32 devices in a mesh: parts: 2 (over x), expert: 16 (over z, y, core).
Axes of the slice: x: 2, y: 2, z: 4, core: 2. Of those that a mesh axis runs over, the one named last changes fastest.
Arguments:
- routes: int32 [4096, 8], P(('parts', 'expert')), parts along dimension 0, may hold values from 0 to 15, all different within a row; in each aligned block of 128 rows (0 to 127, 128 to 255, ...) at most 80 rows name the same one
- probs: float32 [4096, 8], P(('parts', 'expert')), parts along dimension 0, may hold values from 0.05 to 1
- tokens: bfloat16 [4096, 2048], P(('parts', 'expert')), parts along dimension 0, may hold values from -6 to 6
- gate_weight: bfloat16 [16, 2048, 768], P('expert'), may hold values from -0.125 to 0.125
- up_weight: bfloat16 [16, 2048, 768], P('expert'), may hold values from -0.125 to 0.125
- down_weight: bfloat16 [16, 768, 2048], P('expert'), may hold values from -0.21875 to 0.21875
Outputs:
- gram: float32 [32, 768, 768], P(('parts', 'expert')), parts along dimension 0
- mixed: bfloat16 [4096, 2048], P(('parts', 'expert')), parts along dimension 0
The draws below stay inside these ranges and needn't reach their ends.
There are 2 independent parts, one for each index of `parts`. The reference program is written for one: setup_inputs(seed, part) draws one part's arguments, and reference() takes and returns one part's arrays. A program takes and returns all parts, laid end to end along the dimension named above; an argument that names none is the same for every part. Nothing has to cross between parts.
Inputs may be any that keep to these rules, and one draw needn't show every extreme that they name: `routes`: among the rows of one device no expert is named more than 80 times, a bound that some block reaches; every expert is named by some row.
All inputs are finite; a program needn't handle non-finite values.
Results may differ from the reference program's by a relative error of at most 0.006.
Values may be sent and summed in bfloat16 or wider, within the bound.
No kernel may reach another device: no remote copies, remote signals or barrier semaphores. Data moves between devices by JAX's collectives and lax.ppermute only.
A program may use at most 128 MiB of HBM per device.

```python
import math
import jax
import jax.numpy as jnp
import numpy as np
from jax import lax

FW = 768
DW = 2048
TOP = 8
TOK_DEV = 128
EXPERTS = 16
TOKENS = 2048
SLOT = 80
CAP = 512


def block_levels(own_key, shape, split, low, largest):
    gain = 1.0
    for axis_at, parts in split:
        draws = jax.random.uniform(jax.random.fold_in(jax.random.fold_in(own_key, 6), axis_at), (parts,), jnp.float32, low / len(split), largest / len(split))
        gain = gain * jnp.repeat(jnp.exp(draws), shape[axis_at] // parts).reshape((-1,) + (1,) * (len(shape) - 1 - axis_at))
    return gain


def routed_block(own_key, own, number, rows, amount, top, most, lean):
    ranking = jax.random.permutation(own_key, amount)
    packed, ordinary = portions_of(amount, rows * top, most, lean, True), portions_of(amount, rows * top, most, lean, False)
    places = jnp.arange(amount)

    def named(sizes, offset_by):
        used = int((sizes > 0).sum())
        fixed = max(1, used // 4)
        shifted = fixed + (places - fixed + offset_by * (used - fixed)) % max(1, amount - fixed)
        return jnp.zeros((amount,), jnp.int32).at[ranking[jnp.where(places < fixed, places, shifted)]].set(jnp.asarray(sizes, jnp.int32))

    sizes = jnp.where(number % 4 == 0, named(packed, number // 4), named(ordinary, number - number // 4 - 1))
    mixed = jax.random.permutation(jax.random.fold_in(own, 3), amount)
    giver, taker = mixed[0:amount // 2 * 2:2], mixed[1:amount // 2 * 2:2]
    room = jnp.minimum(sizes[giver] - 1, most - sizes[taker]) // 2
    room = jnp.where((giver == ranking[0]) | (taker == ranking[0]) | (sizes[taker] == 0), 0, jnp.maximum(room, 0))
    shifted = jax.random.randint(jax.random.fold_in(own, 4), (amount // 2,), 0, 1 << 20) % (room + 1)
    sizes = sizes.at[giver].add(-shifted).at[taker].add(shifted)
    members = jnp.searchsorted(jnp.cumsum(sizes), jnp.arange(rows * top), side="right").astype(jnp.int32)
    listing = members.reshape(top, rows).T
    listing = listing[jax.random.permutation(jax.random.fold_in(own, 1), rows)]
    offset_by = jax.random.randint(jax.random.fold_in(own, 2), (rows, 1), 0, top)
    return jnp.take_along_axis(listing, (jnp.arange(top)[None, :] + offset_by) % top, axis=1)


def portions_of(amount, total, most, skew, full):
    weights = [(1 << 20) // math.isqrt(standing ** skew) + 1 for standing in range(1, amount + 1)]
    largest = most if full else min(most, max(-(-total // amount), total * weights[0] // sum(weights)))
    least = 1 if total - largest >= amount - 1 else 0
    holding, spare = [largest] + [least] * (amount - 1), total - largest - least * (amount - 1)
    while spare > 0:
        movable = [i for i in range(1, amount) if holding[i] < largest] or [i for i in range(1, amount) if holding[i] < most]
        whole, remaining = sum([weights[i] for i in movable]), spare
        for i in movable:
            addition = min(most - holding[i], max(1, remaining * weights[i] // whole), spare)
            holding[i] = holding[i] + addition
            spare = spare - addition
    return np.array(holding)


def scatter_about(key, shape, spread, reach, split=(), kind=jnp.bfloat16):
    gain = block_levels(key, shape, split, -0.22, 0.18) if split else 1.0
    values = jax.random.normal(key, shape, jnp.float32) * spread * gain
    return jnp.minimum(jnp.maximum(values, -reach), reach).astype(kind)


def setup_inputs(seed: int = 0, part: int = 0) -> dict:
    arg_keys = jax.random.split(jax.random.key(seed), 7)
    own_keys = jax.random.split(jax.random.fold_in(arg_keys[6], part), 7)
    routes_keys = jax.random.split(jax.random.fold_in(own_keys[0], 1), TOKENS // TOK_DEV)
    routes_turns = jax.random.permutation(jax.random.fold_in(own_keys[0], 3), TOKENS // TOK_DEV)
    routes = jax.vmap(lambda own, number: routed_block(jax.random.fold_in(own_keys[0], 2), own, number, TOK_DEV, EXPERTS, TOP, SLOT, 2))(routes_keys, routes_turns).reshape((TOKENS, TOP))
    probs = jnp.clip(0.05 + 0.95 * jax.random.uniform(own_keys[1], (TOKENS, TOP), jnp.float32) ** block_levels(own_keys[1], (TOKENS, TOP), ((0, 16),), -0.2, 0.2), 0.05, 1.0)
    tokens = scatter_about(own_keys[2], (TOKENS, DW), 1.0, 6.0, ((0, 16),))
    gate_weight = scatter_about(arg_keys[3], (EXPERTS, DW, FW), DW ** -0.5, 0.125, ((0, 16),))
    up_weight = scatter_about(arg_keys[4], (EXPERTS, DW, FW), DW ** -0.5, 0.125, ((0, 16),))
    down_weight = scatter_about(arg_keys[5], (EXPERTS, FW, DW), FW ** -0.5, 0.21875, ((0, 16),))
    return dict(routes=routes, probs=probs, tokens=tokens, gate_weight=gate_weight, up_weight=up_weight, down_weight=down_weight)


def reference(routes, probs, tokens, gate_weight, up_weight, down_weight):
    pairs = TOKENS * TOP
    flat_routes = routes.reshape(pairs).astype(jnp.int32)
    onehot = (flat_routes[:, None] == jnp.arange(EXPERTS, dtype=jnp.int32)[None, :]).astype(jnp.int32)
    rank = jnp.sum((jnp.cumsum(onehot, axis=0) - onehot) * onehot, axis=1).astype(jnp.int32)
    kept = rank < CAP
    count = jnp.sum(onehot * kept[:, None].astype(jnp.int32), axis=0).astype(jnp.int32)
    target = jnp.where(kept, rank, CAP).astype(jnp.int32)
    table = jnp.zeros((EXPERTS, CAP), jnp.int32).at[flat_routes, target].set(
        jnp.arange(pairs, dtype=jnp.int32), mode="drop")
    valid = jnp.arange(CAP, dtype=jnp.int32)[None, :] < count[:, None]

    def one_expert(packet):
        rows_index, live, w_gate, w_up, w_down, number = packet
        token_index = (rows_index // TOP).astype(jnp.int32)
        rows = jnp.where(live[:, None], tokens[token_index], jnp.zeros((), tokens.dtype))
        gate = jnp.dot(rows, w_gate, preferred_element_type=jnp.float32)
        up = jnp.dot(rows, w_up, preferred_element_type=jnp.float32)
        act = (jax.nn.silu(gate) * up).astype(jnp.bfloat16)
        square = lax.dot_general(act, act, (((0,), (0,)), ((), ())), preferred_element_type=jnp.float32)
        square = square * (2.0 / number.astype(jnp.float32))
        result = jnp.dot(act, w_down, preferred_element_type=jnp.float32).astype(jnp.bfloat16)
        return square, result

    grams, outputs = lax.map(one_expert, (table, valid, gate_weight, up_weight, down_weight, count))
    picked = outputs[flat_routes, jnp.minimum(rank, CAP - 1)]
    picked = jnp.where(kept[:, None], picked, jnp.zeros((), picked.dtype))
    mixed = jnp.sum(picked.reshape(TOKENS, TOP, DW).astype(jnp.float32) * probs[:, :, None], axis=1)
    return grams, mixed.astype(jnp.bfloat16)
```

```python
import jax
import jax.numpy as jnp
from jax import lax
from jax.sharding import PartitionSpec as P


def gram_of(rows):
    return lax.dot_general(rows, rows, (((0,), (0,)), ((), ())), preferred_element_type=jnp.float32)


def expert_pass(rows, w_gate, w_up, w_down):
    gate = jnp.dot(rows, w_gate, preferred_element_type=jnp.float32)
    up = jnp.dot(rows, w_up, preferred_element_type=jnp.float32)
    act = (jax.nn.silu(gate) * up).astype(jnp.bfloat16)
    gram_sum = gram_of(act)
    made = jnp.dot(act, w_down, preferred_element_type=jnp.float32).astype(jnp.bfloat16)
    return (gram_sum, made)


def small_gather(part, axis):
    size = lax.axis_size(axis)
    copies = jnp.broadcast_to(part[None], (size,) + part.shape)
    return lax.all_to_all(copies, axis, split_axis=0, concat_axis=0, tiled=True)


def shards(routes, probs, tokens, gate_weight, up_weight, down_weight):
    tok_rows, top = routes.shape
    ranks_total = lax.axis_size("expert")
    capacity = tok_rows * top // 2
    expert = lax.axis_index("expert")
    every_token = lax.all_gather(tokens, "expert", tiled=True)
    every_route = small_gather(routes, "expert")
    every_prob = small_gather(probs, "expert")
    names = every_route == expert
    named = jnp.any(names, axis=2).astype(jnp.int32)
    weight = jnp.sum(jnp.where(names, every_prob, 0.0), axis=2).reshape(ranks_total * tok_rows)
    within = jnp.cumsum(named, axis=1) - named
    per_device = jnp.sum(named, axis=1)
    before = jnp.cumsum(per_device) - per_device
    rank = within + before[:, None]
    kept = (named == 1) & (rank < capacity)
    count = jnp.minimum(jnp.sum(per_device), capacity)
    slot = jnp.where(kept, rank, -1).reshape(ranks_total * tok_rows)
    place = jnp.arange(capacity, dtype=jnp.int32)
    select = (place[:, None] == slot[None, :]).astype(jnp.bfloat16)
    rows = jnp.dot(select, every_token, preferred_element_type=jnp.float32).astype(jnp.bfloat16)
    gram_sum, made = expert_pass(rows, gate_weight[0], up_weight[0], down_weight[0])
    gram = gram_sum * (2.0 / count.astype(jnp.float32))
    spread = lax.dot_general(
        select, made, (((0,), (0,)), ((), ())), preferred_element_type=jnp.float32
    )
    partial = (spread * weight[:, None]).astype(jnp.bfloat16)
    mixed = lax.psum_scatter(partial, "expert", scatter_dimension=0, tiled=True)
    return (gram[None], mixed.astype(jnp.bfloat16))


def solution(mesh):
    placed = (
        P(("parts", "expert"), None),
        P(("parts", "expert"), None),
        P(("parts", "expert"), None),
        P("expert", None, None),
        P("expert", None, None),
        P("expert", None, None),
    )
    return jax.shard_map(
        shards,
        mesh=mesh,
        in_specs=placed,
        out_specs=(P(("parts", "expert"), None, None), P(("parts", "expert"), None)),
        check_vma=False,
    )
```

```python
import functools

import jax
import jax.numpy as jnp
from jax import lax
from jax.experimental import pallas as pl
from jax.experimental.pallas import tpu as pltpu
from jax.sharding import PartitionSpec as P


def gram_of(rows):
    return lax.dot_general(rows, rows, (((0,), (0,)), ((), ())), preferred_element_type=jnp.float32)


def expert_pass(rows, w_gate, w_up, w_down):
    gate = jnp.dot(rows, w_gate, preferred_element_type=jnp.float32)
    up = jnp.dot(rows, w_up, preferred_element_type=jnp.float32)
    act = (jax.nn.silu(gate) * up).astype(jnp.bfloat16)
    gram_sum = gram_of(act)
    made = jnp.dot(act, w_down, preferred_element_type=jnp.float32).astype(jnp.bfloat16)
    return (gram_sum, made)


def weights_for_me(routes, probs, experts):
    names = routes.T[None, :, :] == jnp.arange(experts, dtype=jnp.int32)[:, None, None]
    weight = jnp.sum(jnp.where(names, probs.T[None, :, :], 0.0), axis=1)
    mine = jnp.where(jnp.any(names, axis=1), weight, -1.0)
    return lax.all_to_all(mine, "expert", split_axis=0, concat_axis=0, tiled=True)


def summed(*parts):
    total = parts[0].astype(jnp.float32)
    for part in parts[1:]:
        total = total + part.astype(jnp.float32)
    return total.astype(jnp.bfloat16)


def plane_kernel(
    capacity, order, weight, x0, x1, x2, x3, w_gate, w_up, w_down,
    keep, give, act,
    x, rows, made, ranks, gates, ups, downs, x_sem, gate_sem, up_sem, down_sem,
):
    blocks, tok = weight.shape
    features = x.shape[1]
    hidden = act.shape[1]
    slots = act.shape[0]
    wide = 256
    copies = [
        pltpu.make_async_copy(block, x.at[pl.ds(i * tok, tok), :], x_sem.at[i])
        for i, block in enumerate((x0, x1, x2, x3))
    ]
    for copy in copies:
        copy.start()
    gate_copies, up_copies = [], []
    for i in range(hidden // wide):
        span = pl.ds(i * wide, wide)
        gate_copies.append(pltpu.make_async_copy(w_gate.at[:, span], gates.at[i], gate_sem.at[i]))
        up_copies.append(pltpu.make_async_copy(w_up.at[:, span], ups.at[i], up_sem.at[i]))
        gate_copies[i].start()
        up_copies[i].start()
    down_copy = pltpu.make_async_copy(w_down, downs, down_sem)
    down_copy.start()

    named = (weight[...] >= 0.0).astype(jnp.float32)
    lane = lax.broadcasted_iota(jnp.int32, (tok, tok), 0)
    below = (lane < lax.broadcasted_iota(jnp.int32, (tok, tok), 1)).astype(jnp.float32)
    within = jnp.dot(named, below, preferred_element_type=jnp.float32)
    totals = jnp.broadcast_to(jnp.sum(named, axis=1, keepdims=True), (blocks, tok))
    row = lax.broadcasted_iota(jnp.int32, (blocks, blocks), 0)
    earlier = (lax.broadcasted_iota(jnp.int32, (blocks, blocks), 1) < row).astype(jnp.float32)
    before = jnp.dot(earlier, totals, preferred_element_type=jnp.float32)
    rank = within + before
    kept = (named > 0.0) & (rank < capacity)
    first = order[0] // 4 * 4
    block_row = lax.broadcasted_iota(jnp.int32, (blocks, tok), 0)
    start = jnp.sum(jnp.where(block_row == first, before, 0.0), axis=0, keepdims=True)
    ranks[...] = jnp.where(kept, rank - start, -1.0)

    places = [ranks[pl.ds(order[i], 1), :] for i in range(4)]
    shares = [weight[pl.ds(order[i], 1), :] for i in range(4)]
    place = jnp.concatenate(places, axis=1)
    share = jnp.concatenate(shares, axis=1)
    slot = lax.broadcasted_iota(jnp.int32, (slots, 4 * tok), 0).astype(jnp.float32)
    hits = slot == place
    scale = jnp.sum(jnp.where(hits, share, 0.0), axis=1, keepdims=True)
    select = hits.astype(jnp.float32).astype(jnp.bfloat16)
    for copy in copies:
        copy.wait()
    for i in range(features // 512):
        span = pl.ds(i * 512, 512)
        rows[:, span] = jnp.dot(
            select, x[:, span], preferred_element_type=jnp.float32
        ).astype(jnp.bfloat16)
    for i in range(hidden // wide):
        gate_copies[i].wait()
        up_copies[i].wait()
        gate = jnp.dot(rows[...], gates[i], preferred_element_type=jnp.float32)
        up = jnp.dot(rows[...], ups[i], preferred_element_type=jnp.float32)
        act[:, pl.ds(i * wide, wide)] = (gate / (1.0 + jnp.exp(-gate)) * up).astype(jnp.bfloat16)
    down_copy.wait()
    back = select.T
    for i in range(features // 512):
        span = pl.ds(i * 512, 512)
        result = jnp.dot(act[...], downs[:, span], preferred_element_type=jnp.float32)
        made[...] = (result * scale).astype(jnp.bfloat16)
        spread = jnp.dot(back, made[...], preferred_element_type=jnp.float32).astype(jnp.bfloat16)
        keep[:, span] = spread[: 2 * tok]
        give[:, span] = spread[2 * tok :]


def plane_pass(order, weight, xs, w_gate, w_up, w_down, slots, capacity):
    tok, features = xs[0].shape
    hidden = w_gate.shape[1]
    half = jax.ShapeDtypeStruct((2 * tok, features), jnp.bfloat16)
    rows = 4 * slots
    flops = 2 * rows * (3 * features * hidden + 8 * tok * features)
    moved = 2 * (3 * features * hidden + 8 * tok * features)
    return pl.pallas_call(
        functools.partial(plane_kernel, capacity),
        out_shape=(half, half, jax.ShapeDtypeStruct((rows, hidden), jnp.bfloat16)),
        in_specs=[pl.BlockSpec(memory_space=pltpu.SMEM), pl.BlockSpec(memory_space=pltpu.VMEM)]
        + [pl.BlockSpec(memory_space=pl.ANY)] * 7,
        out_specs=[pl.BlockSpec(memory_space=pltpu.VMEM)] * 3,
        scratch_shapes=[
            pltpu.VMEM((4 * tok, features), jnp.bfloat16),
            pltpu.VMEM((rows, features), jnp.bfloat16),
            pltpu.VMEM((rows, 512), jnp.bfloat16),
            pltpu.VMEM(weight.shape, jnp.float32),
            pltpu.VMEM((hidden // 256, features, 256), jnp.bfloat16),
            pltpu.VMEM((hidden // 256, features, 256), jnp.bfloat16),
            pltpu.VMEM((hidden, features), jnp.bfloat16),
            pltpu.SemaphoreType.DMA((4,)),
            pltpu.SemaphoreType.DMA((hidden // 256,)),
            pltpu.SemaphoreType.DMA((hidden // 256,)),
            pltpu.SemaphoreType.DMA,
        ],
        compiler_params=pltpu.CompilerParams(vmem_limit_bytes=32 * 1024 * 1024),
        cost_estimate=pl.CostEstimate(
            flops=flops, bytes_accessed=moved, transcendentals=rows * hidden
        ),
    )(order, weight, *xs, w_gate, w_up, w_down)


def pairs_of(size, planes, step):
    found = []
    for device in range(size):
        z, y, core = device // 4, device // 2 % 2, device % 2
        if z in planes:
            z, y, core = step(z, y, core)
            found.append((device, (z * 2 + y) * 2 + core))
    return found


def staged(routes, probs, tokens, w_gate, w_up, w_down):
    tok, top = routes.shape
    size = lax.axis_size("expert")
    slots = 5 * tok * top // (4 * size)
    capacity = tok * top // 2
    me = lax.axis_index("expert")
    z, y, core = me // 4, me // 2 % 2, me % 2
    middle = (z == 1) | (z == 2)
    every = (0, 1, 2, 3)

    def moved(array, planes, step):
        return lax.ppermute(array, "expert", pairs_of(size, planes, step))

    def pair(z, y, core):
        return z ^ 1, y, core

    def across(z, y, core):
        return 3 - z, y, core

    def column(z, y, core):
        return z, 1 - y, core

    def sibling(z, y, core):
        return z, y, 1 - core

    weight = weights_for_me(routes, probs, size)

    held_1 = moved(tokens, every, pair)
    crossed = moved(tokens, (1, 2), across)
    outward = moved(crossed, (1, 2), pair)
    far_mid = moved(held_1, (1, 2), across)
    far_end = moved(far_mid, (1, 2), pair)
    held = [
        tokens,
        held_1,
        jnp.where(middle, crossed, outward),
        jnp.where(middle, far_mid, far_end),
    ]
    planes = [z, z ^ 1, jnp.where(middle, 3 - z, (3 - z) ^ 1), jnp.where(middle, (3 - z) ^ 1, 3 - z)]
    keeps, gives, acts = [], [], []
    for mine, plane in zip(held, planes):
        other = moved(mine, every, column)
        xs = (mine, other, moved(mine, every, sibling), moved(other, every, sibling))
        base = plane * 4
        order = jnp.stack(
            [
                base + y * 2 + core,
                base + (1 - y) * 2 + core,
                base + y * 2 + 1 - core,
                base + (1 - y) * 2 + 1 - core,
            ]
        ).astype(jnp.int32)
        keep, give, act = plane_pass(order, weight, xs, w_gate, w_up, w_down, slots, capacity)
        keeps.append(keep)
        gives.append(give)
        acts.append(act)

    reduced = [None] * 4
    for k in (3, 2, 1, 0):
        came = moved(gives[k], every, sibling)
        send = summed(keeps[k][tok:], came[tok:])
        crossed = moved(send, every, column)
        reduced[k] = (keeps[k][:tok], came[:tok], crossed)
    far_in = moved(summed(*reduced[3]), (0, 3), pair)
    far_across = moved(summed(*reduced[3], far_in), (1, 2), across)
    near_in = moved(summed(*reduced[2]), (0, 3), pair)
    near_across = moved(summed(*reduced[2], near_in), (1, 2), across)
    last = moved(summed(*reduced[1], far_across), every, pair)
    mixed = summed(*reduced[0], last, near_across)

    count = jnp.minimum(jnp.sum((weight >= 0.0).astype(jnp.float32)), float(capacity))
    gram = gram_of(jnp.concatenate(acts, axis=0)) * (2.0 / count)
    return gram[None], mixed


def gathered(routes, probs, tokens, w_gate, w_up, w_down):
    tok_rows, top = routes.shape
    size = lax.axis_size("expert")
    capacity = tok_rows * top // 2
    every_token = lax.all_gather(tokens, "expert", tiled=True)
    weight = weights_for_me(routes, probs, size)
    named = (weight >= 0.0).astype(jnp.int32)
    within = jnp.cumsum(named, axis=1) - named
    per_device = jnp.sum(named, axis=1)
    before = jnp.cumsum(per_device) - per_device
    rank = within + before[:, None]
    kept = (named == 1) & (rank < capacity)
    count = jnp.minimum(jnp.sum(per_device), capacity)
    slot = jnp.where(kept, rank, -1).reshape(size * tok_rows)
    place = jnp.arange(capacity, dtype=jnp.int32)
    select = (place[:, None] == slot[None, :]).astype(jnp.bfloat16)
    rows = jnp.dot(select, every_token, preferred_element_type=jnp.float32).astype(jnp.bfloat16)
    gram_sum, made = expert_pass(rows, w_gate, w_up, w_down)
    gram = gram_sum * (2.0 / count.astype(jnp.float32))
    spread = lax.dot_general(
        select, made, (((0,), (0,)), ((), ())), preferred_element_type=jnp.float32
    )
    partial = (spread * weight.reshape(size * tok_rows, 1)).astype(jnp.bfloat16)
    mixed = lax.psum_scatter(partial, "expert", scatter_dimension=0, tiled=True)
    return gram[None], mixed.astype(jnp.bfloat16)


def shards(routes, probs, tokens, gate_weight, up_weight, down_weight):
    body = staged if lax.axis_size("expert") == 16 else gathered
    return body(routes, probs, tokens, gate_weight[0], up_weight[0], down_weight[0])


def solution(mesh):
    placed = (
        P(("parts", "expert"), None),
        P(("parts", "expert"), None),
        P(("parts", "expert"), None),
        P("expert", None, None),
        P("expert", None, None),
        P("expert", None, None),
    )
    return jax.shard_map(
        shards,
        mesh=mesh,
        in_specs=placed,
        out_specs=(P(("parts", "expert"), None, None), P(("parts", "expert"), None)),
        check_vma=False,
    )
```

```python
import functools

import jax
import jax.numpy as jnp
from jax import lax
from jax.experimental import pallas as pl
from jax.experimental.pallas import tpu as pltpu
from jax.sharding import PartitionSpec as P


def gram_of(rows):
    return lax.dot_general(rows, rows, (((0,), (0,)), ((), ())), preferred_element_type=jnp.float32)


def expert_pass(rows, w_gate, w_up, w_down):
    gate = jnp.dot(rows, w_gate, preferred_element_type=jnp.float32)
    up = jnp.dot(rows, w_up, preferred_element_type=jnp.float32)
    act = (jax.nn.silu(gate) * up).astype(jnp.bfloat16)
    gram_sum = gram_of(act)
    made = jnp.dot(act, w_down, preferred_element_type=jnp.float32).astype(jnp.bfloat16)
    return (gram_sum, made)


def weights_for_me(routes, probs, experts):
    names = routes.T[None, :, :] == jnp.arange(experts, dtype=jnp.int32)[:, None, None]
    weight = jnp.sum(jnp.where(names, probs.T[None, :, :], 0.0), axis=1)
    mine = jnp.where(jnp.any(names, axis=1), weight, -1.0)
    return lax.all_to_all(mine, "expert", split_axis=0, concat_axis=0, tiled=True)


def summed(*parts):
    total = parts[0].astype(jnp.float32)
    for part in parts[1:]:
        total = total + part.astype(jnp.float32)
    return total.astype(jnp.bfloat16)


def plane_kernel(
    capacity, order, weight, x0, x1, x2, x3, w_gate, w_up, w_down,
    keep, give, act,
    x, rows, made, ranks, gates, ups, downs, x_sem, gate_sem, up_sem, down_sem,
):
    blocks, tok = weight.shape
    features = x.shape[1]
    hidden = act.shape[1]
    slots = act.shape[0]
    wide = 256
    copies = [
        pltpu.make_async_copy(block, x.at[pl.ds(i * tok, tok), :], x_sem.at[i])
        for i, block in enumerate((x0, x1, x2, x3))
    ]
    for copy in copies:
        copy.start()
    gate_copies, up_copies = [], []
    for i in range(hidden // wide):
        span = pl.ds(i * wide, wide)
        gate_copies.append(pltpu.make_async_copy(w_gate.at[:, span], gates.at[i], gate_sem.at[i]))
        up_copies.append(pltpu.make_async_copy(w_up.at[:, span], ups.at[i], up_sem.at[i]))
        gate_copies[i].start()
        up_copies[i].start()
    down_copy = pltpu.make_async_copy(w_down, downs, down_sem)
    down_copy.start()

    named = (weight[...] >= 0.0).astype(jnp.float32)
    lane = lax.broadcasted_iota(jnp.int32, (tok, tok), 0)
    below = (lane < lax.broadcasted_iota(jnp.int32, (tok, tok), 1)).astype(jnp.float32)
    within = jnp.dot(named, below, preferred_element_type=jnp.float32)
    totals = jnp.broadcast_to(jnp.sum(named, axis=1, keepdims=True), (blocks, tok))
    row = lax.broadcasted_iota(jnp.int32, (blocks, blocks), 0)
    earlier = (lax.broadcasted_iota(jnp.int32, (blocks, blocks), 1) < row).astype(jnp.float32)
    before = jnp.dot(earlier, totals, preferred_element_type=jnp.float32)
    rank = within + before
    kept = (named > 0.0) & (rank < capacity)
    first = order[0] // 4 * 4
    block_row = lax.broadcasted_iota(jnp.int32, (blocks, tok), 0)
    start = jnp.sum(jnp.where(block_row == first, before, 0.0), axis=0, keepdims=True)
    ranks[...] = jnp.where(kept, rank - start, -1.0)

    places = [ranks[pl.ds(order[i], 1), :] for i in range(4)]
    shares = [weight[pl.ds(order[i], 1), :] for i in range(4)]
    place = jnp.concatenate(places, axis=1)
    share = jnp.concatenate(shares, axis=1)
    slot = lax.broadcasted_iota(jnp.int32, (slots, 4 * tok), 0).astype(jnp.float32)
    hits = slot == place
    scale = jnp.sum(jnp.where(hits, share, 0.0), axis=1, keepdims=True)
    select = hits.astype(jnp.float32).astype(jnp.bfloat16)
    for copy in copies:
        copy.wait()
    for i in range(features // 512):
        span = pl.ds(i * 512, 512)
        rows[:, span] = jnp.dot(
            select, x[:, span], preferred_element_type=jnp.float32
        ).astype(jnp.bfloat16)
    for i in range(hidden // wide):
        gate_copies[i].wait()
        up_copies[i].wait()
        gate = jnp.dot(rows[...], gates[i], preferred_element_type=jnp.float32)
        up = jnp.dot(rows[...], ups[i], preferred_element_type=jnp.float32)
        act[:, pl.ds(i * wide, wide)] = (gate / (1.0 + jnp.exp(-gate)) * up).astype(jnp.bfloat16)
    down_copy.wait()
    back = select.T
    for i in range(features // 512):
        span = pl.ds(i * 512, 512)
        result = jnp.dot(act[...], downs[:, span], preferred_element_type=jnp.float32)
        made[...] = (result * scale).astype(jnp.bfloat16)
        spread = jnp.dot(back, made[...], preferred_element_type=jnp.float32).astype(jnp.bfloat16)
        keep[:, span] = spread[: 2 * tok]
        give[:, span] = spread[2 * tok :]


def plane_pass(order, weight, xs, w_gate, w_up, w_down, slots, capacity):
    tok, features = xs[0].shape
    hidden = w_gate.shape[1]
    half = jax.ShapeDtypeStruct((2 * tok, features), jnp.bfloat16)
    rows = 4 * slots
    flops = 2 * rows * (3 * features * hidden + 8 * tok * features)
    moved = 2 * (3 * features * hidden + 8 * tok * features)
    return pl.pallas_call(
        functools.partial(plane_kernel, capacity),
        out_shape=(half, half, jax.ShapeDtypeStruct((rows, hidden), jnp.bfloat16)),
        in_specs=[pl.BlockSpec(memory_space=pltpu.SMEM), pl.BlockSpec(memory_space=pltpu.VMEM)]
        + [pl.BlockSpec(memory_space=pl.ANY)] * 4
        + [pl.BlockSpec(memory_space=pltpu.HBM)] * 3,
        out_specs=[pl.BlockSpec(memory_space=pltpu.VMEM)] * 3,
        scratch_shapes=[
            pltpu.VMEM((4 * tok, features), jnp.bfloat16),
            pltpu.VMEM((rows, features), jnp.bfloat16),
            pltpu.VMEM((rows, 512), jnp.bfloat16),
            pltpu.VMEM(weight.shape, jnp.float32),
            pltpu.VMEM((hidden // 256, features, 256), jnp.bfloat16),
            pltpu.VMEM((hidden // 256, features, 256), jnp.bfloat16),
            pltpu.VMEM((hidden, features), jnp.bfloat16),
            pltpu.SemaphoreType.DMA((4,)),
            pltpu.SemaphoreType.DMA((hidden // 256,)),
            pltpu.SemaphoreType.DMA((hidden // 256,)),
            pltpu.SemaphoreType.DMA,
        ],
        compiler_params=pltpu.CompilerParams(vmem_limit_bytes=32 * 1024 * 1024),
        cost_estimate=pl.CostEstimate(
            flops=flops, bytes_accessed=moved, transcendentals=rows * hidden
        ),
    )(order, weight, *xs, w_gate, w_up, w_down)


def pairs_of(size, planes, step):
    found = []
    for device in range(size):
        z, y, core = device // 4, device // 2 % 2, device % 2
        if z in planes:
            z, y, core = step(z, y, core)
            found.append((device, (z * 2 + y) * 2 + core))
    return found


def staged(routes, probs, tokens, w_gate, w_up, w_down):
    tok, top = routes.shape
    size = lax.axis_size("expert")
    slots = 5 * tok * top // (4 * size)
    capacity = tok * top // 2
    me = lax.axis_index("expert")
    z, y, core = me // 4, me // 2 % 2, me % 2
    middle = (z == 1) | (z == 2)
    every = (0, 1, 2, 3)

    def moved(array, planes, step):
        return lax.ppermute(array, "expert", pairs_of(size, planes, step))

    def pair(z, y, core):
        return z ^ 1, y, core

    def across(z, y, core):
        return 3 - z, y, core

    def column(z, y, core):
        return z, 1 - y, core

    def sibling(z, y, core):
        return z, y, 1 - core

    def together(*arrays):
        return lax.optimization_barrier(arrays)

    def sources(plane):
        base = plane * 4
        return jnp.stack(
            [
                base + y * 2 + core,
                base + (1 - y) * 2 + core,
                base + y * 2 + 1 - core,
                base + (1 - y) * 2 + 1 - core,
            ]
        ).astype(jnp.int32)

    def expert(plane, *xs):
        return plane_pass(sources(plane), weight, xs, w_gate, w_up, w_down, slots, capacity)

    weight = weights_for_me(routes, probs, size)
    a0, a1, crossed, b0, c0, weight = together(
        tokens,
        moved(tokens, every, pair),
        moved(tokens, (1, 2), across),
        moved(tokens, every, column),
        moved(tokens, every, sibling),
        weight,
    )
    outward = moved(crossed, (1, 2), pair)
    far_mid = moved(a1, (1, 2), across)
    crossed, outward, far_mid, b1, d0, c1 = together(
        crossed,
        outward,
        far_mid,
        moved(a1, every, column),
        moved(b0, every, sibling),
        moved(a1, every, sibling),
    )
    a2 = jnp.where(middle, crossed, outward)
    far_end = moved(far_mid, (1, 2), pair)
    keep0, give0, act0 = expert(z, a0, b0, c0, d0)
    far_mid, far_end, b2, d1, c2, keep0, give0, act0 = together(
        far_mid,
        far_end,
        moved(a2, every, column),
        moved(b1, every, sibling),
        moved(a2, every, sibling),
        keep0,
        give0,
        act0,
    )
    a3 = jnp.where(middle, far_mid, far_end)
    keep1, give1, act1 = expert(z ^ 1, a1, b1, c1, d1)
    b3, d2, c3, got0, keep1, give1, act1 = together(
        moved(a3, every, column),
        moved(b2, every, sibling),
        moved(a3, every, sibling),
        moved(give0, every, sibling),
        keep1,
        give1,
        act1,
    )
    near = jnp.where(middle, 3 - z, (3 - z) ^ 1)
    keep2, give2, act2 = expert(near, a2, b2, c2, d2)
    d3, got1, keep2, give2, act2 = together(
        moved(b3, every, sibling), moved(give1, every, sibling), keep2, give2, act2
    )
    keep3, give3, act3 = expert(near ^ 1, a3, b3, c3, d3)

    def sent(keep, got):
        return moved(summed(keep[tok:], got[tok:]), every, column)

    keep3, give3, act3, got2 = together(keep3, give3, act3, moved(give2, every, sibling))
    got3 = moved(give3, every, sibling)
    came3, got3 = together(sent(keep3, got3), got3)
    sum3 = summed(keep3[:tok], got3[:tok], came3)
    sum3, far_in, came2 = together(sum3, moved(sum3, (0, 3), pair), sent(keep2, got2))
    sum2 = summed(keep2[:tok], got2[:tok], came2)
    sum2, far_across, near_in, came1 = together(
        sum2,
        moved(summed(sum3, far_in), (1, 2), across),
        moved(sum2, (0, 3), pair),
        sent(keep1, got1),
    )
    near_across = moved(summed(sum2, near_in), (1, 2), across)
    last = moved(summed(keep1[:tok], got1[:tok], came1, far_across), every, pair)
    mixed = summed(keep0[:tok], got0[:tok], sent(keep0, got0), last, near_across)

    acts = jnp.concatenate([act0, act1, act2, act3], axis=0)
    count = jnp.minimum(jnp.sum((weight >= 0.0).astype(jnp.float32)), float(capacity))
    gram = gram_of(acts) * (2.0 / count)
    return gram[None], mixed


def gathered(routes, probs, tokens, w_gate, w_up, w_down):
    tok_rows, top = routes.shape
    size = lax.axis_size("expert")
    capacity = tok_rows * top // 2
    every_token = lax.all_gather(tokens, "expert", tiled=True)
    weight = weights_for_me(routes, probs, size)
    named = (weight >= 0.0).astype(jnp.int32)
    within = jnp.cumsum(named, axis=1) - named
    per_device = jnp.sum(named, axis=1)
    before = jnp.cumsum(per_device) - per_device
    rank = within + before[:, None]
    kept = (named == 1) & (rank < capacity)
    count = jnp.minimum(jnp.sum(per_device), capacity)
    slot = jnp.where(kept, rank, -1).reshape(size * tok_rows)
    place = jnp.arange(capacity, dtype=jnp.int32)
    select = (place[:, None] == slot[None, :]).astype(jnp.bfloat16)
    rows = jnp.dot(select, every_token, preferred_element_type=jnp.float32).astype(jnp.bfloat16)
    gram_sum, made = expert_pass(rows, w_gate, w_up, w_down)
    gram = gram_sum * (2.0 / count.astype(jnp.float32))
    spread = lax.dot_general(
        select, made, (((0,), (0,)), ((), ())), preferred_element_type=jnp.float32
    )
    partial = (spread * weight.reshape(size * tok_rows, 1)).astype(jnp.bfloat16)
    mixed = lax.psum_scatter(partial, "expert", scatter_dimension=0, tiled=True)
    return gram[None], mixed.astype(jnp.bfloat16)


def shards(routes, probs, tokens, gate_weight, up_weight, down_weight):
    body = staged if lax.axis_size("expert") == 16 else gathered
    return body(routes, probs, tokens, gate_weight[0], up_weight[0], down_weight[0])


def solution(mesh):
    placed = (
        P(("parts", "expert"), None),
        P(("parts", "expert"), None),
        P(("parts", "expert"), None),
        P("expert", None, None),
        P("expert", None, None),
        P("expert", None, None),
    )
    return jax.shard_map(
        shards,
        mesh=mesh,
        in_specs=placed,
        out_specs=(P(("parts", "expert"), None, None), P(("parts", "expert"), None)),
        check_vma=False,
    )
```

```python
import jax
import jax.numpy as jnp
from jax import lax
from jax.sharding import PartitionSpec as P


def gram_of(rows):
    return lax.dot_general(rows, rows, (((0,), (0,)), ((), ())), preferred_element_type=jnp.float32)


def expert_pass(rows, w_gate, w_up, w_down):
    gate = jnp.dot(rows, w_gate, preferred_element_type=jnp.float32)
    up = jnp.dot(rows, w_up, preferred_element_type=jnp.float32)
    act = (jax.nn.silu(gate) * up).astype(jnp.bfloat16)
    gram_sum = gram_of(act)
    made = jnp.dot(act, w_down, preferred_element_type=jnp.float32).astype(jnp.bfloat16)
    return (gram_sum, made)


def weights_for_me(routes, probs, experts):
    names = routes.T[None, :, :] == jnp.arange(experts, dtype=jnp.int32)[:, None, None]
    weight = jnp.sum(jnp.where(names, probs.T[None, :, :], 0.0), axis=1)
    mine = jnp.where(jnp.any(names, axis=1), weight, -1.0)
    return lax.all_to_all(mine, "expert", split_axis=0, concat_axis=0, tiled=True)


def shards(routes, probs, tokens, gate_weight, up_weight, down_weight):
    tok_rows, top = routes.shape
    features = tokens.shape[1]
    size = lax.axis_size("expert")
    capacity = tok_rows * top // 2
    core = lax.axis_index("expert") % 2
    groups = [list(range(core, size, 2)) for core in range(2)]
    swap = [(i, i ^ 1) for i in range(size)]

    weight = weights_for_me(routes, probs, size)
    near = lax.all_gather(tokens, "expert", axis_index_groups=groups, tiled=True)
    far = lax.ppermute(near, "expert", swap)

    named = (weight >= 0.0).astype(jnp.int32)
    within = jnp.cumsum(named, axis=1) - named
    per_device = jnp.sum(named, axis=1)
    before = jnp.cumsum(per_device) - per_device
    rank = within + before[:, None]
    kept = (named == 1) & (rank < capacity)
    count = jnp.minimum(jnp.sum(per_device), capacity)
    slot = jnp.where(kept, rank, -1).reshape(size // 2, 2, tok_rows)
    place = jnp.arange(capacity, dtype=jnp.int32)

    def select_of(which):
        own = lax.dynamic_index_in_dim(slot, which, 1, False).reshape(size // 2 * tok_rows)
        return (place[:, None] == own[None, :]).astype(jnp.bfloat16)

    def spread_of(select, which):
        share = lax.dynamic_index_in_dim(
            weight.reshape(size // 2, 2, tok_rows), which, 1, False
        ).reshape(size // 2 * tok_rows, 1)
        spread = lax.dot_general(
            select, made, (((0,), (0,)), ((), ())), preferred_element_type=jnp.float32
        )
        return (spread * share).astype(jnp.bfloat16)

    near_select, far_select = select_of(core), select_of(1 - core)
    near_rows = jnp.dot(near_select, near, preferred_element_type=jnp.float32)
    rows = near_rows + jnp.dot(far_select, far, preferred_element_type=jnp.float32)
    rows = rows.astype(jnp.bfloat16)
    gram_sum, made = expert_pass(rows, gate_weight[0], up_weight[0], down_weight[0])
    gram = gram_sum * (2.0 / count.astype(jnp.float32))
    came = lax.ppermute(spread_of(far_select, 1 - core), "expert", swap)
    partial = spread_of(near_select, core).astype(jnp.float32) + came.astype(jnp.float32)
    mixed = lax.psum_scatter(
        partial.astype(jnp.bfloat16),
        "expert",
        scatter_dimension=0,
        axis_index_groups=groups,
        tiled=True,
    )
    return (gram[None], mixed)


def solution(mesh):
    placed = (
        P(("parts", "expert"), None),
        P(("parts", "expert"), None),
        P(("parts", "expert"), None),
        P("expert", None, None),
        P("expert", None, None),
        P("expert", None, None),
    )
    return jax.shard_map(
        shards,
        mesh=mesh,
        in_specs=placed,
        out_specs=(P(("parts", "expert"), None, None), P(("parts", "expert"), None)),
        check_vma=False,
    )
```

```python
import functools

import jax
import jax.numpy as jnp
from jax import lax
from jax.experimental import pallas as pl
from jax.experimental.pallas import tpu as pltpu
from jax.sharding import PartitionSpec as P


def gram_of(rows):
    return lax.dot_general(rows, rows, (((0,), (0,)), ((), ())), preferred_element_type=jnp.float32)


def expert_pass(rows, w_gate, w_up, w_down):
    gate = jnp.dot(rows, w_gate, preferred_element_type=jnp.float32)
    up = jnp.dot(rows, w_up, preferred_element_type=jnp.float32)
    act = (jax.nn.silu(gate) * up).astype(jnp.bfloat16)
    gram_sum = gram_of(act)
    made = jnp.dot(act, w_down, preferred_element_type=jnp.float32).astype(jnp.bfloat16)
    return (gram_sum, made)


def weights_for_me(routes, probs, experts):
    names = routes.T[None, :, :] == jnp.arange(experts, dtype=jnp.int32)[:, None, None]
    weight = jnp.sum(jnp.where(names, probs.T[None, :, :], 0.0), axis=1)
    mine = jnp.where(jnp.any(names, axis=1), weight, -1.0)
    return lax.all_to_all(mine, "expert", split_axis=0, concat_axis=0, tiled=True)


def summed(*parts):
    total = parts[0].astype(jnp.float32)
    for part in parts[1:]:
        total = total + part.astype(jnp.float32)
    return total.astype(jnp.bfloat16)


def plane_kernel(
    capacity, order, weight, x0, x1, x2, x3, w_gate, w_up, w_down, keep, give, act, rows, ranks
):
    blocks, tok = weight.shape
    features = x0.shape[1]
    slots, hidden = act.shape
    wide = 256
    named = (weight[...] >= 0.0).astype(jnp.float32)
    lane = lax.broadcasted_iota(jnp.int32, (tok, tok), 0)
    below = (lane < lax.broadcasted_iota(jnp.int32, (tok, tok), 1)).astype(jnp.float32)
    within = jnp.dot(named, below, preferred_element_type=jnp.float32)
    totals = jnp.broadcast_to(jnp.sum(named, axis=1, keepdims=True), (blocks, tok))
    row = lax.broadcasted_iota(jnp.int32, (blocks, blocks), 0)
    earlier = (lax.broadcasted_iota(jnp.int32, (blocks, blocks), 1) < row).astype(jnp.float32)
    before = jnp.dot(earlier, totals, preferred_element_type=jnp.float32)
    rank = within + before
    kept = (named > 0.0) & (rank < capacity)
    first = order[0] // 4 * 4
    block_row = lax.broadcasted_iota(jnp.int32, (blocks, tok), 0)
    start = jnp.sum(jnp.where(block_row == first, before, 0.0), axis=0, keepdims=True)
    ranks[...] = jnp.where(kept, rank - start, -1.0)

    places = [ranks[pl.ds(order[i], 1), :] for i in range(4)]
    shares = [weight[pl.ds(order[i], 1), :] for i in range(4)]
    place = jnp.concatenate(places, axis=1)
    share = jnp.concatenate(shares, axis=1)
    slot = lax.broadcasted_iota(jnp.int32, (slots, 4 * tok), 0).astype(jnp.float32)
    hits = slot == place
    scale = jnp.sum(jnp.where(hits, share, 0.0), axis=1, keepdims=True)
    select = hits.astype(jnp.float32).astype(jnp.bfloat16)
    for i in range(features // 512):
        span = pl.ds(i * 512, 512)
        x = jnp.concatenate([x0[:, span], x1[:, span], x2[:, span], x3[:, span]], axis=0)
        rows[:, span] = jnp.dot(select, x, preferred_element_type=jnp.float32).astype(jnp.bfloat16)
    for i in range(hidden // wide):
        span = pl.ds(i * wide, wide)
        gate = jnp.dot(rows[...], w_gate[:, span], preferred_element_type=jnp.float32)
        up = jnp.dot(rows[...], w_up[:, span], preferred_element_type=jnp.float32)
        act[:, span] = (gate / (1.0 + jnp.exp(-gate)) * up).astype(jnp.bfloat16)
    back = select.T
    for i in range(features // 512):
        span = pl.ds(i * 512, 512)
        result = jnp.dot(act[...], w_down[:, span], preferred_element_type=jnp.float32)
        made = (result * scale).astype(jnp.bfloat16)
        spread = jnp.dot(back, made, preferred_element_type=jnp.float32).astype(jnp.bfloat16)
        keep[:, span] = spread[: 2 * tok]
        give[:, span] = spread[2 * tok :]


def plane_pass(order, weight, xs, w_gate, w_up, w_down, slots, capacity):
    tok, features = xs[0].shape
    hidden = w_gate.shape[1]
    half = jax.ShapeDtypeStruct((2 * tok, features), jnp.bfloat16)
    rows = 4 * slots
    flops = 2 * rows * (3 * features * hidden + 8 * tok * features)
    moved = 2 * (3 * features * hidden + 8 * tok * features)
    return pl.pallas_call(
        functools.partial(plane_kernel, capacity),
        out_shape=(half, half, jax.ShapeDtypeStruct((rows, hidden), jnp.bfloat16)),
        in_specs=[pl.BlockSpec(memory_space=pltpu.SMEM)]
        + [pl.BlockSpec(memory_space=pltpu.VMEM)] * 8,
        out_specs=[pl.BlockSpec(memory_space=pltpu.VMEM)] * 3,
        scratch_shapes=[
            pltpu.VMEM((rows, features), jnp.bfloat16),
            pltpu.VMEM(weight.shape, jnp.float32),
        ],
        compiler_params=pltpu.CompilerParams(vmem_limit_bytes=32 * 1024 * 1024),
        cost_estimate=pl.CostEstimate(
            flops=flops, bytes_accessed=moved, transcendentals=rows * hidden
        ),
    )(order, weight, *xs, w_gate, w_up, w_down)


def staged(routes, probs, tokens, w_gate, w_up, w_down):
    tok, top = routes.shape
    size = lax.axis_size("expert")
    slots = 5 * tok * top // (4 * size)
    capacity = tok * top // 2
    half = tok // 2
    me = lax.axis_index("expert")
    z, y, core = me // 4, me // 2 % 2, me % 2

    def swapped(array, bit):
        return lax.ppermute(array, "expert", [(i, i ^ bit) for i in range(size)])

    sibling = functools.partial(swapped, bit=1)
    column = functools.partial(swapped, bit=2)
    pair = functools.partial(swapped, bit=4)
    far = functools.partial(swapped, bit=8)

    def together(*arrays):
        return lax.optimization_barrier(arrays)

    def expert(k, *xs):
        base = (z ^ k) * 4
        order = jnp.stack(
            [
                base + y * 2 + core,
                base + (1 - y) * 2 + core,
                base + y * 2 + 1 - core,
                base + (1 - y) * 2 + 1 - core,
            ]
        ).astype(jnp.int32)
        return plane_pass(order, weight, xs, w_gate, w_up, w_down, slots, capacity)

    weight = weights_for_me(routes, probs, size)
    a0 = tokens
    a1 = pair(a0)
    a2 = far(a0)
    b0 = column(a0)
    c0 = sibling(a0)
    a1, b0, c0, weight = together(a1, b0, c0, weight)
    b1 = column(a1)
    d0 = sibling(b0)
    c1 = sibling(a1)
    keep0, give0, act0 = expert(0, a0, b0, c0, d0)
    a2, b1, c1, keep0, give0, act0 = together(a2, b1, c1, keep0, give0, act0)
    a3 = pair(a2)
    b2 = column(a2)
    d1 = sibling(b1)
    c2 = sibling(a2)
    keep1, give1, act1 = expert(1, a1, b1, c1, d1)
    a3, b2, c2, keep1, give1, act1 = together(a3, b2, c2, keep1, give1, act1)
    b3_low = pair(b2[:half])
    b3_high = column(a3[half:])
    d2 = sibling(b2)
    c3 = sibling(a3)
    got1 = sibling(give1)
    keep2, give2, act2 = expert(2, a2, b2, c2, d2)
    b3_low, b3_high, c3, got1, keep2, give2, act2 = together(
        b3_low, b3_high, c3, got1, keep2, give2, act2
    )
    b3 = jnp.concatenate([b3_low, b3_high], axis=0)
    d3 = sibling(b3)
    came1 = column(summed(keep1[tok:], got1[tok:]))
    got2 = sibling(give2)
    keep3, give3, act3 = expert(3, a3, b3, c3, d3)

    keep3, give3, act3, got2, came1 = together(keep3, give3, act3, got2, came1)
    got3 = sibling(give3)
    got0 = sibling(give0)
    got3, got0 = together(got3, got0)
    low = pair(summed(keep3[tok : tok + half], got3[tok : tok + half]))
    high = column(summed(keep3[tok + half :], got3[tok + half :]))
    low, high = together(low, high)
    far3 = jnp.concatenate(
        [summed(keep3[:half], got3[:half]), summed(keep3[half:tok], got3[half:tok], high)], axis=0
    )
    side2 = jnp.concatenate(
        [
            summed(keep2[tok : tok + half], got2[tok : tok + half], low),
            summed(keep2[tok + half :], got2[tok + half :]),
        ],
        axis=0,
    )
    far3, side2 = together(pair(far3), column(side2))
    last2 = far(summed(keep2[:tok], got2[:tok], far3, side2))
    last1 = pair(summed(keep1[:tok], got1[:tok], came1))
    last0 = column(summed(keep0[tok:], got0[tok:]))
    mixed = summed(keep0[:tok], got0[:tok], last0, last1, last2)

    acts = jnp.concatenate([act0, act1, act2, act3], axis=0)
    count = jnp.minimum(jnp.sum((weight >= 0.0).astype(jnp.float32)), float(capacity))
    gram = gram_of(acts) * (2.0 / count)
    return gram[None], mixed


def gathered(routes, probs, tokens, w_gate, w_up, w_down):
    tok_rows, top = routes.shape
    size = lax.axis_size("expert")
    capacity = tok_rows * top // 2
    every_token = lax.all_gather(tokens, "expert", tiled=True)
    weight = weights_for_me(routes, probs, size)
    named = (weight >= 0.0).astype(jnp.int32)
    within = jnp.cumsum(named, axis=1) - named
    per_device = jnp.sum(named, axis=1)
    before = jnp.cumsum(per_device) - per_device
    rank = within + before[:, None]
    kept = (named == 1) & (rank < capacity)
    count = jnp.minimum(jnp.sum(per_device), capacity)
    slot = jnp.where(kept, rank, -1).reshape(size * tok_rows)
    place = jnp.arange(capacity, dtype=jnp.int32)
    select = (place[:, None] == slot[None, :]).astype(jnp.bfloat16)
    rows = jnp.dot(select, every_token, preferred_element_type=jnp.float32).astype(jnp.bfloat16)
    gram_sum, made = expert_pass(rows, w_gate, w_up, w_down)
    gram = gram_sum * (2.0 / count.astype(jnp.float32))
    spread = lax.dot_general(
        select, made, (((0,), (0,)), ((), ())), preferred_element_type=jnp.float32
    )
    partial = (spread * weight.reshape(size * tok_rows, 1)).astype(jnp.bfloat16)
    mixed = lax.psum_scatter(partial, "expert", scatter_dimension=0, tiled=True)
    return gram[None], mixed.astype(jnp.bfloat16)


def shards(routes, probs, tokens, gate_weight, up_weight, down_weight):
    body = staged if lax.axis_size("expert") == 16 else gathered
    return body(routes, probs, tokens, gate_weight[0], up_weight[0], down_weight[0])


def solution(mesh):
    placed = (
        P(("parts", "expert"), None),
        P(("parts", "expert"), None),
        P(("parts", "expert"), None),
        P("expert", None, None),
        P("expert", None, None),
        P("expert", None, None),
    )
    return jax.shard_map(
        shards,
        mesh=mesh,
        in_specs=placed,
        out_specs=(P(("parts", "expert"), None, None), P(("parts", "expert"), None)),
        check_vma=False,
    )
```

```python
import functools

import jax
import jax.numpy as jnp
from jax import lax
from jax.experimental import pallas as pl
from jax.experimental.pallas import tpu as pltpu
from jax.sharding import PartitionSpec as P


def gram_of(rows):
    return lax.dot_general(rows, rows, (((0,), (0,)), ((), ())), preferred_element_type=jnp.float32)


def expert_pass(rows, w_gate, w_up, w_down):
    gate = jnp.dot(rows, w_gate, preferred_element_type=jnp.float32)
    up = jnp.dot(rows, w_up, preferred_element_type=jnp.float32)
    act = (jax.nn.silu(gate) * up).astype(jnp.bfloat16)
    gram_sum = gram_of(act)
    made = jnp.dot(act, w_down, preferred_element_type=jnp.float32).astype(jnp.bfloat16)
    return (gram_sum, made)


def weights_for_me(routes, probs, experts):
    names = routes.T[None, :, :] == jnp.arange(experts, dtype=jnp.int32)[:, None, None]
    weight = jnp.sum(jnp.where(names, probs.T[None, :, :], 0.0), axis=1)
    mine = jnp.where(jnp.any(names, axis=1), weight, -1.0)
    return lax.all_to_all(mine, "expert", split_axis=0, concat_axis=0, tiled=True)


def summed(*parts):
    total = parts[0].astype(jnp.float32)
    for part in parts[1:]:
        total = total + part.astype(jnp.float32)
    return total.astype(jnp.bfloat16)


def plane_kernel(
    capacity, order, weight, x0, x1, x2, x3, w_gate, w_up, w_down, keep, give, act,
    x, rows, ranks, gates, ups, downs, x_sem, gate_sem, up_sem, down_sem,
):
    blocks, tok = weight.shape
    slots, hidden = act.shape
    tiles, features, wide = gates.shape
    cuts, _, cut = downs.shape
    x_copies = [
        pltpu.make_async_copy(block, x.at[pl.ds(i * tok, tok), :], x_sem.at[i])
        for i, block in enumerate((x0, x1, x2, x3))
    ]
    gate_copies = [
        pltpu.make_async_copy(w_gate.at[:, pl.ds(i * wide, wide)], gates.at[i], gate_sem.at[i])
        for i in range(tiles)
    ]
    up_copies = [
        pltpu.make_async_copy(w_up.at[:, pl.ds(i * wide, wide)], ups.at[i], up_sem.at[i])
        for i in range(tiles)
    ]
    down_copies = [
        pltpu.make_async_copy(w_down.at[:, pl.ds(i * cut, cut)], downs.at[i], down_sem.at[i])
        for i in range(cuts)
    ]
    for copy in x_copies:
        copy.start()
    for gate_copy, up_copy in zip(gate_copies, up_copies):
        gate_copy.start()
        up_copy.start()
    for copy in down_copies:
        copy.start()

    named = (weight[...] >= 0.0).astype(jnp.float32)
    lane = lax.broadcasted_iota(jnp.int32, (tok, tok), 0)
    below = (lane < lax.broadcasted_iota(jnp.int32, (tok, tok), 1)).astype(jnp.float32)
    within = jnp.dot(named, below, preferred_element_type=jnp.float32)
    totals = jnp.broadcast_to(jnp.sum(named, axis=1, keepdims=True), (blocks, tok))
    row = lax.broadcasted_iota(jnp.int32, (blocks, blocks), 0)
    earlier = (lax.broadcasted_iota(jnp.int32, (blocks, blocks), 1) < row).astype(jnp.float32)
    before = jnp.dot(earlier, totals, preferred_element_type=jnp.float32)
    rank = within + before
    kept = (named > 0.0) & (rank < capacity)
    first = order[0] // 4 * 4
    block_row = lax.broadcasted_iota(jnp.int32, (blocks, tok), 0)
    start = jnp.sum(jnp.where(block_row == first, before, 0.0), axis=0, keepdims=True)
    ranks[...] = jnp.where(kept, rank - start, -1.0)

    places = [ranks[pl.ds(order[i], 1), :] for i in range(4)]
    shares = [weight[pl.ds(order[i], 1), :] for i in range(4)]
    place = jnp.concatenate(places, axis=1)
    share = jnp.concatenate(shares, axis=1)
    slot = lax.broadcasted_iota(jnp.int32, (slots, 4 * tok), 0).astype(jnp.float32)
    hits = slot == place
    scale = jnp.sum(jnp.where(hits, share, 0.0), axis=1, keepdims=True)
    select = hits.astype(jnp.float32).astype(jnp.bfloat16)
    for copy in x_copies:
        copy.wait()
    for i in range(cuts):
        span = pl.ds(i * cut, cut)
        rows[:, span] = jnp.dot(
            select, x[:, span], preferred_element_type=jnp.float32
        ).astype(jnp.bfloat16)
    for i in range(tiles):
        gate_copies[i].wait()
        gate = jnp.dot(rows[...], gates[i], preferred_element_type=jnp.float32)
        up_copies[i].wait()
        up = jnp.dot(rows[...], ups[i], preferred_element_type=jnp.float32)
        act[:, pl.ds(i * wide, wide)] = (gate / (1.0 + jnp.exp(-gate)) * up).astype(jnp.bfloat16)
    back = select.T
    for i in range(cuts):
        span = pl.ds(i * cut, cut)
        down_copies[i].wait()
        result = jnp.dot(act[...], downs[i], preferred_element_type=jnp.float32)
        made = (result * scale).astype(jnp.bfloat16)
        spread = jnp.dot(back, made, preferred_element_type=jnp.float32).astype(jnp.bfloat16)
        keep[:, span] = spread[: 2 * tok]
        give[:, span] = spread[2 * tok :]


def plane_pass(order, weight, xs, w_gate, w_up, w_down, slots, capacity):
    tok, features = xs[0].shape
    hidden = w_gate.shape[1]
    half = jax.ShapeDtypeStruct((2 * tok, features), jnp.bfloat16)
    rows = 4 * slots
    wide, cut = 256, 512
    tiles, cuts = hidden // wide, features // cut
    flops = 2 * rows * (3 * features * hidden + 8 * tok * features)
    moved = 2 * (3 * features * hidden + 8 * tok * features)
    return pl.pallas_call(
        functools.partial(plane_kernel, capacity),
        out_shape=(half, half, jax.ShapeDtypeStruct((rows, hidden), jnp.bfloat16)),
        in_specs=[pl.BlockSpec(memory_space=pltpu.SMEM), pl.BlockSpec(memory_space=pltpu.VMEM)]
        + [pl.BlockSpec(memory_space=pl.ANY)] * 7,
        out_specs=[pl.BlockSpec(memory_space=pltpu.VMEM)] * 3,
        scratch_shapes=[
            pltpu.VMEM((4 * tok, features), jnp.bfloat16),
            pltpu.VMEM((rows, features), jnp.bfloat16),
            pltpu.VMEM(weight.shape, jnp.float32),
            pltpu.VMEM((tiles, features, wide), jnp.bfloat16),
            pltpu.VMEM((tiles, features, wide), jnp.bfloat16),
            pltpu.VMEM((cuts, hidden, cut), jnp.bfloat16),
            pltpu.SemaphoreType.DMA((4,)),
            pltpu.SemaphoreType.DMA((tiles,)),
            pltpu.SemaphoreType.DMA((tiles,)),
            pltpu.SemaphoreType.DMA((cuts,)),
        ],
        compiler_params=pltpu.CompilerParams(vmem_limit_bytes=58 * 1024 * 1024),
        cost_estimate=pl.CostEstimate(
            flops=flops, bytes_accessed=moved, transcendentals=rows * hidden
        ),
    )(order, weight, *xs, w_gate, w_up, w_down)


def staged(routes, probs, tokens, w_gate, w_up, w_down):
    tok, top = routes.shape
    size = lax.axis_size("expert")
    slots = 5 * tok * top // (4 * size)
    capacity = tok * top // 2
    half = tok // 2
    me = lax.axis_index("expert")
    z, y, core = me // 4, me // 2 % 2, me % 2

    def swapped(array, bit):
        return lax.ppermute(array, "expert", [(i, i ^ bit) for i in range(size)])

    sibling = functools.partial(swapped, bit=1)
    column = functools.partial(swapped, bit=2)
    pair = functools.partial(swapped, bit=4)
    far = functools.partial(swapped, bit=8)

    def together(*arrays):
        return lax.optimization_barrier(arrays)

    def expert(k, *xs):
        base = (z ^ k) * 4
        order = jnp.stack(
            [
                base + y * 2 + core,
                base + (1 - y) * 2 + core,
                base + y * 2 + 1 - core,
                base + (1 - y) * 2 + 1 - core,
            ]
        ).astype(jnp.int32)
        return plane_pass(order, weight, xs, w_gate, w_up, w_down, slots, capacity)

    weight = weights_for_me(routes, probs, size)
    a0 = tokens
    a1, low, b0, c0, weight = together(
        pair(a0), far(a0[:half]), column(a0), sibling(a0), weight
    )
    b1 = column(a1)
    high = far(a0[half:])
    d0 = sibling(b0)
    c1 = sibling(a1)
    keep0, give0, act0 = expert(0, a0, b0, c0, d0)
    high, b1, c1, keep0, give0, act0 = together(high, b1, c1, keep0, give0, act0)
    a2 = jnp.concatenate([low, high], axis=0)
    a3 = pair(a2)
    b2 = column(a2)
    d1 = sibling(b1)
    c2 = sibling(a2)
    keep1, give1, act1 = expert(1, a1, b1, c1, d1)
    a3, b2, c2, keep1, give1, act1 = together(a3, b2, c2, keep1, give1, act1)
    b3_low = pair(b2[:half])
    b3_high = column(a3[half:])
    d2 = sibling(b2)
    c3 = sibling(a3)
    got1 = sibling(give1)
    keep2, give2, act2 = expert(2, a2, b2, c2, d2)
    b3_low, b3_high, c3, got1, keep2, give2, act2 = together(
        b3_low, b3_high, c3, got1, keep2, give2, act2
    )
    b3 = jnp.concatenate([b3_low, b3_high], axis=0)
    d3 = sibling(b3)
    came1 = column(summed(keep1[tok:], got1[tok:]))
    got2 = sibling(give2)
    keep3, give3, act3 = expert(3, a3, b3, c3, d3)

    keep3, give3, act3, got2, came1 = together(keep3, give3, act3, got2, came1)
    got3 = sibling(give3)
    got0 = sibling(give0)
    got3, got0 = together(got3, got0)
    low = pair(summed(keep3[tok : tok + half], got3[tok : tok + half]))
    high = column(summed(keep3[tok + half :], got3[tok + half :]))
    low, high = together(low, high)
    far3 = jnp.concatenate(
        [summed(keep3[:half], got3[:half]), summed(keep3[half:tok], got3[half:tok], high)], axis=0
    )
    side2 = jnp.concatenate(
        [
            summed(keep2[tok : tok + half], got2[tok : tok + half], low),
            summed(keep2[tok + half :], got2[tok + half :]),
        ],
        axis=0,
    )
    far3, side2 = together(pair(far3), column(side2))
    last2 = far(summed(keep2[:tok], got2[:tok], far3, side2))
    last1 = pair(summed(keep1[:tok], got1[:tok], came1))
    last0 = column(summed(keep0[tok:], got0[tok:]))
    mixed = summed(keep0[:tok], got0[:tok], last0, last1, last2)

    acts = jnp.concatenate([act0, act1, act2, act3], axis=0)
    count = jnp.minimum(jnp.sum((weight >= 0.0).astype(jnp.float32)), float(capacity))
    gram = gram_of(acts) * (2.0 / count)
    return gram[None], mixed


def gathered(routes, probs, tokens, w_gate, w_up, w_down):
    tok_rows, top = routes.shape
    size = lax.axis_size("expert")
    capacity = tok_rows * top // 2
    every_token = lax.all_gather(tokens, "expert", tiled=True)
    weight = weights_for_me(routes, probs, size)
    named = (weight >= 0.0).astype(jnp.int32)
    within = jnp.cumsum(named, axis=1) - named
    per_device = jnp.sum(named, axis=1)
    before = jnp.cumsum(per_device) - per_device
    rank = within + before[:, None]
    kept = (named == 1) & (rank < capacity)
    count = jnp.minimum(jnp.sum(per_device), capacity)
    slot = jnp.where(kept, rank, -1).reshape(size * tok_rows)
    place = jnp.arange(capacity, dtype=jnp.int32)
    select = (place[:, None] == slot[None, :]).astype(jnp.bfloat16)
    rows = jnp.dot(select, every_token, preferred_element_type=jnp.float32).astype(jnp.bfloat16)
    gram_sum, made = expert_pass(rows, w_gate, w_up, w_down)
    gram = gram_sum * (2.0 / count.astype(jnp.float32))
    spread = lax.dot_general(
        select, made, (((0,), (0,)), ((), ())), preferred_element_type=jnp.float32
    )
    partial = (spread * weight.reshape(size * tok_rows, 1)).astype(jnp.bfloat16)
    mixed = lax.psum_scatter(partial, "expert", scatter_dimension=0, tiled=True)
    return gram[None], mixed.astype(jnp.bfloat16)


def shards(routes, probs, tokens, gate_weight, up_weight, down_weight):
    body = staged if lax.axis_size("expert") == 16 else gathered
    return body(routes, probs, tokens, gate_weight[0], up_weight[0], down_weight[0])


def solution(mesh):
    placed = (
        P(("parts", "expert"), None),
        P(("parts", "expert"), None),
        P(("parts", "expert"), None),
        P("expert", None, None),
        P("expert", None, None),
        P("expert", None, None),
    )
    return jax.shard_map(
        shards,
        mesh=mesh,
        in_specs=placed,
        out_specs=(P(("parts", "expert"), None, None), P(("parts", "expert"), None)),
        check_vma=False,
    )
```

```python
import functools

import jax
import jax.numpy as jnp
from jax import lax
from jax.experimental import pallas as pl
from jax.experimental.pallas import tpu as pltpu
from jax.sharding import PartitionSpec as P


def gram_of(rows):
    return lax.dot_general(rows, rows, (((0,), (0,)), ((), ())), preferred_element_type=jnp.float32)


def expert_pass(rows, w_gate, w_up, w_down):
    gate = jnp.dot(rows, w_gate, preferred_element_type=jnp.float32)
    up = jnp.dot(rows, w_up, preferred_element_type=jnp.float32)
    act = (jax.nn.silu(gate) * up).astype(jnp.bfloat16)
    gram_sum = gram_of(act)
    made = jnp.dot(act, w_down, preferred_element_type=jnp.float32).astype(jnp.bfloat16)
    return (gram_sum, made)


def weights_for_me(routes, probs, experts):
    names = routes.T[None, :, :] == jnp.arange(experts, dtype=jnp.int32)[:, None, None]
    weight = jnp.sum(jnp.where(names, probs.T[None, :, :], 0.0), axis=1)
    mine = jnp.where(jnp.any(names, axis=1), weight, -1.0)
    return lax.all_to_all(mine, "expert", split_axis=0, concat_axis=0, tiled=True)


def summed(*parts):
    total = parts[0].astype(jnp.float32)
    for part in parts[1:]:
        total = total + part.astype(jnp.float32)
    return total.astype(jnp.bfloat16)


def plane_kernel(capacity, k, parts, spots, weight, *refs):
    xs, refs = refs[:parts], refs[parts:]
    w_gate, w_up, w_down, keep, give, act_out = refs[:6]
    x, rows, act, out, ranks, gates, ups, downs, x_sem, gate_sem, up_sem, down_sem, out_sem = refs[6:]
    blocks, tok = weight.shape
    slots, hidden = act.shape
    tiles, features, wide = gates.shape
    cuts, _, cut = downs.shape
    x_copies, at = [], 0
    for i, block in enumerate(xs):
        target = x.at[pl.ds(at, block.shape[0]), :]
        x_copies.append(pltpu.make_async_copy(block, target, x_sem.at[i]))
        at += block.shape[0]
    loads = []
    for i in range(tiles):
        span = pl.ds(i * wide, wide)
        loads.append(pltpu.make_async_copy(w_gate.at[:, span], gates.at[i], gate_sem.at[i]))
        loads.append(pltpu.make_async_copy(w_up.at[:, span], ups.at[i], up_sem.at[i]))
    for i in range(cuts):
        span = pl.ds(i * cut, cut)
        loads.append(pltpu.make_async_copy(w_down.at[:, span], downs.at[i], down_sem.at[i]))
    for copy in x_copies:
        copy.start()
    loads[0].start()
    loads[1].start()

    named = (weight[...] >= 0.0).astype(jnp.float32)
    lane = lax.broadcasted_iota(jnp.int32, (tok, tok), 0)
    below = (lane < lax.broadcasted_iota(jnp.int32, (tok, tok), 1)).astype(jnp.float32)
    within = jnp.dot(named, below, preferred_element_type=jnp.float32)
    totals = jnp.broadcast_to(jnp.sum(named, axis=1, keepdims=True), (blocks, tok))
    row = lax.broadcasted_iota(jnp.int32, (blocks, blocks), 0)
    earlier = (lax.broadcasted_iota(jnp.int32, (blocks, blocks), 1) < row).astype(jnp.float32)
    before = jnp.dot(earlier, totals, preferred_element_type=jnp.float32)
    rank = within + before
    kept = (named > 0.0) & (rank < capacity)
    order = [spots[4 * k + i] for i in range(4)]
    first = order[0] // 4 * 4
    block_row = lax.broadcasted_iota(jnp.int32, (blocks, tok), 0)
    start = jnp.sum(jnp.where(block_row == first, before, 0.0), axis=0, keepdims=True)
    ranks[...] = jnp.where(kept, rank - start, -1.0)
    place = jnp.concatenate([ranks[pl.ds(i, 1), :] for i in order], axis=1)
    share = jnp.concatenate([weight[pl.ds(i, 1), :] for i in order], axis=1)
    slot = lax.broadcasted_iota(jnp.int32, (slots, 4 * tok), 0).astype(jnp.float32)
    hits = slot == place
    scale = jnp.sum(jnp.where(hits, share, 0.0), axis=1, keepdims=True)
    select = hits.astype(jnp.float32).astype(jnp.bfloat16)
    for copy in x_copies:
        copy.wait()
    for load in loads[2 : 2 * tiles]:
        load.start()
    for i in range(cuts):
        span = pl.ds(i * cut, cut)
        rows[:, span] = jnp.dot(
            select, x[:, span], preferred_element_type=jnp.float32
        ).astype(jnp.bfloat16)
    for load in loads[2 * tiles :]:
        load.start()
    act_copy = pltpu.make_async_copy(act, act_out, out_sem.at[2 * cuts])
    for i in range(tiles):
        loads[2 * i].wait()
        gate = jnp.dot(rows[...], gates[i], preferred_element_type=jnp.float32)
        loads[2 * i + 1].wait()
        up = jnp.dot(rows[...], ups[i], preferred_element_type=jnp.float32)
        act[:, pl.ds(i * wide, wide)] = (gate / (1.0 + jnp.exp(-gate)) * up).astype(jnp.bfloat16)
    act_copy.start()
    back = select.T
    out_copies = []
    for i in range(cuts):
        span = pl.ds(i * cut, cut)
        loads[2 * tiles + i].wait()
        result = jnp.dot(act[...], downs[i], preferred_element_type=jnp.float32)
        made = (result * scale).astype(jnp.bfloat16)
        out[i] = jnp.dot(back, made, preferred_element_type=jnp.float32).astype(jnp.bfloat16)
        for half, target in enumerate((keep, give)):
            source = out.at[i, pl.ds(half * 2 * tok, 2 * tok), :]
            copy = pltpu.make_async_copy(source, target.at[:, span], out_sem.at[2 * i + half])
            copy.start()
            out_copies.append(copy)
    act_copy.wait()
    for copy in out_copies:
        copy.wait()


def plane_pass(k, spots, weight, xs, w_gate, w_up, w_down, slots, capacity):
    tok, features = weight.shape[1], w_gate.shape[0]
    hidden = w_gate.shape[1]
    half = jax.ShapeDtypeStruct((2 * tok, features), jnp.bfloat16)
    rows = 4 * slots
    wide, cut = 256, 512
    tiles, cuts = hidden // wide, features // cut
    flops = 2 * rows * (3 * features * hidden + 8 * tok * features)
    moved = 2 * (3 * features * hidden + 8 * tok * features)
    return pl.pallas_call(
        functools.partial(plane_kernel, capacity, k, len(xs)),
        out_shape=(half, half, jax.ShapeDtypeStruct((rows, hidden), jnp.bfloat16)),
        in_specs=[pl.BlockSpec(memory_space=pltpu.SMEM), pl.BlockSpec(memory_space=pltpu.VMEM)]
        + [pl.BlockSpec(memory_space=pl.ANY)] * (len(xs) + 3),
        out_specs=[pl.BlockSpec(memory_space=pl.ANY)] * 3,
        scratch_shapes=[
            pltpu.VMEM((4 * tok, features), jnp.bfloat16),
            pltpu.VMEM((rows, features), jnp.bfloat16),
            pltpu.VMEM((rows, hidden), jnp.bfloat16),
            pltpu.VMEM((cuts, 4 * tok, cut), jnp.bfloat16),
            pltpu.VMEM(weight.shape, jnp.float32),
            pltpu.VMEM((tiles, features, wide), jnp.bfloat16),
            pltpu.VMEM((tiles, features, wide), jnp.bfloat16),
            pltpu.VMEM((cuts, hidden, cut), jnp.bfloat16),
            pltpu.SemaphoreType.DMA((len(xs),)),
            pltpu.SemaphoreType.DMA((tiles,)),
            pltpu.SemaphoreType.DMA((tiles,)),
            pltpu.SemaphoreType.DMA((cuts,)),
            pltpu.SemaphoreType.DMA((2 * cuts + 1,)),
        ],
        compiler_params=pltpu.CompilerParams(vmem_limit_bytes=58 * 1024 * 1024),
        cost_estimate=pl.CostEstimate(
            flops=flops, bytes_accessed=moved, transcendentals=rows * hidden
        ),
    )(spots, weight, *xs, w_gate, w_up, w_down)


def staged(routes, probs, tokens, w_gate, w_up, w_down):
    tok, top = routes.shape
    size = lax.axis_size("expert")
    slots = 5 * tok * top // (4 * size)
    capacity = tok * top // 2
    half = tok // 2
    me = lax.axis_index("expert")
    z, y, core = me // 4, me // 2 % 2, me % 2

    def swapped(array, bit):
        return lax.ppermute(array, "expert", [(i, i ^ bit) for i in range(size)])

    sibling = functools.partial(swapped, bit=1)
    column = functools.partial(swapped, bit=2)
    pair = functools.partial(swapped, bit=4)
    far = functools.partial(swapped, bit=8)

    def together(*arrays):
        return lax.optimization_barrier(arrays)

    spots = jnp.stack(
        [
            (z ^ k) * 4 + (y ^ column_bit) * 2 + (core ^ core_bit)
            for k in range(4)
            for core_bit in range(2)
            for column_bit in range(2)
        ]
    ).astype(jnp.int32)

    def expert(k, *xs):
        return plane_pass(k, spots, weight, xs, w_gate, w_up, w_down, slots, capacity)

    weight = weights_for_me(routes, probs, size)
    a0 = tokens
    a1, low, b0, c0, weight = together(
        pair(a0), far(a0[:half]), column(a0), sibling(a0), weight
    )
    b1 = column(a1)
    high = far(a0[half:])
    d0 = sibling(b0)
    c1 = sibling(a1)
    keep0, give0, act0 = expert(0, a0, b0, c0, d0)
    high, b1, c1, keep0, give0, act0 = together(high, b1, c1, keep0, give0, act0)
    a2 = jnp.concatenate([low, high], axis=0)
    a3 = pair(a2)
    b2 = column(a2)
    d1 = sibling(b1)
    c2 = sibling(a2)
    keep1, give1, act1 = expert(1, a1, b1, c1, d1)
    a3, b2, c2, keep1, give1, act1 = together(a3, b2, c2, keep1, give1, act1)
    b3_low = pair(b2[:half])
    b3_high = column(a3[half:])
    d2 = sibling(b2)
    c3 = sibling(a3)
    got1 = sibling(give1)
    keep2, give2, act2 = expert(2, a2, b2, c2, d2)
    b3_low, b3_high, c3, got1, keep2, give2, act2 = together(
        b3_low, b3_high, c3, got1, keep2, give2, act2
    )
    d3_low = sibling(b3_low)
    d3_high = sibling(b3_high)
    came1 = column(summed(keep1[tok:], got1[tok:]))
    got2 = sibling(give2)
    keep3, give3, act3 = expert(3, a3, b3_low, b3_high, c3, d3_low, d3_high)

    keep3, give3, act3, got2, came1 = together(keep3, give3, act3, got2, came1)
    got3 = sibling(give3)
    got0 = sibling(give0)
    got3, got0 = together(got3, got0)
    low = pair(summed(keep3[tok : tok + half], got3[tok : tok + half]))
    high = column(summed(keep3[tok + half :], got3[tok + half :]))
    low, high = together(low, high)
    far3 = jnp.concatenate(
        [summed(keep3[:half], got3[:half]), summed(keep3[half:tok], got3[half:tok], high)], axis=0
    )
    side2 = jnp.concatenate(
        [
            summed(keep2[tok : tok + half], got2[tok : tok + half], low),
            summed(keep2[tok + half :], got2[tok + half :]),
        ],
        axis=0,
    )
    near1 = summed(keep1[:tok], got1[:tok], came1)
    side0 = summed(keep0[tok:], got0[tok:])
    far3, side2, near1, side0 = together(pair(far3), column(side2), near1, side0)
    last2 = far(summed(keep2[:tok], got2[:tok], far3, side2))
    last1 = pair(near1)
    last0 = column(side0)
    mixed = summed(keep0[:tok], got0[:tok], last0, last1, last2)

    acts = jnp.concatenate([act0, act1, act2, act3], axis=0)
    count = jnp.minimum(jnp.sum((weight >= 0.0).astype(jnp.float32)), float(capacity))
    gram = gram_of(acts) * (2.0 / count)
    return gram[None], mixed


def gathered(routes, probs, tokens, w_gate, w_up, w_down):
    tok_rows, top = routes.shape
    size = lax.axis_size("expert")
    capacity = tok_rows * top // 2
    every_token = lax.all_gather(tokens, "expert", tiled=True)
    weight = weights_for_me(routes, probs, size)
    named = (weight >= 0.0).astype(jnp.int32)
    within = jnp.cumsum(named, axis=1) - named
    per_device = jnp.sum(named, axis=1)
    before = jnp.cumsum(per_device) - per_device
    rank = within + before[:, None]
    kept = (named == 1) & (rank < capacity)
    count = jnp.minimum(jnp.sum(per_device), capacity)
    slot = jnp.where(kept, rank, -1).reshape(size * tok_rows)
    place = jnp.arange(capacity, dtype=jnp.int32)
    select = (place[:, None] == slot[None, :]).astype(jnp.bfloat16)
    rows = jnp.dot(select, every_token, preferred_element_type=jnp.float32).astype(jnp.bfloat16)
    gram_sum, made = expert_pass(rows, w_gate, w_up, w_down)
    gram = gram_sum * (2.0 / count.astype(jnp.float32))
    spread = lax.dot_general(
        select, made, (((0,), (0,)), ((), ())), preferred_element_type=jnp.float32
    )
    partial = (spread * weight.reshape(size * tok_rows, 1)).astype(jnp.bfloat16)
    mixed = lax.psum_scatter(partial, "expert", scatter_dimension=0, tiled=True)
    return gram[None], mixed.astype(jnp.bfloat16)


def shards(routes, probs, tokens, gate_weight, up_weight, down_weight):
    body = staged if lax.axis_size("expert") == 16 else gathered
    return body(routes, probs, tokens, gate_weight[0], up_weight[0], down_weight[0])


def solution(mesh):
    placed = (
        P(("parts", "expert"), None),
        P(("parts", "expert"), None),
        P(("parts", "expert"), None),
        P("expert", None, None),
        P("expert", None, None),
        P("expert", None, None),
    )
    return jax.shard_map(
        shards,
        mesh=mesh,
        in_specs=placed,
        out_specs=(P(("parts", "expert"), None, None), P(("parts", "expert"), None)),
        check_vma=False,
    )
```

```python
import functools

import jax
import jax.numpy as jnp
from jax import lax
from jax.experimental import pallas as pl
from jax.experimental.pallas import tpu as pltpu
from jax.sharding import PartitionSpec as P


def gram_of(rows):
    return lax.dot_general(rows, rows, (((0,), (0,)), ((), ())), preferred_element_type=jnp.float32)


def expert_pass(rows, w_gate, w_up, w_down):
    gate = jnp.dot(rows, w_gate, preferred_element_type=jnp.float32)
    up = jnp.dot(rows, w_up, preferred_element_type=jnp.float32)
    act = (jax.nn.silu(gate) * up).astype(jnp.bfloat16)
    gram_sum = gram_of(act)
    made = jnp.dot(act, w_down, preferred_element_type=jnp.float32).astype(jnp.bfloat16)
    return (gram_sum, made)


def weights_for_me(routes, probs, experts):
    names = routes.T[None, :, :] == jnp.arange(experts, dtype=jnp.int32)[:, None, None]
    weight = jnp.sum(jnp.where(names, probs.T[None, :, :], 0.0), axis=1)
    mine = jnp.where(jnp.any(names, axis=1), weight, -1.0)
    return lax.all_to_all(mine, "expert", split_axis=0, concat_axis=0, tiled=True)


def summed(*parts):
    total = parts[0].astype(jnp.float32)
    for part in parts[1:]:
        total = total + part.astype(jnp.float32)
    return total.astype(jnp.bfloat16)


def plane_kernel(capacity, k, parts, spots, weight, *refs):
    xs, refs = refs[:parts], refs[parts:]
    w_gate, w_up, w_down, keep, give, act_out = refs[:6]
    x, rows, act, gated, made, out, ranks, gates, ups, downs = refs[6:16]
    x_sem, gate_sem, up_sem, down_sem, out_sem = refs[16:]
    blocks, tok = weight.shape
    slots, hidden = act.shape
    features = x.shape[1]
    wide, cut = 256, 512
    x_copies, at = [], 0
    for i, block in enumerate(xs):
        target = x.at[pl.ds(at, block.shape[0]), :]
        x_copies.append(pltpu.make_async_copy(block, target, x_sem.at[i]))
        at += block.shape[0]

    def loads(source, target, sems):
        count = sems.shape[0]
        some = source.shape[0] // count
        return [
            pltpu.make_async_copy(
                source.at[pl.ds(i * some, some), :], target.at[pl.ds(i * some, some), :], sems.at[i]
            )
            for i in range(count)
        ]

    gate_copies = loads(w_gate, gates, gate_sem)
    up_copies = loads(w_up, ups, up_sem)
    down_copies = loads(w_down, downs, down_sem)
    for copy in x_copies + gate_copies:
        copy.start()

    named = (weight[...] >= 0.0).astype(jnp.float32)
    lane = lax.broadcasted_iota(jnp.int32, (tok, tok), 0)
    below = (lane < lax.broadcasted_iota(jnp.int32, (tok, tok), 1)).astype(jnp.float32)
    within = jnp.dot(named, below, preferred_element_type=jnp.float32)
    totals = jnp.broadcast_to(jnp.sum(named, axis=1, keepdims=True), (blocks, tok))
    row = lax.broadcasted_iota(jnp.int32, (blocks, blocks), 0)
    earlier = (lax.broadcasted_iota(jnp.int32, (blocks, blocks), 1) < row).astype(jnp.float32)
    before = jnp.dot(earlier, totals, preferred_element_type=jnp.float32)
    rank = within + before
    kept = (named > 0.0) & (rank < capacity)
    order = [spots[4 * k + i] for i in range(4)]
    first = order[0] // 4 * 4
    block_row = lax.broadcasted_iota(jnp.int32, (blocks, tok), 0)
    start = jnp.sum(jnp.where(block_row == first, before, 0.0), axis=0, keepdims=True)
    ranks[...] = jnp.where(kept, rank - start, -1.0)
    place = jnp.concatenate([ranks[pl.ds(i, 1), :] for i in order], axis=1)
    share = jnp.concatenate([weight[pl.ds(i, 1), :] for i in order], axis=1)
    slot = lax.broadcasted_iota(jnp.int32, (slots, 4 * tok), 0).astype(jnp.float32)
    hits = slot == place
    scale = jnp.sum(jnp.where(hits, share, 0.0), axis=1, keepdims=True)
    select = hits.astype(jnp.float32).astype(jnp.bfloat16)
    for copy in x_copies:
        copy.wait()
    for copy in up_copies:
        copy.start()
    for i in range(features // cut):
        span = pl.ds(i * cut, cut)
        rows[:, span] = jnp.dot(
            select, x[:, span], preferred_element_type=jnp.float32
        ).astype(jnp.bfloat16)
    for copy in gate_copies:
        copy.wait()
    for copy in down_copies:
        copy.start()
    for i in range(hidden // wide):
        span = pl.ds(i * wide, wide)
        gate = jnp.dot(rows[...], gates[:, span], preferred_element_type=jnp.float32)
        gated[:, span] = gate / (1.0 + jnp.exp(-gate))
    for copy in up_copies:
        copy.wait()
    for i in range(hidden // wide):
        span = pl.ds(i * wide, wide)
        up = jnp.dot(rows[...], ups[:, span], preferred_element_type=jnp.float32)
        act[:, span] = (gated[:, span] * up).astype(jnp.bfloat16)
    act_copy = pltpu.make_async_copy(act, act_out, out_sem.at[2])
    act_copy.start()
    for copy in down_copies:
        copy.wait()
    for i in range(features // cut):
        span = pl.ds(i * cut, cut)
        result = jnp.dot(act[...], downs[:, span], preferred_element_type=jnp.float32)
        made[:, span] = (result * scale).astype(jnp.bfloat16)
    back = select.T
    out_copies = []
    for half, target in ((1, give), (0, keep)):
        for i in range(features // cut):
            span = pl.ds(i * cut, cut)
            out[half, :, span] = jnp.dot(
                back[half * 2 * tok : (half + 1) * 2 * tok],
                made[:, span],
                preferred_element_type=jnp.float32,
            ).astype(jnp.bfloat16)
        copy = pltpu.make_async_copy(out.at[half], target, out_sem.at[half])
        copy.start()
        out_copies.append(copy)
    act_copy.wait()
    for copy in out_copies:
        copy.wait()


def plane_pass(k, spots, weight, xs, w_gate, w_up, w_down, slots, capacity):
    tok, features = weight.shape[1], w_gate.shape[0]
    hidden = w_gate.shape[1]
    half = jax.ShapeDtypeStruct((2 * tok, features), jnp.bfloat16)
    rows = 4 * slots
    flops = 2 * rows * (3 * features * hidden + 8 * tok * features)
    moved = 2 * (3 * features * hidden + 8 * tok * features)
    return pl.pallas_call(
        functools.partial(plane_kernel, capacity, k, len(xs)),
        out_shape=(half, half, jax.ShapeDtypeStruct((rows, hidden), jnp.bfloat16)),
        in_specs=[pl.BlockSpec(memory_space=pltpu.SMEM), pl.BlockSpec(memory_space=pltpu.VMEM)]
        + [pl.BlockSpec(memory_space=pl.ANY)] * (len(xs) + 3),
        out_specs=[pl.BlockSpec(memory_space=pl.ANY)] * 3,
        scratch_shapes=[
            pltpu.VMEM((4 * tok, features), jnp.bfloat16),
            pltpu.VMEM((rows, features), jnp.bfloat16),
            pltpu.VMEM((rows, hidden), jnp.bfloat16),
            pltpu.VMEM((rows, hidden), jnp.float32),
            pltpu.VMEM((rows, features), jnp.bfloat16),
            pltpu.VMEM((2, 2 * tok, features), jnp.bfloat16),
            pltpu.VMEM(weight.shape, jnp.float32),
            pltpu.VMEM((features, hidden), jnp.bfloat16),
            pltpu.VMEM((features, hidden), jnp.bfloat16),
            pltpu.VMEM((hidden, features), jnp.bfloat16),
            pltpu.SemaphoreType.DMA((len(xs),)),
            pltpu.SemaphoreType.DMA((4,)),
            pltpu.SemaphoreType.DMA((4,)),
            pltpu.SemaphoreType.DMA((4,)),
            pltpu.SemaphoreType.DMA((3,)),
        ],
        compiler_params=pltpu.CompilerParams(vmem_limit_bytes=58 * 1024 * 1024),
        cost_estimate=pl.CostEstimate(
            flops=flops, bytes_accessed=moved, transcendentals=rows * hidden
        ),
    )(spots, weight, *xs, w_gate, w_up, w_down)


def staged(routes, probs, tokens, w_gate, w_up, w_down):
    tok, top = routes.shape
    size = lax.axis_size("expert")
    slots = 5 * tok * top // (4 * size)
    capacity = tok * top // 2
    half = tok // 2
    me = lax.axis_index("expert")
    z, y, core = me // 4, me // 2 % 2, me % 2

    def swapped(array, bit):
        return lax.ppermute(array, "expert", [(i, i ^ bit) for i in range(size)])

    sibling = functools.partial(swapped, bit=1)
    column = functools.partial(swapped, bit=2)
    pair = functools.partial(swapped, bit=4)
    far = functools.partial(swapped, bit=8)

    def together(*arrays):
        return lax.optimization_barrier(arrays)

    spots = jnp.stack(
        [
            (z ^ k) * 4 + (y ^ column_bit) * 2 + (core ^ core_bit)
            for k in range(4)
            for core_bit in range(2)
            for column_bit in range(2)
        ]
    ).astype(jnp.int32)

    def expert(k, *xs):
        return plane_pass(k, spots, weight, xs, w_gate, w_up, w_down, slots, capacity)

    weight = weights_for_me(routes, probs, size)
    a0 = tokens
    a1, low, b0, c0, weight = together(
        pair(a0), far(a0[:half]), column(a0), sibling(a0), weight
    )
    b1 = column(a1)
    high = far(a0[half:])
    d0 = sibling(b0)
    c1 = sibling(a1)
    keep0, give0, act0 = expert(0, a0, b0, c0, d0)
    high, b1, c1, keep0, give0, act0 = together(high, b1, c1, keep0, give0, act0)
    a2 = jnp.concatenate([low, high], axis=0)
    a3 = pair(a2)
    b2 = column(a2)
    d1 = sibling(b1)
    c2 = sibling(a2)
    keep1, give1, act1 = expert(1, a1, b1, c1, d1)
    a3, b2, c2, keep1, give1, act1 = together(a3, b2, c2, keep1, give1, act1)
    b3_low = pair(b2[:half])
    b3_high = column(a3[half:])
    d2 = sibling(b2)
    c3 = sibling(a3)
    got1 = sibling(give1)
    keep2, give2, act2 = expert(2, a2, b2, c2, d2)
    b3_low, b3_high, c3, got1, keep2, give2, act2 = together(
        b3_low, b3_high, c3, got1, keep2, give2, act2
    )
    d3_low = sibling(b3_low)
    d3_high = sibling(b3_high)
    came1 = column(summed(keep1[tok:], got1[tok:]))
    got2 = sibling(give2)
    keep3, give3, act3 = expert(3, a3, b3_low, b3_high, c3, d3_low, d3_high)

    keep3, give3, act3, got2, came1 = together(keep3, give3, act3, got2, came1)
    got3 = sibling(give3)
    got0 = sibling(give0)
    got3, got0 = together(got3, got0)
    low = pair(summed(keep3[tok : tok + half], got3[tok : tok + half]))
    high = column(summed(keep3[tok + half :], got3[tok + half :]))
    low, high = together(low, high)
    far3 = jnp.concatenate(
        [summed(keep3[:half], got3[:half]), summed(keep3[half:tok], got3[half:tok], high)], axis=0
    )
    side2 = jnp.concatenate(
        [
            summed(keep2[tok : tok + half], got2[tok : tok + half], low),
            summed(keep2[tok + half :], got2[tok + half :]),
        ],
        axis=0,
    )
    near1 = summed(keep1[:tok], got1[:tok], came1)
    side0 = summed(keep0[tok:], got0[tok:])
    far3, side2, near1, side0 = together(pair(far3), column(side2), near1, side0)
    last2 = far(summed(keep2[:tok], got2[:tok], far3, side2))
    last1 = pair(near1)
    last0 = column(side0)
    mixed = summed(keep0[:tok], got0[:tok], last0, last1, last2)

    acts = jnp.concatenate([act0, act1, act2, act3], axis=0)
    count = jnp.minimum(jnp.sum((weight >= 0.0).astype(jnp.float32)), float(capacity))
    gram = gram_of(acts) * (2.0 / count)
    return gram[None], mixed


def gathered(routes, probs, tokens, w_gate, w_up, w_down):
    tok_rows, top = routes.shape
    size = lax.axis_size("expert")
    capacity = tok_rows * top // 2
    every_token = lax.all_gather(tokens, "expert", tiled=True)
    weight = weights_for_me(routes, probs, size)
    named = (weight >= 0.0).astype(jnp.int32)
    within = jnp.cumsum(named, axis=1) - named
    per_device = jnp.sum(named, axis=1)
    before = jnp.cumsum(per_device) - per_device
    rank = within + before[:, None]
    kept = (named == 1) & (rank < capacity)
    count = jnp.minimum(jnp.sum(per_device), capacity)
    slot = jnp.where(kept, rank, -1).reshape(size * tok_rows)
    place = jnp.arange(capacity, dtype=jnp.int32)
    select = (place[:, None] == slot[None, :]).astype(jnp.bfloat16)
    rows = jnp.dot(select, every_token, preferred_element_type=jnp.float32).astype(jnp.bfloat16)
    gram_sum, made = expert_pass(rows, w_gate, w_up, w_down)
    gram = gram_sum * (2.0 / count.astype(jnp.float32))
    spread = lax.dot_general(
        select, made, (((0,), (0,)), ((), ())), preferred_element_type=jnp.float32
    )
    partial = (spread * weight.reshape(size * tok_rows, 1)).astype(jnp.bfloat16)
    mixed = lax.psum_scatter(partial, "expert", scatter_dimension=0, tiled=True)
    return gram[None], mixed.astype(jnp.bfloat16)


def shards(routes, probs, tokens, gate_weight, up_weight, down_weight):
    body = staged if lax.axis_size("expert") == 16 else gathered
    return body(routes, probs, tokens, gate_weight[0], up_weight[0], down_weight[0])


def solution(mesh):
    placed = (
        P(("parts", "expert"), None),
        P(("parts", "expert"), None),
        P(("parts", "expert"), None),
        P("expert", None, None),
        P("expert", None, None),
        P("expert", None, None),
    )
    return jax.shard_map(
        shards,
        mesh=mesh,
        in_specs=placed,
        out_specs=(P(("parts", "expert"), None, None), P(("parts", "expert"), None)),
        check_vma=False,
    )
```

```python
import functools

import jax
import jax.numpy as jnp
from jax import lax
from jax.experimental import pallas as pl
from jax.experimental.pallas import tpu as pltpu
from jax.sharding import PartitionSpec as P


def gram_of(rows):
    return lax.dot_general(rows, rows, (((0,), (0,)), ((), ())), preferred_element_type=jnp.float32)


def expert_pass(rows, w_gate, w_up, w_down):
    gate = jnp.dot(rows, w_gate, preferred_element_type=jnp.float32)
    up = jnp.dot(rows, w_up, preferred_element_type=jnp.float32)
    act = (jax.nn.silu(gate) * up).astype(jnp.bfloat16)
    gram_sum = gram_of(act)
    made = jnp.dot(act, w_down, preferred_element_type=jnp.float32).astype(jnp.bfloat16)
    return (gram_sum, made)


def weights_for_me(routes, probs, experts):
    names = routes.T[None, :, :] == jnp.arange(experts, dtype=jnp.int32)[:, None, None]
    weight = jnp.sum(jnp.where(names, probs.T[None, :, :], 0.0), axis=1)
    mine = jnp.where(jnp.any(names, axis=1), weight, -1.0)
    return lax.all_to_all(mine, "expert", split_axis=0, concat_axis=0, tiled=True)


def summed(*parts):
    total = parts[0].astype(jnp.float32)
    for part in parts[1:]:
        total = total + part.astype(jnp.float32)
    return total.astype(jnp.bfloat16)


def plane_kernel(capacity, k, parts, spots, weight, *refs):
    xs, refs = refs[:parts], refs[parts:]
    w_gate, w_up, w_down, keep, give, act, rows, ranks = refs
    blocks, tok = weight.shape
    slots, hidden = act.shape
    features = rows.shape[1]
    wide, cut = 256, 512
    named = (weight[...] >= 0.0).astype(jnp.float32)
    lane = lax.broadcasted_iota(jnp.int32, (tok, tok), 0)
    below = (lane < lax.broadcasted_iota(jnp.int32, (tok, tok), 1)).astype(jnp.float32)
    within = jnp.dot(named, below, preferred_element_type=jnp.float32)
    totals = jnp.broadcast_to(jnp.sum(named, axis=1, keepdims=True), (blocks, tok))
    row = lax.broadcasted_iota(jnp.int32, (blocks, blocks), 0)
    earlier = (lax.broadcasted_iota(jnp.int32, (blocks, blocks), 1) < row).astype(jnp.float32)
    before = jnp.dot(earlier, totals, preferred_element_type=jnp.float32)
    rank = within + before
    kept = (named > 0.0) & (rank < capacity)
    order = [spots[4 * k + i] for i in range(4)]
    first = order[0] // 4 * 4
    block_row = lax.broadcasted_iota(jnp.int32, (blocks, tok), 0)
    start = jnp.sum(jnp.where(block_row == first, before, 0.0), axis=0, keepdims=True)
    ranks[...] = jnp.where(kept, rank - start, -1.0)
    place = jnp.concatenate([ranks[pl.ds(i, 1), :] for i in order], axis=1)
    share = jnp.concatenate([weight[pl.ds(i, 1), :] for i in order], axis=1)
    slot = lax.broadcasted_iota(jnp.int32, (slots, 4 * tok), 0).astype(jnp.float32)
    hits = slot == place
    scale = jnp.sum(jnp.where(hits, share, 0.0), axis=1, keepdims=True)
    select = hits.astype(jnp.float32).astype(jnp.bfloat16)
    for i in range(features // cut):
        span = pl.ds(i * cut, cut)
        x = jnp.concatenate([block[:, span] for block in xs], axis=0)
        rows[:, span] = jnp.dot(select, x, preferred_element_type=jnp.float32).astype(jnp.bfloat16)
    for i in range(hidden // wide):
        span = pl.ds(i * wide, wide)
        gate = jnp.dot(rows[...], w_gate[:, span], preferred_element_type=jnp.float32)
        up = jnp.dot(rows[...], w_up[:, span], preferred_element_type=jnp.float32)
        act[:, span] = (gate / (1.0 + jnp.exp(-gate)) * up).astype(jnp.bfloat16)
    back = select.T
    for i in range(features // cut):
        span = pl.ds(i * cut, cut)
        result = jnp.dot(act[...], w_down[:, span], preferred_element_type=jnp.float32)
        made = (result * scale).astype(jnp.bfloat16)
        spread = jnp.dot(back, made, preferred_element_type=jnp.float32).astype(jnp.bfloat16)
        keep[:, span] = spread[: 2 * tok]
        give[:, span] = spread[2 * tok :]


def plane_pass(k, spots, weight, xs, w_gate, w_up, w_down, slots, capacity):
    tok, features = weight.shape[1], w_gate.shape[0]
    hidden = w_gate.shape[1]
    half = jax.ShapeDtypeStruct((2 * tok, features), jnp.bfloat16)
    rows = 4 * slots
    flops = 2 * rows * (3 * features * hidden + 8 * tok * features)
    moved = 2 * (3 * features * hidden + 8 * tok * features)
    return pl.pallas_call(
        functools.partial(plane_kernel, capacity, k, len(xs)),
        out_shape=(half, half, jax.ShapeDtypeStruct((rows, hidden), jnp.bfloat16)),
        in_specs=[pl.BlockSpec(memory_space=pltpu.SMEM)]
        + [pl.BlockSpec(memory_space=pltpu.VMEM)] * (len(xs) + 4),
        out_specs=[pl.BlockSpec(memory_space=pltpu.VMEM)] * 3,
        scratch_shapes=[
            pltpu.VMEM((rows, features), jnp.bfloat16),
            pltpu.VMEM(weight.shape, jnp.float32),
        ],
        compiler_params=pltpu.CompilerParams(vmem_limit_bytes=12 * 1024 * 1024),
        cost_estimate=pl.CostEstimate(
            flops=flops, bytes_accessed=moved, transcendentals=rows * hidden
        ),
    )(spots, weight, *xs, w_gate, w_up, w_down)


def staged(routes, probs, tokens, w_gate, w_up, w_down):
    tok, top = routes.shape
    size = lax.axis_size("expert")
    slots = 5 * tok * top // (4 * size)
    capacity = tok * top // 2
    half = tok // 2
    me = lax.axis_index("expert")
    z, y, core = me // 4, me // 2 % 2, me % 2

    def swapped(array, bit):
        return lax.ppermute(array, "expert", [(i, i ^ bit) for i in range(size)])

    sibling = functools.partial(swapped, bit=1)
    column = functools.partial(swapped, bit=2)
    pair = functools.partial(swapped, bit=4)
    far = functools.partial(swapped, bit=8)

    def together(*arrays):
        return lax.optimization_barrier(arrays)

    spots = jnp.stack(
        [
            (z ^ k) * 4 + (y ^ column_bit) * 2 + (core ^ core_bit)
            for k in range(4)
            for core_bit in range(2)
            for column_bit in range(2)
        ]
    ).astype(jnp.int32)

    def expert(k, *xs):
        return plane_pass(k, spots, weight, xs, w_gate, w_up, w_down, slots, capacity)

    weight = weights_for_me(routes, probs, size)
    a0 = tokens
    a1, low, b0, c0, weight = together(
        pair(a0), far(a0[:half]), column(a0), sibling(a0), weight
    )
    b1 = column(a1)
    high = far(a0[half:])
    d0 = sibling(b0)
    c1 = sibling(a1)
    keep0, give0, act0 = expert(0, a0, b0, c0, d0)
    high, b1, c1, keep0, give0, act0 = together(high, b1, c1, keep0, give0, act0)
    a2 = jnp.concatenate([low, high], axis=0)
    a3 = pair(a2)
    b2 = column(a2)
    d1 = sibling(b1)
    c2 = sibling(a2)
    keep1, give1, act1 = expert(1, a1, b1, c1, d1)
    a3, b2, c2, keep1, give1, act1 = together(a3, b2, c2, keep1, give1, act1)
    b3_low = pair(b2[:half])
    b3_high = column(a3[half:])
    d2 = sibling(b2)
    c3 = sibling(a3)
    got1 = sibling(give1)
    keep2, give2, act2 = expert(2, a2, b2, c2, d2)
    b3_low, b3_high, c3, got1, keep2, give2, act2 = together(
        b3_low, b3_high, c3, got1, keep2, give2, act2
    )
    d3_low = sibling(b3_low)
    d3_high = sibling(b3_high)
    came1 = column(summed(keep1[tok:], got1[tok:]))
    got2 = sibling(give2)
    keep3, give3, act3 = expert(3, a3, b3_low, b3_high, c3, d3_low, d3_high)

    keep3, give3, act3, got2, came1 = together(keep3, give3, act3, got2, came1)
    got3 = sibling(give3)
    got0 = sibling(give0)
    got3, got0 = together(got3, got0)
    low = pair(summed(keep3[tok : tok + half], got3[tok : tok + half]))
    high = column(summed(keep3[tok + half :], got3[tok + half :]))
    low, high = together(low, high)
    far3 = jnp.concatenate(
        [summed(keep3[:half], got3[:half]), summed(keep3[half:tok], got3[half:tok], high)], axis=0
    )
    side2 = jnp.concatenate(
        [
            summed(keep2[tok : tok + half], got2[tok : tok + half], low),
            summed(keep2[tok + half :], got2[tok + half :]),
        ],
        axis=0,
    )
    near1 = summed(keep1[:tok], got1[:tok], came1)
    side0 = summed(keep0[tok:], got0[tok:])
    far3, side2, near1, side0 = together(pair(far3), column(side2), near1, side0)
    last2 = far(summed(keep2[:tok], got2[:tok], far3, side2))
    last1 = pair(near1)
    last0 = column(side0)
    mixed = summed(keep0[:tok], got0[:tok], last0, last1, last2)

    acts = jnp.concatenate([act0, act1, act2, act3], axis=0)
    count = jnp.minimum(jnp.sum((weight >= 0.0).astype(jnp.float32)), float(capacity))
    gram = gram_of(acts) * (2.0 / count)
    return gram[None], mixed


def gathered(routes, probs, tokens, w_gate, w_up, w_down):
    tok_rows, top = routes.shape
    size = lax.axis_size("expert")
    capacity = tok_rows * top // 2
    every_token = lax.all_gather(tokens, "expert", tiled=True)
    weight = weights_for_me(routes, probs, size)
    named = (weight >= 0.0).astype(jnp.int32)
    within = jnp.cumsum(named, axis=1) - named
    per_device = jnp.sum(named, axis=1)
    before = jnp.cumsum(per_device) - per_device
    rank = within + before[:, None]
    kept = (named == 1) & (rank < capacity)
    count = jnp.minimum(jnp.sum(per_device), capacity)
    slot = jnp.where(kept, rank, -1).reshape(size * tok_rows)
    place = jnp.arange(capacity, dtype=jnp.int32)
    select = (place[:, None] == slot[None, :]).astype(jnp.bfloat16)
    rows = jnp.dot(select, every_token, preferred_element_type=jnp.float32).astype(jnp.bfloat16)
    gram_sum, made = expert_pass(rows, w_gate, w_up, w_down)
    gram = gram_sum * (2.0 / count.astype(jnp.float32))
    spread = lax.dot_general(
        select, made, (((0,), (0,)), ((), ())), preferred_element_type=jnp.float32
    )
    partial = (spread * weight.reshape(size * tok_rows, 1)).astype(jnp.bfloat16)
    mixed = lax.psum_scatter(partial, "expert", scatter_dimension=0, tiled=True)
    return gram[None], mixed.astype(jnp.bfloat16)


def shards(routes, probs, tokens, gate_weight, up_weight, down_weight):
    body = staged if lax.axis_size("expert") == 16 else gathered
    return body(routes, probs, tokens, gate_weight[0], up_weight[0], down_weight[0])


def solution(mesh):
    placed = (
        P(("parts", "expert"), None),
        P(("parts", "expert"), None),
        P(("parts", "expert"), None),
        P("expert", None, None),
        P("expert", None, None),
        P("expert", None, None),
    )
    return jax.shard_map(
        shards,
        mesh=mesh,
        in_specs=placed,
        out_specs=(P(("parts", "expert"), None, None), P(("parts", "expert"), None)),
        check_vma=False,
    )
```

```python
import functools

import jax
import jax.numpy as jnp
from jax import lax
from jax.experimental import pallas as pl
from jax.experimental.pallas import tpu as pltpu
from jax.sharding import PartitionSpec as P


def gram_of(rows):
    return lax.dot_general(rows, rows, (((0,), (0,)), ((), ())), preferred_element_type=jnp.float32)


def expert_pass(rows, w_gate, w_up, w_down):
    gate = jnp.dot(rows, w_gate, preferred_element_type=jnp.float32)
    up = jnp.dot(rows, w_up, preferred_element_type=jnp.float32)
    act = (jax.nn.silu(gate) * up).astype(jnp.bfloat16)
    gram_sum = gram_of(act)
    made = jnp.dot(act, w_down, preferred_element_type=jnp.float32).astype(jnp.bfloat16)
    return (gram_sum, made)


def weights_for_me(routes, probs, experts):
    names = routes.T[None, :, :] == jnp.arange(experts, dtype=jnp.int32)[:, None, None]
    weight = jnp.sum(jnp.where(names, probs.T[None, :, :], 0.0), axis=1)
    mine = jnp.where(jnp.any(names, axis=1), weight, -1.0)
    return lax.all_to_all(mine, "expert", split_axis=0, concat_axis=0, tiled=True)


def summed(*parts):
    total = parts[0].astype(jnp.float32)
    for part in parts[1:]:
        total = total + part.astype(jnp.float32)
    return total.astype(jnp.bfloat16)


def plane_kernel(capacity, k, parts, spots, weight, *refs):
    xs, refs = refs[:parts], refs[parts:]
    w_gate, w_up, w_down, keep, give, act, rows, ranks = refs
    blocks, tok = weight.shape
    slots, hidden = act.shape
    features = rows.shape[1]
    wide, cut = 256, 512
    named = (weight[...] >= 0.0).astype(jnp.float32)
    lane = lax.broadcasted_iota(jnp.int32, (tok, tok), 0)
    below = (lane < lax.broadcasted_iota(jnp.int32, (tok, tok), 1)).astype(jnp.float32)
    within = jnp.dot(named, below, preferred_element_type=jnp.float32)
    totals = jnp.broadcast_to(jnp.sum(named, axis=1, keepdims=True), (blocks, tok))
    row = lax.broadcasted_iota(jnp.int32, (blocks, blocks), 0)
    earlier = (lax.broadcasted_iota(jnp.int32, (blocks, blocks), 1) < row).astype(jnp.float32)
    before = jnp.dot(earlier, totals, preferred_element_type=jnp.float32)
    rank = within + before
    kept = (named > 0.0) & (rank < capacity)
    order = [spots[4 * k + i] for i in range(4)]
    first = order[0] // 4 * 4
    block_row = lax.broadcasted_iota(jnp.int32, (blocks, tok), 0)
    start = jnp.sum(jnp.where(block_row == first, before, 0.0), axis=0, keepdims=True)
    ranks[...] = jnp.where(kept, rank - start, -1.0)
    place = jnp.concatenate([ranks[pl.ds(i, 1), :] for i in order], axis=1)
    share = jnp.concatenate([weight[pl.ds(i, 1), :] for i in order], axis=1)
    slot = lax.broadcasted_iota(jnp.int32, (slots, 4 * tok), 0).astype(jnp.float32)
    hits = slot == place
    scale = jnp.sum(jnp.where(hits, share, 0.0), axis=1, keepdims=True)
    select = hits.astype(jnp.float32).astype(jnp.bfloat16)
    for i in range(features // cut):
        span = pl.ds(i * cut, cut)
        x = jnp.concatenate([block[:, span] for block in xs], axis=0)
        rows[:, span] = jnp.dot(select, x, preferred_element_type=jnp.float32).astype(jnp.bfloat16)
    for i in range(hidden // wide):
        span = pl.ds(i * wide, wide)
        gate = jnp.dot(rows[...], w_gate[:, span], preferred_element_type=jnp.float32)
        up = jnp.dot(rows[...], w_up[:, span], preferred_element_type=jnp.float32)
        act[:, span] = (gate / (1.0 + jnp.exp(-gate)) * up).astype(jnp.bfloat16)
    back = select.T
    for i in range(features // cut):
        span = pl.ds(i * cut, cut)
        result = jnp.dot(act[...], w_down[:, span], preferred_element_type=jnp.float32)
        made = (result * scale).astype(jnp.bfloat16)
        spread = jnp.dot(back, made, preferred_element_type=jnp.float32).astype(jnp.bfloat16)
        keep[:, span] = spread[: 2 * tok]
        give[:, span] = spread[2 * tok :]


def plane_pass(k, spots, weight, xs, w_gate, w_up, w_down, slots, capacity):
    tok, features = weight.shape[1], w_gate.shape[0]
    hidden = w_gate.shape[1]
    half = jax.ShapeDtypeStruct((2 * tok, features), jnp.bfloat16)
    rows = 4 * slots
    flops = 2 * rows * (3 * features * hidden + 8 * tok * features)
    moved = 2 * (3 * features * hidden + 8 * tok * features)
    return pl.pallas_call(
        functools.partial(plane_kernel, capacity, k, len(xs)),
        out_shape=(half, half, jax.ShapeDtypeStruct((rows, hidden), jnp.bfloat16)),
        in_specs=[pl.BlockSpec(memory_space=pltpu.SMEM)]
        + [pl.BlockSpec(memory_space=pltpu.VMEM)] * (len(xs) + 4),
        out_specs=[pl.BlockSpec(memory_space=pltpu.VMEM)] * 3,
        scratch_shapes=[
            pltpu.VMEM((rows, features), jnp.bfloat16),
            pltpu.VMEM(weight.shape, jnp.float32),
        ],
        compiler_params=pltpu.CompilerParams(vmem_limit_bytes=12 * 1024 * 1024),
        cost_estimate=pl.CostEstimate(
            flops=flops, bytes_accessed=moved, transcendentals=rows * hidden
        ),
    )(spots, weight, *xs, w_gate, w_up, w_down)


def staged(routes, probs, tokens, w_gate, w_up, w_down):
    tok, top = routes.shape
    size = lax.axis_size("expert")
    slots = 5 * tok * top // (4 * size)
    capacity = tok * top // 2
    half = tok // 2
    me = lax.axis_index("expert")
    z, y, core = me // 4, me // 2 % 2, me % 2

    def swapped(array, bit):
        return lax.ppermute(array, "expert", [(i, i ^ bit) for i in range(size)])

    sibling = functools.partial(swapped, bit=1)
    column = functools.partial(swapped, bit=2)
    pair = functools.partial(swapped, bit=4)
    far = functools.partial(swapped, bit=8)

    def together(*arrays):
        return lax.optimization_barrier(arrays)

    spots = jnp.stack(
        [
            (z ^ k) * 4 + (y ^ column_bit) * 2 + (core ^ core_bit)
            for k in range(4)
            for core_bit in range(2)
            for column_bit in range(2)
        ]
    ).astype(jnp.int32)

    def expert(k, *xs):
        return plane_pass(k, spots, weight, xs, w_gate, w_up, w_down, slots, capacity)

    weight = weights_for_me(routes, probs, size)
    a0 = tokens
    a1, a2, b0, c0, weight = together(pair(a0), far(a0), column(a0), sibling(a0), weight)
    a3 = pair(a2)
    b1 = column(a1)
    d0 = sibling(b0)
    c1 = sibling(a1)
    keep0, give0, act0 = expert(0, a0, b0, c0, d0)
    a3, b1, c1, keep0, give0, act0 = together(a3, b1, c1, keep0, give0, act0)
    b2 = column(a2)
    b3_low = far(b1[:half])
    d1 = sibling(b1)
    c2 = sibling(a2)
    got0 = sibling(give0)
    keep1, give1, act1 = expert(1, a1, b1, c1, d1)
    b2, b3_low, c2, got0, keep1, give1, act1 = together(b2, b3_low, c2, got0, keep1, give1, act1)
    b3_high = column(a3[half:])
    d2 = sibling(b2)
    c3 = sibling(a3)
    d3_low = sibling(b3_low)
    got1 = sibling(give1)
    keep2, give2, act2 = expert(2, a2, b2, c2, d2)
    b3_high, c3, d3_low, got1, keep2, give2, act2 = together(
        b3_high, c3, d3_low, got1, keep2, give2, act2
    )
    d3_high = sibling(b3_high)
    got2 = sibling(give2)
    came1 = column(summed(keep1[tok:], got1[tok:]))
    keep3, give3, act3 = expert(3, a3, b3_low, b3_high, c3, d3_low, d3_high)
    keep3, give3, act3, got2 = together(keep3, give3, act3, got2)

    got3, came1 = together(sibling(give3), came1)
    low = pair(summed(keep3[tok : tok + half], got3[tok : tok + half]))
    high = column(summed(keep3[tok + half :], got3[tok + half :]))
    low, high = together(low, high)
    far3 = jnp.concatenate(
        [summed(keep3[:half], got3[:half]), summed(keep3[half:tok], got3[half:tok], high)], axis=0
    )
    side2 = jnp.concatenate(
        [
            summed(keep2[tok : tok + half], got2[tok : tok + half], low),
            summed(keep2[tok + half :], got2[tok + half :]),
        ],
        axis=0,
    )
    near1 = summed(keep1[:tok], got1[:tok], came1)
    side0 = summed(keep0[tok:], got0[tok:])
    far3, side2, near1, side0 = together(pair(far3), column(side2), near1, side0)
    far2, near1, side0 = together(
        summed(keep2[:tok], got2[:tok], far3, side2), near1, side0
    )
    mixed = summed(keep0[:tok], got0[:tok], far(far2), pair(near1), column(side0))

    acts = jnp.concatenate([act0, act1, act2, act3], axis=0)
    count = jnp.minimum(jnp.sum((weight >= 0.0).astype(jnp.float32)), float(capacity))
    gram = gram_of(acts) * (2.0 / count)
    return gram[None], mixed


def gathered(routes, probs, tokens, w_gate, w_up, w_down):
    tok_rows, top = routes.shape
    size = lax.axis_size("expert")
    capacity = tok_rows * top // 2
    every_token = lax.all_gather(tokens, "expert", tiled=True)
    weight = weights_for_me(routes, probs, size)
    named = (weight >= 0.0).astype(jnp.int32)
    within = jnp.cumsum(named, axis=1) - named
    per_device = jnp.sum(named, axis=1)
    before = jnp.cumsum(per_device) - per_device
    rank = within + before[:, None]
    kept = (named == 1) & (rank < capacity)
    count = jnp.minimum(jnp.sum(per_device), capacity)
    slot = jnp.where(kept, rank, -1).reshape(size * tok_rows)
    place = jnp.arange(capacity, dtype=jnp.int32)
    select = (place[:, None] == slot[None, :]).astype(jnp.bfloat16)
    rows = jnp.dot(select, every_token, preferred_element_type=jnp.float32).astype(jnp.bfloat16)
    gram_sum, made = expert_pass(rows, w_gate, w_up, w_down)
    gram = gram_sum * (2.0 / count.astype(jnp.float32))
    spread = lax.dot_general(
        select, made, (((0,), (0,)), ((), ())), preferred_element_type=jnp.float32
    )
    partial = (spread * weight.reshape(size * tok_rows, 1)).astype(jnp.bfloat16)
    mixed = lax.psum_scatter(partial, "expert", scatter_dimension=0, tiled=True)
    return gram[None], mixed.astype(jnp.bfloat16)


def shards(routes, probs, tokens, gate_weight, up_weight, down_weight):
    body = staged if lax.axis_size("expert") == 16 else gathered
    return body(routes, probs, tokens, gate_weight[0], up_weight[0], down_weight[0])


def solution(mesh):
    placed = (
        P(("parts", "expert"), None),
        P(("parts", "expert"), None),
        P(("parts", "expert"), None),
        P("expert", None, None),
        P("expert", None, None),
        P("expert", None, None),
    )
    return jax.shard_map(
        shards,
        mesh=mesh,
        in_specs=placed,
        out_specs=(P(("parts", "expert"), None, None), P(("parts", "expert"), None)),
        check_vma=False,
    )
```

```python
import functools

import jax
import jax.numpy as jnp
from jax import lax
from jax.experimental import pallas as pl
from jax.experimental.pallas import tpu as pltpu
from jax.sharding import PartitionSpec as P


def gram_of(rows):
    return lax.dot_general(rows, rows, (((0,), (0,)), ((), ())), preferred_element_type=jnp.float32)


def expert_pass(rows, w_gate, w_up, w_down):
    gate = jnp.dot(rows, w_gate, preferred_element_type=jnp.float32)
    up = jnp.dot(rows, w_up, preferred_element_type=jnp.float32)
    act = (jax.nn.silu(gate) * up).astype(jnp.bfloat16)
    gram_sum = gram_of(act)
    made = jnp.dot(act, w_down, preferred_element_type=jnp.float32).astype(jnp.bfloat16)
    return (gram_sum, made)


def weights_for_me(routes, probs, experts):
    names = routes.T[None, :, :] == jnp.arange(experts, dtype=jnp.int32)[:, None, None]
    weight = jnp.sum(jnp.where(names, probs.T[None, :, :], 0.0), axis=1)
    mine = jnp.where(jnp.any(names, axis=1), weight, -1.0)
    return lax.all_to_all(mine, "expert", split_axis=0, concat_axis=0, tiled=True)


def summed(*parts):
    total = parts[0].astype(jnp.float32)
    for part in parts[1:]:
        total = total + part.astype(jnp.float32)
    return total.astype(jnp.bfloat16)


def plane_kernel(capacity, k, parts, spots, weight, *refs):
    xs, refs = refs[:parts], refs[parts:]
    w_gate, w_up, w_down, keep, give, act, rows, ranks = refs
    blocks, tok = weight.shape
    slots, hidden = act.shape
    features = rows.shape[1]
    wide, cut = 256, 512
    named = (weight[...] >= 0.0).astype(jnp.float32)
    lane = lax.broadcasted_iota(jnp.int32, (tok, tok), 0)
    below = (lane < lax.broadcasted_iota(jnp.int32, (tok, tok), 1)).astype(jnp.float32)
    within = jnp.dot(named, below, preferred_element_type=jnp.float32)
    totals = jnp.broadcast_to(jnp.sum(named, axis=1, keepdims=True), (blocks, tok))
    row = lax.broadcasted_iota(jnp.int32, (blocks, blocks), 0)
    earlier = (lax.broadcasted_iota(jnp.int32, (blocks, blocks), 1) < row).astype(jnp.float32)
    before = jnp.dot(earlier, totals, preferred_element_type=jnp.float32)
    rank = within + before
    kept = (named > 0.0) & (rank < capacity)
    order = [spots[4 * k + i] for i in range(4)]
    first = order[0] // 4 * 4
    block_row = lax.broadcasted_iota(jnp.int32, (blocks, tok), 0)
    start = jnp.sum(jnp.where(block_row == first, before, 0.0), axis=0, keepdims=True)
    ranks[...] = jnp.where(kept, rank - start, -1.0)
    place = jnp.concatenate([ranks[pl.ds(i, 1), :] for i in order], axis=1)
    share = jnp.concatenate([weight[pl.ds(i, 1), :] for i in order], axis=1)
    slot = lax.broadcasted_iota(jnp.int32, (slots, 4 * tok), 0).astype(jnp.float32)
    hits = slot == place
    scale = jnp.sum(jnp.where(hits, share, 0.0), axis=1, keepdims=True)
    select = hits.astype(jnp.float32).astype(jnp.bfloat16)
    for i in range(features // cut):
        span = pl.ds(i * cut, cut)
        x = jnp.concatenate([block[:, span] for block in xs], axis=0)
        rows[:, span] = jnp.dot(select, x, preferred_element_type=jnp.float32).astype(jnp.bfloat16)
    for i in range(hidden // wide):
        span = pl.ds(i * wide, wide)
        gate = jnp.dot(rows[...], w_gate[:, span], preferred_element_type=jnp.float32)
        up = jnp.dot(rows[...], w_up[:, span], preferred_element_type=jnp.float32)
        act[:, span] = (gate / (1.0 + jnp.exp(-gate)) * up).astype(jnp.bfloat16)
    back = select.T
    for i in range(features // cut):
        span = pl.ds(i * cut, cut)
        result = jnp.dot(act[...], w_down[:, span], preferred_element_type=jnp.float32)
        made = (result * scale).astype(jnp.bfloat16)
        spread = jnp.dot(back, made, preferred_element_type=jnp.float32).astype(jnp.bfloat16)
        keep[:, span] = spread[: 2 * tok]
        give[:, span] = spread[2 * tok :]


def plane_pass(k, spots, weight, xs, w_gate, w_up, w_down, slots, capacity):
    tok, features = weight.shape[1], w_gate.shape[0]
    hidden = w_gate.shape[1]
    half = jax.ShapeDtypeStruct((2 * tok, features), jnp.bfloat16)
    rows = 4 * slots
    flops = 2 * rows * (3 * features * hidden + 8 * tok * features)
    moved = 2 * (3 * features * hidden + 8 * tok * features)
    return pl.pallas_call(
        functools.partial(plane_kernel, capacity, k, len(xs)),
        out_shape=(half, half, jax.ShapeDtypeStruct((rows, hidden), jnp.bfloat16)),
        in_specs=[pl.BlockSpec(memory_space=pltpu.SMEM)]
        + [pl.BlockSpec(memory_space=pltpu.VMEM)] * (len(xs) + 4),
        out_specs=[pl.BlockSpec(memory_space=pltpu.VMEM)] * 3,
        scratch_shapes=[
            pltpu.VMEM((rows, features), jnp.bfloat16),
            pltpu.VMEM(weight.shape, jnp.float32),
        ],
        compiler_params=pltpu.CompilerParams(vmem_limit_bytes=12 * 1024 * 1024),
        cost_estimate=pl.CostEstimate(
            flops=flops, bytes_accessed=moved, transcendentals=rows * hidden
        ),
    )(spots, weight, *xs, w_gate, w_up, w_down)


def staged(routes, probs, tokens, w_gate, w_up, w_down):
    tok, top = routes.shape
    size = lax.axis_size("expert")
    slots = 5 * tok * top // (4 * size)
    capacity = tok * top // 2
    half = tok // 2
    me = lax.axis_index("expert")
    z, y, core = me // 4, me // 2 % 2, me % 2

    def swapped(array, bit):
        return lax.ppermute(array, "expert", [(i, i ^ bit) for i in range(size)])

    sibling = functools.partial(swapped, bit=1)
    column = functools.partial(swapped, bit=2)
    pair = functools.partial(swapped, bit=4)
    far = functools.partial(swapped, bit=8)

    def together(*arrays):
        return lax.optimization_barrier(arrays)

    spots = jnp.stack(
        [
            (z ^ k) * 4 + (y ^ column_bit) * 2 + (core ^ core_bit)
            for k in range(4)
            for core_bit in range(2)
            for column_bit in range(2)
        ]
    ).astype(jnp.int32)

    def expert(k, *xs):
        return plane_pass(k, spots, weight, xs, w_gate, w_up, w_down, slots, capacity)

    weight = weights_for_me(routes, probs, size)
    a0 = tokens
    a1, b0, c0, weight = together(pair(a0), column(a0), sibling(a0), weight)
    a2 = far(a0)
    b1 = column(a1)
    d0 = sibling(b0)
    c1 = sibling(a1)
    keep0, give0, act0 = expert(0, a0, b0, c0, d0)
    a2, b1, c1, keep0, give0, act0 = together(a2, b1, c1, keep0, give0, act0)
    a3 = pair(a2)
    b2 = column(a2)
    d1 = sibling(b1)
    c2 = sibling(a2)
    got0 = sibling(give0)
    keep1, give1, act1 = expert(1, a1, b1, c1, d1)
    got1 = sibling(give1)
    a3, b2, c2, got0, got1, keep1, act1 = together(a3, b2, c2, got0, got1, keep1, act1)
    b3 = pair(b2)
    came1 = column(summed(keep1[tok:], got1[tok:]))
    d2 = sibling(b2)
    c3 = sibling(a3)
    keep2, give2, act2 = expert(2, a2, b2, c2, d2)
    b3, came1, c3, keep2, give2, act2 = together(b3, came1, c3, keep2, give2, act2)
    d3 = sibling(b3)
    got2 = sibling(give2)
    keep3, give3, act3 = expert(3, a3, b3, c3, d3)
    keep3, give3, act3, got2 = together(keep3, give3, act3, got2)

    got3 = sibling(give3)
    low = pair(summed(keep3[tok : tok + half], got3[tok : tok + half]))
    high = column(summed(keep3[tok + half :], got3[tok + half :]))
    low, high = together(low, high)
    far3 = jnp.concatenate(
        [summed(keep3[:half], got3[:half]), summed(keep3[half:tok], got3[half:tok], high)], axis=0
    )
    side2 = jnp.concatenate(
        [
            summed(keep2[tok : tok + half], got2[tok : tok + half], low),
            summed(keep2[tok + half :], got2[tok + half :]),
        ],
        axis=0,
    )
    near1 = summed(keep1[:tok], got1[:tok], came1)
    side0 = summed(keep0[tok:], got0[tok:])
    far3, side2, near1, side0 = together(pair(far3), column(side2), near1, side0)
    far2, near1, side0 = together(
        summed(keep2[:tok], got2[:tok], far3, side2), near1, side0
    )
    mixed = summed(keep0[:tok], got0[:tok], far(far2), pair(near1), column(side0))

    acts = jnp.concatenate([act0, act1, act2, act3], axis=0)
    count = jnp.minimum(jnp.sum((weight >= 0.0).astype(jnp.float32)), float(capacity))
    gram = gram_of(acts) * (2.0 / count)
    return gram[None], mixed


def gathered(routes, probs, tokens, w_gate, w_up, w_down):
    tok_rows, top = routes.shape
    size = lax.axis_size("expert")
    capacity = tok_rows * top // 2
    every_token = lax.all_gather(tokens, "expert", tiled=True)
    weight = weights_for_me(routes, probs, size)
    named = (weight >= 0.0).astype(jnp.int32)
    within = jnp.cumsum(named, axis=1) - named
    per_device = jnp.sum(named, axis=1)
    before = jnp.cumsum(per_device) - per_device
    rank = within + before[:, None]
    kept = (named == 1) & (rank < capacity)
    count = jnp.minimum(jnp.sum(per_device), capacity)
    slot = jnp.where(kept, rank, -1).reshape(size * tok_rows)
    place = jnp.arange(capacity, dtype=jnp.int32)
    select = (place[:, None] == slot[None, :]).astype(jnp.bfloat16)
    rows = jnp.dot(select, every_token, preferred_element_type=jnp.float32).astype(jnp.bfloat16)
    gram_sum, made = expert_pass(rows, w_gate, w_up, w_down)
    gram = gram_sum * (2.0 / count.astype(jnp.float32))
    spread = lax.dot_general(
        select, made, (((0,), (0,)), ((), ())), preferred_element_type=jnp.float32
    )
    partial = (spread * weight.reshape(size * tok_rows, 1)).astype(jnp.bfloat16)
    mixed = lax.psum_scatter(partial, "expert", scatter_dimension=0, tiled=True)
    return gram[None], mixed.astype(jnp.bfloat16)


def shards(routes, probs, tokens, gate_weight, up_weight, down_weight):
    body = staged if lax.axis_size("expert") == 16 else gathered
    return body(routes, probs, tokens, gate_weight[0], up_weight[0], down_weight[0])


def solution(mesh):
    placed = (
        P(("parts", "expert"), None),
        P(("parts", "expert"), None),
        P(("parts", "expert"), None),
        P("expert", None, None),
        P("expert", None, None),
        P("expert", None, None),
    )
    return jax.shard_map(
        shards,
        mesh=mesh,
        in_specs=placed,
        out_specs=(P(("parts", "expert"), None, None), P(("parts", "expert"), None)),
        check_vma=False,
    )
```

```python
import functools

import jax
import jax.numpy as jnp
from jax import lax
from jax.experimental import pallas as pl
from jax.experimental.pallas import tpu as pltpu
from jax.sharding import PartitionSpec as P


def gram_of(rows):
    return lax.dot_general(rows, rows, (((0,), (0,)), ((), ())), preferred_element_type=jnp.float32)


def expert_pass(rows, w_gate, w_up, w_down):
    gate = jnp.dot(rows, w_gate, preferred_element_type=jnp.float32)
    up = jnp.dot(rows, w_up, preferred_element_type=jnp.float32)
    act = (jax.nn.silu(gate) * up).astype(jnp.bfloat16)
    gram_sum = gram_of(act)
    made = jnp.dot(act, w_down, preferred_element_type=jnp.float32).astype(jnp.bfloat16)
    return (gram_sum, made)


def weights_for_me(routes, probs, experts):
    names = routes.T[None, :, :] == jnp.arange(experts, dtype=jnp.int32)[:, None, None]
    weight = jnp.sum(jnp.where(names, probs.T[None, :, :], 0.0), axis=1)
    mine = jnp.where(jnp.any(names, axis=1), weight, -1.0)
    return lax.all_to_all(mine, "expert", split_axis=0, concat_axis=0, tiled=True)


def table_kernel(routes, probs, w_gate, w_up, w_down, mine):
    names, shares = routes[...], probs[...]
    for e in range(mine.shape[0]):
        hit = (names == e).astype(jnp.float32)
        named = jnp.sum(hit, axis=0, keepdims=True)
        share = jnp.sum(hit * shares, axis=0, keepdims=True)
        mine[pl.ds(e, 1), :] = jnp.where(named > 0.0, share, -1.0)


def table_pass(routes, probs, experts, w_gate, w_up, w_down):
    mine = pl.pallas_call(
        table_kernel,
        out_shape=jax.ShapeDtypeStruct((experts, routes.shape[0]), jnp.float32),
        in_specs=[pl.BlockSpec(memory_space=pltpu.VMEM)] * 5,
        out_specs=pl.BlockSpec(memory_space=pltpu.VMEM),
        compiler_params=pltpu.CompilerParams(vmem_limit_bytes=4 * 1024 * 1024),
    )(routes.T, probs.T, w_gate, w_up, w_down)
    return lax.all_to_all(mine, "expert", split_axis=0, concat_axis=0, tiled=True)


def summed(*parts):
    total = parts[0].astype(jnp.float32)
    for part in parts[1:]:
        total = total + part.astype(jnp.float32)
    return total.astype(jnp.bfloat16)


def plane_kernel(capacity, k, parts, spots, weight, *refs):
    xs, refs = refs[:parts], refs[parts:]
    w_gate, w_up, w_down, keep, give, act, rows, ranks = refs
    blocks, tok = weight.shape
    slots, hidden = act.shape
    features = rows.shape[1]
    wide, cut = 256, 512
    named = (weight[...] >= 0.0).astype(jnp.float32)
    lane = lax.broadcasted_iota(jnp.int32, (tok, tok), 0)
    below = (lane < lax.broadcasted_iota(jnp.int32, (tok, tok), 1)).astype(jnp.float32)
    within = jnp.dot(named, below, preferred_element_type=jnp.float32)
    totals = jnp.broadcast_to(jnp.sum(named, axis=1, keepdims=True), (blocks, tok))
    row = lax.broadcasted_iota(jnp.int32, (blocks, blocks), 0)
    earlier = (lax.broadcasted_iota(jnp.int32, (blocks, blocks), 1) < row).astype(jnp.float32)
    before = jnp.dot(earlier, totals, preferred_element_type=jnp.float32)
    rank = within + before
    kept = (named > 0.0) & (rank < capacity)
    order = [spots[4 * k + i] for i in range(4)]
    first = order[0] // 4 * 4
    block_row = lax.broadcasted_iota(jnp.int32, (blocks, tok), 0)
    start = jnp.sum(jnp.where(block_row == first, before, 0.0), axis=0, keepdims=True)
    ranks[...] = jnp.where(kept, rank - start, -1.0)
    place = jnp.concatenate([ranks[pl.ds(i, 1), :] for i in order], axis=1)
    share = jnp.concatenate([weight[pl.ds(i, 1), :] for i in order], axis=1)
    slot = lax.broadcasted_iota(jnp.int32, (slots, 4 * tok), 0).astype(jnp.float32)
    hits = slot == place
    scale = jnp.sum(jnp.where(hits, share, 0.0), axis=1, keepdims=True)
    select = hits.astype(jnp.float32).astype(jnp.bfloat16)
    for i in range(features // cut):
        span = pl.ds(i * cut, cut)
        x = jnp.concatenate([block[:, span] for block in xs], axis=0)
        rows[:, span] = jnp.dot(select, x, preferred_element_type=jnp.float32).astype(jnp.bfloat16)
    for i in range(hidden // wide):
        span = pl.ds(i * wide, wide)
        gate = jnp.dot(rows[...], w_gate[:, span], preferred_element_type=jnp.float32)
        up = jnp.dot(rows[...], w_up[:, span], preferred_element_type=jnp.float32)
        act[:, span] = (gate / (1.0 + jnp.exp(-gate)) * up).astype(jnp.bfloat16)
    back = select.T
    for i in range(features // cut):
        span = pl.ds(i * cut, cut)
        result = jnp.dot(act[...], w_down[:, span], preferred_element_type=jnp.float32)
        made = (result * scale).astype(jnp.bfloat16)
        spread = jnp.dot(back, made, preferred_element_type=jnp.float32).astype(jnp.bfloat16)
        keep[:, span] = spread[: 2 * tok]
        give[:, span] = spread[2 * tok :]


def plane_pass(k, spots, weight, xs, w_gate, w_up, w_down, slots, capacity):
    tok, features = weight.shape[1], w_gate.shape[0]
    hidden = w_gate.shape[1]
    half = jax.ShapeDtypeStruct((2 * tok, features), jnp.bfloat16)
    rows = 4 * slots
    flops = 2 * rows * (3 * features * hidden + 8 * tok * features)
    moved = 2 * (3 * features * hidden + 8 * tok * features)
    return pl.pallas_call(
        functools.partial(plane_kernel, capacity, k, len(xs)),
        out_shape=(half, half, jax.ShapeDtypeStruct((rows, hidden), jnp.bfloat16)),
        in_specs=[pl.BlockSpec(memory_space=pltpu.SMEM)]
        + [pl.BlockSpec(memory_space=pltpu.VMEM)] * (len(xs) + 4),
        out_specs=[pl.BlockSpec(memory_space=pltpu.VMEM)] * 3,
        scratch_shapes=[
            pltpu.VMEM((rows, features), jnp.bfloat16),
            pltpu.VMEM(weight.shape, jnp.float32),
        ],
        compiler_params=pltpu.CompilerParams(vmem_limit_bytes=12 * 1024 * 1024),
        cost_estimate=pl.CostEstimate(
            flops=flops, bytes_accessed=moved, transcendentals=rows * hidden
        ),
    )(spots, weight, *xs, w_gate, w_up, w_down)


def staged(routes, probs, tokens, w_gate, w_up, w_down):
    tok, top = routes.shape
    size = lax.axis_size("expert")
    slots = 5 * tok * top // (4 * size)
    capacity = tok * top // 2
    half = tok // 2
    me = lax.axis_index("expert")
    z, y, core = me // 4, me // 2 % 2, me % 2

    def swapped(array, bit):
        return lax.ppermute(array, "expert", [(i, i ^ bit) for i in range(size)])

    sibling = functools.partial(swapped, bit=1)
    column = functools.partial(swapped, bit=2)
    pair = functools.partial(swapped, bit=4)
    far = functools.partial(swapped, bit=8)

    def together(*arrays):
        return lax.optimization_barrier(arrays)

    spots = jnp.stack(
        [
            (z ^ k) * 4 + (y ^ column_bit) * 2 + (core ^ core_bit)
            for k in range(4)
            for core_bit in range(2)
            for column_bit in range(2)
        ]
    ).astype(jnp.int32)

    def expert(k, *xs):
        return plane_pass(k, spots, weight, xs, w_gate, w_up, w_down, slots, capacity)

    weight = table_pass(routes, probs, size, w_gate, w_up, w_down)
    a0 = tokens
    a1, low, b0, c0, weight = together(
        pair(a0), far(a0[:half]), column(a0), sibling(a0), weight
    )
    high = far(a0[half:])
    b1 = column(a1)
    d0 = sibling(b0)
    c1 = sibling(a1)
    keep0, give0, act0 = expert(0, a0, b0, c0, d0)
    high, b1, c1, keep0, give0, act0 = together(high, b1, c1, keep0, give0, act0)
    a2 = jnp.concatenate([low, high], axis=0)
    a3 = pair(a2)
    b2 = column(a2)
    d1 = sibling(b1)
    c2 = sibling(a2)
    keep1, give1, act1 = expert(1, a1, b1, c1, d1)
    a3, b2, c2, keep1, give1, act1 = together(a3, b2, c2, keep1, give1, act1)
    b3 = pair(b2)
    got1 = sibling(give1)
    came1 = column(summed(keep1[tok:], got1[tok:]))
    d2 = sibling(b2)
    c3 = sibling(a3)
    keep2, give2, act2 = expert(2, a2, b2, c2, d2)
    b3, came1, c3, keep2, give2, act2 = together(b3, came1, c3, keep2, give2, act2)
    d3 = sibling(b3)
    got2 = sibling(give2)
    keep3, give3, act3 = expert(3, a3, b3, c3, d3)
    keep3, give3, act3, got2 = together(keep3, give3, act3, got2)
    got0 = sibling(give0)

    got3 = sibling(give3)
    low = pair(summed(keep3[tok : tok + half], got3[tok : tok + half]))
    high = column(summed(keep3[tok + half :], got3[tok + half :]))
    low, high = together(low, high)
    far3 = jnp.concatenate(
        [summed(keep3[:half], got3[:half]), summed(keep3[half:tok], got3[half:tok], high)], axis=0
    )
    side2 = jnp.concatenate(
        [
            summed(keep2[tok : tok + half], got2[tok : tok + half], low),
            summed(keep2[tok + half :], got2[tok + half :]),
        ],
        axis=0,
    )
    near1 = summed(keep1[:tok], got1[:tok], came1)
    side0 = summed(keep0[tok:], got0[tok:])
    far3, side2, near1, side0 = together(pair(far3), column(side2), near1, side0)
    far2, near1, side0 = together(
        summed(keep2[:tok], got2[:tok], far3, side2), near1, side0
    )
    mixed = summed(keep0[:tok], got0[:tok], far(far2), pair(near1), column(side0))

    acts = jnp.concatenate([act0, act1, act2, act3], axis=0)
    count = jnp.minimum(jnp.sum((weight >= 0.0).astype(jnp.float32)), float(capacity))
    gram = gram_of(acts) * (2.0 / count)
    return gram[None], mixed


def gathered(routes, probs, tokens, w_gate, w_up, w_down):
    tok_rows, top = routes.shape
    size = lax.axis_size("expert")
    capacity = tok_rows * top // 2
    every_token = lax.all_gather(tokens, "expert", tiled=True)
    weight = weights_for_me(routes, probs, size)
    named = (weight >= 0.0).astype(jnp.int32)
    within = jnp.cumsum(named, axis=1) - named
    per_device = jnp.sum(named, axis=1)
    before = jnp.cumsum(per_device) - per_device
    rank = within + before[:, None]
    kept = (named == 1) & (rank < capacity)
    count = jnp.minimum(jnp.sum(per_device), capacity)
    slot = jnp.where(kept, rank, -1).reshape(size * tok_rows)
    place = jnp.arange(capacity, dtype=jnp.int32)
    select = (place[:, None] == slot[None, :]).astype(jnp.bfloat16)
    rows = jnp.dot(select, every_token, preferred_element_type=jnp.float32).astype(jnp.bfloat16)
    gram_sum, made = expert_pass(rows, w_gate, w_up, w_down)
    gram = gram_sum * (2.0 / count.astype(jnp.float32))
    spread = lax.dot_general(
        select, made, (((0,), (0,)), ((), ())), preferred_element_type=jnp.float32
    )
    partial = (spread * weight.reshape(size * tok_rows, 1)).astype(jnp.bfloat16)
    mixed = lax.psum_scatter(partial, "expert", scatter_dimension=0, tiled=True)
    return gram[None], mixed.astype(jnp.bfloat16)


def shards(routes, probs, tokens, gate_weight, up_weight, down_weight):
    body = staged if lax.axis_size("expert") == 16 else gathered
    return body(routes, probs, tokens, gate_weight[0], up_weight[0], down_weight[0])


def solution(mesh):
    placed = (
        P(("parts", "expert"), None),
        P(("parts", "expert"), None),
        P(("parts", "expert"), None),
        P("expert", None, None),
        P("expert", None, None),
        P("expert", None, None),
    )
    return jax.shard_map(
        shards,
        mesh=mesh,
        in_specs=placed,
        out_specs=(P(("parts", "expert"), None, None), P(("parts", "expert"), None)),
        check_vma=False,
    )
```

```python
import functools

import jax
import jax.numpy as jnp
from jax import lax
from jax.experimental import pallas as pl
from jax.experimental.pallas import tpu as pltpu
from jax.sharding import PartitionSpec as P


def gram_of(rows):
    return lax.dot_general(rows, rows, (((0,), (0,)), ((), ())), preferred_element_type=jnp.float32)


def expert_pass(rows, w_gate, w_up, w_down):
    gate = jnp.dot(rows, w_gate, preferred_element_type=jnp.float32)
    up = jnp.dot(rows, w_up, preferred_element_type=jnp.float32)
    act = (jax.nn.silu(gate) * up).astype(jnp.bfloat16)
    gram_sum = gram_of(act)
    made = jnp.dot(act, w_down, preferred_element_type=jnp.float32).astype(jnp.bfloat16)
    return (gram_sum, made)


def weights_for_me(routes, probs, experts):
    names = routes.T[None, :, :] == jnp.arange(experts, dtype=jnp.int32)[:, None, None]
    weight = jnp.sum(jnp.where(names, probs.T[None, :, :], 0.0), axis=1)
    mine = jnp.where(jnp.any(names, axis=1), weight, -1.0)
    return lax.all_to_all(mine, "expert", split_axis=0, concat_axis=0, tiled=True)


def table_kernel(routes, probs, w_gate, w_up, w_down, mine):
    names, shares = routes[...], probs[...]
    for e in range(mine.shape[0]):
        hit = (names == e).astype(jnp.float32)
        named = jnp.sum(hit, axis=0, keepdims=True)
        share = jnp.sum(hit * shares, axis=0, keepdims=True)
        mine[pl.ds(e, 1), :] = jnp.where(named > 0.0, share, -1.0)


def table_pass(routes, probs, experts, w_gate, w_up, w_down):
    mine = pl.pallas_call(
        table_kernel,
        out_shape=jax.ShapeDtypeStruct((experts, routes.shape[0]), jnp.float32),
        in_specs=[pl.BlockSpec(memory_space=pltpu.VMEM)] * 5,
        out_specs=pl.BlockSpec(memory_space=pltpu.VMEM),
        compiler_params=pltpu.CompilerParams(vmem_limit_bytes=4 * 1024 * 1024),
    )(routes.T, probs.T, w_gate, w_up, w_down)
    return lax.all_to_all(mine, "expert", split_axis=0, concat_axis=0, tiled=True)


def summed(*parts):
    total = parts[0].astype(jnp.float32)
    for part in parts[1:]:
        total = total + part.astype(jnp.float32)
    return total.astype(jnp.bfloat16)


def fill_tables(capacity, spots, weight, ranks, tables):
    blocks, tok = weight.shape
    named = (weight[...] >= 0.0).astype(jnp.float32)
    lane = lax.broadcasted_iota(jnp.int32, (tok, tok), 0)
    below = (lane < lax.broadcasted_iota(jnp.int32, (tok, tok), 1)).astype(jnp.float32)
    within = jnp.dot(named, below, preferred_element_type=jnp.float32)
    totals = jnp.broadcast_to(jnp.sum(named, axis=1, keepdims=True), (blocks, tok))
    row = lax.broadcasted_iota(jnp.int32, (blocks, blocks), 0)
    earlier = (lax.broadcasted_iota(jnp.int32, (blocks, blocks), 1) < row).astype(jnp.float32)
    before = jnp.dot(earlier, totals, preferred_element_type=jnp.float32)
    rank = within + before
    kept = (named > 0.0) & (rank < capacity)
    first = lax.broadcasted_iota(jnp.int32, (blocks, blocks), 0) // 4 * 4
    column = lax.broadcasted_iota(jnp.int32, (blocks, blocks), 1)
    start = jnp.dot((column < first).astype(jnp.float32), totals, preferred_element_type=jnp.float32)
    ranks[...] = jnp.where(kept, rank - start, -1.0)
    for k in range(blocks // 4):
        for i in range(4):
            span = pl.ds(i * tok, tok)
            tables[pl.ds(k, 1), span] = ranks[pl.ds(spots[4 * k + i], 1), :]
            tables[pl.ds(blocks // 4 + k, 1), span] = weight[pl.ds(spots[4 * k + i], 1), :]


def plane_kernel(k, tables, *refs):
    *xs, w_gate, w_up, w_down, keep, give, act, rows = refs
    slots, hidden = act.shape
    features = rows.shape[1]
    half, width = keep.shape[0], tables.shape[1]
    wide, cut = 256, 512
    place = tables[pl.ds(k, 1), :]
    share = tables[pl.ds(tables.shape[0] // 2 + k, 1), :]
    slot = lax.broadcasted_iota(jnp.int32, (slots, width), 0).astype(jnp.float32)
    hits = slot == place
    scale = jnp.sum(jnp.where(hits, share, 0.0), axis=1, keepdims=True)
    select = hits.astype(jnp.float32).astype(jnp.bfloat16)
    for i in range(features // cut):
        span = pl.ds(i * cut, cut)
        x = jnp.concatenate([block[:, span] for block in xs], axis=0)
        rows[:, span] = jnp.dot(select, x, preferred_element_type=jnp.float32).astype(jnp.bfloat16)
    for i in range(hidden // wide):
        span = pl.ds(i * wide, wide)
        gate = jnp.dot(rows[...], w_gate[:, span], preferred_element_type=jnp.float32)
        up = jnp.dot(rows[...], w_up[:, span], preferred_element_type=jnp.float32)
        act[:, span] = (gate / (1.0 + jnp.exp(-gate)) * up).astype(jnp.bfloat16)
    back = select.T
    for i in range(features // cut):
        span = pl.ds(i * cut, cut)
        result = jnp.dot(act[...], w_down[:, span], preferred_element_type=jnp.float32)
        made = (result * scale).astype(jnp.bfloat16)
        spread = jnp.dot(back, made, preferred_element_type=jnp.float32).astype(jnp.bfloat16)
        keep[:, span] = spread[:half]
        give[:, span] = spread[half:]


def first_kernel(capacity, spots, weight, *refs):
    *plane, tables, rows, ranks = refs
    fill_tables(capacity, spots, weight, ranks, tables)
    plane_kernel(0, tables, *plane, rows)


def plane_pass(k, tables, xs, w_gate, w_up, w_down, slots, first=None):
    tok, features = xs[0].shape
    hidden = w_gate.shape[1]
    rows = 4 * slots
    half = jax.ShapeDtypeStruct((2 * tok, features), jnp.bfloat16)
    outs = (half, half, jax.ShapeDtypeStruct((rows, hidden), jnp.bfloat16))
    scratch = [pltpu.VMEM((rows, features), jnp.bfloat16)]
    vmem = pl.BlockSpec(memory_space=pltpu.VMEM)
    if first is None:
        body, inputs, specs = functools.partial(plane_kernel, k), (tables,), [vmem]
    else:
        capacity, spots, weight = first
        body = functools.partial(first_kernel, capacity)
        inputs, specs = (spots, weight), [pl.BlockSpec(memory_space=pltpu.SMEM), vmem]
        outs += (jax.ShapeDtypeStruct((weight.shape[0] // 2, 4 * tok), jnp.float32),)
        scratch.append(pltpu.VMEM(weight.shape, jnp.float32))
    flops = 2 * rows * (3 * features * hidden + 8 * tok * features)
    moved = 2 * (3 * features * hidden + 8 * tok * features)
    return pl.pallas_call(
        body,
        out_shape=outs,
        in_specs=specs + [vmem] * (len(xs) + 3),
        out_specs=[vmem] * len(outs),
        scratch_shapes=scratch,
        compiler_params=pltpu.CompilerParams(vmem_limit_bytes=12 * 1024 * 1024),
        cost_estimate=pl.CostEstimate(
            flops=flops, bytes_accessed=moved, transcendentals=rows * hidden
        ),
    )(*inputs, *xs, w_gate, w_up, w_down)


def mix_kernel(keep, got, side, near_low, far_low, near_high, far_high, mixed):
    most, tok = near_low.shape[0], mixed.shape[0]
    for start, stop, near, far in ((0, most, near_low, far_low), (most, tok, near_high, far_high)):
        total = keep[start:stop, :].astype(jnp.float32) + got[start:stop, :].astype(jnp.float32)
        total = total + side[start:stop, :].astype(jnp.float32) + near[...].astype(jnp.float32)
        mixed[start:stop, :] = (total + far[...].astype(jnp.float32)).astype(mixed.dtype)


def mix_pass(*parts):
    side = parts[2]
    vmem = pl.BlockSpec(memory_space=pltpu.VMEM)
    return pl.pallas_call(
        mix_kernel,
        out_shape=jax.ShapeDtypeStruct(side.shape, side.dtype),
        in_specs=[vmem] * len(parts),
        out_specs=vmem,
        compiler_params=pltpu.CompilerParams(vmem_limit_bytes=12 * 1024 * 1024),
    )(*parts)


def staged(routes, probs, tokens, w_gate, w_up, w_down):
    tok, top = routes.shape
    size = lax.axis_size("expert")
    slots = 5 * tok * top // (4 * size)
    capacity = tok * top // 2
    half = tok // 2
    me = lax.axis_index("expert")
    z, y, core = me // 4, me // 2 % 2, me % 2

    def swapped(array, bit):
        return lax.ppermute(array, "expert", [(i, i ^ bit) for i in range(size)])

    sibling = functools.partial(swapped, bit=1)
    column = functools.partial(swapped, bit=2)
    pair = functools.partial(swapped, bit=4)
    far = functools.partial(swapped, bit=8)

    def together(*arrays):
        return lax.optimization_barrier(arrays)

    spots = jnp.stack(
        [
            (z ^ k) * 4 + (y ^ column_bit) * 2 + (core ^ core_bit)
            for k in range(4)
            for core_bit in range(2)
            for column_bit in range(2)
        ]
    ).astype(jnp.int32)

    def expert(k, tables, *xs, first=None):
        return plane_pass(k, tables, xs, w_gate, w_up, w_down, slots, first)

    weight = table_pass(routes, probs, size, w_gate, w_up, w_down)
    a0 = tokens
    a1, low, b0, c0, weight = together(
        pair(a0), far(a0[:half]), column(a0), sibling(a0), weight
    )
    high = far(a0[half:])
    b1 = column(a1)
    d0 = sibling(b0)
    c1 = sibling(a1)
    keep0, give0, act0, tables = expert(
        0, None, a0, b0, c0, d0, first=(capacity, spots, weight)
    )
    high, b1, c1, keep0, give0, act0, tables = together(
        high, b1, c1, keep0, give0, act0, tables
    )
    a2 = jnp.concatenate([low, high], axis=0)
    a3 = pair(a2)
    b2 = column(a2)
    d1 = sibling(b1)
    c2 = sibling(a2)
    keep1, give1, act1 = expert(1, tables, a1, b1, c1, d1)
    a3, b2, c2, keep1, give1, act1 = together(a3, b2, c2, keep1, give1, act1)
    b3 = pair(b2)
    got1 = sibling(give1)
    came1 = column(summed(keep1[tok:], got1[tok:]))
    d2 = sibling(b2)
    c3 = sibling(a3)
    keep2, give2, act2 = expert(2, tables, a2, b2, c2, d2)
    b3, came1, c3, keep2, give2, act2 = together(b3, came1, c3, keep2, give2, act2)
    near1 = summed(keep1[:tok], got1[:tok], came1)
    most = 5 * tok // 8
    d3 = sibling(b3)
    got2 = sibling(give2)
    near1_low = pair(near1[:most])
    keep3, give3, act3 = expert(3, tables, a3, b3, c3, d3)
    keep3, give3, act3, got2, near1, near1_low = together(
        keep3, give3, act3, got2, near1, near1_low
    )
    got0 = sibling(give0)

    def own(keep, got, start, stop, *more):
        return summed(keep[start:stop], got[start:stop], *more)

    got3 = sibling(give3)
    low = pair(own(keep3, got3, tok, tok + most))
    high = column(own(keep3, got3, tok + most, 2 * tok))
    side_high = column(own(keep2, got2, tok + most, 2 * tok))
    sum3 = own(keep3, got3, 0, most)
    low, high, side_high, got0, sum3 = together(low, high, side_high, got0, sum3)
    far3_high = far(own(keep3, got3, most, tok, high))
    far2_high = far(own(keep2, got2, most, tok, side_high))
    pair3_low = pair(sum3)
    side_low = column(own(keep2, got2, tok, tok + most, low))
    side0 = own(keep0, got0, tok, 2 * tok)
    far3_high, far2_high, pair3_low, side_low, side0 = together(
        far3_high, far2_high, pair3_low, side_low, side0
    )
    sum2 = own(keep2, got2, 0, most, pair3_low, side_low)
    sum1 = summed(near1[most:], far3_high)
    sum2, sum1, side0 = together(sum2, sum1, side0)
    far2_low = far(sum2)
    near1_high = pair(sum1)
    last0 = column(side0)
    mixed = mix_pass(keep0, got0, last0, near1_low, far2_low, near1_high, far2_high)

    acts = jnp.concatenate([act0, act1, act2, act3], axis=0)
    count = jnp.minimum(jnp.sum((weight >= 0.0).astype(jnp.float32)), float(capacity))
    gram = gram_of(acts) * (2.0 / count)
    return gram[None], mixed


def gathered(routes, probs, tokens, w_gate, w_up, w_down):
    tok_rows, top = routes.shape
    size = lax.axis_size("expert")
    capacity = tok_rows * top // 2
    every_token = lax.all_gather(tokens, "expert", tiled=True)
    weight = weights_for_me(routes, probs, size)
    named = (weight >= 0.0).astype(jnp.int32)
    within = jnp.cumsum(named, axis=1) - named
    per_device = jnp.sum(named, axis=1)
    before = jnp.cumsum(per_device) - per_device
    rank = within + before[:, None]
    kept = (named == 1) & (rank < capacity)
    count = jnp.minimum(jnp.sum(per_device), capacity)
    slot = jnp.where(kept, rank, -1).reshape(size * tok_rows)
    place = jnp.arange(capacity, dtype=jnp.int32)
    select = (place[:, None] == slot[None, :]).astype(jnp.bfloat16)
    rows = jnp.dot(select, every_token, preferred_element_type=jnp.float32).astype(jnp.bfloat16)
    gram_sum, made = expert_pass(rows, w_gate, w_up, w_down)
    gram = gram_sum * (2.0 / count.astype(jnp.float32))
    spread = lax.dot_general(
        select, made, (((0,), (0,)), ((), ())), preferred_element_type=jnp.float32
    )
    partial = (spread * weight.reshape(size * tok_rows, 1)).astype(jnp.bfloat16)
    mixed = lax.psum_scatter(partial, "expert", scatter_dimension=0, tiled=True)
    return gram[None], mixed.astype(jnp.bfloat16)


def shards(routes, probs, tokens, gate_weight, up_weight, down_weight):
    body = staged if lax.axis_size("expert") == 16 else gathered
    return body(routes, probs, tokens, gate_weight[0], up_weight[0], down_weight[0])


def solution(mesh):
    placed = (
        P(("parts", "expert"), None),
        P(("parts", "expert"), None),
        P(("parts", "expert"), None),
        P("expert", None, None),
        P("expert", None, None),
        P("expert", None, None),
    )
    return jax.shard_map(
        shards,
        mesh=mesh,
        in_specs=placed,
        out_specs=(P(("parts", "expert"), None, None), P(("parts", "expert"), None)),
        check_vma=False,
    )
```

```python
import functools

import jax
import jax.numpy as jnp
from jax import lax
from jax.experimental import pallas as pl
from jax.experimental.pallas import tpu as pltpu
from jax.sharding import PartitionSpec as P


def gram_of(rows):
    return lax.dot_general(rows, rows, (((0,), (0,)), ((), ())), preferred_element_type=jnp.float32)


def expert_pass(rows, w_gate, w_up, w_down):
    gate = jnp.dot(rows, w_gate, preferred_element_type=jnp.float32)
    up = jnp.dot(rows, w_up, preferred_element_type=jnp.float32)
    act = (jax.nn.silu(gate) * up).astype(jnp.bfloat16)
    gram_sum = gram_of(act)
    made = jnp.dot(act, w_down, preferred_element_type=jnp.float32).astype(jnp.bfloat16)
    return (gram_sum, made)


def weights_for_me(routes, probs, experts):
    names = routes.T[None, :, :] == jnp.arange(experts, dtype=jnp.int32)[:, None, None]
    weight = jnp.sum(jnp.where(names, probs.T[None, :, :], 0.0), axis=1)
    mine = jnp.where(jnp.any(names, axis=1), weight, -1.0)
    return lax.all_to_all(mine, "expert", split_axis=0, concat_axis=0, tiled=True)


def table_kernel(routes, probs, w_gate, w_up, w_down, mine):
    names, shares = routes[...], probs[...]
    for e in range(mine.shape[0]):
        hit = (names == e).astype(jnp.float32)
        named = jnp.sum(hit, axis=0, keepdims=True)
        share = jnp.sum(hit * shares, axis=0, keepdims=True)
        mine[pl.ds(e, 1), :] = jnp.where(named > 0.0, share, -1.0)


def table_pass(routes, probs, experts, w_gate, w_up, w_down):
    mine = pl.pallas_call(
        table_kernel,
        out_shape=jax.ShapeDtypeStruct((experts, routes.shape[0]), jnp.float32),
        in_specs=[pl.BlockSpec(memory_space=pltpu.VMEM)] * 5,
        out_specs=pl.BlockSpec(memory_space=pltpu.VMEM),
        compiler_params=pltpu.CompilerParams(vmem_limit_bytes=4 * 1024 * 1024),
    )(routes.T, probs.T, w_gate, w_up, w_down)
    return lax.all_to_all(mine, "expert", split_axis=0, concat_axis=0, tiled=True)


def summed(*parts):
    total = parts[0].astype(jnp.float32)
    for part in parts[1:]:
        total = total + part.astype(jnp.float32)
    return total.astype(jnp.bfloat16)


def fill_tables(capacity, spots, weight, ranks, tables):
    blocks, tok = weight.shape
    named = (weight[...] >= 0.0).astype(jnp.float32)
    lane = lax.broadcasted_iota(jnp.int32, (tok, tok), 0)
    below = (lane < lax.broadcasted_iota(jnp.int32, (tok, tok), 1)).astype(jnp.float32)
    within = jnp.dot(named, below, preferred_element_type=jnp.float32)
    totals = jnp.broadcast_to(jnp.sum(named, axis=1, keepdims=True), (blocks, tok))
    row = lax.broadcasted_iota(jnp.int32, (blocks, blocks), 0)
    earlier = (lax.broadcasted_iota(jnp.int32, (blocks, blocks), 1) < row).astype(jnp.float32)
    before = jnp.dot(earlier, totals, preferred_element_type=jnp.float32)
    rank = within + before
    kept = (named > 0.0) & (rank < capacity)
    first = lax.broadcasted_iota(jnp.int32, (blocks, blocks), 0) // 4 * 4
    column = lax.broadcasted_iota(jnp.int32, (blocks, blocks), 1)
    start = jnp.dot((column < first).astype(jnp.float32), totals, preferred_element_type=jnp.float32)
    ranks[...] = jnp.where(kept, rank - start, -1.0)
    for k in range(blocks // 4):
        for i in range(4):
            span = pl.ds(i * tok, tok)
            tables[pl.ds(k, 1), span] = ranks[pl.ds(spots[4 * k + i], 1), :]
            tables[pl.ds(blocks // 4 + k, 1), span] = weight[pl.ds(spots[4 * k + i], 1), :]


def plane_kernel(k, gives, tables, *refs):
    *xs, w_gate, w_up, w_down, keep = refs[: -gives - 2]
    *gives, act, rows = refs[-gives - 2 :]
    slots, hidden = act.shape
    features = rows.shape[1]
    half, width = keep.shape[0], tables.shape[1]
    wide, cut = 256, 512
    place = tables[pl.ds(k, 1), :]
    share = tables[pl.ds(tables.shape[0] // 2 + k, 1), :]
    slot = lax.broadcasted_iota(jnp.int32, (slots, width), 0).astype(jnp.float32)
    hits = slot == place
    scale = jnp.sum(jnp.where(hits, share, 0.0), axis=1, keepdims=True)
    select = hits.astype(jnp.float32).astype(jnp.bfloat16)
    for i in range(features // cut):
        span = pl.ds(i * cut, cut)
        x = jnp.concatenate([block[:, span] for block in xs], axis=0)
        rows[:, span] = jnp.dot(select, x, preferred_element_type=jnp.float32).astype(jnp.bfloat16)
    for i in range(hidden // wide):
        span = pl.ds(i * wide, wide)
        gate = jnp.dot(rows[...], w_gate[:, span], preferred_element_type=jnp.float32)
        up = jnp.dot(rows[...], w_up[:, span], preferred_element_type=jnp.float32)
        act[:, span] = (gate / (1.0 + jnp.exp(-gate)) * up).astype(jnp.bfloat16)
    back = select.T
    for i in range(features // cut):
        span = pl.ds(i * cut, cut)
        result = jnp.dot(act[...], w_down[:, span], preferred_element_type=jnp.float32)
        made = (result * scale).astype(jnp.bfloat16)
        spread = jnp.dot(back, made, preferred_element_type=jnp.float32).astype(jnp.bfloat16)
        keep[:, span] = spread[:half]
        start = half
        for give in gives:
            give[:, span] = spread[start : start + give.shape[0]]
            start += give.shape[0]


def first_kernel(capacity, spots, weight, *refs):
    *plane, tables, rows, ranks = refs
    fill_tables(capacity, spots, weight, ranks, tables)
    plane_kernel(0, 1, tables, *plane, rows)


def plane_pass(k, tables, xs, w_gate, w_up, w_down, slots, first=None, pieces=None):
    tok, features = xs[0].shape
    hidden = w_gate.shape[1]
    rows = 4 * slots
    pieces = pieces or (2 * tok,)
    outs = tuple(
        jax.ShapeDtypeStruct((some, features), jnp.bfloat16) for some in (2 * tok, *pieces)
    )
    outs += (jax.ShapeDtypeStruct((rows, hidden), jnp.bfloat16),)
    scratch = [pltpu.VMEM((rows, features), jnp.bfloat16)]
    vmem = pl.BlockSpec(memory_space=pltpu.VMEM)
    if first is None:
        body, inputs, specs = functools.partial(plane_kernel, k, len(pieces)), (tables,), [vmem]
    else:
        capacity, spots, weight = first
        body = functools.partial(first_kernel, capacity)
        inputs, specs = (spots, weight), [pl.BlockSpec(memory_space=pltpu.SMEM), vmem]
        outs += (jax.ShapeDtypeStruct((weight.shape[0] // 2, 4 * tok), jnp.float32),)
        scratch.append(pltpu.VMEM(weight.shape, jnp.float32))
    flops = 2 * rows * (3 * features * hidden + 8 * tok * features)
    moved = 2 * (3 * features * hidden + 8 * tok * features)
    return pl.pallas_call(
        body,
        out_shape=outs,
        in_specs=specs + [vmem] * (len(xs) + 3),
        out_specs=[vmem] * len(outs),
        scratch_shapes=scratch,
        compiler_params=pltpu.CompilerParams(vmem_limit_bytes=12 * 1024 * 1024),
        cost_estimate=pl.CostEstimate(
            flops=flops, bytes_accessed=moved, transcendentals=rows * hidden
        ),
    )(*inputs, *xs, w_gate, w_up, w_down)


def high_kernel(keep3, got3, high3, keep2, got2, high2, both):
    tok, least = keep3.shape[0] // 2, high3.shape[0]
    for i, parts in enumerate(((keep3, got3, high3), (keep2, got2, high2))):
        keep, got = (part[tok - least : tok, :].astype(jnp.float32) for part in parts[:2])
        total = keep + got + parts[2][...].astype(jnp.float32)
        both[i * least : (i + 1) * least, :] = total.astype(both.dtype)


def high_pass(*parts):
    least, features = parts[2].shape
    vmem = pl.BlockSpec(memory_space=pltpu.VMEM)
    return pl.pallas_call(
        high_kernel,
        out_shape=jax.ShapeDtypeStruct((2 * least, features), parts[2].dtype),
        in_specs=[vmem] * len(parts),
        out_specs=vmem,
        compiler_params=pltpu.CompilerParams(vmem_limit_bytes=12 * 1024 * 1024),
    )(*parts)


def mix_kernel(keep, got, side, near_low, near_mid, near_high, far_low, far_high, mixed):
    least, most, tok = near_low.shape[0], far_low.shape[0], mixed.shape[0]
    for start, stop, near, far in (
        (0, least, near_low, far_low[:least, :]),
        (least, most, near_mid, far_low[least:, :]),
        (most, tok, near_high, far_high[tok - most :, :]),
    ):
        total = keep[start:stop, :].astype(jnp.float32) + got[start:stop, :].astype(jnp.float32)
        total = total + side[start:stop, :].astype(jnp.float32) + near[...].astype(jnp.float32)
        mixed[start:stop, :] = (total + far.astype(jnp.float32)).astype(mixed.dtype)


def mix_pass(*parts):
    side = parts[2]
    vmem = pl.BlockSpec(memory_space=pltpu.VMEM)
    return pl.pallas_call(
        mix_kernel,
        out_shape=jax.ShapeDtypeStruct(side.shape, side.dtype),
        in_specs=[vmem] * len(parts),
        out_specs=vmem,
        compiler_params=pltpu.CompilerParams(vmem_limit_bytes=12 * 1024 * 1024),
    )(*parts)


def staged(routes, probs, tokens, w_gate, w_up, w_down):
    tok, top = routes.shape
    size = lax.axis_size("expert")
    slots = 5 * tok * top // (4 * size)
    capacity = tok * top // 2
    half = tok // 2
    me = lax.axis_index("expert")
    z, y, core = me // 4, me // 2 % 2, me % 2

    def swapped(array, bit):
        return lax.ppermute(array, "expert", [(i, i ^ bit) for i in range(size)])

    sibling = functools.partial(swapped, bit=1)
    column = functools.partial(swapped, bit=2)
    pair = functools.partial(swapped, bit=4)
    far = functools.partial(swapped, bit=8)

    def together(*arrays):
        return lax.optimization_barrier(arrays)

    spots = jnp.stack(
        [
            (z ^ k) * 4 + (y ^ column_bit) * 2 + (core ^ core_bit)
            for k in range(4)
            for core_bit in range(2)
            for column_bit in range(2)
        ]
    ).astype(jnp.int32)

    def expert(k, tables, *xs, first=None, pieces=None):
        return plane_pass(k, tables, xs, w_gate, w_up, w_down, slots, first, pieces)

    weight = table_pass(routes, probs, size, w_gate, w_up, w_down)
    a0 = tokens
    a1, low, b0, c0, weight = together(
        pair(a0), far(a0[:half]), column(a0), sibling(a0), weight
    )
    high = far(a0[half:])
    b1 = column(a1)
    d0 = sibling(b0)
    c1 = sibling(a1)
    keep0, give0, act0, tables = expert(
        0, None, a0, b0, c0, d0, first=(capacity, spots, weight)
    )
    high, b1, c1, keep0, give0, act0, tables = together(
        high, b1, c1, keep0, give0, act0, tables
    )
    a2 = jnp.concatenate([low, high], axis=0)
    a3 = pair(a2)
    b2 = column(a2)
    d1 = sibling(b1)
    c2 = sibling(a2)
    keep1, give1, *give1_side, act1 = expert(1, tables, a1, b1, c1, d1, pieces=(tok, tok))
    got1_side = [sibling(piece) for piece in give1_side]
    a3, b2, c2, keep1, give1, act1, *got1_side = together(
        a3, b2, c2, keep1, give1, act1, *got1_side
    )
    b3 = pair(b2)
    came1 = column(summed(keep1[tok:], jnp.concatenate(got1_side, axis=0)))
    got1 = sibling(give1)
    d2 = sibling(b2)
    c3 = sibling(a3)
    keep2, give2, act2 = expert(2, tables, a2, b2, c2, d2)
    b3, came1, c3, got1, keep2, give2, act2 = together(b3, came1, c3, got1, keep2, give2, act2)
    d3 = sibling(b3)
    near1 = summed(keep1[:tok], got1, came1)
    most = 5 * tok // 8
    least = tok - most
    got2 = sibling(give2)
    near1_low = pair(near1[:least])
    keep3, give3, act3 = expert(3, tables, a3, b3, c3, d3)
    keep3, give3, act3, got2, near1, near1_low = together(
        keep3, give3, act3, got2, near1, near1_low
    )
    got0 = sibling(give0)

    def own(keep, got, start, stop, *more):
        return summed(keep[start:stop], got[start:stop], *more)

    got3 = sibling(give3)
    low = pair(own(keep3, got3, tok, tok + most))
    high = column(own(keep3, got3, tok + most, 2 * tok))
    side_high = column(own(keep2, got2, tok + most, 2 * tok))
    near1_mid = pair(near1[least:most])
    sum3 = own(keep3, got3, 0, most)
    side0 = own(keep0, got0, tok, 2 * tok)
    low, high, side_high, near1_mid, sum3, side0 = together(
        low, high, side_high, near1_mid, sum3, side0
    )
    far_high = far(high_pass(keep3, got3, high, keep2, got2, side_high))
    pair3_low = pair(sum3)
    side_low = column(own(keep2, got2, tok, tok + most, low))
    last0 = column(side0)
    acts = jnp.concatenate([act0, act1, act2, act3], axis=0)
    count = jnp.minimum(jnp.sum((weight >= 0.0).astype(jnp.float32)), float(capacity))
    gram = gram_of(acts) * (2.0 / count)
    far_high, pair3_low, side_low, last0, gram = together(
        far_high, pair3_low, side_low, last0, gram
    )
    far2_low = far(own(keep2, got2, 0, most, pair3_low, side_low))
    near1_high = pair(summed(near1[most:], far_high[:least]))
    mixed = mix_pass(
        keep0, got0, last0, near1_low, near1_mid, near1_high, far2_low, far_high
    )

    return gram[None], mixed


def gathered(routes, probs, tokens, w_gate, w_up, w_down):
    tok_rows, top = routes.shape
    size = lax.axis_size("expert")
    capacity = tok_rows * top // 2
    every_token = lax.all_gather(tokens, "expert", tiled=True)
    weight = weights_for_me(routes, probs, size)
    named = (weight >= 0.0).astype(jnp.int32)
    within = jnp.cumsum(named, axis=1) - named
    per_device = jnp.sum(named, axis=1)
    before = jnp.cumsum(per_device) - per_device
    rank = within + before[:, None]
    kept = (named == 1) & (rank < capacity)
    count = jnp.minimum(jnp.sum(per_device), capacity)
    slot = jnp.where(kept, rank, -1).reshape(size * tok_rows)
    place = jnp.arange(capacity, dtype=jnp.int32)
    select = (place[:, None] == slot[None, :]).astype(jnp.bfloat16)
    rows = jnp.dot(select, every_token, preferred_element_type=jnp.float32).astype(jnp.bfloat16)
    gram_sum, made = expert_pass(rows, w_gate, w_up, w_down)
    gram = gram_sum * (2.0 / count.astype(jnp.float32))
    spread = lax.dot_general(
        select, made, (((0,), (0,)), ((), ())), preferred_element_type=jnp.float32
    )
    partial = (spread * weight.reshape(size * tok_rows, 1)).astype(jnp.bfloat16)
    mixed = lax.psum_scatter(partial, "expert", scatter_dimension=0, tiled=True)
    return gram[None], mixed.astype(jnp.bfloat16)


def shards(routes, probs, tokens, gate_weight, up_weight, down_weight):
    body = staged if lax.axis_size("expert") == 16 else gathered
    return body(routes, probs, tokens, gate_weight[0], up_weight[0], down_weight[0])


def solution(mesh):
    placed = (
        P(("parts", "expert"), None),
        P(("parts", "expert"), None),
        P(("parts", "expert"), None),
        P("expert", None, None),
        P("expert", None, None),
        P("expert", None, None),
    )
    return jax.shard_map(
        shards,
        mesh=mesh,
        in_specs=placed,
        out_specs=(P(("parts", "expert"), None, None), P(("parts", "expert"), None)),
        check_vma=False,
    )
```

```python
import functools

import jax
import jax.numpy as jnp
from jax import lax
from jax.experimental import pallas as pl
from jax.experimental.pallas import tpu as pltpu
from jax.sharding import PartitionSpec as P


def gram_of(rows):
    return lax.dot_general(rows, rows, (((0,), (0,)), ((), ())), preferred_element_type=jnp.float32)


def expert_pass(rows, w_gate, w_up, w_down):
    gate = jnp.dot(rows, w_gate, preferred_element_type=jnp.float32)
    up = jnp.dot(rows, w_up, preferred_element_type=jnp.float32)
    act = (jax.nn.silu(gate) * up).astype(jnp.bfloat16)
    gram_sum = gram_of(act)
    made = jnp.dot(act, w_down, preferred_element_type=jnp.float32).astype(jnp.bfloat16)
    return (gram_sum, made)


def weights_for_me(routes, probs, experts):
    names = routes.T[None, :, :] == jnp.arange(experts, dtype=jnp.int32)[:, None, None]
    weight = jnp.sum(jnp.where(names, probs.T[None, :, :], 0.0), axis=1)
    mine = jnp.where(jnp.any(names, axis=1), weight, -1.0)
    return lax.all_to_all(mine, "expert", split_axis=0, concat_axis=0, tiled=True)


def table_kernel(routes, probs, mine):
    names, shares = routes[...], probs[...]
    for e in range(mine.shape[0]):
        hit = (names == e).astype(jnp.float32)
        named = jnp.sum(hit, axis=0, keepdims=True)
        share = jnp.sum(hit * shares, axis=0, keepdims=True)
        mine[pl.ds(e, 1), :] = jnp.where(named > 0.0, share, -1.0)


def table_pass(routes, probs, experts):
    mine = pl.pallas_call(
        table_kernel,
        out_shape=jax.ShapeDtypeStruct((experts, routes.shape[0]), jnp.float32),
        in_specs=[pl.BlockSpec(memory_space=pltpu.VMEM)] * 2,
        out_specs=pl.BlockSpec(memory_space=pltpu.VMEM),
        compiler_params=pltpu.CompilerParams(vmem_limit_bytes=4 * 1024 * 1024),
    )(routes.T, probs.T)
    return lax.all_to_all(mine, "expert", split_axis=0, concat_axis=0, tiled=True)


def summed(*parts):
    total = parts[0].astype(jnp.float32)
    for part in parts[1:]:
        total = total + part.astype(jnp.float32)
    return total.astype(jnp.bfloat16)


def ranks_kernel(capacity, spots, weight, w_gate, w_up, w_down, tables, ranks):
    blocks, tok = weight.shape
    planes = blocks // 4
    named = (weight[...] >= 0.0).astype(jnp.float32)
    lane = lax.broadcasted_iota(jnp.int32, (tok, tok), 0)
    below = (lane < lax.broadcasted_iota(jnp.int32, (tok, tok), 1)).astype(jnp.float32)
    within = jnp.dot(named, below, preferred_element_type=jnp.float32)
    totals = jnp.broadcast_to(jnp.sum(named, axis=1, keepdims=True), (blocks, tok))
    row = lax.broadcasted_iota(jnp.int32, (blocks, blocks), 0)
    column = lax.broadcasted_iota(jnp.int32, (blocks, blocks), 1)
    earlier = (column < row).astype(jnp.float32)
    before = jnp.dot(earlier, totals, preferred_element_type=jnp.float32)
    rank = within + before
    kept = (named > 0.0) & (rank < capacity)
    first = (column < row // 4 * 4).astype(jnp.float32)
    start = jnp.dot(first, totals, preferred_element_type=jnp.float32)
    ranks[...] = jnp.where(kept, rank - start, -1.0)
    for k in range(planes):
        for i in range(4):
            span = pl.ds(i * tok, tok)
            tables[pl.ds(k, 1), span] = ranks[pl.ds(spots[4 * k + i], 1), :]
            tables[pl.ds(planes + k, 1), span] = weight[pl.ds(spots[4 * k + i], 1), :]
    count = jnp.minimum(jnp.sum(totals[:, :1], axis=0, keepdims=True), float(capacity))
    tables[2 * planes :, :] = jnp.broadcast_to(2.0 / count, tables[2 * planes :, :].shape)


def ranks_pass(capacity, spots, weight, w_gate, w_up, w_down):
    blocks, tok = weight.shape
    vmem = pl.BlockSpec(memory_space=pltpu.VMEM)
    return pl.pallas_call(
        functools.partial(ranks_kernel, capacity),
        out_shape=jax.ShapeDtypeStruct((blocks // 4 * 2 + 8, 4 * tok), jnp.float32),
        in_specs=[pl.BlockSpec(memory_space=pltpu.SMEM)] + [vmem] * 4,
        out_specs=vmem,
        scratch_shapes=[pltpu.VMEM(weight.shape, jnp.float32)],
        compiler_params=pltpu.CompilerParams(vmem_limit_bytes=4 * 1024 * 1024),
    )(spots, weight, w_gate, w_up, w_down)


def plane_kernel(k, gives, tables, *refs):
    *xs, w_gate, w_up, w_down, keep = refs[: -gives - 2]
    *gives, act, rows = refs[-gives - 2 :]
    slots, hidden = act.shape
    features = rows.shape[1]
    half, width = keep.shape[0], tables.shape[1]
    wide, cut = 256, 512
    place = tables[pl.ds(k, 1), :]
    share = tables[pl.ds(4 + k, 1), :]
    slot = lax.broadcasted_iota(jnp.int32, (slots, width), 0).astype(jnp.float32)
    hits = slot == place
    scale = jnp.sum(jnp.where(hits, share, 0.0), axis=1, keepdims=True)
    select = hits.astype(jnp.float32).astype(jnp.bfloat16)
    for i in range(features // cut):
        span = pl.ds(i * cut, cut)
        x = jnp.concatenate([block[:, span] for block in xs], axis=0)
        rows[:, span] = jnp.dot(select, x, preferred_element_type=jnp.float32).astype(jnp.bfloat16)
    for i in range(hidden // wide):
        span = pl.ds(i * wide, wide)
        gate = jnp.dot(rows[...], w_gate[:, span], preferred_element_type=jnp.float32)
        up = jnp.dot(rows[...], w_up[:, span], preferred_element_type=jnp.float32)
        act[:, span] = (gate / (1.0 + jnp.exp(-gate)) * up).astype(jnp.bfloat16)
    back = select.T
    for i in range(features // cut):
        span = pl.ds(i * cut, cut)
        result = jnp.dot(act[...], w_down[:, span], preferred_element_type=jnp.float32)
        made = (result * scale).astype(jnp.bfloat16)
        spread = jnp.dot(back, made, preferred_element_type=jnp.float32).astype(jnp.bfloat16)
        keep[:, span] = spread[:half]
        start = half
        for give in gives:
            give[:, span] = spread[start : start + give.shape[0]]
            start += give.shape[0]


def plane_pass(k, tables, xs, w_gate, w_up, w_down, slots, pieces=None):
    tok, features = xs[0].shape
    hidden = w_gate.shape[1]
    rows = 4 * slots
    pieces = pieces or (2 * tok,)
    outs = tuple(
        jax.ShapeDtypeStruct((some, features), jnp.bfloat16) for some in (2 * tok, *pieces)
    )
    outs += (jax.ShapeDtypeStruct((rows, hidden), jnp.bfloat16),)
    vmem = pl.BlockSpec(memory_space=pltpu.VMEM)
    flops = 2 * rows * (3 * features * hidden + 8 * tok * features)
    moved = 2 * (3 * features * hidden + 8 * tok * features)
    return pl.pallas_call(
        functools.partial(plane_kernel, k, len(pieces)),
        out_shape=outs,
        in_specs=[vmem] * (len(xs) + 4),
        out_specs=[vmem] * len(outs),
        scratch_shapes=[pltpu.VMEM((rows, features), jnp.bfloat16)],
        compiler_params=pltpu.CompilerParams(vmem_limit_bytes=12 * 1024 * 1024),
        cost_estimate=pl.CostEstimate(
            flops=flops, bytes_accessed=moved, transcendentals=rows * hidden
        ),
    )(tables, *xs, w_gate, w_up, w_down)


def high_kernel(keep3, got3, high3, keep2, got2, high2, both):
    tok, least = keep3.shape[0] // 2, high3.shape[0]
    for i, parts in enumerate(((keep3, got3, high3), (keep2, got2, high2))):
        keep, got = (part[tok - least : tok, :].astype(jnp.float32) for part in parts[:2])
        total = keep + got + parts[2][...].astype(jnp.float32)
        both[i * least : (i + 1) * least, :] = total.astype(both.dtype)


def high_pass(*parts):
    least, features = parts[2].shape
    vmem = pl.BlockSpec(memory_space=pltpu.VMEM)
    return pl.pallas_call(
        high_kernel,
        out_shape=jax.ShapeDtypeStruct((2 * least, features), parts[2].dtype),
        in_specs=[vmem] * len(parts),
        out_specs=vmem,
        compiler_params=pltpu.CompilerParams(vmem_limit_bytes=12 * 1024 * 1024),
    )(*parts)


def mix_kernel(keep, got, side, near_low, near_high, far_low, far_high, mixed):
    most, tok = near_low.shape[0], mixed.shape[0]
    for start, stop, near, far in (
        (0, most, near_low, far_low[...]),
        (most, tok, near_high, far_high[tok - most :, :]),
    ):
        total = keep[start:stop, :].astype(jnp.float32) + got[start:stop, :].astype(jnp.float32)
        total = total + side[start:stop, :].astype(jnp.float32) + near[...].astype(jnp.float32)
        mixed[start:stop, :] = (total + far.astype(jnp.float32)).astype(mixed.dtype)


def mix_pass(*parts):
    side = parts[2]
    vmem = pl.BlockSpec(memory_space=pltpu.VMEM)
    return pl.pallas_call(
        mix_kernel,
        out_shape=jax.ShapeDtypeStruct(side.shape, side.dtype),
        in_specs=[vmem] * len(parts),
        out_specs=vmem,
        compiler_params=pltpu.CompilerParams(vmem_limit_bytes=12 * 1024 * 1024),
    )(*parts)


def staged(routes, probs, tokens, w_gate, w_up, w_down):
    tok, top = routes.shape
    size = lax.axis_size("expert")
    slots = 5 * tok * top // (4 * size)
    capacity = tok * top // 2
    half = tok // 2
    me = lax.axis_index("expert")
    z, y, core = me // 4, me // 2 % 2, me % 2

    def swapped(array, bit):
        return lax.ppermute(array, "expert", [(i, i ^ bit) for i in range(size)])

    sibling = functools.partial(swapped, bit=1)
    column = functools.partial(swapped, bit=2)
    pair = functools.partial(swapped, bit=4)
    far = functools.partial(swapped, bit=8)

    def together(*arrays):
        return lax.optimization_barrier(arrays)

    spots = jnp.stack(
        [
            (z ^ k) * 4 + (y ^ column_bit) * 2 + (core ^ core_bit)
            for k in range(4)
            for core_bit in range(2)
            for column_bit in range(2)
        ]
    ).astype(jnp.int32)

    def expert(k, *xs, pieces=None):
        return plane_pass(k, tables, xs, w_gate, w_up, w_down, slots, pieces)

    a0, weight = together(tokens, table_pass(routes, probs, size))
    tables = ranks_pass(capacity, spots, weight, w_gate, w_up, w_down)
    a1, low, b0, c0, tables = together(
        pair(a0), far(a0[:half]), column(a0), sibling(a0), tables
    )
    high = far(a0[half:])
    b1 = column(a1)
    d0 = sibling(b0)
    c1 = sibling(a1)
    keep0, give0, act0 = expert(0, a0, b0, c0, d0)
    high, b1, c1, keep0, give0, act0 = together(high, b1, c1, keep0, give0, act0)
    a2 = jnp.concatenate([low, high], axis=0)
    a3 = pair(a2)
    b2 = column(a2)
    d1 = sibling(b1)
    c2 = sibling(a2)
    keep1, give1, *give1_side, act1 = expert(1, a1, b1, c1, d1, pieces=(tok, tok))
    got1_side = [sibling(piece) for piece in give1_side]
    a3, b2, c2, keep1, give1, act1, *got1_side = together(
        a3, b2, c2, keep1, give1, act1, *got1_side
    )
    b3 = pair(b2)
    came1 = column(summed(keep1[tok:], jnp.concatenate(got1_side, axis=0)))
    got1 = sibling(give1)
    d2 = sibling(b2)
    c3 = sibling(a3)
    keep2, give2, act2 = expert(2, a2, b2, c2, d2)
    b3, came1, c3, got1, keep2, give2, act2 = together(b3, came1, c3, got1, keep2, give2, act2)
    d3 = sibling(b3)
    near1 = summed(keep1[:tok], got1, came1)
    most = 5 * tok // 8
    least = tok - most

    def own(keep, got, start, stop, *more):
        return summed(keep[start:stop], got[start:stop], *more)

    near1_low = pair(near1[:most])
    got2 = sibling(give2)
    side_high = column(own(keep2, got2, tok + most, 2 * tok))
    keep3, give3, act3 = expert(3, a3, b3, c3, d3)
    keep3, give3, act3, got2, near1, near1_low, side_high = together(
        keep3, give3, act3, got2, near1, near1_low, side_high
    )
    got0 = sibling(give0)
    got3 = sibling(give3)
    low = pair(own(keep3, got3, tok, tok + most))
    high = column(own(keep3, got3, tok + most, 2 * tok))
    sum3 = own(keep3, got3, 0, most)
    side0 = own(keep0, got0, tok, 2 * tok)
    low, high, sum3, side0 = together(low, high, sum3, side0)
    far_high = far(high_pass(keep3, got3, high, keep2, got2, side_high))
    pair3_low = pair(sum3)
    side_low = column(own(keep2, got2, tok, tok + most, low))
    gram = gram_of(jnp.concatenate([act0, act1, act2, act3], axis=0)) * tables[8, 0]
    far_high, pair3_low, side_low, side0, gram = together(
        far_high, pair3_low, side_low, side0, gram
    )
    far2_low = far(own(keep2, got2, 0, most, pair3_low, side_low))
    near1_high = pair(summed(near1[most:], far_high[:least]))
    last0 = column(side0)
    mixed = mix_pass(
        keep0, got0, last0, near1_low, near1_high, far2_low, far_high
    )

    return gram[None], mixed


def gathered(routes, probs, tokens, w_gate, w_up, w_down):
    tok_rows, top = routes.shape
    size = lax.axis_size("expert")
    capacity = tok_rows * top // 2
    every_token = lax.all_gather(tokens, "expert", tiled=True)
    weight = weights_for_me(routes, probs, size)
    named = (weight >= 0.0).astype(jnp.int32)
    within = jnp.cumsum(named, axis=1) - named
    per_device = jnp.sum(named, axis=1)
    before = jnp.cumsum(per_device) - per_device
    rank = within + before[:, None]
    kept = (named == 1) & (rank < capacity)
    count = jnp.minimum(jnp.sum(per_device), capacity)
    slot = jnp.where(kept, rank, -1).reshape(size * tok_rows)
    place = jnp.arange(capacity, dtype=jnp.int32)
    select = (place[:, None] == slot[None, :]).astype(jnp.bfloat16)
    rows = jnp.dot(select, every_token, preferred_element_type=jnp.float32).astype(jnp.bfloat16)
    gram_sum, made = expert_pass(rows, w_gate, w_up, w_down)
    gram = gram_sum * (2.0 / count.astype(jnp.float32))
    spread = lax.dot_general(
        select, made, (((0,), (0,)), ((), ())), preferred_element_type=jnp.float32
    )
    partial = (spread * weight.reshape(size * tok_rows, 1)).astype(jnp.bfloat16)
    mixed = lax.psum_scatter(partial, "expert", scatter_dimension=0, tiled=True)
    return gram[None], mixed.astype(jnp.bfloat16)


def shards(routes, probs, tokens, gate_weight, up_weight, down_weight):
    body = staged if lax.axis_size("expert") == 16 else gathered
    return body(routes, probs, tokens, gate_weight[0], up_weight[0], down_weight[0])


def solution(mesh):
    placed = (
        P(("parts", "expert"), None),
        P(("parts", "expert"), None),
        P(("parts", "expert"), None),
        P("expert", None, None),
        P("expert", None, None),
        P("expert", None, None),
    )
    return jax.shard_map(
        shards,
        mesh=mesh,
        in_specs=placed,
        out_specs=(P(("parts", "expert"), None, None), P(("parts", "expert"), None)),
        check_vma=False,
    )
```

```python
import functools

import jax
import jax.numpy as jnp
from jax import lax
from jax.experimental import pallas as pl
from jax.experimental.pallas import tpu as pltpu
from jax.sharding import PartitionSpec as P


def gram_of(rows):
    return lax.dot_general(rows, rows, (((0,), (0,)), ((), ())), preferred_element_type=jnp.float32)


def expert_pass(rows, w_gate, w_up, w_down):
    gate = jnp.dot(rows, w_gate, preferred_element_type=jnp.float32)
    up = jnp.dot(rows, w_up, preferred_element_type=jnp.float32)
    act = (jax.nn.silu(gate) * up).astype(jnp.bfloat16)
    gram_sum = gram_of(act)
    made = jnp.dot(act, w_down, preferred_element_type=jnp.float32).astype(jnp.bfloat16)
    return (gram_sum, made)


def weights_for_me(routes, probs, experts):
    names = routes.T[None, :, :] == jnp.arange(experts, dtype=jnp.int32)[:, None, None]
    weight = jnp.sum(jnp.where(names, probs.T[None, :, :], 0.0), axis=1)
    mine = jnp.where(jnp.any(names, axis=1), weight, -1.0)
    return lax.all_to_all(mine, "expert", split_axis=0, concat_axis=0, tiled=True)


def table_kernel(routes, probs, mine):
    names, shares = routes[...], probs[...]
    for e in range(mine.shape[0]):
        hit = (names == e).astype(jnp.float32)
        named = jnp.sum(hit, axis=0, keepdims=True)
        share = jnp.sum(hit * shares, axis=0, keepdims=True)
        mine[pl.ds(e, 1), :] = jnp.where(named > 0.0, share, -1.0)


def table_pass(routes, probs, experts):
    mine = pl.pallas_call(
        table_kernel,
        out_shape=jax.ShapeDtypeStruct((experts, routes.shape[0]), jnp.float32),
        in_specs=[pl.BlockSpec(memory_space=pltpu.VMEM)] * 2,
        out_specs=pl.BlockSpec(memory_space=pltpu.VMEM),
        compiler_params=pltpu.CompilerParams(vmem_limit_bytes=4 * 1024 * 1024),
    )(routes.T, probs.T)
    return lax.all_to_all(mine, "expert", split_axis=0, concat_axis=0, tiled=True)


def summed(*parts):
    total = parts[0].astype(jnp.float32)
    for part in parts[1:]:
        total = total + part.astype(jnp.float32)
    return total.astype(jnp.bfloat16)


def ranks_kernel(capacity, spots, weight, w_gate, w_up, w_down, tables, ranks):
    blocks, tok = weight.shape
    planes = blocks // 4
    named = (weight[...] >= 0.0).astype(jnp.float32)
    lane = lax.broadcasted_iota(jnp.int32, (tok, tok), 0)
    below = (lane < lax.broadcasted_iota(jnp.int32, (tok, tok), 1)).astype(jnp.float32)
    within = jnp.dot(named, below, preferred_element_type=jnp.float32)
    totals = jnp.broadcast_to(jnp.sum(named, axis=1, keepdims=True), (blocks, tok))
    row = lax.broadcasted_iota(jnp.int32, (blocks, blocks), 0)
    column = lax.broadcasted_iota(jnp.int32, (blocks, blocks), 1)
    earlier = (column < row).astype(jnp.float32)
    before = jnp.dot(earlier, totals, preferred_element_type=jnp.float32)
    rank = within + before
    kept = (named > 0.0) & (rank < capacity)
    first = (column < row // 4 * 4).astype(jnp.float32)
    start = jnp.dot(first, totals, preferred_element_type=jnp.float32)
    ranks[...] = jnp.where(kept, rank - start, -1.0)
    for k in range(planes):
        for i in range(4):
            span = pl.ds(i * tok, tok)
            tables[pl.ds(k, 1), span] = ranks[pl.ds(spots[4 * k + i], 1), :]
            tables[pl.ds(planes + k, 1), span] = weight[pl.ds(spots[4 * k + i], 1), :]
    count = jnp.minimum(jnp.sum(totals[:, :1], axis=0, keepdims=True), float(capacity))
    tables[2 * planes :, :] = jnp.broadcast_to(2.0 / count, tables[2 * planes :, :].shape)


def ranks_pass(capacity, spots, weight, w_gate, w_up, w_down):
    blocks, tok = weight.shape
    vmem = pl.BlockSpec(memory_space=pltpu.VMEM)
    return pl.pallas_call(
        functools.partial(ranks_kernel, capacity),
        out_shape=jax.ShapeDtypeStruct((blocks // 4 * 2 + 8, 4 * tok), jnp.float32),
        in_specs=[pl.BlockSpec(memory_space=pltpu.SMEM)] + [vmem] * 4,
        out_specs=vmem,
        scratch_shapes=[pltpu.VMEM(weight.shape, jnp.float32)],
        compiler_params=pltpu.CompilerParams(vmem_limit_bytes=4 * 1024 * 1024),
    )(spots, weight, w_gate, w_up, w_down)


def plane_kernel(k, gives, tables, *refs):
    *xs, w_gate, w_up, w_down, keep = refs[: -gives - 2]
    *gives, act, rows = refs[-gives - 2 :]
    slots, hidden = act.shape
    features = rows.shape[1]
    half, width = keep.shape[0], tables.shape[1]
    wide, cut = 256, 512
    place = tables[pl.ds(k, 1), :]
    share = tables[pl.ds(4 + k, 1), :]
    slot = lax.broadcasted_iota(jnp.int32, (slots, width), 0).astype(jnp.float32)
    hits = slot == place
    scale = jnp.sum(jnp.where(hits, share, 0.0), axis=1, keepdims=True)
    select = hits.astype(jnp.float32).astype(jnp.bfloat16)
    for i in range(features // cut):
        span = pl.ds(i * cut, cut)
        x = jnp.concatenate([block[:, span] for block in xs], axis=0)
        rows[:, span] = jnp.dot(select, x, preferred_element_type=jnp.float32).astype(jnp.bfloat16)
    for i in range(hidden // wide):
        span = pl.ds(i * wide, wide)
        gate = jnp.dot(rows[...], w_gate[:, span], preferred_element_type=jnp.float32)
        up = jnp.dot(rows[...], w_up[:, span], preferred_element_type=jnp.float32)
        act[:, span] = (gate / (1.0 + jnp.exp(-gate)) * up).astype(jnp.bfloat16)
    back = select.T
    for i in range(features // cut):
        span = pl.ds(i * cut, cut)
        result = jnp.dot(act[...], w_down[:, span], preferred_element_type=jnp.float32)
        made = (result * scale).astype(jnp.bfloat16)
        spread = jnp.dot(back, made, preferred_element_type=jnp.float32).astype(jnp.bfloat16)
        keep[:, span] = spread[:half]
        start = half
        for give in gives:
            give[:, span] = spread[start : start + give.shape[0]]
            start += give.shape[0]


def plane_pass(k, tables, xs, w_gate, w_up, w_down, slots, pieces=None):
    tok, features = xs[0].shape
    hidden = w_gate.shape[1]
    rows = 4 * slots
    pieces = pieces or (2 * tok,)
    outs = tuple(
        jax.ShapeDtypeStruct((some, features), jnp.bfloat16) for some in (2 * tok, *pieces)
    )
    outs += (jax.ShapeDtypeStruct((rows, hidden), jnp.bfloat16),)
    vmem = pl.BlockSpec(memory_space=pltpu.VMEM)
    flops = 2 * rows * (3 * features * hidden + 8 * tok * features)
    moved = 2 * (3 * features * hidden + 8 * tok * features)
    return pl.pallas_call(
        functools.partial(plane_kernel, k, len(pieces)),
        out_shape=outs,
        in_specs=[vmem] * (len(xs) + 4),
        out_specs=[vmem] * len(outs),
        scratch_shapes=[pltpu.VMEM((rows, features), jnp.bfloat16)],
        compiler_params=pltpu.CompilerParams(vmem_limit_bytes=12 * 1024 * 1024),
        cost_estimate=pl.CostEstimate(
            flops=flops, bytes_accessed=moved, transcendentals=rows * hidden
        ),
    )(tables, *xs, w_gate, w_up, w_down)


def mix_kernel(keep, got, side, near_low, near_high, far_low, far_high, mixed):
    most, tok = near_low.shape[0], mixed.shape[0]
    for start, stop, near, far in (
        (0, most, near_low, far_low),
        (most, tok, near_high, far_high),
    ):
        total = keep[start:stop, :].astype(jnp.float32) + got[start:stop, :].astype(jnp.float32)
        total = total + side[start:stop, :].astype(jnp.float32) + near[...].astype(jnp.float32)
        mixed[start:stop, :] = (total + far[...].astype(jnp.float32)).astype(mixed.dtype)


def mix_pass(*parts):
    side = parts[2]
    vmem = pl.BlockSpec(memory_space=pltpu.VMEM)
    return pl.pallas_call(
        mix_kernel,
        out_shape=jax.ShapeDtypeStruct(side.shape, side.dtype),
        in_specs=[vmem] * len(parts),
        out_specs=vmem,
        compiler_params=pltpu.CompilerParams(vmem_limit_bytes=12 * 1024 * 1024),
    )(*parts)


def staged(routes, probs, tokens, w_gate, w_up, w_down):
    tok, top = routes.shape
    size = lax.axis_size("expert")
    slots = 5 * tok * top // (4 * size)
    capacity = tok * top // 2
    half = tok // 2
    me = lax.axis_index("expert")
    z, y, core = me // 4, me // 2 % 2, me % 2

    def swapped(array, bit):
        return lax.ppermute(array, "expert", [(i, i ^ bit) for i in range(size)])

    sibling = functools.partial(swapped, bit=1)
    column = functools.partial(swapped, bit=2)
    pair = functools.partial(swapped, bit=4)
    far = functools.partial(swapped, bit=8)

    def together(*arrays):
        return lax.optimization_barrier(arrays)

    spots = jnp.stack(
        [
            (z ^ k) * 4 + (y ^ column_bit) * 2 + (core ^ core_bit)
            for k in range(4)
            for core_bit in range(2)
            for column_bit in range(2)
        ]
    ).astype(jnp.int32)

    def expert(k, *xs, pieces=None):
        return plane_pass(k, tables, xs, w_gate, w_up, w_down, slots, pieces)

    weight = table_pass(routes, probs, size)
    a0 = tokens
    a1, low, b0, c0, weight = together(
        pair(a0), far(a0[:half]), column(a0), sibling(a0), weight
    )
    tables = ranks_pass(capacity, spots, weight, w_gate, w_up, w_down)
    high = far(a0[half:])
    b1 = column(a1)
    d0 = sibling(b0)
    c1 = sibling(a1)
    keep0, give0, act0 = expert(0, a0, b0, c0, d0)
    high, b1, c1, keep0, give0, act0, tables = together(
        high, b1, c1, keep0, give0, act0, tables
    )
    a2 = jnp.concatenate([low, high], axis=0)
    a3 = pair(a2)
    b2 = column(a2)
    d1 = sibling(b1)
    c2 = sibling(a2)
    keep1, give1, *give1_side, act1 = expert(1, a1, b1, c1, d1, pieces=(tok, tok))
    got1_side = [sibling(piece) for piece in give1_side]
    a3, b2, c2, keep1, give1, act1, *got1_side = together(
        a3, b2, c2, keep1, give1, act1, *got1_side
    )
    b3 = pair(b2)
    came1 = column(summed(keep1[tok:], jnp.concatenate(got1_side, axis=0)))
    got1 = sibling(give1)
    d2 = sibling(b2)
    c3 = sibling(a3)
    keep2, give2, act2 = expert(2, a2, b2, c2, d2)
    b3, came1, c3, got1, keep2, give2, act2 = together(b3, came1, c3, got1, keep2, give2, act2)
    d3 = sibling(b3)
    near1 = summed(keep1[:tok], got1, came1)

    def own(keep, got, start, stop, *more):
        return summed(keep[start:stop], got[start:stop], *more)

    near1_low = pair(near1[:half])
    got2 = sibling(give2)
    side_high = column(own(keep2, got2, tok + half, 2 * tok))
    keep3, give3, act3 = expert(3, a3, b3, c3, d3)
    keep3, give3, act3, got2, near1, near1_low, side_high = together(
        keep3, give3, act3, got2, near1, near1_low, side_high
    )
    far2_high = far(own(keep2, got2, half, tok, side_high))
    got0 = sibling(give0)
    got3 = sibling(give3)
    low = pair(own(keep3, got3, tok, tok + half))
    high = column(own(keep3, got3, tok + half, 2 * tok))
    sum3 = own(keep3, got3, 0, half)
    side0 = own(keep0, got0, tok, 2 * tok)
    low, high, far2_high, sum3, side0 = together(low, high, far2_high, sum3, side0)
    far3_high = far(own(keep3, got3, half, tok, high))
    pair3_low = pair(sum3)
    side_low = column(own(keep2, got2, tok, tok + half, low))
    gram = gram_of(jnp.concatenate([act0, act1, act2, act3], axis=0)) * tables[8, 0]
    far3_high, pair3_low, side_low, side0, gram = together(
        far3_high, pair3_low, side_low, side0, gram
    )
    far2_low = far(own(keep2, got2, 0, half, pair3_low, side_low))
    near1_high = pair(summed(near1[half:], far3_high))
    last0 = column(side0)
    mixed = mix_pass(
        keep0, got0, last0, near1_low, near1_high, far2_low, far2_high
    )

    return gram[None], mixed


def gathered(routes, probs, tokens, w_gate, w_up, w_down):
    tok_rows, top = routes.shape
    size = lax.axis_size("expert")
    capacity = tok_rows * top // 2
    every_token = lax.all_gather(tokens, "expert", tiled=True)
    weight = weights_for_me(routes, probs, size)
    named = (weight >= 0.0).astype(jnp.int32)
    within = jnp.cumsum(named, axis=1) - named
    per_device = jnp.sum(named, axis=1)
    before = jnp.cumsum(per_device) - per_device
    rank = within + before[:, None]
    kept = (named == 1) & (rank < capacity)
    count = jnp.minimum(jnp.sum(per_device), capacity)
    slot = jnp.where(kept, rank, -1).reshape(size * tok_rows)
    place = jnp.arange(capacity, dtype=jnp.int32)
    select = (place[:, None] == slot[None, :]).astype(jnp.bfloat16)
    rows = jnp.dot(select, every_token, preferred_element_type=jnp.float32).astype(jnp.bfloat16)
    gram_sum, made = expert_pass(rows, w_gate, w_up, w_down)
    gram = gram_sum * (2.0 / count.astype(jnp.float32))
    spread = lax.dot_general(
        select, made, (((0,), (0,)), ((), ())), preferred_element_type=jnp.float32
    )
    partial = (spread * weight.reshape(size * tok_rows, 1)).astype(jnp.bfloat16)
    mixed = lax.psum_scatter(partial, "expert", scatter_dimension=0, tiled=True)
    return gram[None], mixed.astype(jnp.bfloat16)


def shards(routes, probs, tokens, gate_weight, up_weight, down_weight):
    body = staged if lax.axis_size("expert") == 16 else gathered
    return body(routes, probs, tokens, gate_weight[0], up_weight[0], down_weight[0])


def solution(mesh):
    placed = (
        P(("parts", "expert"), None),
        P(("parts", "expert"), None),
        P(("parts", "expert"), None),
        P("expert", None, None),
        P("expert", None, None),
        P("expert", None, None),
    )
    return jax.shard_map(
        shards,
        mesh=mesh,
        in_specs=placed,
        out_specs=(P(("parts", "expert"), None, None), P(("parts", "expert"), None)),
        check_vma=False,
    )
```

```python
import functools

import jax
import jax.numpy as jnp
from jax import lax
from jax.experimental import pallas as pl
from jax.experimental.pallas import tpu as pltpu
from jax.sharding import PartitionSpec as P


def gram_of(rows):
    return lax.dot_general(rows, rows, (((0,), (0,)), ((), ())), preferred_element_type=jnp.float32)


def expert_pass(rows, w_gate, w_up, w_down):
    gate = jnp.dot(rows, w_gate, preferred_element_type=jnp.float32)
    up = jnp.dot(rows, w_up, preferred_element_type=jnp.float32)
    act = (jax.nn.silu(gate) * up).astype(jnp.bfloat16)
    gram_sum = gram_of(act)
    made = jnp.dot(act, w_down, preferred_element_type=jnp.float32).astype(jnp.bfloat16)
    return (gram_sum, made)


def weights_for_me(routes, probs, experts):
    names = routes.T[None, :, :] == jnp.arange(experts, dtype=jnp.int32)[:, None, None]
    weight = jnp.sum(jnp.where(names, probs.T[None, :, :], 0.0), axis=1)
    mine = jnp.where(jnp.any(names, axis=1), weight, -1.0)
    return lax.all_to_all(mine, "expert", split_axis=0, concat_axis=0, tiled=True)


def prepare_kernel(routes, probs, tokens, mine, low, high, names, shares, sems):
    half = low.shape[0]
    pairs = (
        (routes, names),
        (probs, shares),
        (tokens.at[pl.ds(0, half), :], low),
        (tokens.at[pl.ds(half, half), :], high),
    )
    copies = [pltpu.make_async_copy(*pair, sems.at[i]) for i, pair in enumerate(pairs)]
    for copy in copies:
        copy.start()
    for copy in copies[:2]:
        copy.wait()
    for e in range(mine.shape[0]):
        hit = (names[...] == e).astype(jnp.float32)
        named = jnp.sum(hit, axis=0, keepdims=True)
        share = jnp.sum(hit * shares[...], axis=0, keepdims=True)
        mine[pl.ds(e, 1), :] = jnp.where(named > 0.0, share, -1.0)
    for copy in copies[2:]:
        copy.wait()


def prepare_pass(routes, probs, tokens, experts):
    tok, top = routes.shape
    half = jax.ShapeDtypeStruct((tok // 2, tokens.shape[1]), tokens.dtype)
    vmem = pl.BlockSpec(memory_space=pltpu.VMEM)
    return pl.pallas_call(
        prepare_kernel,
        out_shape=(jax.ShapeDtypeStruct((experts, tok), jnp.float32), half, half),
        in_specs=[pl.BlockSpec(memory_space=pl.ANY)] * 3,
        out_specs=[vmem] * 3,
        scratch_shapes=[
            pltpu.VMEM((top, tok), routes.dtype),
            pltpu.VMEM((top, tok), probs.dtype),
            pltpu.SemaphoreType.DMA((4,)),
        ],
        compiler_params=pltpu.CompilerParams(vmem_limit_bytes=4 * 1024 * 1024),
    )(routes.T, probs.T, tokens)


def summed(*parts):
    total = parts[0].astype(jnp.float32)
    for part in parts[1:]:
        total = total + part.astype(jnp.float32)
    return total.astype(jnp.bfloat16)


def ranks_kernel(capacity, spots, weight, tables, ranks):
    blocks, tok = weight.shape
    planes = blocks // 4
    named = (weight[...] >= 0.0).astype(jnp.float32)
    lane = lax.broadcasted_iota(jnp.int32, (tok, tok), 0)
    below = (lane < lax.broadcasted_iota(jnp.int32, (tok, tok), 1)).astype(jnp.float32)
    within = jnp.dot(named, below, preferred_element_type=jnp.float32)
    totals = jnp.broadcast_to(jnp.sum(named, axis=1, keepdims=True), (blocks, tok))
    row = lax.broadcasted_iota(jnp.int32, (blocks, blocks), 0)
    column = lax.broadcasted_iota(jnp.int32, (blocks, blocks), 1)
    earlier = (column < row).astype(jnp.float32)
    before = jnp.dot(earlier, totals, preferred_element_type=jnp.float32)
    rank = within + before
    kept = (named > 0.0) & (rank < capacity)
    first = (column < row // 4 * 4).astype(jnp.float32)
    start = jnp.dot(first, totals, preferred_element_type=jnp.float32)
    ranks[...] = jnp.where(kept, rank - start, -1.0)
    for k in range(planes):
        for i in range(4):
            span = pl.ds(i * tok, tok)
            tables[pl.ds(k, 1), span] = ranks[pl.ds(spots[4 * k + i], 1), :]
            tables[pl.ds(planes + k, 1), span] = weight[pl.ds(spots[4 * k + i], 1), :]
    count = jnp.minimum(jnp.sum(totals[:, :1], axis=0, keepdims=True), float(capacity))
    tables[2 * planes :, :] = jnp.broadcast_to(2.0 / count, tables[2 * planes :, :].shape)


def ranks_pass(capacity, spots, weight):
    blocks, tok = weight.shape
    vmem = pl.BlockSpec(memory_space=pltpu.VMEM)
    return pl.pallas_call(
        functools.partial(ranks_kernel, capacity),
        out_shape=jax.ShapeDtypeStruct((blocks // 4 * 2 + 8, 4 * tok), jnp.float32),
        in_specs=[pl.BlockSpec(memory_space=pltpu.SMEM), vmem],
        out_specs=vmem,
        scratch_shapes=[pltpu.VMEM(weight.shape, jnp.float32)],
        compiler_params=pltpu.CompilerParams(vmem_limit_bytes=4 * 1024 * 1024),
    )(spots, weight)


def plane_kernel(k, gives, tables, *refs):
    *xs, w_gate, w_up, w_down, keep = refs[: -gives - 2]
    *gives, act, rows = refs[-gives - 2 :]
    slots, hidden = act.shape
    features = rows.shape[1]
    half, width = keep.shape[0], tables.shape[1]
    wide, cut = 256, 512
    place = tables[pl.ds(k, 1), :]
    share = tables[pl.ds(4 + k, 1), :]
    slot = lax.broadcasted_iota(jnp.int32, (slots, width), 0).astype(jnp.float32)
    hits = slot == place
    scale = jnp.sum(jnp.where(hits, share, 0.0), axis=1, keepdims=True)
    select = hits.astype(jnp.float32).astype(jnp.bfloat16)
    for i in range(features // cut):
        span = pl.ds(i * cut, cut)
        x = jnp.concatenate([block[:, span] for block in xs], axis=0)
        rows[:, span] = jnp.dot(select, x, preferred_element_type=jnp.float32).astype(jnp.bfloat16)
    for i in range(hidden // wide):
        span = pl.ds(i * wide, wide)
        gate = jnp.dot(rows[...], w_gate[:, span], preferred_element_type=jnp.float32)
        up = jnp.dot(rows[...], w_up[:, span], preferred_element_type=jnp.float32)
        act[:, span] = (gate / (1.0 + jnp.exp(-gate)) * up).astype(jnp.bfloat16)
    back = select.T
    for i in range(features // cut):
        span = pl.ds(i * cut, cut)
        result = jnp.dot(act[...], w_down[:, span], preferred_element_type=jnp.float32)
        made = (result * scale).astype(jnp.bfloat16)
        spread = jnp.dot(back, made, preferred_element_type=jnp.float32).astype(jnp.bfloat16)
        keep[:, span] = spread[:half]
        start = half
        for give in gives:
            give[:, span] = spread[start : start + give.shape[0]]
            start += give.shape[0]


def plane_pass(k, tables, xs, w_gate, w_up, w_down, slots, pieces=None):
    tok, features = xs[0].shape
    hidden = w_gate.shape[1]
    rows = 4 * slots
    pieces = pieces or (2 * tok,)
    outs = tuple(
        jax.ShapeDtypeStruct((some, features), jnp.bfloat16) for some in (2 * tok, *pieces)
    )
    outs += (jax.ShapeDtypeStruct((rows, hidden), jnp.bfloat16),)
    vmem = pl.BlockSpec(memory_space=pltpu.VMEM)
    flops = 2 * rows * (3 * features * hidden + 8 * tok * features)
    moved = 2 * (3 * features * hidden + 8 * tok * features)
    return pl.pallas_call(
        functools.partial(plane_kernel, k, len(pieces)),
        out_shape=outs,
        in_specs=[vmem] * (len(xs) + 4),
        out_specs=[vmem] * len(outs),
        scratch_shapes=[pltpu.VMEM((rows, features), jnp.bfloat16)],
        compiler_params=pltpu.CompilerParams(vmem_limit_bytes=12 * 1024 * 1024),
        cost_estimate=pl.CostEstimate(
            flops=flops, bytes_accessed=moved, transcendentals=rows * hidden
        ),
    )(tables, *xs, w_gate, w_up, w_down)


def mix_kernel(keep, got, side, near_low, near_high, far_low, far_high, mixed):
    most, tok = near_low.shape[0], mixed.shape[0]
    for start, stop, near, far in (
        (0, most, near_low, far_low),
        (most, tok, near_high, far_high),
    ):
        total = keep[start:stop, :].astype(jnp.float32) + got[start:stop, :].astype(jnp.float32)
        total = total + side[start:stop, :].astype(jnp.float32) + near[...].astype(jnp.float32)
        mixed[start:stop, :] = (total + far[...].astype(jnp.float32)).astype(mixed.dtype)


def mix_pass(*parts):
    side = parts[2]
    vmem = pl.BlockSpec(memory_space=pltpu.VMEM)
    return pl.pallas_call(
        mix_kernel,
        out_shape=jax.ShapeDtypeStruct(side.shape, side.dtype),
        in_specs=[vmem] * len(parts),
        out_specs=vmem,
        compiler_params=pltpu.CompilerParams(vmem_limit_bytes=12 * 1024 * 1024),
    )(*parts)


def staged(routes, probs, tokens, w_gate, w_up, w_down):
    tok, top = routes.shape
    size = lax.axis_size("expert")
    slots = 5 * tok * top // (4 * size)
    capacity = tok * top // 2
    half = tok // 2
    me = lax.axis_index("expert")
    z, y, core = me // 4, me // 2 % 2, me % 2

    def swapped(array, bit):
        return lax.ppermute(array, "expert", [(i, i ^ bit) for i in range(size)])

    sibling = functools.partial(swapped, bit=1)
    column = functools.partial(swapped, bit=2)
    pair = functools.partial(swapped, bit=4)
    far = functools.partial(swapped, bit=8)

    def together(*arrays):
        return lax.optimization_barrier(arrays)

    spots = jnp.stack(
        [
            (z ^ k) * 4 + (y ^ column_bit) * 2 + (core ^ core_bit)
            for k in range(4)
            for core_bit in range(2)
            for column_bit in range(2)
        ]
    ).astype(jnp.int32)

    def expert(k, *xs, pieces=None):
        return plane_pass(k, tables, xs, w_gate, w_up, w_down, slots, pieces)

    mine, a0_low, a0_high = prepare_pass(routes, probs, tokens, size)
    a0 = tokens
    a1, low, b0, c0, weight, a0_high = together(
        pair(a0),
        far(a0_low),
        column(a0),
        sibling(a0),
        lax.all_to_all(mine, "expert", split_axis=0, concat_axis=0, tiled=True),
        a0_high,
    )
    tables = ranks_pass(capacity, spots, weight)
    high = far(a0_high)
    b1 = column(a1)
    d0 = sibling(b0)
    c1 = sibling(a1)
    keep0, give0, act0 = expert(0, a0, b0, c0, d0)
    high, b1, c1, keep0, give0, act0, tables = together(
        high, b1, c1, keep0, give0, act0, tables
    )
    a2 = jnp.concatenate([low, high], axis=0)
    a3 = pair(a2)
    b2 = column(a2)
    d1 = sibling(b1)
    c2 = sibling(a2)
    keep1, give1, *give1_side, act1 = expert(1, a1, b1, c1, d1, pieces=(tok, tok))
    got1_side = [sibling(piece) for piece in give1_side]
    a3, b2, c2, keep1, give1, act1, *got1_side = together(
        a3, b2, c2, keep1, give1, act1, *got1_side
    )
    b3 = pair(b2)
    came1 = column(summed(keep1[tok:], jnp.concatenate(got1_side, axis=0)))
    got1 = sibling(give1)
    d2 = sibling(b2)
    c3 = sibling(a3)
    keep2, give2, act2 = expert(2, a2, b2, c2, d2)
    b3, came1, c3, got1, keep2, give2, act2 = together(b3, came1, c3, got1, keep2, give2, act2)
    d3 = sibling(b3)
    near1 = summed(keep1[:tok], got1, came1)

    def own(keep, got, start, stop, *more):
        return summed(keep[start:stop], got[start:stop], *more)

    near1_low = pair(near1[:half])
    got2 = sibling(give2)
    side_high = column(own(keep2, got2, tok + half, 2 * tok))
    keep3, give3, act3 = expert(3, a3, b3, c3, d3)
    keep3, give3, act3, got2, near1, near1_low, side_high = together(
        keep3, give3, act3, got2, near1, near1_low, side_high
    )
    far2_high = far(own(keep2, got2, half, tok, side_high))
    got0 = sibling(give0)
    got3 = sibling(give3)
    came3 = column(own(keep3, got3, tok, 2 * tok))
    side0 = own(keep0, got0, tok, 2 * tok)
    side2 = own(keep2, got2, tok, tok + half)
    came3, far2_high, side0, side2 = together(came3, far2_high, side0, side2)
    far3_high = far(own(keep3, got3, half, tok, came3[half:]))
    pair3_low = pair(own(keep3, got3, 0, half, came3[:half]))
    side_low = column(side2)
    gram = gram_of(jnp.concatenate([act0, act1, act2, act3], axis=0)) * tables[8, 0]
    far3_high, pair3_low, side_low, side0, gram = together(
        far3_high, pair3_low, side_low, side0, gram
    )
    far2_low = far(own(keep2, got2, 0, half, pair3_low, side_low))
    near1_high = pair(summed(near1[half:], far3_high))
    last0 = column(side0)
    mixed = mix_pass(
        keep0, got0, last0, near1_low, near1_high, far2_low, far2_high
    )

    return gram[None], mixed


def gathered(routes, probs, tokens, w_gate, w_up, w_down):
    tok_rows, top = routes.shape
    size = lax.axis_size("expert")
    capacity = tok_rows * top // 2
    every_token = lax.all_gather(tokens, "expert", tiled=True)
    weight = weights_for_me(routes, probs, size)
    named = (weight >= 0.0).astype(jnp.int32)
    within = jnp.cumsum(named, axis=1) - named
    per_device = jnp.sum(named, axis=1)
    before = jnp.cumsum(per_device) - per_device
    rank = within + before[:, None]
    kept = (named == 1) & (rank < capacity)
    count = jnp.minimum(jnp.sum(per_device), capacity)
    slot = jnp.where(kept, rank, -1).reshape(size * tok_rows)
    place = jnp.arange(capacity, dtype=jnp.int32)
    select = (place[:, None] == slot[None, :]).astype(jnp.bfloat16)
    rows = jnp.dot(select, every_token, preferred_element_type=jnp.float32).astype(jnp.bfloat16)
    gram_sum, made = expert_pass(rows, w_gate, w_up, w_down)
    gram = gram_sum * (2.0 / count.astype(jnp.float32))
    spread = lax.dot_general(
        select, made, (((0,), (0,)), ((), ())), preferred_element_type=jnp.float32
    )
    partial = (spread * weight.reshape(size * tok_rows, 1)).astype(jnp.bfloat16)
    mixed = lax.psum_scatter(partial, "expert", scatter_dimension=0, tiled=True)
    return gram[None], mixed.astype(jnp.bfloat16)


def shards(routes, probs, tokens, gate_weight, up_weight, down_weight):
    body = staged if lax.axis_size("expert") == 16 else gathered
    return body(routes, probs, tokens, gate_weight[0], up_weight[0], down_weight[0])


def solution(mesh):
    placed = (
        P(("parts", "expert"), None),
        P(("parts", "expert"), None),
        P(("parts", "expert"), None),
        P("expert", None, None),
        P("expert", None, None),
        P("expert", None, None),
    )
    return jax.shard_map(
        shards,
        mesh=mesh,
        in_specs=placed,
        out_specs=(P(("parts", "expert"), None, None), P(("parts", "expert"), None)),
        check_vma=False,
    )
```

```python
import functools

import jax
import jax.numpy as jnp
from jax import lax
from jax.experimental import pallas as pl
from jax.experimental.pallas import tpu as pltpu
from jax.sharding import PartitionSpec as P


def gram_of(rows):
    return lax.dot_general(rows, rows, (((0,), (0,)), ((), ())), preferred_element_type=jnp.float32)


def expert_pass(rows, w_gate, w_up, w_down):
    gate = jnp.dot(rows, w_gate, preferred_element_type=jnp.float32)
    up = jnp.dot(rows, w_up, preferred_element_type=jnp.float32)
    act = (jax.nn.silu(gate) * up).astype(jnp.bfloat16)
    gram_sum = gram_of(act)
    made = jnp.dot(act, w_down, preferred_element_type=jnp.float32).astype(jnp.bfloat16)
    return (gram_sum, made)


def weights_for_me(routes, probs, experts):
    names = routes.T[None, :, :] == jnp.arange(experts, dtype=jnp.int32)[:, None, None]
    weight = jnp.sum(jnp.where(names, probs.T[None, :, :], 0.0), axis=1)
    mine = jnp.where(jnp.any(names, axis=1), weight, -1.0)
    return lax.all_to_all(mine, "expert", split_axis=0, concat_axis=0, tiled=True)


def prepare_kernel(routes, probs, tokens, mine, low, high, names, shares, sems):
    half = low.shape[0]
    pairs = (
        (routes, names),
        (probs, shares),
        (tokens.at[pl.ds(0, half), :], low),
        (tokens.at[pl.ds(half, half), :], high),
    )
    copies = [pltpu.make_async_copy(*pair, sems.at[i]) for i, pair in enumerate(pairs)]
    for copy in copies:
        copy.start()
    for copy in copies[:2]:
        copy.wait()
    for e in range(mine.shape[0]):
        hit = (names[...] == e).astype(jnp.float32)
        named = jnp.sum(hit, axis=0, keepdims=True)
        share = jnp.sum(hit * shares[...], axis=0, keepdims=True)
        mine[pl.ds(e, 1), :] = jnp.where(named > 0.0, share, -1.0)
    for copy in copies[2:]:
        copy.wait()


def prepare_pass(routes, probs, tokens, experts):
    tok, top = routes.shape
    half = jax.ShapeDtypeStruct((tok // 2, tokens.shape[1]), tokens.dtype)
    vmem = pl.BlockSpec(memory_space=pltpu.VMEM)
    return pl.pallas_call(
        prepare_kernel,
        out_shape=(jax.ShapeDtypeStruct((experts, tok), jnp.float32), half, half),
        in_specs=[pl.BlockSpec(memory_space=pl.ANY)] * 3,
        out_specs=[vmem] * 3,
        scratch_shapes=[
            pltpu.VMEM((top, tok), routes.dtype),
            pltpu.VMEM((top, tok), probs.dtype),
            pltpu.SemaphoreType.DMA((4,)),
        ],
        compiler_params=pltpu.CompilerParams(vmem_limit_bytes=4 * 1024 * 1024),
    )(routes.T, probs.T, tokens)


def summed(*parts):
    total = parts[0].astype(jnp.float32)
    for part in parts[1:]:
        total = total + part.astype(jnp.float32)
    return total.astype(jnp.bfloat16)


def ranks_kernel(capacity, spots, weight, tables, ranks, chip_ranks):
    blocks, tok = weight.shape
    planes = blocks // 4
    named = (weight[...] >= 0.0).astype(jnp.float32)
    lane = lax.broadcasted_iota(jnp.int32, (tok, tok), 0)
    below = (lane < lax.broadcasted_iota(jnp.int32, (tok, tok), 1)).astype(jnp.float32)
    within = jnp.dot(named, below, preferred_element_type=jnp.float32)
    totals = jnp.broadcast_to(jnp.sum(named, axis=1, keepdims=True), (blocks, tok))
    row = lax.broadcasted_iota(jnp.int32, (blocks, blocks), 0)
    column = lax.broadcasted_iota(jnp.int32, (blocks, blocks), 1)
    earlier = (column < row).astype(jnp.float32)
    before = jnp.dot(earlier, totals, preferred_element_type=jnp.float32)
    rank = within + before
    kept = (named > 0.0) & (rank < capacity)
    first = (column < row // 4 * 4).astype(jnp.float32)
    start = jnp.dot(first, totals, preferred_element_type=jnp.float32)
    ranks[...] = jnp.where(kept, rank - start, -1.0)
    first = (column < row // 2 * 2).astype(jnp.float32)
    start = jnp.dot(first, totals, preferred_element_type=jnp.float32)
    chip_ranks[...] = jnp.where(kept, rank - start, -1.0)
    for i in range(4):
        span = pl.ds(i * tok, tok)
        tables[pl.ds(2 * planes, 1), span] = chip_ranks[pl.ds(spots[4 * planes - 4 + i], 1), :]
    for k in range(planes):
        for i in range(4):
            span = pl.ds(i * tok, tok)
            tables[pl.ds(k, 1), span] = ranks[pl.ds(spots[4 * k + i], 1), :]
            tables[pl.ds(planes + k, 1), span] = weight[pl.ds(spots[4 * k + i], 1), :]
    count = jnp.minimum(jnp.sum(totals[:, :1], axis=0, keepdims=True), float(capacity))
    rest = (tables.shape[0] - 2 * planes - 1, tables.shape[1])
    tables[2 * planes + 1 :, :] = jnp.broadcast_to(2.0 / count, rest)


def ranks_pass(capacity, spots, weight):
    blocks, tok = weight.shape
    vmem = pl.BlockSpec(memory_space=pltpu.VMEM)
    return pl.pallas_call(
        functools.partial(ranks_kernel, capacity),
        out_shape=jax.ShapeDtypeStruct((blocks // 4 * 2 + 8, 4 * tok), jnp.float32),
        in_specs=[pl.BlockSpec(memory_space=pltpu.SMEM), vmem],
        out_specs=vmem,
        scratch_shapes=[pltpu.VMEM(weight.shape, jnp.float32)] * 2,
        compiler_params=pltpu.CompilerParams(vmem_limit_bytes=4 * 1024 * 1024),
    )(spots, weight)


def plane_kernel(k, picked, gives, tables, *refs):
    *xs, w_gate, w_up, w_down, keep = refs[: -gives - 2]
    *gives, act, rows = refs[-gives - 2 :]
    slots, hidden = act.shape
    features = rows.shape[1]
    half, width = keep.shape[0], tables.shape[1]
    wide, cut = 256, 512
    place = tables[pl.ds(8 if picked else k, 1), :]
    share = tables[pl.ds(4 + k, 1), :]
    if picked:
        tok = width // 4
        place, share = (
            jnp.concatenate([row[:, i * tok : (i + 1) * tok] for i in picked], axis=1)
            for row in (place, share)
        )
        width = 2 * tok
    slot = lax.broadcasted_iota(jnp.int32, (slots, width), 0).astype(jnp.float32)
    hits = slot == place
    scale = jnp.sum(jnp.where(hits, share, 0.0), axis=1, keepdims=True)
    select = hits.astype(jnp.float32).astype(jnp.bfloat16)
    for i in range(features // cut):
        span = pl.ds(i * cut, cut)
        x = jnp.concatenate([block[:, span] for block in xs], axis=0)
        rows[:, span] = jnp.dot(select, x, preferred_element_type=jnp.float32).astype(jnp.bfloat16)
    for i in range(hidden // wide):
        span = pl.ds(i * wide, wide)
        gate = jnp.dot(rows[...], w_gate[:, span], preferred_element_type=jnp.float32)
        up = jnp.dot(rows[...], w_up[:, span], preferred_element_type=jnp.float32)
        act[:, span] = (gate / (1.0 + jnp.exp(-gate)) * up).astype(jnp.bfloat16)
    back = select.T
    for i in range(features // cut):
        span = pl.ds(i * cut, cut)
        result = jnp.dot(act[...], w_down[:, span], preferred_element_type=jnp.float32)
        made = (result * scale).astype(jnp.bfloat16)
        spread = jnp.dot(back, made, preferred_element_type=jnp.float32).astype(jnp.bfloat16)
        keep[:, span] = spread[:half]
        start = half
        for give in gives:
            give[:, span] = spread[start : start + give.shape[0]]
            start += give.shape[0]


def plane_pass(k, tables, xs, w_gate, w_up, w_down, slots, pieces=None, picked=None):
    tok, features = xs[0].shape
    hidden = w_gate.shape[1]
    blocks = 2 if picked else 4
    rows = blocks * slots
    half = blocks // 2 * tok
    pieces = pieces or (half,)
    outs = tuple(jax.ShapeDtypeStruct((some, features), jnp.bfloat16) for some in (half, *pieces))
    outs += (jax.ShapeDtypeStruct((rows, hidden), jnp.bfloat16),)
    vmem = pl.BlockSpec(memory_space=pltpu.VMEM)
    flops = 2 * rows * (3 * features * hidden + 2 * blocks * tok * features)
    moved = 2 * (3 * features * hidden + 2 * blocks * tok * features)
    return pl.pallas_call(
        functools.partial(plane_kernel, k, picked, len(pieces)),
        out_shape=outs,
        in_specs=[vmem] * (len(xs) + 4),
        out_specs=[vmem] * len(outs),
        scratch_shapes=[pltpu.VMEM((rows, features), jnp.bfloat16)],
        compiler_params=pltpu.CompilerParams(vmem_limit_bytes=12 * 1024 * 1024),
        cost_estimate=pl.CostEstimate(
            flops=flops, bytes_accessed=moved, transcendentals=rows * hidden
        ),
    )(tables, *xs, w_gate, w_up, w_down)


def gram_kernel(tables, *refs):
    *acts, gram = refs
    wide = 256
    scale = tables[9:10, :1]
    rows = jnp.concatenate([act[...] for act in acts], axis=0)
    for i in range(gram.shape[0] // wide):
        some = rows[:, i * wide : (i + 1) * wide]
        gram[pl.ds(i * wide, wide), :] = gram_of_two(some, rows) * scale


def gram_of_two(left, right):
    return lax.dot_general(left, right, (((0,), (0,)), ((), ())), preferred_element_type=jnp.float32)


def gram_pass(tables, *acts):
    hidden = acts[0].shape[1]
    rows = sum(act.shape[0] for act in acts)
    vmem = pl.BlockSpec(memory_space=pltpu.VMEM)
    return pl.pallas_call(
        gram_kernel,
        out_shape=jax.ShapeDtypeStruct((hidden, hidden), jnp.float32),
        in_specs=[vmem] * (len(acts) + 1),
        out_specs=vmem,
        compiler_params=pltpu.CompilerParams(vmem_limit_bytes=16 * 1024 * 1024),
        cost_estimate=pl.CostEstimate(
            flops=2 * rows * hidden * hidden,
            bytes_accessed=4 * hidden * hidden + 2 * rows * hidden,
            transcendentals=0,
        ),
    )(tables, *acts)


def mix_kernel(keep, got, side, near_low, near_high, far_low, far_high, mixed):
    most, tok = near_low.shape[0], mixed.shape[0]
    for start, stop, near, far in (
        (0, most, near_low, far_low),
        (most, tok, near_high, far_high),
    ):
        total = keep[start:stop, :].astype(jnp.float32) + got[start:stop, :].astype(jnp.float32)
        total = total + side[start:stop, :].astype(jnp.float32) + near[...].astype(jnp.float32)
        mixed[start:stop, :] = (total + far[...].astype(jnp.float32)).astype(mixed.dtype)


def mix_pass(*parts):
    side = parts[2]
    vmem = pl.BlockSpec(memory_space=pltpu.VMEM)
    return pl.pallas_call(
        mix_kernel,
        out_shape=jax.ShapeDtypeStruct(side.shape, side.dtype),
        in_specs=[vmem] * len(parts),
        out_specs=vmem,
        compiler_params=pltpu.CompilerParams(vmem_limit_bytes=12 * 1024 * 1024),
    )(*parts)


def staged(routes, probs, tokens, w_gate, w_up, w_down):
    tok, top = routes.shape
    size = lax.axis_size("expert")
    slots = 5 * tok * top // (4 * size)
    capacity = tok * top // 2
    half = tok // 2
    me = lax.axis_index("expert")
    z, y, core = me // 4, me // 2 % 2, me % 2

    def swapped(array, bit):
        return lax.ppermute(array, "expert", [(i, i ^ bit) for i in range(size)])

    sibling = functools.partial(swapped, bit=1)
    column = functools.partial(swapped, bit=2)
    pair = functools.partial(swapped, bit=4)
    far = functools.partial(swapped, bit=8)

    def together(*arrays):
        return lax.optimization_barrier(arrays)

    spots = jnp.stack(
        [
            (z ^ k) * 4 + (y ^ column_bit) * 2 + (core ^ core_bit)
            for k in range(4)
            for core_bit in range(2)
            for column_bit in range(2)
        ]
    ).astype(jnp.int32)

    def expert(k, *xs, pieces=None, picked=None):
        return plane_pass(k, tables, xs, w_gate, w_up, w_down, slots, pieces, picked)

    mine, a0_low, a0_high = prepare_pass(routes, probs, tokens, size)
    a0 = tokens
    a1, low, b0, c0, weight, a0_high = together(
        pair(a0),
        far(a0_low),
        column(a0),
        sibling(a0),
        lax.all_to_all(mine, "expert", split_axis=0, concat_axis=0, tiled=True),
        a0_high,
    )
    tables = ranks_pass(capacity, spots, weight)
    high = far(a0_high)
    b1 = column(a1)
    d0 = sibling(b0)
    c1 = sibling(a1)
    keep0, give0, act0 = expert(0, a0, b0, c0, d0)
    high, b1, c1, keep0, give0, act0, tables = together(
        high, b1, c1, keep0, give0, act0, tables
    )
    a2 = jnp.concatenate([low, high], axis=0)
    a3 = pair(a2)
    b2 = column(a2)
    d1 = sibling(b1)
    c2 = sibling(a2)
    keep1, give1, *give1_side, act1 = expert(1, a1, b1, c1, d1, pieces=(tok, tok))
    got1_side = [sibling(piece) for piece in give1_side]
    a3, b2, c2, keep1, give1, act1, *got1_side = together(
        a3, b2, c2, keep1, give1, act1, *got1_side
    )
    b3 = pair(b2)
    came1 = column(summed(keep1[tok:], jnp.concatenate(got1_side, axis=0)))
    got1 = sibling(give1)
    d2 = sibling(b2)
    c3 = sibling(a3)
    keep2, give2, give2_side, act2 = expert(2, a2, b2, c2, d2, pieces=(tok, tok))
    got2_side = sibling(give2_side)
    keep3, give3, act3 = expert(3, a3, c3, picked=(0, 2))
    b3, came1, got1, got2_side, keep2, give2, act2, keep3, give3, act3 = together(
        b3, came1, got1, got2_side, keep2, give2, act2, keep3, give3, act3
    )
    d3 = sibling(b3)
    near1 = summed(keep1[:tok], got1, came1)

    side_high = column(summed(keep2[tok + half :], got2_side[half:]))
    got0, got2, got3 = sibling(give0), sibling(give2), sibling(give3)
    keep3_side, give3_side, act4 = expert(3, b3, d3, picked=(1, 3))
    keep3_side, give3_side, act4, got0, got2, got3, side_high, near1 = together(
        keep3_side, give3_side, act4, got0, got2, got3, side_high, near1
    )
    far2_high = far(summed(keep2[half:tok], got2[half:], side_high))
    got3_side = sibling(give3_side)
    came3_low = column(summed(keep3_side[:half], got3_side[:half]))
    came3_high = column(summed(keep3_side[half:], got3_side[half:]))
    near1_low = pair(near1[:half])
    side0 = summed(keep0[tok:], got0[tok:])
    side2 = summed(keep2[tok : tok + half], got2_side[:half])
    came3_low, came3_high, far2_high, near1_low, side0, side2 = together(
        came3_low, came3_high, far2_high, near1_low, side0, side2
    )
    far3_high = far(summed(keep3[half:], got3[half:], came3_high))
    pair3_low = pair(summed(keep3[:half], got3[:half], came3_low))
    side_low = column(side2)
    gram = gram_pass(tables, act0, act1, act2, act3, act4)
    far3_high, pair3_low, side_low, side0, gram = together(
        far3_high, pair3_low, side_low, side0, gram
    )
    far2_low = far(summed(keep2[:half], got2[:half], pair3_low, side_low))
    near1_high = pair(summed(near1[half:], far3_high))
    last0 = column(side0)
    mixed = mix_pass(
        keep0, got0, last0, near1_low, near1_high, far2_low, far2_high
    )

    return gram[None], mixed


def gathered(routes, probs, tokens, w_gate, w_up, w_down):
    tok_rows, top = routes.shape
    size = lax.axis_size("expert")
    capacity = tok_rows * top // 2
    every_token = lax.all_gather(tokens, "expert", tiled=True)
    weight = weights_for_me(routes, probs, size)
    named = (weight >= 0.0).astype(jnp.int32)
    within = jnp.cumsum(named, axis=1) - named
    per_device = jnp.sum(named, axis=1)
    before = jnp.cumsum(per_device) - per_device
    rank = within + before[:, None]
    kept = (named == 1) & (rank < capacity)
    count = jnp.minimum(jnp.sum(per_device), capacity)
    slot = jnp.where(kept, rank, -1).reshape(size * tok_rows)
    place = jnp.arange(capacity, dtype=jnp.int32)
    select = (place[:, None] == slot[None, :]).astype(jnp.bfloat16)
    rows = jnp.dot(select, every_token, preferred_element_type=jnp.float32).astype(jnp.bfloat16)
    gram_sum, made = expert_pass(rows, w_gate, w_up, w_down)
    gram = gram_sum * (2.0 / count.astype(jnp.float32))
    spread = lax.dot_general(
        select, made, (((0,), (0,)), ((), ())), preferred_element_type=jnp.float32
    )
    partial = (spread * weight.reshape(size * tok_rows, 1)).astype(jnp.bfloat16)
    mixed = lax.psum_scatter(partial, "expert", scatter_dimension=0, tiled=True)
    return gram[None], mixed.astype(jnp.bfloat16)


def shards(routes, probs, tokens, gate_weight, up_weight, down_weight):
    body = staged if lax.axis_size("expert") == 16 else gathered
    return body(routes, probs, tokens, gate_weight[0], up_weight[0], down_weight[0])


def solution(mesh):
    placed = (
        P(("parts", "expert"), None),
        P(("parts", "expert"), None),
        P(("parts", "expert"), None),
        P("expert", None, None),
        P("expert", None, None),
        P("expert", None, None),
    )
    return jax.shard_map(
        shards,
        mesh=mesh,
        in_specs=placed,
        out_specs=(P(("parts", "expert"), None, None), P(("parts", "expert"), None)),
        check_vma=False,
    )
```

```python
import functools

import jax
import jax.numpy as jnp
from jax import lax
from jax.experimental import pallas as pl
from jax.experimental.pallas import tpu as pltpu
from jax.sharding import PartitionSpec as P


def gram_of(rows):
    return lax.dot_general(rows, rows, (((0,), (0,)), ((), ())), preferred_element_type=jnp.float32)


def expert_pass(rows, w_gate, w_up, w_down):
    gate = jnp.dot(rows, w_gate, preferred_element_type=jnp.float32)
    up = jnp.dot(rows, w_up, preferred_element_type=jnp.float32)
    act = (jax.nn.silu(gate) * up).astype(jnp.bfloat16)
    gram_sum = gram_of(act)
    made = jnp.dot(act, w_down, preferred_element_type=jnp.float32).astype(jnp.bfloat16)
    return (gram_sum, made)


def weights_for_me(routes, probs, experts):
    names = routes.T[None, :, :] == jnp.arange(experts, dtype=jnp.int32)[:, None, None]
    weight = jnp.sum(jnp.where(names, probs.T[None, :, :], 0.0), axis=1)
    mine = jnp.where(jnp.any(names, axis=1), weight, -1.0)
    return lax.all_to_all(mine, "expert", split_axis=0, concat_axis=0, tiled=True)


def prepare_kernel(routes, probs, tokens, mine, low, high, names, shares, sems):
    half = low.shape[0]
    pairs = (
        (routes, names),
        (probs, shares),
        (tokens.at[pl.ds(0, half), :], low),
        (tokens.at[pl.ds(half, half), :], high),
    )
    copies = [pltpu.make_async_copy(*pair, sems.at[i]) for i, pair in enumerate(pairs)]
    for copy in copies:
        copy.start()
    for copy in copies[:2]:
        copy.wait()
    for e in range(mine.shape[0]):
        hit = (names[...] == e).astype(jnp.float32)
        named = jnp.sum(hit, axis=0, keepdims=True)
        share = jnp.sum(hit * shares[...], axis=0, keepdims=True)
        mine[pl.ds(e, 1), :] = jnp.where(named > 0.0, share, -1.0)
    for copy in copies[2:]:
        copy.wait()


def prepare_pass(routes, probs, tokens, experts):
    tok, top = routes.shape
    half = jax.ShapeDtypeStruct((tok // 2, tokens.shape[1]), tokens.dtype)
    vmem = pl.BlockSpec(memory_space=pltpu.VMEM)
    return pl.pallas_call(
        prepare_kernel,
        out_shape=(jax.ShapeDtypeStruct((experts, tok), jnp.float32), half, half),
        in_specs=[pl.BlockSpec(memory_space=pl.ANY)] * 3,
        out_specs=[vmem] * 3,
        scratch_shapes=[
            pltpu.VMEM((top, tok), routes.dtype),
            pltpu.VMEM((top, tok), probs.dtype),
            pltpu.SemaphoreType.DMA((4,)),
        ],
        compiler_params=pltpu.CompilerParams(vmem_limit_bytes=4 * 1024 * 1024),
    )(routes.T, probs.T, tokens)


def summed(*parts):
    total = parts[0].astype(jnp.float32)
    for part in parts[1:]:
        total = total + part.astype(jnp.float32)
    return total.astype(jnp.bfloat16)


def ranks_kernel(capacity, spots, weight, w_gate, w_up, w_down, tables, ranks, chip_ranks):
    blocks, tok = weight.shape
    planes = blocks // 4
    named = (weight[...] >= 0.0).astype(jnp.float32)
    lane = lax.broadcasted_iota(jnp.int32, (tok, tok), 0)
    below = (lane < lax.broadcasted_iota(jnp.int32, (tok, tok), 1)).astype(jnp.float32)
    within = jnp.dot(named, below, preferred_element_type=jnp.float32)
    totals = jnp.broadcast_to(jnp.sum(named, axis=1, keepdims=True), (blocks, tok))
    row = lax.broadcasted_iota(jnp.int32, (blocks, blocks), 0)
    column = lax.broadcasted_iota(jnp.int32, (blocks, blocks), 1)
    earlier = (column < row).astype(jnp.float32)
    before = jnp.dot(earlier, totals, preferred_element_type=jnp.float32)
    rank = within + before
    kept = (named > 0.0) & (rank < capacity)
    first = (column < row // 4 * 4).astype(jnp.float32)
    start = jnp.dot(first, totals, preferred_element_type=jnp.float32)
    ranks[...] = jnp.where(kept, rank - start, -1.0)
    first = (column < row // 2 * 2).astype(jnp.float32)
    start = jnp.dot(first, totals, preferred_element_type=jnp.float32)
    chip_ranks[...] = jnp.where(kept, rank - start, -1.0)
    for i in range(4):
        span = pl.ds(i * tok, tok)
        tables[pl.ds(2 * planes, 1), span] = chip_ranks[pl.ds(spots[4 * planes - 4 + i], 1), :]
    for k in range(planes):
        for i in range(4):
            span = pl.ds(i * tok, tok)
            tables[pl.ds(k, 1), span] = ranks[pl.ds(spots[4 * k + i], 1), :]
            tables[pl.ds(planes + k, 1), span] = weight[pl.ds(spots[4 * k + i], 1), :]
    count = jnp.minimum(jnp.sum(totals[:, :1], axis=0, keepdims=True), float(capacity))
    rest = (tables.shape[0] - 2 * planes - 1, tables.shape[1])
    tables[2 * planes + 1 :, :] = jnp.broadcast_to(2.0 / count, rest)


def ranks_pass(capacity, spots, weight, w_gate, w_up, w_down):
    blocks, tok = weight.shape
    vmem = pl.BlockSpec(memory_space=pltpu.VMEM)
    return pl.pallas_call(
        functools.partial(ranks_kernel, capacity),
        out_shape=jax.ShapeDtypeStruct((blocks // 4 * 2 + 8, 4 * tok), jnp.float32),
        in_specs=[pl.BlockSpec(memory_space=pltpu.SMEM)] + [vmem] * 4,
        out_specs=vmem,
        scratch_shapes=[pltpu.VMEM(weight.shape, jnp.float32)] * 2,
        compiler_params=pltpu.CompilerParams(vmem_limit_bytes=4 * 1024 * 1024),
    )(spots, weight, w_gate, w_up, w_down)


def plane_kernel(k, picked, gives, tables, *refs):
    *xs, w_gate, w_up, w_down, keep = refs[: -gives - 2]
    *gives, act, rows = refs[-gives - 2 :]
    slots, hidden = act.shape
    features = rows.shape[1]
    half, width = keep.shape[0], tables.shape[1]
    wide, cut = 256, 512
    place = tables[pl.ds(8 if picked else k, 1), :]
    share = tables[pl.ds(4 + k, 1), :]
    if picked:
        tok = width // 4
        place, share = (
            jnp.concatenate([row[:, i * tok : (i + 1) * tok] for i in picked], axis=1)
            for row in (place, share)
        )
        width = 2 * tok
    slot = lax.broadcasted_iota(jnp.int32, (slots, width), 0).astype(jnp.float32)
    hits = slot == place
    scale = jnp.sum(jnp.where(hits, share, 0.0), axis=1, keepdims=True)
    select = hits.astype(jnp.float32).astype(jnp.bfloat16)
    for i in range(features // cut):
        span = pl.ds(i * cut, cut)
        x = jnp.concatenate([block[:, span] for block in xs], axis=0)
        rows[:, span] = jnp.dot(select, x, preferred_element_type=jnp.float32).astype(jnp.bfloat16)
    for i in range(hidden // wide):
        span = pl.ds(i * wide, wide)
        gate = jnp.dot(rows[...], w_gate[:, span], preferred_element_type=jnp.float32)
        up = jnp.dot(rows[...], w_up[:, span], preferred_element_type=jnp.float32)
        act[:, span] = (gate / (1.0 + jnp.exp(-gate)) * up).astype(jnp.bfloat16)
    back = select.T
    for i in range(features // cut):
        span = pl.ds(i * cut, cut)
        result = jnp.dot(act[...], w_down[:, span], preferred_element_type=jnp.float32)
        made = (result * scale).astype(jnp.bfloat16)
        spread = jnp.dot(back, made, preferred_element_type=jnp.float32).astype(jnp.bfloat16)
        keep[:, span] = spread[:half]
        start = half
        for give in gives:
            give[:, span] = spread[start : start + give.shape[0]]
            start += give.shape[0]


def plane_pass(k, tables, xs, w_gate, w_up, w_down, slots, pieces=None, picked=None):
    tok, features = xs[0].shape
    hidden = w_gate.shape[1]
    blocks = 2 if picked else 4
    rows = blocks * slots
    half = blocks // 2 * tok
    pieces = pieces or (half,)
    outs = tuple(jax.ShapeDtypeStruct((some, features), jnp.bfloat16) for some in (half, *pieces))
    outs += (jax.ShapeDtypeStruct((rows, hidden), jnp.bfloat16),)
    vmem = pl.BlockSpec(memory_space=pltpu.VMEM)
    flops = 2 * rows * (3 * features * hidden + 2 * blocks * tok * features)
    moved = 2 * (3 * features * hidden + 2 * blocks * tok * features)
    return pl.pallas_call(
        functools.partial(plane_kernel, k, picked, len(pieces)),
        out_shape=outs,
        in_specs=[vmem] * (len(xs) + 4),
        out_specs=[vmem] * len(outs),
        scratch_shapes=[pltpu.VMEM((rows, features), jnp.bfloat16)],
        compiler_params=pltpu.CompilerParams(vmem_limit_bytes=12 * 1024 * 1024),
        cost_estimate=pl.CostEstimate(
            flops=flops, bytes_accessed=moved, transcendentals=rows * hidden
        ),
    )(tables, *xs, w_gate, w_up, w_down)


def late_kernel(keep3, got3, keep2, got2, side2, near1, low3, high3, high2, low1):
    half, tok = low3.shape[0], keep3.shape[0]

    def total(*parts):
        return sum(part.astype(jnp.float32) for part in parts).astype(low3.dtype)

    low3[...] = total(keep3[:half, :], got3[:half, :])
    high3[...] = total(keep3[half:, :], got3[half:, :])
    high2[...] = total(keep2[half:tok, :], got2[half:, :], side2[...])
    low1[...] = near1[:half, :]


def late_pass(*parts):
    side = parts[4]
    vmem = pl.BlockSpec(memory_space=pltpu.VMEM)
    return pl.pallas_call(
        late_kernel,
        out_shape=[jax.ShapeDtypeStruct(side.shape, side.dtype)] * 4,
        in_specs=[vmem] * len(parts),
        out_specs=[vmem] * 4,
        compiler_params=pltpu.CompilerParams(vmem_limit_bytes=12 * 1024 * 1024),
    )(*parts)


def gram_kernel(tables, *refs):
    *acts, gram = refs
    wide = 256
    scale = tables[9:10, :1]
    rows = jnp.concatenate([act[...] for act in acts], axis=0)
    for i in range(gram.shape[0] // wide):
        some = rows[:, i * wide : (i + 1) * wide]
        gram[pl.ds(i * wide, wide), :] = gram_of_two(some, rows) * scale


def gram_of_two(left, right):
    return lax.dot_general(left, right, (((0,), (0,)), ((), ())), preferred_element_type=jnp.float32)


def gram_pass(tables, *acts):
    hidden = acts[0].shape[1]
    rows = sum(act.shape[0] for act in acts)
    vmem = pl.BlockSpec(memory_space=pltpu.VMEM)
    return pl.pallas_call(
        gram_kernel,
        out_shape=jax.ShapeDtypeStruct((hidden, hidden), jnp.float32),
        in_specs=[vmem] * (len(acts) + 1),
        out_specs=vmem,
        compiler_params=pltpu.CompilerParams(vmem_limit_bytes=16 * 1024 * 1024),
        cost_estimate=pl.CostEstimate(
            flops=2 * rows * hidden * hidden,
            bytes_accessed=4 * hidden * hidden + 2 * rows * hidden,
            transcendentals=0,
        ),
    )(tables, *acts)


def mix_kernel(keep, got, side, near_low, near_high, far_low, far_high, mixed):
    most, tok = near_low.shape[0], mixed.shape[0]
    for start, stop, near, far in (
        (0, most, near_low, far_low),
        (most, tok, near_high, far_high),
    ):
        total = keep[start:stop, :].astype(jnp.float32) + got[start:stop, :].astype(jnp.float32)
        total = total + side[start:stop, :].astype(jnp.float32) + near[...].astype(jnp.float32)
        mixed[start:stop, :] = (total + far[...].astype(jnp.float32)).astype(mixed.dtype)


def mix_pass(*parts):
    side = parts[2]
    vmem = pl.BlockSpec(memory_space=pltpu.VMEM)
    return pl.pallas_call(
        mix_kernel,
        out_shape=jax.ShapeDtypeStruct(side.shape, side.dtype),
        in_specs=[vmem] * len(parts),
        out_specs=vmem,
        compiler_params=pltpu.CompilerParams(vmem_limit_bytes=12 * 1024 * 1024),
    )(*parts)


def staged(routes, probs, tokens, w_gate, w_up, w_down):
    tok, top = routes.shape
    size = lax.axis_size("expert")
    slots = 5 * tok * top // (4 * size)
    capacity = tok * top // 2
    half = tok // 2
    me = lax.axis_index("expert")
    z, y, core = me // 4, me // 2 % 2, me % 2

    def swapped(array, bit):
        return lax.ppermute(array, "expert", [(i, i ^ bit) for i in range(size)])

    sibling = functools.partial(swapped, bit=1)
    column = functools.partial(swapped, bit=2)
    pair = functools.partial(swapped, bit=4)
    far = functools.partial(swapped, bit=8)

    def together(*arrays):
        return lax.optimization_barrier(arrays)

    spots = jnp.stack(
        [
            (z ^ k) * 4 + (y ^ column_bit) * 2 + (core ^ core_bit)
            for k in range(4)
            for core_bit in range(2)
            for column_bit in range(2)
        ]
    ).astype(jnp.int32)

    def expert(k, *xs, pieces=None, picked=None):
        return plane_pass(k, tables, xs, w_gate, w_up, w_down, slots, pieces, picked)

    mine, a0_low, a0_high = prepare_pass(routes, probs, tokens, size)
    a0 = tokens
    a1, low, b0, c0, weight, a0_high = together(
        pair(a0),
        far(a0_low),
        column(a0),
        sibling(a0),
        lax.all_to_all(mine, "expert", split_axis=0, concat_axis=0, tiled=True),
        a0_high,
    )
    tables = ranks_pass(capacity, spots, weight, w_gate, w_up, w_down)
    high = far(a0_high)
    b1 = column(a1)
    d0 = sibling(b0)
    c1 = sibling(a1)
    high, b1, c1, d0, tables = together(high, b1, c1, d0, tables)
    a2 = jnp.concatenate([low, high], axis=0)
    a3 = pair(a2)
    b2 = column(a2)
    d1 = sibling(b1)
    c2 = sibling(a2)
    keep0, give0, act0 = expert(0, a0, b0, c0, d0)
    keep1, give1, *give1_side, act1 = expert(1, a1, b1, c1, d1, pieces=(tok, tok))
    got1_side = [sibling(piece) for piece in give1_side]
    a3, b2, c2, keep0, give0, act0, keep1, give1, act1, *got1_side = together(
        a3, b2, c2, keep0, give0, act0, keep1, give1, act1, *got1_side
    )
    b3 = pair(b2)
    came1 = column(summed(keep1[tok:], jnp.concatenate(got1_side, axis=0)))
    got1 = sibling(give1)
    d2 = sibling(b2)
    c3 = sibling(a3)
    keep2, give2, give2_side, act2 = expert(2, a2, b2, c2, d2, pieces=(tok, tok))
    got2_side = sibling(give2_side)
    keep3, give3, act3 = expert(3, a3, c3, picked=(0, 2))
    b3, came1, got1, got2_side, keep2, give2, act2, keep3, give3, act3 = together(
        b3, came1, got1, got2_side, keep2, give2, act2, keep3, give3, act3
    )
    d3 = sibling(b3)
    near1 = summed(keep1[:tok], got1, came1)

    side_high = column(summed(keep2[tok + half :], got2_side[half:]))
    got0, got2, got3 = sibling(give0), sibling(give2), sibling(give3)
    keep3_side, give3_side, act4 = expert(3, b3, d3, picked=(1, 3))
    keep3_side, give3_side, act4, got0, got2, got3, near1 = together(
        keep3_side, give3_side, act4, got0, got2, got3, near1
    )
    got3_side = sibling(give3_side)
    came3_low, came3_high, far2_high, near1_low = late_pass(
        keep3_side, got3_side, keep2, got2, side_high, near1
    )
    came3_low, came3_high = column(came3_low), column(came3_high)
    far2_high = far(far2_high)
    near1_low = pair(near1_low)
    side0 = summed(keep0[tok:], got0[tok:])
    side2 = summed(keep2[tok : tok + half], got2_side[:half])
    came3_low, came3_high, far2_high, near1_low, side0, side2 = together(
        came3_low, came3_high, far2_high, near1_low, side0, side2
    )
    far3_high = far(summed(keep3[half:], got3[half:], came3_high))
    pair3_low = pair(summed(keep3[:half], got3[:half], came3_low))
    side_low = column(side2)
    gram = gram_pass(tables, act0, act1, act2, act3, act4)
    far3_high, pair3_low, side_low, side0, gram = together(
        far3_high, pair3_low, side_low, side0, gram
    )
    far2_low = far(summed(keep2[:half], got2[:half], pair3_low, side_low))
    near1_high = pair(summed(near1[half:], far3_high))
    last0 = column(side0)
    mixed = mix_pass(
        keep0, got0, last0, near1_low, near1_high, far2_low, far2_high
    )

    return gram[None], mixed


def gathered(routes, probs, tokens, w_gate, w_up, w_down):
    tok_rows, top = routes.shape
    size = lax.axis_size("expert")
    capacity = tok_rows * top // 2
    every_token = lax.all_gather(tokens, "expert", tiled=True)
    weight = weights_for_me(routes, probs, size)
    named = (weight >= 0.0).astype(jnp.int32)
    within = jnp.cumsum(named, axis=1) - named
    per_device = jnp.sum(named, axis=1)
    before = jnp.cumsum(per_device) - per_device
    rank = within + before[:, None]
    kept = (named == 1) & (rank < capacity)
    count = jnp.minimum(jnp.sum(per_device), capacity)
    slot = jnp.where(kept, rank, -1).reshape(size * tok_rows)
    place = jnp.arange(capacity, dtype=jnp.int32)
    select = (place[:, None] == slot[None, :]).astype(jnp.bfloat16)
    rows = jnp.dot(select, every_token, preferred_element_type=jnp.float32).astype(jnp.bfloat16)
    gram_sum, made = expert_pass(rows, w_gate, w_up, w_down)
    gram = gram_sum * (2.0 / count.astype(jnp.float32))
    spread = lax.dot_general(
        select, made, (((0,), (0,)), ((), ())), preferred_element_type=jnp.float32
    )
    partial = (spread * weight.reshape(size * tok_rows, 1)).astype(jnp.bfloat16)
    mixed = lax.psum_scatter(partial, "expert", scatter_dimension=0, tiled=True)
    return gram[None], mixed.astype(jnp.bfloat16)


def shards(routes, probs, tokens, gate_weight, up_weight, down_weight):
    body = staged if lax.axis_size("expert") == 16 else gathered
    return body(routes, probs, tokens, gate_weight[0], up_weight[0], down_weight[0])


def solution(mesh):
    placed = (
        P(("parts", "expert"), None),
        P(("parts", "expert"), None),
        P(("parts", "expert"), None),
        P("expert", None, None),
        P("expert", None, None),
        P("expert", None, None),
    )
    return jax.shard_map(
        shards,
        mesh=mesh,
        in_specs=placed,
        out_specs=(P(("parts", "expert"), None, None), P(("parts", "expert"), None)),
        check_vma=False,
    )
```

```python
import functools

import jax
import jax.numpy as jnp
from jax import lax
from jax.experimental import pallas as pl
from jax.experimental.pallas import tpu as pltpu
from jax.sharding import PartitionSpec as P


def gram_of(rows):
    return lax.dot_general(rows, rows, (((0,), (0,)), ((), ())), preferred_element_type=jnp.float32)


def expert_pass(rows, w_gate, w_up, w_down):
    gate = jnp.dot(rows, w_gate, preferred_element_type=jnp.float32)
    up = jnp.dot(rows, w_up, preferred_element_type=jnp.float32)
    act = (jax.nn.silu(gate) * up).astype(jnp.bfloat16)
    gram_sum = gram_of(act)
    made = jnp.dot(act, w_down, preferred_element_type=jnp.float32).astype(jnp.bfloat16)
    return (gram_sum, made)


def weights_for_me(routes, probs, experts):
    names = routes.T[None, :, :] == jnp.arange(experts, dtype=jnp.int32)[:, None, None]
    weight = jnp.sum(jnp.where(names, probs.T[None, :, :], 0.0), axis=1)
    mine = jnp.where(jnp.any(names, axis=1), weight, -1.0)
    return lax.all_to_all(mine, "expert", split_axis=0, concat_axis=0, tiled=True)


def prepare_kernel(routes, probs, tokens, mine, low, high, names, shares, sems):
    half = low.shape[0]
    pairs = (
        (routes, names),
        (probs, shares),
        (tokens.at[pl.ds(0, half), :], low),
        (tokens.at[pl.ds(half, half), :], high),
    )
    copies = [pltpu.make_async_copy(*pair, sems.at[i]) for i, pair in enumerate(pairs)]
    for copy in copies:
        copy.start()
    for copy in copies[:2]:
        copy.wait()
    for e in range(mine.shape[0]):
        hit = (names[...] == e).astype(jnp.float32)
        named = jnp.sum(hit, axis=0, keepdims=True)
        share = jnp.sum(hit * shares[...], axis=0, keepdims=True)
        mine[pl.ds(e, 1), :] = jnp.where(named > 0.0, share, -1.0)
    for copy in copies[2:]:
        copy.wait()


def prepare_pass(routes, probs, tokens, experts):
    tok, top = routes.shape
    half = jax.ShapeDtypeStruct((tok // 2, tokens.shape[1]), tokens.dtype)
    vmem = pl.BlockSpec(memory_space=pltpu.VMEM)
    return pl.pallas_call(
        prepare_kernel,
        out_shape=(jax.ShapeDtypeStruct((experts, tok), jnp.float32), half, half),
        in_specs=[pl.BlockSpec(memory_space=pl.ANY)] * 3,
        out_specs=[vmem] * 3,
        scratch_shapes=[
            pltpu.VMEM((top, tok), routes.dtype),
            pltpu.VMEM((top, tok), probs.dtype),
            pltpu.SemaphoreType.DMA((4,)),
        ],
        compiler_params=pltpu.CompilerParams(vmem_limit_bytes=4 * 1024 * 1024),
    )(routes.T, probs.T, tokens)


def summed(*parts):
    total = parts[0].astype(jnp.float32)
    for part in parts[1:]:
        total = total + part.astype(jnp.float32)
    return total.astype(jnp.bfloat16)


def ranks_kernel(capacity, spots, weight, tables, ranks, chip_ranks):
    blocks, tok = weight.shape
    planes = blocks // 4
    named = (weight[...] >= 0.0).astype(jnp.float32)
    lane = lax.broadcasted_iota(jnp.int32, (tok, tok), 0)
    below = (lane < lax.broadcasted_iota(jnp.int32, (tok, tok), 1)).astype(jnp.float32)
    within = jnp.dot(named, below, preferred_element_type=jnp.float32)
    totals = jnp.broadcast_to(jnp.sum(named, axis=1, keepdims=True), (blocks, tok))
    row = lax.broadcasted_iota(jnp.int32, (blocks, blocks), 0)
    column = lax.broadcasted_iota(jnp.int32, (blocks, blocks), 1)
    earlier = (column < row).astype(jnp.float32)
    before = jnp.dot(earlier, totals, preferred_element_type=jnp.float32)
    rank = within + before
    kept = (named > 0.0) & (rank < capacity)
    first = (column < row // 4 * 4).astype(jnp.float32)
    start = jnp.dot(first, totals, preferred_element_type=jnp.float32)
    ranks[...] = jnp.where(kept, rank - start, -1.0)
    first = (column < row // 2 * 2).astype(jnp.float32)
    start = jnp.dot(first, totals, preferred_element_type=jnp.float32)
    chip_ranks[...] = jnp.where(kept, rank - start, -1.0)
    for i in range(4):
        span = pl.ds(i * tok, tok)
        tables[pl.ds(2 * planes, 1), span] = chip_ranks[pl.ds(spots[4 * planes - 4 + i], 1), :]
    for k in range(planes):
        for i in range(4):
            span = pl.ds(i * tok, tok)
            tables[pl.ds(k, 1), span] = ranks[pl.ds(spots[4 * k + i], 1), :]
            tables[pl.ds(planes + k, 1), span] = weight[pl.ds(spots[4 * k + i], 1), :]
    count = jnp.minimum(jnp.sum(totals[:, :1], axis=0, keepdims=True), float(capacity))
    rest = (tables.shape[0] - 2 * planes - 1, tables.shape[1])
    tables[2 * planes + 1 :, :] = jnp.broadcast_to(2.0 / count, rest)


def ranks_pass(capacity, spots, weight):
    blocks, tok = weight.shape
    vmem = pl.BlockSpec(memory_space=pltpu.VMEM)
    return pl.pallas_call(
        functools.partial(ranks_kernel, capacity),
        out_shape=jax.ShapeDtypeStruct((blocks // 4 * 2 + 8, 4 * tok), jnp.float32),
        in_specs=[pl.BlockSpec(memory_space=pltpu.SMEM), vmem],
        out_specs=vmem,
        scratch_shapes=[pltpu.VMEM(weight.shape, jnp.float32)] * 2,
        compiler_params=pltpu.CompilerParams(vmem_limit_bytes=4 * 1024 * 1024),
    )(spots, weight)


def plane_kernel(k, picked, gives, tables, *refs):
    *xs, w_gate, w_up, w_down, keep = refs[: -gives - 2]
    *gives, act, rows = refs[-gives - 2 :]
    slots, hidden = act.shape
    features = rows.shape[1]
    half, width = keep.shape[0], tables.shape[1]
    wide, cut = 256, 512
    place = tables[pl.ds(8 if picked else k, 1), :]
    share = tables[pl.ds(4 + k, 1), :]
    if picked:
        tok = width // 4
        place, share = (
            jnp.concatenate([row[:, i * tok : (i + 1) * tok] for i in picked], axis=1)
            for row in (place, share)
        )
        width = 2 * tok
    slot = lax.broadcasted_iota(jnp.int32, (slots, width), 0).astype(jnp.float32)
    hits = slot == place
    scale = jnp.sum(jnp.where(hits, share, 0.0), axis=1, keepdims=True)
    select = hits.astype(jnp.float32).astype(jnp.bfloat16)
    for i in range(features // cut):
        span = pl.ds(i * cut, cut)
        x = jnp.concatenate([block[:, span] for block in xs], axis=0)
        rows[:, span] = jnp.dot(select, x, preferred_element_type=jnp.float32).astype(jnp.bfloat16)
    for i in range(hidden // wide):
        span = pl.ds(i * wide, wide)
        gate = jnp.dot(rows[...], w_gate[:, span], preferred_element_type=jnp.float32)
        up = jnp.dot(rows[...], w_up[:, span], preferred_element_type=jnp.float32)
        act[:, span] = (gate / (1.0 + jnp.exp(-gate)) * up).astype(jnp.bfloat16)
    back = select.T
    for i in range(features // cut):
        span = pl.ds(i * cut, cut)
        result = jnp.dot(act[...], w_down[:, span], preferred_element_type=jnp.float32)
        made = (result * scale).astype(jnp.bfloat16)
        spread = jnp.dot(back, made, preferred_element_type=jnp.float32).astype(jnp.bfloat16)
        keep[:, span] = spread[:half]
        start = half
        for give in gives:
            give[:, span] = spread[start : start + give.shape[0]]
            start += give.shape[0]


def plane_pass(k, tables, xs, w_gate, w_up, w_down, slots, pieces=None, picked=None):
    tok, features = xs[0].shape
    hidden = w_gate.shape[1]
    blocks = 2 if picked else 4
    rows = blocks * slots
    half = blocks // 2 * tok
    pieces = pieces or (half,)
    outs = tuple(jax.ShapeDtypeStruct((some, features), jnp.bfloat16) for some in (half, *pieces))
    outs += (jax.ShapeDtypeStruct((rows, hidden), jnp.bfloat16),)
    vmem = pl.BlockSpec(memory_space=pltpu.VMEM)
    flops = 2 * rows * (3 * features * hidden + 2 * blocks * tok * features)
    moved = 2 * (3 * features * hidden + 2 * blocks * tok * features)
    return pl.pallas_call(
        functools.partial(plane_kernel, k, picked, len(pieces)),
        out_shape=outs,
        in_specs=[vmem] * (len(xs) + 4),
        out_specs=[vmem] * len(outs),
        scratch_shapes=[pltpu.VMEM((rows, features), jnp.bfloat16)],
        compiler_params=pltpu.CompilerParams(vmem_limit_bytes=12 * 1024 * 1024),
        cost_estimate=pl.CostEstimate(
            flops=flops, bytes_accessed=moved, transcendentals=rows * hidden
        ),
    )(tables, *xs, w_gate, w_up, w_down)


def gram_kernel(tables, *refs):
    *acts, gram = refs
    wide = 256
    scale = tables[9:10, :1]
    rows = jnp.concatenate([act[...] for act in acts], axis=0)
    for i in range(gram.shape[0] // wide):
        some = rows[:, i * wide : (i + 1) * wide]
        gram[pl.ds(i * wide, wide), :] = gram_of_two(some, rows) * scale


def gram_of_two(left, right):
    return lax.dot_general(left, right, (((0,), (0,)), ((), ())), preferred_element_type=jnp.float32)


def gram_pass(tables, *acts):
    hidden = acts[0].shape[1]
    rows = sum(act.shape[0] for act in acts)
    vmem = pl.BlockSpec(memory_space=pltpu.VMEM)
    return pl.pallas_call(
        gram_kernel,
        out_shape=jax.ShapeDtypeStruct((hidden, hidden), jnp.float32),
        in_specs=[vmem] * (len(acts) + 1),
        out_specs=vmem,
        compiler_params=pltpu.CompilerParams(vmem_limit_bytes=16 * 1024 * 1024),
        cost_estimate=pl.CostEstimate(
            flops=2 * rows * hidden * hidden,
            bytes_accessed=4 * hidden * hidden + 2 * rows * hidden,
            transcendentals=0,
        ),
    )(tables, *acts)


def mix_kernel(keep, got, side, near_low, near_high, far_low, far_high, mixed):
    most, tok = near_low.shape[0], mixed.shape[0]
    for start, stop, near, far in (
        (0, most, near_low, far_low),
        (most, tok, near_high, far_high),
    ):
        total = keep[start:stop, :].astype(jnp.float32) + got[start:stop, :].astype(jnp.float32)
        total = total + side[start:stop, :].astype(jnp.float32) + near[...].astype(jnp.float32)
        mixed[start:stop, :] = (total + far[...].astype(jnp.float32)).astype(mixed.dtype)


def mix_pass(*parts):
    side = parts[2]
    vmem = pl.BlockSpec(memory_space=pltpu.VMEM)
    return pl.pallas_call(
        mix_kernel,
        out_shape=jax.ShapeDtypeStruct(side.shape, side.dtype),
        in_specs=[vmem] * len(parts),
        out_specs=vmem,
        compiler_params=pltpu.CompilerParams(vmem_limit_bytes=12 * 1024 * 1024),
    )(*parts)


def staged(routes, probs, tokens, w_gate, w_up, w_down):
    tok, top = routes.shape
    size = lax.axis_size("expert")
    slots = 5 * tok * top // (4 * size)
    capacity = tok * top // 2
    half = tok // 2
    me = lax.axis_index("expert")
    z, y, core = me // 4, me // 2 % 2, me % 2

    def swapped(array, bit):
        return lax.ppermute(array, "expert", [(i, i ^ bit) for i in range(size)])

    sibling = functools.partial(swapped, bit=1)
    column = functools.partial(swapped, bit=2)
    pair = functools.partial(swapped, bit=4)
    far = functools.partial(swapped, bit=8)

    def together(*arrays):
        return lax.optimization_barrier(arrays)

    spots = jnp.stack(
        [
            (z ^ k) * 4 + (y ^ column_bit) * 2 + (core ^ core_bit)
            for k in range(4)
            for core_bit in range(2)
            for column_bit in range(2)
        ]
    ).astype(jnp.int32)

    def expert(k, *xs, pieces=None, picked=None):
        return plane_pass(k, tables, xs, w_gate, w_up, w_down, slots, pieces, picked)

    mine, a0_low, a0_high = prepare_pass(routes, probs, tokens, size)
    a0 = tokens
    a1, low, b0, c0, weight, a0_high = together(
        pair(a0),
        far(a0_low),
        column(a0),
        sibling(a0),
        lax.all_to_all(mine, "expert", split_axis=0, concat_axis=0, tiled=True),
        a0_high,
    )
    tables = ranks_pass(capacity, spots, weight)
    high = far(a0_high)
    b1 = column(a1)
    d0 = sibling(b0)
    c1 = sibling(a1)
    keep0, give0, act0 = expert(0, a0, b0, c0, d0)
    high, b1, c1, keep0, give0, act0, tables = together(
        high, b1, c1, keep0, give0, act0, tables
    )
    a2 = jnp.concatenate([low, high], axis=0)
    a3 = pair(a2)
    b2 = column(a2)
    d1 = sibling(b1)
    c2 = sibling(a2)
    keep1, give1, give1_side, act1 = expert(1, a1, b1, c1, d1, pieces=(tok, tok))
    got1_side = sibling(give1_side)
    a3, b2, c2, keep1, give1, act1, got1_side = together(
        a3, b2, c2, keep1, give1, act1, got1_side
    )
    b3 = pair(b2)
    came1_low = column(summed(keep1[tok : tok + half], got1_side[:half]))
    got1 = sibling(give1)
    d2 = sibling(b2)
    c3 = sibling(a3)
    keep2, give2, give2_low, give2_high, act2 = expert(
        2, a2, b2, c2, d2, pieces=(tok, half, half)
    )
    got2_high = sibling(give2_high)
    keep3, give3, act3 = expert(3, a3, c3, picked=(0, 2))
    got0 = sibling(give0)
    b3, came1_low, got0, got1, got2_high, keep2, give2, give2_low, act2, keep3, give3, act3 = (
        together(
            b3, came1_low, got0, got1, got2_high, keep2, give2, give2_low, act2, keep3, give3, act3
        )
    )
    d3 = sibling(b3)
    near1 = summed(keep1[:half], got1[:half], came1_low)

    side_high = column(summed(keep2[tok + half :], got2_high))
    got2 = sibling(give2)
    keep3_side, give3_side, act4 = expert(3, b3, d3, picked=(1, 3))
    keep3_side, give3_side, act4, got2, side_high, near1 = together(
        keep3_side, give3_side, act4, got2, side_high, near1
    )
    got2_low, got3 = sibling(give2_low), sibling(give3)
    far2_high = far(summed(keep2[half:tok], got2[half:], side_high))
    got3_side = sibling(give3_side)
    came3_low = column(summed(keep3_side[:half], got3_side[:half]))
    came3_high = column(summed(keep3_side[half:], got3_side[half:]))
    near1_low = pair(near1)
    side0 = summed(keep0[tok:], got0[tok:])
    side1 = summed(keep1[tok + half :], got1_side[half:])
    came3_low, came3_high, far2_high, near1_low, side0, side1, got2_low, got3 = together(
        came3_low, came3_high, far2_high, near1_low, side0, side1, got2_low, got3
    )
    far3_high = far(summed(keep3[half:], got3[half:], came3_high))
    pair3_low = pair(summed(keep3[:half], got3[:half], came3_low))
    side_low = column(summed(keep2[tok : tok + half], got2_low))
    came1_high = column(side1)
    gram = gram_pass(tables, act0, act1, act2, act3, act4)
    far3_high, pair3_low, side_low, came1_high, side0, gram = together(
        far3_high, pair3_low, side_low, came1_high, side0, gram
    )
    far2_low = summed(keep2[:half], got2[:half], pair3_low, side_low)
    far2_low, far3_high, came1_high, side0 = together(far2_low, far3_high, came1_high, side0)
    far2_low = far(far2_low)
    near1_high = pair(summed(keep1[half:tok], got1[half:], came1_high, far3_high))
    last0 = column(side0)
    mixed = mix_pass(
        keep0, got0, last0, near1_low, near1_high, far2_low, far2_high
    )

    return gram[None], mixed


def gathered(routes, probs, tokens, w_gate, w_up, w_down):
    tok_rows, top = routes.shape
    size = lax.axis_size("expert")
    capacity = tok_rows * top // 2
    every_token = lax.all_gather(tokens, "expert", tiled=True)
    weight = weights_for_me(routes, probs, size)
    named = (weight >= 0.0).astype(jnp.int32)
    within = jnp.cumsum(named, axis=1) - named
    per_device = jnp.sum(named, axis=1)
    before = jnp.cumsum(per_device) - per_device
    rank = within + before[:, None]
    kept = (named == 1) & (rank < capacity)
    count = jnp.minimum(jnp.sum(per_device), capacity)
    slot = jnp.where(kept, rank, -1).reshape(size * tok_rows)
    place = jnp.arange(capacity, dtype=jnp.int32)
    select = (place[:, None] == slot[None, :]).astype(jnp.bfloat16)
    rows = jnp.dot(select, every_token, preferred_element_type=jnp.float32).astype(jnp.bfloat16)
    gram_sum, made = expert_pass(rows, w_gate, w_up, w_down)
    gram = gram_sum * (2.0 / count.astype(jnp.float32))
    spread = lax.dot_general(
        select, made, (((0,), (0,)), ((), ())), preferred_element_type=jnp.float32
    )
    partial = (spread * weight.reshape(size * tok_rows, 1)).astype(jnp.bfloat16)
    mixed = lax.psum_scatter(partial, "expert", scatter_dimension=0, tiled=True)
    return gram[None], mixed.astype(jnp.bfloat16)


def shards(routes, probs, tokens, gate_weight, up_weight, down_weight):
    body = staged if lax.axis_size("expert") == 16 else gathered
    return body(routes, probs, tokens, gate_weight[0], up_weight[0], down_weight[0])


def solution(mesh):
    placed = (
        P(("parts", "expert"), None),
        P(("parts", "expert"), None),
        P(("parts", "expert"), None),
        P("expert", None, None),
        P("expert", None, None),
        P("expert", None, None),
    )
    return jax.shard_map(
        shards,
        mesh=mesh,
        in_specs=placed,
        out_specs=(P(("parts", "expert"), None, None), P(("parts", "expert"), None)),
        check_vma=False,
    )
```

```python
import functools

import jax
import jax.numpy as jnp
from jax import lax
from jax.experimental import pallas as pl
from jax.experimental.pallas import tpu as pltpu
from jax.sharding import PartitionSpec as P


def gram_of(rows):
    return lax.dot_general(rows, rows, (((0,), (0,)), ((), ())), preferred_element_type=jnp.float32)


def expert_pass(rows, w_gate, w_up, w_down):
    gate = jnp.dot(rows, w_gate, preferred_element_type=jnp.float32)
    up = jnp.dot(rows, w_up, preferred_element_type=jnp.float32)
    act = (jax.nn.silu(gate) * up).astype(jnp.bfloat16)
    gram_sum = gram_of(act)
    made = jnp.dot(act, w_down, preferred_element_type=jnp.float32).astype(jnp.bfloat16)
    return (gram_sum, made)


def weights_for_me(routes, probs, experts):
    names = routes.T[None, :, :] == jnp.arange(experts, dtype=jnp.int32)[:, None, None]
    weight = jnp.sum(jnp.where(names, probs.T[None, :, :], 0.0), axis=1)
    mine = jnp.where(jnp.any(names, axis=1), weight, -1.0)
    return lax.all_to_all(mine, "expert", split_axis=0, concat_axis=0, tiled=True)


def prepare_kernel(routes, probs, tokens, mine, low, high, names, shares, sems):
    half = low.shape[0]
    pairs = (
        (routes, names),
        (probs, shares),
        (tokens.at[pl.ds(0, half), :], low),
        (tokens.at[pl.ds(half, half), :], high),
    )
    copies = [pltpu.make_async_copy(*pair, sems.at[i]) for i, pair in enumerate(pairs)]
    for copy in copies:
        copy.start()
    for copy in copies[:2]:
        copy.wait()
    for e in range(mine.shape[0]):
        hit = (names[...] == e).astype(jnp.float32)
        named = jnp.sum(hit, axis=0, keepdims=True)
        share = jnp.sum(hit * shares[...], axis=0, keepdims=True)
        mine[pl.ds(e, 1), :] = jnp.where(named > 0.0, share, -1.0)
    for copy in copies[2:]:
        copy.wait()


def prepare_pass(routes, probs, tokens, experts):
    tok, top = routes.shape
    half = jax.ShapeDtypeStruct((tok // 2, tokens.shape[1]), tokens.dtype)
    vmem = pl.BlockSpec(memory_space=pltpu.VMEM)
    return pl.pallas_call(
        prepare_kernel,
        out_shape=(jax.ShapeDtypeStruct((experts, tok), jnp.float32), half, half),
        in_specs=[pl.BlockSpec(memory_space=pl.ANY)] * 3,
        out_specs=[vmem] * 3,
        scratch_shapes=[
            pltpu.VMEM((top, tok), routes.dtype),
            pltpu.VMEM((top, tok), probs.dtype),
            pltpu.SemaphoreType.DMA((4,)),
        ],
        compiler_params=pltpu.CompilerParams(vmem_limit_bytes=4 * 1024 * 1024),
    )(routes.T, probs.T, tokens)


def summed(*parts):
    total = parts[0].astype(jnp.float32)
    for part in parts[1:]:
        total = total + part.astype(jnp.float32)
    return total.astype(jnp.bfloat16)


def ranks_kernel(capacity, spots, weight, tables, ranks, chip_ranks):
    blocks, tok = weight.shape
    planes = blocks // 4
    named = (weight[...] >= 0.0).astype(jnp.float32)
    lane = lax.broadcasted_iota(jnp.int32, (tok, tok), 0)
    below = (lane < lax.broadcasted_iota(jnp.int32, (tok, tok), 1)).astype(jnp.float32)
    within = jnp.dot(named, below, preferred_element_type=jnp.float32)
    totals = jnp.broadcast_to(jnp.sum(named, axis=1, keepdims=True), (blocks, tok))
    row = lax.broadcasted_iota(jnp.int32, (blocks, blocks), 0)
    column = lax.broadcasted_iota(jnp.int32, (blocks, blocks), 1)
    earlier = (column < row).astype(jnp.float32)
    before = jnp.dot(earlier, totals, preferred_element_type=jnp.float32)
    rank = within + before
    kept = (named > 0.0) & (rank < capacity)
    first = (column < row // 4 * 4).astype(jnp.float32)
    start = jnp.dot(first, totals, preferred_element_type=jnp.float32)
    ranks[...] = jnp.where(kept, rank - start, -1.0)
    first = (column < row // 2 * 2).astype(jnp.float32)
    start = jnp.dot(first, totals, preferred_element_type=jnp.float32)
    chip_ranks[...] = jnp.where(kept, rank - start, -1.0)
    for i in range(4):
        span = pl.ds(i * tok, tok)
        tables[pl.ds(2 * planes, 1), span] = chip_ranks[pl.ds(spots[4 * planes - 4 + i], 1), :]
    for k in range(planes):
        for i in range(4):
            span = pl.ds(i * tok, tok)
            tables[pl.ds(k, 1), span] = ranks[pl.ds(spots[4 * k + i], 1), :]
            tables[pl.ds(planes + k, 1), span] = weight[pl.ds(spots[4 * k + i], 1), :]
    count = jnp.minimum(jnp.sum(totals[:, :1], axis=0, keepdims=True), float(capacity))
    rest = (tables.shape[0] - 2 * planes - 1, tables.shape[1])
    tables[2 * planes + 1 :, :] = jnp.broadcast_to(2.0 / count, rest)


def ranks_pass(capacity, spots, weight):
    blocks, tok = weight.shape
    vmem = pl.BlockSpec(memory_space=pltpu.VMEM)
    return pl.pallas_call(
        functools.partial(ranks_kernel, capacity),
        out_shape=jax.ShapeDtypeStruct((blocks // 4 * 2 + 8, 4 * tok), jnp.float32),
        in_specs=[pl.BlockSpec(memory_space=pltpu.SMEM), vmem],
        out_specs=vmem,
        scratch_shapes=[pltpu.VMEM(weight.shape, jnp.float32)] * 2,
        compiler_params=pltpu.CompilerParams(vmem_limit_bytes=4 * 1024 * 1024),
    )(spots, weight)


def plane_kernel(k, picked, gives, tables, *refs):
    *xs, w_gate, w_up, w_down, keep = refs[: -gives - 2]
    *gives, act, rows = refs[-gives - 2 :]
    slots, hidden = act.shape
    features = rows.shape[1]
    half, width = keep.shape[0], tables.shape[1]
    wide, cut = 256, 512
    place = tables[pl.ds(8 if picked else k, 1), :]
    share = tables[pl.ds(4 + k, 1), :]
    if picked:
        tok = width // 4
        place, share = (
            jnp.concatenate([row[:, i * tok : (i + 1) * tok] for i in picked], axis=1)
            for row in (place, share)
        )
        width = 2 * tok
    slot = lax.broadcasted_iota(jnp.int32, (slots, width), 0).astype(jnp.float32)
    hits = slot == place
    scale = jnp.sum(jnp.where(hits, share, 0.0), axis=1, keepdims=True)
    select = hits.astype(jnp.float32).astype(jnp.bfloat16)
    for i in range(features // cut):
        span = pl.ds(i * cut, cut)
        x = jnp.concatenate([block[:, span] for block in xs], axis=0)
        rows[:, span] = jnp.dot(select, x, preferred_element_type=jnp.float32).astype(jnp.bfloat16)
    for i in range(hidden // wide):
        span = pl.ds(i * wide, wide)
        gate = jnp.dot(rows[...], w_gate[:, span], preferred_element_type=jnp.float32)
        up = jnp.dot(rows[...], w_up[:, span], preferred_element_type=jnp.float32)
        act[:, span] = (gate / (1.0 + jnp.exp(-gate)) * up).astype(jnp.bfloat16)
    back = select.T
    for i in range(features // cut):
        span = pl.ds(i * cut, cut)
        result = jnp.dot(act[...], w_down[:, span], preferred_element_type=jnp.float32)
        made = (result * scale).astype(jnp.bfloat16)
        spread = jnp.dot(back, made, preferred_element_type=jnp.float32).astype(jnp.bfloat16)
        keep[:, span] = spread[:half]
        start = half
        for give in gives:
            give[:, span] = spread[start : start + give.shape[0]]
            start += give.shape[0]


def plane_pass(k, tables, xs, w_gate, w_up, w_down, slots, pieces=None, picked=None):
    tok, features = xs[0].shape
    hidden = w_gate.shape[1]
    blocks = 2 if picked else 4
    rows = blocks * slots
    half = blocks // 2 * tok
    pieces = pieces or (half,)
    outs = tuple(jax.ShapeDtypeStruct((some, features), jnp.bfloat16) for some in (half, *pieces))
    outs += (jax.ShapeDtypeStruct((rows, hidden), jnp.bfloat16),)
    vmem = pl.BlockSpec(memory_space=pltpu.VMEM)
    flops = 2 * rows * (3 * features * hidden + 2 * blocks * tok * features)
    moved = 2 * (3 * features * hidden + 2 * blocks * tok * features)
    return pl.pallas_call(
        functools.partial(plane_kernel, k, picked, len(pieces)),
        out_shape=outs,
        in_specs=[vmem] * (len(xs) + 4),
        out_specs=[vmem] * len(outs),
        scratch_shapes=[pltpu.VMEM((rows, features), jnp.bfloat16)],
        compiler_params=pltpu.CompilerParams(vmem_limit_bytes=12 * 1024 * 1024),
        cost_estimate=pl.CostEstimate(
            flops=flops, bytes_accessed=moved, transcendentals=rows * hidden
        ),
    )(tables, *xs, w_gate, w_up, w_down)


def gram_kernel(tables, *refs):
    *acts, gram = refs
    wide = 256
    scale = tables[9:10, :1]
    rows = jnp.concatenate([act[...] for act in acts], axis=0)
    for i in range(gram.shape[0] // wide):
        some = rows[:, i * wide : (i + 1) * wide]
        gram[pl.ds(i * wide, wide), :] = gram_of_two(some, rows) * scale


def gram_of_two(left, right):
    return lax.dot_general(left, right, (((0,), (0,)), ((), ())), preferred_element_type=jnp.float32)


def gram_pass(tables, *acts):
    hidden = acts[0].shape[1]
    rows = sum(act.shape[0] for act in acts)
    vmem = pl.BlockSpec(memory_space=pltpu.VMEM)
    return pl.pallas_call(
        gram_kernel,
        out_shape=jax.ShapeDtypeStruct((hidden, hidden), jnp.float32),
        in_specs=[vmem] * (len(acts) + 1),
        out_specs=vmem,
        compiler_params=pltpu.CompilerParams(vmem_limit_bytes=16 * 1024 * 1024),
        cost_estimate=pl.CostEstimate(
            flops=2 * rows * hidden * hidden,
            bytes_accessed=4 * hidden * hidden + 2 * rows * hidden,
            transcendentals=0,
        ),
    )(tables, *acts)


def mix_kernel(
    keep, got, side_low, side_high, near_low, near_high, far_low, far_high, mixed
):
    most, tok = near_low.shape[0], mixed.shape[0]
    for start, stop, *parts in (
        (0, most, side_low, near_low, far_low),
        (most, tok, side_high, near_high, far_high),
    ):
        total = keep[start:stop, :].astype(jnp.float32) + got[start:stop, :].astype(jnp.float32)
        for part in parts:
            total = total + part[...].astype(jnp.float32)
        mixed[start:stop, :] = total.astype(mixed.dtype)


def mix_pass(*parts):
    tok = 2 * parts[2].shape[0]
    vmem = pl.BlockSpec(memory_space=pltpu.VMEM)
    return pl.pallas_call(
        mix_kernel,
        out_shape=jax.ShapeDtypeStruct((tok, parts[2].shape[1]), parts[2].dtype),
        in_specs=[vmem] * len(parts),
        out_specs=vmem,
        compiler_params=pltpu.CompilerParams(vmem_limit_bytes=12 * 1024 * 1024),
    )(*parts)


def staged(routes, probs, tokens, w_gate, w_up, w_down):
    tok, top = routes.shape
    size = lax.axis_size("expert")
    slots = 5 * tok * top // (4 * size)
    capacity = tok * top // 2
    half = tok // 2
    me = lax.axis_index("expert")
    z, y, core = me // 4, me // 2 % 2, me % 2

    def swapped(array, bit):
        return lax.ppermute(array, "expert", [(i, i ^ bit) for i in range(size)])

    sibling = functools.partial(swapped, bit=1)
    column = functools.partial(swapped, bit=2)
    pair = functools.partial(swapped, bit=4)
    far = functools.partial(swapped, bit=8)

    def together(*arrays):
        return lax.optimization_barrier(arrays)

    spots = jnp.stack(
        [
            (z ^ k) * 4 + (y ^ column_bit) * 2 + (core ^ core_bit)
            for k in range(4)
            for core_bit in range(2)
            for column_bit in range(2)
        ]
    ).astype(jnp.int32)

    def expert(k, *xs, pieces=None, picked=None):
        return plane_pass(k, tables, xs, w_gate, w_up, w_down, slots, pieces, picked)

    mine, a0_low, a0_high = prepare_pass(routes, probs, tokens, size)
    a0 = tokens
    a1, low, b0, c0, a0_high, mine = together(
        pair(a0), far(a0_low), column(a0), sibling(a0), a0_high, mine
    )
    weight = lax.all_to_all(mine, "expert", split_axis=0, concat_axis=0, tiled=True)
    high = far(a0_high)
    b1 = column(a1)
    d0 = sibling(b0)
    c1 = sibling(a1)
    high, b1, c1, d0, weight = together(high, b1, c1, d0, weight)
    tables = ranks_pass(capacity, spots, weight)
    a2 = jnp.concatenate([low, high], axis=0)
    a3 = pair(a2)
    b2 = column(a2)
    d1 = sibling(b1)
    c2 = sibling(a2)
    keep1, give1, give1_side, act1 = expert(1, a1, b1, c1, d1, pieces=(tok, tok))
    got1_side = sibling(give1_side)
    a3, b2, c2, keep1, give1, act1, got1_side, tables = together(
        a3, b2, c2, keep1, give1, act1, got1_side, tables
    )
    b3 = pair(b2)
    came1_low = column(summed(keep1[tok : tok + half], got1_side[:half]))
    got1 = sibling(give1)
    d2 = sibling(b2)
    c3 = sibling(a3)
    keep2, give2, give2_low, give2_high, act2 = expert(
        2, a2, b2, c2, d2, pieces=(tok, half, half)
    )
    got2_high = sibling(give2_high)
    keep3, give3, act3 = expert(3, a3, c3, picked=(0, 2))
    b3, came1_low, got1, got2_high, keep2, give2, give2_low, act2, keep3, give3, act3 = (
        together(
            b3, came1_low, got1, got2_high, keep2, give2, give2_low, act2, keep3, give3, act3
        )
    )
    d3 = sibling(b3)
    near1 = summed(keep1[:half], got1[:half], came1_low)

    side_high = column(summed(keep2[tok + half :], got2_high))
    got2 = sibling(give2)
    keep3_side, give3_side, act4 = expert(3, b3, d3, picked=(1, 3))
    keep3_side, give3_side, act4, got2, side_high, near1 = together(
        keep3_side, give3_side, act4, got2, side_high, near1
    )
    got2_low, got3 = sibling(give2_low), sibling(give3)
    far2_high = far(summed(keep2[half:tok], got2[half:], side_high))
    got3_side = sibling(give3_side)
    came3_low = column(summed(keep3_side[:half], got3_side[:half]))
    came3_high = column(summed(keep3_side[half:], got3_side[half:]))
    near1_low = pair(near1)
    keep0, give0, act0 = expert(0, a0, b0, c0, d0)
    side1 = summed(keep1[tok + half :], got1_side[half:])
    came3_low, came3_high, far2_high, near1_low, side1, got2_low, got3, keep0, give0, act0 = (
        together(
            came3_low, came3_high, far2_high, near1_low, side1, got2_low, got3, keep0, give0, act0
        )
    )
    got0 = sibling(give0)
    far3_high = far(summed(keep3[half:], got3[half:], came3_high))
    pair3_low = pair(summed(keep3[:half], got3[:half], came3_low))
    side_low = column(summed(keep2[tok : tok + half], got2_low))
    came1_high = column(side1)
    gram = gram_pass(tables, act0, act1, act2, act3, act4)
    far3_high, pair3_low, side_low, came1_high, got0, gram = together(
        far3_high, pair3_low, side_low, came1_high, got0, gram
    )
    far2_low = summed(keep2[:half], got2[:half], pair3_low, side_low)
    far2_low, far3_high, came1_high, got0 = together(far2_low, far3_high, came1_high, got0)
    far2_low = far(far2_low)
    near1_high = pair(summed(keep1[half:tok], got1[half:], came1_high, far3_high))
    last0_low = column(summed(keep0[tok : tok + half], got0[tok : tok + half]))
    last0_high = column(summed(keep0[tok + half :], got0[tok + half :]))
    mixed = mix_pass(
        keep0, got0, last0_low, last0_high, near1_low, near1_high, far2_low, far2_high
    )

    return gram[None], mixed


def gathered(routes, probs, tokens, w_gate, w_up, w_down):
    tok_rows, top = routes.shape
    size = lax.axis_size("expert")
    capacity = tok_rows * top // 2
    every_token = lax.all_gather(tokens, "expert", tiled=True)
    weight = weights_for_me(routes, probs, size)
    named = (weight >= 0.0).astype(jnp.int32)
    within = jnp.cumsum(named, axis=1) - named
    per_device = jnp.sum(named, axis=1)
    before = jnp.cumsum(per_device) - per_device
    rank = within + before[:, None]
    kept = (named == 1) & (rank < capacity)
    count = jnp.minimum(jnp.sum(per_device), capacity)
    slot = jnp.where(kept, rank, -1).reshape(size * tok_rows)
    place = jnp.arange(capacity, dtype=jnp.int32)
    select = (place[:, None] == slot[None, :]).astype(jnp.bfloat16)
    rows = jnp.dot(select, every_token, preferred_element_type=jnp.float32).astype(jnp.bfloat16)
    gram_sum, made = expert_pass(rows, w_gate, w_up, w_down)
    gram = gram_sum * (2.0 / count.astype(jnp.float32))
    spread = lax.dot_general(
        select, made, (((0,), (0,)), ((), ())), preferred_element_type=jnp.float32
    )
    partial = (spread * weight.reshape(size * tok_rows, 1)).astype(jnp.bfloat16)
    mixed = lax.psum_scatter(partial, "expert", scatter_dimension=0, tiled=True)
    return gram[None], mixed.astype(jnp.bfloat16)


def shards(routes, probs, tokens, gate_weight, up_weight, down_weight):
    body = staged if lax.axis_size("expert") == 16 else gathered
    return body(routes, probs, tokens, gate_weight[0], up_weight[0], down_weight[0])


def solution(mesh):
    placed = (
        P(("parts", "expert"), None),
        P(("parts", "expert"), None),
        P(("parts", "expert"), None),
        P("expert", None, None),
        P("expert", None, None),
        P("expert", None, None),
    )
    return jax.shard_map(
        shards,
        mesh=mesh,
        in_specs=placed,
        out_specs=(P(("parts", "expert"), None, None), P(("parts", "expert"), None)),
        check_vma=False,
    )
```

```python
import functools

import jax
import jax.numpy as jnp
from jax import lax
from jax.experimental import pallas as pl
from jax.experimental.pallas import tpu as pltpu
from jax.sharding import PartitionSpec as P


def gram_of(rows):
    return lax.dot_general(rows, rows, (((0,), (0,)), ((), ())), preferred_element_type=jnp.float32)


def expert_pass(rows, w_gate, w_up, w_down):
    gate = jnp.dot(rows, w_gate, preferred_element_type=jnp.float32)
    up = jnp.dot(rows, w_up, preferred_element_type=jnp.float32)
    act = (jax.nn.silu(gate) * up).astype(jnp.bfloat16)
    gram_sum = gram_of(act)
    made = jnp.dot(act, w_down, preferred_element_type=jnp.float32).astype(jnp.bfloat16)
    return (gram_sum, made)


def weights_for_me(routes, probs, experts):
    names = routes.T[None, :, :] == jnp.arange(experts, dtype=jnp.int32)[:, None, None]
    weight = jnp.sum(jnp.where(names, probs.T[None, :, :], 0.0), axis=1)
    mine = jnp.where(jnp.any(names, axis=1), weight, -1.0)
    return lax.all_to_all(mine, "expert", split_axis=0, concat_axis=0, tiled=True)


def prepare_kernel(routes, probs, tokens, mine, low, high, names, shares, sems):
    half = low.shape[0]
    pairs = (
        (routes, names),
        (probs, shares),
        (tokens.at[pl.ds(0, half), :], low),
        (tokens.at[pl.ds(half, half), :], high),
    )
    copies = [pltpu.make_async_copy(*pair, sems.at[i]) for i, pair in enumerate(pairs)]
    for copy in copies:
        copy.start()
    for copy in copies[:2]:
        copy.wait()
    for e in range(mine.shape[0]):
        hit = (names[...] == e).astype(jnp.float32)
        named = jnp.sum(hit, axis=0, keepdims=True)
        share = jnp.sum(hit * shares[...], axis=0, keepdims=True)
        mine[pl.ds(e, 1), :] = jnp.where(named > 0.0, share, -1.0)
    for copy in copies[2:]:
        copy.wait()


def prepare_pass(routes, probs, tokens, experts):
    tok, top = routes.shape
    half = jax.ShapeDtypeStruct((tok // 2, tokens.shape[1]), tokens.dtype)
    vmem = pl.BlockSpec(memory_space=pltpu.VMEM)
    return pl.pallas_call(
        prepare_kernel,
        out_shape=(jax.ShapeDtypeStruct((experts, tok), jnp.float32), half, half),
        in_specs=[pl.BlockSpec(memory_space=pl.ANY)] * 3,
        out_specs=[vmem] * 3,
        scratch_shapes=[
            pltpu.VMEM((top, tok), routes.dtype),
            pltpu.VMEM((top, tok), probs.dtype),
            pltpu.SemaphoreType.DMA((4,)),
        ],
        compiler_params=pltpu.CompilerParams(vmem_limit_bytes=4 * 1024 * 1024),
    )(routes.T, probs.T, tokens)


def summed(*parts):
    total = parts[0].astype(jnp.float32)
    for part in parts[1:]:
        total = total + part.astype(jnp.float32)
    return total.astype(jnp.bfloat16)


def ranks_kernel(capacity, spots, weight, tables, ranks, chip_ranks):
    blocks, tok = weight.shape
    planes = blocks // 4
    named = (weight[...] >= 0.0).astype(jnp.float32)
    lane = lax.broadcasted_iota(jnp.int32, (tok, tok), 0)
    below = (lane < lax.broadcasted_iota(jnp.int32, (tok, tok), 1)).astype(jnp.float32)
    within = jnp.dot(named, below, preferred_element_type=jnp.float32)
    totals = jnp.broadcast_to(jnp.sum(named, axis=1, keepdims=True), (blocks, tok))
    row = lax.broadcasted_iota(jnp.int32, (blocks, blocks), 0)
    column = lax.broadcasted_iota(jnp.int32, (blocks, blocks), 1)
    earlier = (column < row).astype(jnp.float32)
    before = jnp.dot(earlier, totals, preferred_element_type=jnp.float32)
    rank = within + before
    kept = (named > 0.0) & (rank < capacity)
    first = (column < row // 4 * 4).astype(jnp.float32)
    start = jnp.dot(first, totals, preferred_element_type=jnp.float32)
    ranks[...] = jnp.where(kept, rank - start, -1.0)
    first = (column < row // 2 * 2).astype(jnp.float32)
    start = jnp.dot(first, totals, preferred_element_type=jnp.float32)
    chip_ranks[...] = jnp.where(kept, rank - start, -1.0)
    for i in range(4):
        span = pl.ds(i * tok, tok)
        tables[pl.ds(2 * planes, 1), span] = chip_ranks[pl.ds(spots[4 * planes - 4 + i], 1), :]
    for k in range(planes):
        for i in range(4):
            span = pl.ds(i * tok, tok)
            tables[pl.ds(k, 1), span] = ranks[pl.ds(spots[4 * k + i], 1), :]
            tables[pl.ds(planes + k, 1), span] = weight[pl.ds(spots[4 * k + i], 1), :]
    count = jnp.minimum(jnp.sum(totals[:, :1], axis=0, keepdims=True), float(capacity))
    rest = (tables.shape[0] - 2 * planes - 1, tables.shape[1])
    tables[2 * planes + 1 :, :] = jnp.broadcast_to(2.0 / count, rest)


def ranks_pass(capacity, spots, weight):
    blocks, tok = weight.shape
    vmem = pl.BlockSpec(memory_space=pltpu.VMEM)
    return pl.pallas_call(
        functools.partial(ranks_kernel, capacity),
        out_shape=jax.ShapeDtypeStruct((blocks // 4 * 2 + 8, 4 * tok), jnp.float32),
        in_specs=[pl.BlockSpec(memory_space=pltpu.SMEM), vmem],
        out_specs=vmem,
        scratch_shapes=[pltpu.VMEM(weight.shape, jnp.float32)] * 2,
        compiler_params=pltpu.CompilerParams(vmem_limit_bytes=4 * 1024 * 1024),
    )(spots, weight)


def plane_kernel(k, picked, gives, tables, *refs):
    *xs, w_gate, w_up, w_down, keep = refs[: -gives - 2]
    *gives, act, rows = refs[-gives - 2 :]
    slots, hidden = act.shape
    features = rows.shape[1]
    half, width = keep.shape[0], tables.shape[1]
    wide, cut = 256, 512
    place = tables[pl.ds(8 if picked else k, 1), :]
    share = tables[pl.ds(4 + k, 1), :]
    if picked:
        tok = width // 4
        place, share = (
            jnp.concatenate([row[:, i * tok : (i + 1) * tok] for i in picked], axis=1)
            for row in (place, share)
        )
        width = 2 * tok
    slot = lax.broadcasted_iota(jnp.int32, (slots, width), 0).astype(jnp.float32)
    hits = slot == place
    scale = jnp.sum(jnp.where(hits, share, 0.0), axis=1, keepdims=True)
    select = hits.astype(jnp.float32).astype(jnp.bfloat16)
    for i in range(features // cut):
        span = pl.ds(i * cut, cut)
        x = jnp.concatenate([block[:, span] for block in xs], axis=0)
        rows[:, span] = jnp.dot(select, x, preferred_element_type=jnp.float32).astype(jnp.bfloat16)
    for i in range(hidden // wide):
        span = pl.ds(i * wide, wide)
        gate = jnp.dot(rows[...], w_gate[:, span], preferred_element_type=jnp.float32)
        up = jnp.dot(rows[...], w_up[:, span], preferred_element_type=jnp.float32)
        act[:, span] = (gate / (1.0 + jnp.exp(-gate)) * up).astype(jnp.bfloat16)
    back = select.T
    for i in range(features // cut):
        span = pl.ds(i * cut, cut)
        result = jnp.dot(act[...], w_down[:, span], preferred_element_type=jnp.float32)
        made = (result * scale).astype(jnp.bfloat16)
        spread = jnp.dot(back, made, preferred_element_type=jnp.float32).astype(jnp.bfloat16)
        keep[:, span] = spread[:half]
        start = half
        for give in gives:
            give[:, span] = spread[start : start + give.shape[0]]
            start += give.shape[0]


def plane_pass(k, tables, xs, w_gate, w_up, w_down, slots, pieces=None, picked=None):
    tok, features = xs[0].shape
    hidden = w_gate.shape[1]
    blocks = 2 if picked else 4
    rows = blocks * slots
    half = blocks // 2 * tok
    pieces = pieces or (half,)
    outs = tuple(jax.ShapeDtypeStruct((some, features), jnp.bfloat16) for some in (half, *pieces))
    outs += (jax.ShapeDtypeStruct((rows, hidden), jnp.bfloat16),)
    vmem = pl.BlockSpec(memory_space=pltpu.VMEM)
    flops = 2 * rows * (3 * features * hidden + 2 * blocks * tok * features)
    moved = 2 * (3 * features * hidden + 2 * blocks * tok * features)
    return pl.pallas_call(
        functools.partial(plane_kernel, k, picked, len(pieces)),
        out_shape=outs,
        in_specs=[vmem] * (len(xs) + 4),
        out_specs=[vmem] * len(outs),
        scratch_shapes=[pltpu.VMEM((rows, features), jnp.bfloat16)],
        compiler_params=pltpu.CompilerParams(vmem_limit_bytes=12 * 1024 * 1024),
        cost_estimate=pl.CostEstimate(
            flops=flops, bytes_accessed=moved, transcendentals=rows * hidden
        ),
    )(tables, *xs, w_gate, w_up, w_down)


def gram_kernel(tables, *refs):
    *acts, gram = refs
    wide = 256
    scale = tables[9:10, :1]
    rows = jnp.concatenate([act[...] for act in acts], axis=0)
    for i in range(gram.shape[0] // wide):
        some = rows[:, i * wide : (i + 1) * wide]
        gram[pl.ds(i * wide, wide), :] = gram_of_two(some, rows) * scale


def gram_of_two(left, right):
    return lax.dot_general(left, right, (((0,), (0,)), ((), ())), preferred_element_type=jnp.float32)


def gram_pass(tables, *acts):
    hidden = acts[0].shape[1]
    rows = sum(act.shape[0] for act in acts)
    vmem = pl.BlockSpec(memory_space=pltpu.VMEM)
    return pl.pallas_call(
        gram_kernel,
        out_shape=jax.ShapeDtypeStruct((hidden, hidden), jnp.float32),
        in_specs=[vmem] * (len(acts) + 1),
        out_specs=vmem,
        compiler_params=pltpu.CompilerParams(vmem_limit_bytes=16 * 1024 * 1024),
        cost_estimate=pl.CostEstimate(
            flops=2 * rows * hidden * hidden,
            bytes_accessed=4 * hidden * hidden + 2 * rows * hidden,
            transcendentals=0,
        ),
    )(tables, *acts)


def mix_kernel(far_low, far_high, near_high, near_low, side, keep, got, mixed):
    most, tok = near_low.shape[0], mixed.shape[0]
    for start, stop, near, far in (
        (0, most, near_low, far_low),
        (most, tok, near_high, far_high),
    ):
        total = keep[start:stop, :].astype(jnp.float32) + got[start:stop, :].astype(jnp.float32)
        total = total + side[start:stop, :].astype(jnp.float32) + near[...].astype(jnp.float32)
        mixed[start:stop, :] = (total + far[...].astype(jnp.float32)).astype(mixed.dtype)


def mix_pass(*parts):
    side = parts[4]
    vmem = pl.BlockSpec(memory_space=pltpu.VMEM)
    return pl.pallas_call(
        mix_kernel,
        out_shape=jax.ShapeDtypeStruct(side.shape, side.dtype),
        in_specs=[vmem] * len(parts),
        out_specs=vmem,
        compiler_params=pltpu.CompilerParams(vmem_limit_bytes=12 * 1024 * 1024),
    )(*parts)


def staged(routes, probs, tokens, w_gate, w_up, w_down):
    tok, top = routes.shape
    size = lax.axis_size("expert")
    slots = 5 * tok * top // (4 * size)
    capacity = tok * top // 2
    half = tok // 2
    me = lax.axis_index("expert")
    z, y, core = me // 4, me // 2 % 2, me % 2

    def swapped(array, bit):
        return lax.ppermute(array, "expert", [(i, i ^ bit) for i in range(size)])

    sibling = functools.partial(swapped, bit=1)
    column = functools.partial(swapped, bit=2)
    pair = functools.partial(swapped, bit=4)
    far = functools.partial(swapped, bit=8)

    def together(*arrays):
        return lax.optimization_barrier(arrays)

    spots = jnp.stack(
        [
            (z ^ k) * 4 + (y ^ column_bit) * 2 + (core ^ core_bit)
            for k in range(4)
            for core_bit in range(2)
            for column_bit in range(2)
        ]
    ).astype(jnp.int32)

    def expert(k, *xs, pieces=None, picked=None):
        return plane_pass(k, tables, xs, w_gate, w_up, w_down, slots, pieces, picked)

    mine, a0_low, a0_high = prepare_pass(routes, probs, tokens, size)
    a0 = tokens
    a1, low, b0, c0, weight, a0_high = together(
        pair(a0),
        far(a0_low),
        column(a0),
        sibling(a0),
        lax.all_to_all(mine, "expert", split_axis=0, concat_axis=0, tiled=True),
        a0_high,
    )
    tables = ranks_pass(capacity, spots, weight)
    high = far(a0_high)
    b1 = column(a1)
    d0 = sibling(b0)
    c1 = sibling(a1)
    keep0, give0, act0 = expert(0, a0, b0, c0, d0)
    high, b1, c1, keep0, give0, act0, tables = together(
        high, b1, c1, keep0, give0, act0, tables
    )
    a2 = jnp.concatenate([low, high], axis=0)
    a3 = pair(a2)
    b2 = column(a2)
    d1 = sibling(b1)
    c2 = sibling(a2)
    keep1, give1, give1_side, act1 = expert(1, a1, b1, c1, d1, pieces=(tok, tok))
    got1_side = sibling(give1_side)
    a3, b2, c2, keep1, give1, act1, got1_side = together(
        a3, b2, c2, keep1, give1, act1, got1_side
    )
    b3 = pair(b2)
    came1_low = column(summed(keep1[tok : tok + half], got1_side[:half]))
    got1 = sibling(give1)
    d2 = sibling(b2)
    c3 = sibling(a3)
    keep2, give2, give2_low, give2_high, act2 = expert(
        2, a2, b2, c2, d2, pieces=(tok, half, half)
    )
    got2_high = sibling(give2_high)
    keep3, give3, act3 = expert(3, a3, c3, picked=(0, 2))
    got0 = sibling(give0)
    b3, came1_low, got0, got1, got2_high, keep2, give2, give2_low, act2, keep3, give3, act3 = (
        together(
            b3, came1_low, got0, got1, got2_high, keep2, give2, give2_low, act2, keep3, give3, act3
        )
    )
    d3 = sibling(b3)
    near1 = summed(keep1[:half], got1[:half], came1_low)

    side_high = column(summed(keep2[tok + half :], got2_high))
    got2 = sibling(give2)
    keep3_side, give3_side, act4 = expert(3, b3, d3, picked=(1, 3))
    keep3_side, give3_side, act4, got2, side_high, near1 = together(
        keep3_side, give3_side, act4, got2, side_high, near1
    )
    got2_low, got3 = sibling(give2_low), sibling(give3)
    far2_high = far(summed(keep2[half:tok], got2[half:], side_high))
    got3_side = sibling(give3_side)
    came3_low = column(summed(keep3_side[:half], got3_side[:half]))
    came3_high = column(summed(keep3_side[half:], got3_side[half:]))
    near1_low = pair(near1)
    side0 = summed(keep0[tok:], got0[tok:])
    side1 = summed(keep1[tok + half :], got1_side[half:])
    came3_low, came3_high, far2_high, near1_low, side0, side1, got2_low, got3 = together(
        came3_low, came3_high, far2_high, near1_low, side0, side1, got2_low, got3
    )
    far3_high = far(summed(keep3[half:], got3[half:], came3_high))
    pair3_low = pair(summed(keep3[:half], got3[:half], came3_low))
    side_low = column(summed(keep2[tok : tok + half], got2_low))
    came1_high = column(side1)
    gram = gram_pass(tables, act0, act1, act2, act3, act4)
    far3_high, pair3_low, side_low, came1_high, side0, gram = together(
        far3_high, pair3_low, side_low, came1_high, side0, gram
    )
    far2_low = summed(keep2[:half], got2[:half], pair3_low, side_low)
    far2_low, far3_high, came1_high, side0 = together(far2_low, far3_high, came1_high, side0)
    far2_low = far(far2_low)
    near1_high = pair(summed(keep1[half:tok], got1[half:], came1_high, far3_high))
    last0 = column(side0)
    mixed = mix_pass(
        far2_low, far2_high, near1_high, near1_low, last0, keep0, got0
    )

    return gram[None], mixed


def gathered(routes, probs, tokens, w_gate, w_up, w_down):
    tok_rows, top = routes.shape
    size = lax.axis_size("expert")
    capacity = tok_rows * top // 2
    every_token = lax.all_gather(tokens, "expert", tiled=True)
    weight = weights_for_me(routes, probs, size)
    named = (weight >= 0.0).astype(jnp.int32)
    within = jnp.cumsum(named, axis=1) - named
    per_device = jnp.sum(named, axis=1)
    before = jnp.cumsum(per_device) - per_device
    rank = within + before[:, None]
    kept = (named == 1) & (rank < capacity)
    count = jnp.minimum(jnp.sum(per_device), capacity)
    slot = jnp.where(kept, rank, -1).reshape(size * tok_rows)
    place = jnp.arange(capacity, dtype=jnp.int32)
    select = (place[:, None] == slot[None, :]).astype(jnp.bfloat16)
    rows = jnp.dot(select, every_token, preferred_element_type=jnp.float32).astype(jnp.bfloat16)
    gram_sum, made = expert_pass(rows, w_gate, w_up, w_down)
    gram = gram_sum * (2.0 / count.astype(jnp.float32))
    spread = lax.dot_general(
        select, made, (((0,), (0,)), ((), ())), preferred_element_type=jnp.float32
    )
    partial = (spread * weight.reshape(size * tok_rows, 1)).astype(jnp.bfloat16)
    mixed = lax.psum_scatter(partial, "expert", scatter_dimension=0, tiled=True)
    return gram[None], mixed.astype(jnp.bfloat16)


def shards(routes, probs, tokens, gate_weight, up_weight, down_weight):
    body = staged if lax.axis_size("expert") == 16 else gathered
    return body(routes, probs, tokens, gate_weight[0], up_weight[0], down_weight[0])


def solution(mesh):
    placed = (
        P(("parts", "expert"), None),
        P(("parts", "expert"), None),
        P(("parts", "expert"), None),
        P("expert", None, None),
        P("expert", None, None),
        P("expert", None, None),
    )
    return jax.shard_map(
        shards,
        mesh=mesh,
        in_specs=placed,
        out_specs=(P(("parts", "expert"), None, None), P(("parts", "expert"), None)),
        check_vma=False,
    )
```

```python
import functools

import jax
import jax.numpy as jnp
from jax import lax
from jax.experimental import pallas as pl
from jax.experimental.pallas import tpu as pltpu
from jax.sharding import PartitionSpec as P


def gram_of(rows):
    return lax.dot_general(rows, rows, (((0,), (0,)), ((), ())), preferred_element_type=jnp.float32)


def expert_pass(rows, w_gate, w_up, w_down):
    gate = jnp.dot(rows, w_gate, preferred_element_type=jnp.float32)
    up = jnp.dot(rows, w_up, preferred_element_type=jnp.float32)
    act = (jax.nn.silu(gate) * up).astype(jnp.bfloat16)
    gram_sum = gram_of(act)
    made = jnp.dot(act, w_down, preferred_element_type=jnp.float32).astype(jnp.bfloat16)
    return (gram_sum, made)


def weights_for_me(routes, probs, experts):
    names = routes.T[None, :, :] == jnp.arange(experts, dtype=jnp.int32)[:, None, None]
    weight = jnp.sum(jnp.where(names, probs.T[None, :, :], 0.0), axis=1)
    mine = jnp.where(jnp.any(names, axis=1), weight, -1.0)
    return lax.all_to_all(mine, "expert", split_axis=0, concat_axis=0, tiled=True)


def table_kernel(routes, probs, mine):
    names, shares = routes[...], probs[...]
    for e in range(mine.shape[0]):
        hit = (names == e).astype(jnp.float32)
        named = jnp.sum(hit, axis=0, keepdims=True)
        share = jnp.sum(hit * shares, axis=0, keepdims=True)
        mine[pl.ds(e, 1), :] = jnp.where(named > 0.0, share, -1.0)


def table_pass(routes, probs, experts):
    vmem = pl.BlockSpec(memory_space=pltpu.VMEM)
    return pl.pallas_call(
        table_kernel,
        out_shape=jax.ShapeDtypeStruct((experts, routes.shape[0]), jnp.float32),
        in_specs=[vmem] * 2,
        out_specs=vmem,
        compiler_params=pltpu.CompilerParams(vmem_limit_bytes=4 * 1024 * 1024),
    )(routes.T, probs.T)


def summed(*parts):
    total = parts[0].astype(jnp.float32)
    for part in parts[1:]:
        total = total + part.astype(jnp.float32)
    return total.astype(jnp.bfloat16)


def ranks_kernel(capacity, spots, weight, tables, ranks, chip_ranks):
    blocks, tok = weight.shape
    planes = blocks // 4
    named = (weight[...] >= 0.0).astype(jnp.float32)
    lane = lax.broadcasted_iota(jnp.int32, (tok, tok), 0)
    below = (lane < lax.broadcasted_iota(jnp.int32, (tok, tok), 1)).astype(jnp.float32)
    within = jnp.dot(named, below, preferred_element_type=jnp.float32)
    totals = jnp.broadcast_to(jnp.sum(named, axis=1, keepdims=True), (blocks, tok))
    row = lax.broadcasted_iota(jnp.int32, (blocks, blocks), 0)
    column = lax.broadcasted_iota(jnp.int32, (blocks, blocks), 1)
    earlier = (column < row).astype(jnp.float32)
    before = jnp.dot(earlier, totals, preferred_element_type=jnp.float32)
    rank = within + before
    kept = (named > 0.0) & (rank < capacity)
    first = (column < row // 4 * 4).astype(jnp.float32)
    start = jnp.dot(first, totals, preferred_element_type=jnp.float32)
    ranks[...] = jnp.where(kept, rank - start, -1.0)
    first = (column < row // 2 * 2).astype(jnp.float32)
    start = jnp.dot(first, totals, preferred_element_type=jnp.float32)
    chip_ranks[...] = jnp.where(kept, rank - start, -1.0)
    for i in range(4):
        span = pl.ds(i * tok, tok)
        tables[pl.ds(2 * planes, 1), span] = chip_ranks[pl.ds(spots[4 * planes - 4 + i], 1), :]
    for k in range(planes):
        for i in range(4):
            span = pl.ds(i * tok, tok)
            tables[pl.ds(k, 1), span] = ranks[pl.ds(spots[4 * k + i], 1), :]
            tables[pl.ds(planes + k, 1), span] = weight[pl.ds(spots[4 * k + i], 1), :]
    count = jnp.minimum(jnp.sum(totals[:, :1], axis=0, keepdims=True), float(capacity))
    rest = (tables.shape[0] - 2 * planes - 1, tables.shape[1])
    tables[2 * planes + 1 :, :] = jnp.broadcast_to(2.0 / count, rest)


def ranks_pass(capacity, spots, weight):
    blocks, tok = weight.shape
    vmem = pl.BlockSpec(memory_space=pltpu.VMEM)
    return pl.pallas_call(
        functools.partial(ranks_kernel, capacity),
        out_shape=jax.ShapeDtypeStruct((blocks // 4 * 2 + 8, 4 * tok), jnp.float32),
        in_specs=[pl.BlockSpec(memory_space=pltpu.SMEM), vmem],
        out_specs=vmem,
        scratch_shapes=[pltpu.VMEM(weight.shape, jnp.float32)] * 2,
        compiler_params=pltpu.CompilerParams(vmem_limit_bytes=4 * 1024 * 1024),
    )(spots, weight)


def plane_kernel(k, picked, gives, tables, *refs):
    *xs, w_gate, w_up, w_down, keep = refs[: -gives - 2]
    *gives, act, rows = refs[-gives - 2 :]
    slots, hidden = act.shape
    features = rows.shape[1]
    half, width = keep.shape[0], tables.shape[1]
    wide, cut = 256, 512
    place = tables[pl.ds(8 if picked else k, 1), :]
    share = tables[pl.ds(4 + k, 1), :]
    if picked:
        tok = width // 4
        place, share = (
            jnp.concatenate([row[:, i * tok : (i + 1) * tok] for i in picked], axis=1)
            for row in (place, share)
        )
        width = 2 * tok
    slot = lax.broadcasted_iota(jnp.int32, (slots, width), 0).astype(jnp.float32)
    hits = slot == place
    scale = jnp.sum(jnp.where(hits, share, 0.0), axis=1, keepdims=True)
    select = hits.astype(jnp.float32).astype(jnp.bfloat16)
    for i in range(features // cut):
        span = pl.ds(i * cut, cut)
        x = jnp.concatenate([block[:, span] for block in xs], axis=0)
        rows[:, span] = jnp.dot(select, x, preferred_element_type=jnp.float32).astype(jnp.bfloat16)
    for i in range(hidden // wide):
        span = pl.ds(i * wide, wide)
        gate = jnp.dot(rows[...], w_gate[:, span], preferred_element_type=jnp.float32)
        up = jnp.dot(rows[...], w_up[:, span], preferred_element_type=jnp.float32)
        act[:, span] = (gate / (1.0 + jnp.exp(-gate)) * up).astype(jnp.bfloat16)
    back = select.T
    for i in range(features // cut):
        span = pl.ds(i * cut, cut)
        result = jnp.dot(act[...], w_down[:, span], preferred_element_type=jnp.float32)
        made = (result * scale).astype(jnp.bfloat16)
        spread = jnp.dot(back, made, preferred_element_type=jnp.float32).astype(jnp.bfloat16)
        keep[:, span] = spread[:half]
        start = half
        for give in gives:
            give[:, span] = spread[start : start + give.shape[0]]
            start += give.shape[0]


def plane_pass(k, tables, xs, w_gate, w_up, w_down, slots, pieces=None, picked=None):
    tok, features = xs[0].shape
    hidden = w_gate.shape[1]
    blocks = 2 if picked else 4
    rows = blocks * slots
    half = blocks // 2 * tok
    pieces = pieces or (half,)
    outs = tuple(jax.ShapeDtypeStruct((some, features), jnp.bfloat16) for some in (half, *pieces))
    outs += (jax.ShapeDtypeStruct((rows, hidden), jnp.bfloat16),)
    vmem = pl.BlockSpec(memory_space=pltpu.VMEM)
    flops = 2 * rows * (3 * features * hidden + 2 * blocks * tok * features)
    moved = 2 * (3 * features * hidden + 2 * blocks * tok * features)
    return pl.pallas_call(
        functools.partial(plane_kernel, k, picked, len(pieces)),
        out_shape=outs,
        in_specs=[vmem] * (len(xs) + 4),
        out_specs=[vmem] * len(outs),
        scratch_shapes=[pltpu.VMEM((rows, features), jnp.bfloat16)],
        compiler_params=pltpu.CompilerParams(vmem_limit_bytes=12 * 1024 * 1024),
        cost_estimate=pl.CostEstimate(
            flops=flops, bytes_accessed=moved, transcendentals=rows * hidden
        ),
    )(tables, *xs, w_gate, w_up, w_down)


def gram_kernel(tables, *refs):
    *acts, gram = refs
    wide = 256
    scale = tables[9:10, :1]
    rows = jnp.concatenate([act[...] for act in acts], axis=0)
    for i in range(gram.shape[0] // wide):
        some = rows[:, i * wide : (i + 1) * wide]
        gram[pl.ds(i * wide, wide), :] = gram_of_two(some, rows) * scale


def gram_of_two(left, right):
    return lax.dot_general(left, right, (((0,), (0,)), ((), ())), preferred_element_type=jnp.float32)


def gram_pass(tables, *acts):
    hidden = acts[0].shape[1]
    rows = sum(act.shape[0] for act in acts)
    vmem = pl.BlockSpec(memory_space=pltpu.VMEM)
    return pl.pallas_call(
        gram_kernel,
        out_shape=jax.ShapeDtypeStruct((hidden, hidden), jnp.float32),
        in_specs=[vmem] * (len(acts) + 1),
        out_specs=vmem,
        compiler_params=pltpu.CompilerParams(vmem_limit_bytes=16 * 1024 * 1024),
        cost_estimate=pl.CostEstimate(
            flops=2 * rows * hidden * hidden,
            bytes_accessed=4 * hidden * hidden + 2 * rows * hidden,
            transcendentals=0,
        ),
    )(tables, *acts)


def mix_kernel(far_low, far_high, near_high, near_low, side, keep, got, mixed):
    most, tok = near_low.shape[0], mixed.shape[0]
    for start, stop, near, far in (
        (0, most, near_low, far_low),
        (most, tok, near_high, far_high),
    ):
        total = keep[start:stop, :].astype(jnp.float32) + got[start:stop, :].astype(jnp.float32)
        total = total + side[start:stop, :].astype(jnp.float32) + near[...].astype(jnp.float32)
        mixed[start:stop, :] = (total + far[...].astype(jnp.float32)).astype(mixed.dtype)


def mix_pass(*parts):
    side = parts[4]
    vmem = pl.BlockSpec(memory_space=pltpu.VMEM)
    return pl.pallas_call(
        mix_kernel,
        out_shape=jax.ShapeDtypeStruct(side.shape, side.dtype),
        in_specs=[vmem] * len(parts),
        out_specs=vmem,
        compiler_params=pltpu.CompilerParams(vmem_limit_bytes=12 * 1024 * 1024),
    )(*parts)


def staged(routes, probs, tokens, w_gate, w_up, w_down):
    tok, top = routes.shape
    size = lax.axis_size("expert")
    slots = 5 * tok * top // (4 * size)
    capacity = tok * top // 2
    half = tok // 2
    me = lax.axis_index("expert")
    z, y, core = me // 4, me // 2 % 2, me % 2

    def swapped(array, bit):
        return lax.ppermute(array, "expert", [(i, i ^ bit) for i in range(size)])

    sibling = functools.partial(swapped, bit=1)
    column = functools.partial(swapped, bit=2)
    pair = functools.partial(swapped, bit=4)
    far = functools.partial(swapped, bit=8)

    def together(*arrays):
        return lax.optimization_barrier(arrays)

    spots = jnp.stack(
        [
            (z ^ k) * 4 + (y ^ column_bit) * 2 + (core ^ core_bit)
            for k in range(4)
            for core_bit in range(2)
            for column_bit in range(2)
        ]
    ).astype(jnp.int32)

    def expert(k, *xs, pieces=None, picked=None):
        return plane_pass(k, tables, xs, w_gate, w_up, w_down, slots, pieces, picked)

    def far_of(which, array):
        pairs = [(i, i ^ 8) for i in range(size) if i % 2 == which]
        return lax.ppermute(array, "expert", pairs)

    mine = table_pass(routes, probs, size)
    a0 = tokens
    a1, far_0, b0, c0, weight = together(
        pair(a0),
        far_of(0, a0),
        column(a0),
        sibling(a0),
        lax.all_to_all(mine, "expert", split_axis=0, concat_axis=0, tiled=True),
    )
    tables = ranks_pass(capacity, spots, weight)
    far_1 = far_of(1, a0)
    b1 = column(a1)
    d0 = sibling(b0)
    c1 = sibling(a1)
    keep0, give0, act0 = expert(0, a0, b0, c0, d0)
    far_1, b1, c1, keep0, give0, act0, tables = together(
        far_1, b1, c1, keep0, give0, act0, tables
    )
    a2 = jnp.where(core == 0, far_0, far_1)
    a3 = pair(a2)
    b2 = column(a2)
    d1 = sibling(b1)
    c2 = sibling(a2)
    keep1, give1, give1_side, act1 = expert(1, a1, b1, c1, d1, pieces=(tok, tok))
    got1_side = sibling(give1_side)
    a3, b2, c2, keep1, give1, act1, got1_side = together(
        a3, b2, c2, keep1, give1, act1, got1_side
    )
    b3 = pair(b2)
    came1_low = column(summed(keep1[tok : tok + half], got1_side[:half]))
    got1 = sibling(give1)
    d2 = sibling(b2)
    c3 = sibling(a3)
    keep2, give2, give2_low, give2_high, act2 = expert(
        2, a2, b2, c2, d2, pieces=(tok, half, half)
    )
    got2_high = sibling(give2_high)
    keep3, give3, act3 = expert(3, a3, c3, picked=(0, 2))
    got0 = sibling(give0)
    b3, came1_low, got0, got1, got2_high, keep2, give2, give2_low, act2, keep3, give3, act3 = (
        together(
            b3, came1_low, got0, got1, got2_high, keep2, give2, give2_low, act2, keep3, give3, act3
        )
    )
    d3 = sibling(b3)
    near1 = summed(keep1[:half], got1[:half], came1_low)

    side_high = column(summed(keep2[tok + half :], got2_high))
    got2 = sibling(give2)
    keep3_side, give3_side, act4 = expert(3, b3, d3, picked=(1, 3))
    keep3_side, give3_side, act4, got2, side_high, near1 = together(
        keep3_side, give3_side, act4, got2, side_high, near1
    )
    got2_low, got3 = sibling(give2_low), sibling(give3)
    far2_high = far(summed(keep2[half:tok], got2[half:], side_high))
    got3_side = sibling(give3_side)
    came3_low = column(summed(keep3_side[:half], got3_side[:half]))
    came3_high = column(summed(keep3_side[half:], got3_side[half:]))
    near1_low = pair(near1)
    side0 = summed(keep0[tok:], got0[tok:])
    side1 = summed(keep1[tok + half :], got1_side[half:])
    came3_low, came3_high, far2_high, near1_low, side0, side1, got2_low, got3 = together(
        came3_low, came3_high, far2_high, near1_low, side0, side1, got2_low, got3
    )
    far3_high = far(summed(keep3[half:], got3[half:], came3_high))
    pair3_low = pair(summed(keep3[:half], got3[:half], came3_low))
    side_low = column(summed(keep2[tok : tok + half], got2_low))
    came1_high = column(side1)
    gram = gram_pass(tables, act0, act1, act2, act3, act4)
    far3_high, pair3_low, side_low, came1_high, side0, gram = together(
        far3_high, pair3_low, side_low, came1_high, side0, gram
    )
    far2_low = summed(keep2[:half], got2[:half], pair3_low, side_low)
    far2_low, far3_high, came1_high, side0 = together(far2_low, far3_high, came1_high, side0)
    far2_low = far(far2_low)
    near1_high = pair(summed(keep1[half:tok], got1[half:], came1_high, far3_high))
    last0 = column(side0)
    mixed = mix_pass(
        far2_low, far2_high, near1_high, near1_low, last0, keep0, got0
    )

    return gram[None], mixed


def gathered(routes, probs, tokens, w_gate, w_up, w_down):
    tok_rows, top = routes.shape
    size = lax.axis_size("expert")
    capacity = tok_rows * top // 2
    every_token = lax.all_gather(tokens, "expert", tiled=True)
    weight = weights_for_me(routes, probs, size)
    named = (weight >= 0.0).astype(jnp.int32)
    within = jnp.cumsum(named, axis=1) - named
    per_device = jnp.sum(named, axis=1)
    before = jnp.cumsum(per_device) - per_device
    rank = within + before[:, None]
    kept = (named == 1) & (rank < capacity)
    count = jnp.minimum(jnp.sum(per_device), capacity)
    slot = jnp.where(kept, rank, -1).reshape(size * tok_rows)
    place = jnp.arange(capacity, dtype=jnp.int32)
    select = (place[:, None] == slot[None, :]).astype(jnp.bfloat16)
    rows = jnp.dot(select, every_token, preferred_element_type=jnp.float32).astype(jnp.bfloat16)
    gram_sum, made = expert_pass(rows, w_gate, w_up, w_down)
    gram = gram_sum * (2.0 / count.astype(jnp.float32))
    spread = lax.dot_general(
        select, made, (((0,), (0,)), ((), ())), preferred_element_type=jnp.float32
    )
    partial = (spread * weight.reshape(size * tok_rows, 1)).astype(jnp.bfloat16)
    mixed = lax.psum_scatter(partial, "expert", scatter_dimension=0, tiled=True)
    return gram[None], mixed.astype(jnp.bfloat16)


def shards(routes, probs, tokens, gate_weight, up_weight, down_weight):
    body = staged if lax.axis_size("expert") == 16 else gathered
    return body(routes, probs, tokens, gate_weight[0], up_weight[0], down_weight[0])


def solution(mesh):
    placed = (
        P(("parts", "expert"), None),
        P(("parts", "expert"), None),
        P(("parts", "expert"), None),
        P("expert", None, None),
        P("expert", None, None),
        P("expert", None, None),
    )
    return jax.shard_map(
        shards,
        mesh=mesh,
        in_specs=placed,
        out_specs=(P(("parts", "expert"), None, None), P(("parts", "expert"), None)),
        check_vma=False,
    )
```

```python
import functools

import jax
import jax.numpy as jnp
from jax import lax
from jax.experimental import pallas as pl
from jax.experimental.pallas import tpu as pltpu
from jax.sharding import PartitionSpec as P


def gram_of(rows):
    return lax.dot_general(rows, rows, (((0,), (0,)), ((), ())), preferred_element_type=jnp.float32)


def expert_pass(rows, w_gate, w_up, w_down):
    gate = jnp.dot(rows, w_gate, preferred_element_type=jnp.float32)
    up = jnp.dot(rows, w_up, preferred_element_type=jnp.float32)
    act = (jax.nn.silu(gate) * up).astype(jnp.bfloat16)
    gram_sum = gram_of(act)
    made = jnp.dot(act, w_down, preferred_element_type=jnp.float32).astype(jnp.bfloat16)
    return (gram_sum, made)


def weights_for_me(routes, probs, experts):
    names = routes.T[None, :, :] == jnp.arange(experts, dtype=jnp.int32)[:, None, None]
    weight = jnp.sum(jnp.where(names, probs.T[None, :, :], 0.0), axis=1)
    mine = jnp.where(jnp.any(names, axis=1), weight, -1.0)
    return lax.all_to_all(mine, "expert", split_axis=0, concat_axis=0, tiled=True)


def prepare_kernel(routes, probs, tokens, mine, low, high, names, shares, sems):
    half = low.shape[0]
    pairs = (
        (routes, names),
        (probs, shares),
        (tokens.at[pl.ds(0, half), :], low),
        (tokens.at[pl.ds(half, half), :], high),
    )
    copies = [pltpu.make_async_copy(*pair, sems.at[i]) for i, pair in enumerate(pairs)]
    for copy in copies:
        copy.start()
    for copy in copies[:2]:
        copy.wait()
    for e in range(mine.shape[0]):
        hit = (names[...] == e).astype(jnp.float32)
        named = jnp.sum(hit, axis=0, keepdims=True)
        share = jnp.sum(hit * shares[...], axis=0, keepdims=True)
        mine[pl.ds(e, 1), :] = jnp.where(named > 0.0, share, -1.0)
    for copy in copies[2:]:
        copy.wait()


def prepare_pass(routes, probs, tokens, experts):
    tok, top = routes.shape
    half = jax.ShapeDtypeStruct((tok // 2, tokens.shape[1]), tokens.dtype)
    vmem = pl.BlockSpec(memory_space=pltpu.VMEM)
    return pl.pallas_call(
        prepare_kernel,
        out_shape=(jax.ShapeDtypeStruct((experts, tok), jnp.float32), half, half),
        in_specs=[pl.BlockSpec(memory_space=pl.ANY)] * 3,
        out_specs=[vmem] * 3,
        scratch_shapes=[
            pltpu.VMEM((top, tok), routes.dtype),
            pltpu.VMEM((top, tok), probs.dtype),
            pltpu.SemaphoreType.DMA((4,)),
        ],
        compiler_params=pltpu.CompilerParams(vmem_limit_bytes=4 * 1024 * 1024),
    )(routes.T, probs.T, tokens)


def summed(*parts):
    total = parts[0].astype(jnp.float32)
    for part in parts[1:]:
        total = total + part.astype(jnp.float32)
    return total.astype(jnp.bfloat16)


def ranks_kernel(capacity, spots, weight, tables, ranks, chip_ranks):
    blocks, tok = weight.shape
    planes = blocks // 4
    named = (weight[...] >= 0.0).astype(jnp.float32)
    lane = lax.broadcasted_iota(jnp.int32, (tok, tok), 0)
    below = (lane < lax.broadcasted_iota(jnp.int32, (tok, tok), 1)).astype(jnp.float32)
    within = jnp.dot(named, below, preferred_element_type=jnp.float32)
    totals = jnp.broadcast_to(jnp.sum(named, axis=1, keepdims=True), (blocks, tok))
    row = lax.broadcasted_iota(jnp.int32, (blocks, blocks), 0)
    column = lax.broadcasted_iota(jnp.int32, (blocks, blocks), 1)
    earlier = (column < row).astype(jnp.float32)
    before = jnp.dot(earlier, totals, preferred_element_type=jnp.float32)
    rank = within + before
    kept = (named > 0.0) & (rank < capacity)
    first = (column < row // 4 * 4).astype(jnp.float32)
    start = jnp.dot(first, totals, preferred_element_type=jnp.float32)
    ranks[...] = jnp.where(kept, rank - start, -1.0)
    first = (column < row // 2 * 2).astype(jnp.float32)
    start = jnp.dot(first, totals, preferred_element_type=jnp.float32)
    chip_ranks[...] = jnp.where(kept, rank - start, -1.0)
    for i in range(4):
        span = pl.ds(i * tok, tok)
        tables[pl.ds(2 * planes, 1), span] = chip_ranks[pl.ds(spots[4 * planes - 4 + i], 1), :]
    for k in range(planes):
        for i in range(4):
            span = pl.ds(i * tok, tok)
            tables[pl.ds(k, 1), span] = ranks[pl.ds(spots[4 * k + i], 1), :]
            tables[pl.ds(planes + k, 1), span] = weight[pl.ds(spots[4 * k + i], 1), :]
    count = jnp.minimum(jnp.sum(totals[:, :1], axis=0, keepdims=True), float(capacity))
    rest = (tables.shape[0] - 2 * planes - 1, tables.shape[1])
    tables[2 * planes + 1 :, :] = jnp.broadcast_to(2.0 / count, rest)


def ranks_pass(capacity, spots, weight):
    blocks, tok = weight.shape
    vmem = pl.BlockSpec(memory_space=pltpu.VMEM)
    return pl.pallas_call(
        functools.partial(ranks_kernel, capacity),
        out_shape=jax.ShapeDtypeStruct((blocks // 4 * 2 + 8, 4 * tok), jnp.float32),
        in_specs=[pl.BlockSpec(memory_space=pltpu.SMEM), vmem],
        out_specs=vmem,
        scratch_shapes=[pltpu.VMEM(weight.shape, jnp.float32)] * 2,
        compiler_params=pltpu.CompilerParams(vmem_limit_bytes=4 * 1024 * 1024),
    )(spots, weight)


def plane_kernel(k, picked, gives, tables, *refs):
    *xs, w_gate, w_up, w_down, keep = refs[: -gives - 2]
    *gives, act, rows = refs[-gives - 2 :]
    slots, hidden = act.shape
    features = rows.shape[1]
    half, width = keep.shape[0], tables.shape[1]
    wide, cut = 256, 512
    place = tables[pl.ds(8 if picked else k, 1), :]
    share = tables[pl.ds(4 + k, 1), :]
    if picked:
        tok = width // 4
        place, share = (
            jnp.concatenate([row[:, i * tok : (i + 1) * tok] for i in picked], axis=1)
            for row in (place, share)
        )
        width = 2 * tok
    slot = lax.broadcasted_iota(jnp.int32, (slots, width), 0).astype(jnp.float32)
    hits = slot == place
    scale = jnp.sum(jnp.where(hits, share, 0.0), axis=1, keepdims=True)
    select = hits.astype(jnp.float32).astype(jnp.bfloat16)
    for i in range(features // cut):
        span = pl.ds(i * cut, cut)
        x = jnp.concatenate([block[:, span] for block in xs], axis=0)
        rows[:, span] = jnp.dot(select, x, preferred_element_type=jnp.float32).astype(jnp.bfloat16)
    for i in range(hidden // wide):
        span = pl.ds(i * wide, wide)
        gate = jnp.dot(rows[...], w_gate[:, span], preferred_element_type=jnp.float32)
        up = jnp.dot(rows[...], w_up[:, span], preferred_element_type=jnp.float32)
        act[:, span] = (gate / (1.0 + jnp.exp(-gate)) * up).astype(jnp.bfloat16)
    back = select.T
    for i in range(features // cut):
        span = pl.ds(i * cut, cut)
        result = jnp.dot(act[...], w_down[:, span], preferred_element_type=jnp.float32)
        made = (result * scale).astype(jnp.bfloat16)
        spread = jnp.dot(back, made, preferred_element_type=jnp.float32).astype(jnp.bfloat16)
        keep[:, span] = spread[:half]
        start = half
        for give in gives:
            give[:, span] = spread[start : start + give.shape[0]]
            start += give.shape[0]


def plane_pass(k, tables, xs, w_gate, w_up, w_down, slots, pieces=None, picked=None):
    tok, features = xs[0].shape
    hidden = w_gate.shape[1]
    blocks = 2 if picked else 4
    rows = blocks * slots
    half = blocks // 2 * tok
    pieces = pieces or (half,)
    outs = tuple(jax.ShapeDtypeStruct((some, features), jnp.bfloat16) for some in (half, *pieces))
    outs += (jax.ShapeDtypeStruct((rows, hidden), jnp.bfloat16),)
    vmem = pl.BlockSpec(memory_space=pltpu.VMEM)
    flops = 2 * rows * (3 * features * hidden + 2 * blocks * tok * features)
    moved = 2 * (3 * features * hidden + 2 * blocks * tok * features)
    return pl.pallas_call(
        functools.partial(plane_kernel, k, picked, len(pieces)),
        out_shape=outs,
        in_specs=[vmem] * (len(xs) + 4),
        out_specs=[vmem] * len(outs),
        scratch_shapes=[pltpu.VMEM((rows, features), jnp.bfloat16)],
        compiler_params=pltpu.CompilerParams(vmem_limit_bytes=12 * 1024 * 1024),
        cost_estimate=pl.CostEstimate(
            flops=flops, bytes_accessed=moved, transcendentals=rows * hidden
        ),
    )(tables, *xs, w_gate, w_up, w_down)


def gram_kernel(tables, *refs):
    *acts, gram = refs
    wide = 256
    scale = tables[9:10, :1]
    rows = jnp.concatenate([act[...] for act in acts], axis=0)
    for i in range(gram.shape[0] // wide):
        some = rows[:, i * wide : (i + 1) * wide]
        gram[pl.ds(i * wide, wide), :] = gram_of_two(some, rows) * scale


def gram_of_two(left, right):
    return lax.dot_general(left, right, (((0,), (0,)), ((), ())), preferred_element_type=jnp.float32)


def gram_pass(tables, *acts):
    hidden = acts[0].shape[1]
    rows = sum(act.shape[0] for act in acts)
    vmem = pl.BlockSpec(memory_space=pltpu.VMEM)
    return pl.pallas_call(
        gram_kernel,
        out_shape=jax.ShapeDtypeStruct((hidden, hidden), jnp.float32),
        in_specs=[vmem] * (len(acts) + 1),
        out_specs=vmem,
        compiler_params=pltpu.CompilerParams(vmem_limit_bytes=16 * 1024 * 1024),
        cost_estimate=pl.CostEstimate(
            flops=2 * rows * hidden * hidden,
            bytes_accessed=4 * hidden * hidden + 2 * rows * hidden,
            transcendentals=0,
        ),
    )(tables, *acts)


def mix_kernel(far_low, far_high, near_high, near_low, side, keep, got, mixed):
    most, tok = near_low.shape[0], mixed.shape[0]
    for start, stop, near, far in (
        (0, most, near_low, far_low),
        (most, tok, near_high, far_high),
    ):
        total = keep[start:stop, :].astype(jnp.float32) + got[start:stop, :].astype(jnp.float32)
        total = total + side[start:stop, :].astype(jnp.float32) + near[...].astype(jnp.float32)
        mixed[start:stop, :] = (total + far[...].astype(jnp.float32)).astype(mixed.dtype)


def mix_pass(*parts):
    side = parts[4]
    vmem = pl.BlockSpec(memory_space=pltpu.VMEM)
    return pl.pallas_call(
        mix_kernel,
        out_shape=jax.ShapeDtypeStruct(side.shape, side.dtype),
        in_specs=[vmem] * len(parts),
        out_specs=vmem,
        compiler_params=pltpu.CompilerParams(vmem_limit_bytes=12 * 1024 * 1024),
    )(*parts)


def staged(routes, probs, tokens, w_gate, w_up, w_down):
    tok, top = routes.shape
    size = lax.axis_size("expert")
    slots = 5 * tok * top // (4 * size)
    capacity = tok * top // 2
    half = tok // 2
    me = lax.axis_index("expert")
    z, y, core = me // 4, me // 2 % 2, me % 2

    def swapped(array, bit):
        return lax.ppermute(array, "expert", [(i, i ^ bit) for i in range(size)])

    sibling = functools.partial(swapped, bit=1)
    column = functools.partial(swapped, bit=2)
    pair = functools.partial(swapped, bit=4)
    far = functools.partial(swapped, bit=8)

    def together(*arrays):
        return lax.optimization_barrier(arrays)

    spots = jnp.stack(
        [
            (z ^ k) * 4 + (y ^ column_bit) * 2 + (core ^ core_bit)
            for k in range(4)
            for core_bit in range(2)
            for column_bit in range(2)
        ]
    ).astype(jnp.int32)

    def expert(k, *xs, pieces=None, picked=None):
        return plane_pass(k, tables, xs, w_gate, w_up, w_down, slots, pieces, picked)

    mine, a0_low, a0_high = prepare_pass(routes, probs, tokens, size)
    a0 = tokens
    a1, low, b0, c0, weight, a0_high = together(
        pair(a0),
        far(a0_low),
        column(a0),
        sibling(a0),
        lax.all_to_all(mine, "expert", split_axis=0, concat_axis=0, tiled=True),
        a0_high,
    )
    tables = ranks_pass(capacity, spots, weight)
    high = far(a0_high)
    b1 = column(a1)
    d0 = sibling(b0)
    c1 = sibling(a1)
    keep0, give0, act0 = expert(0, a0, b0, c0, d0)
    high, b1, c1, keep0, give0, act0, tables = together(
        high, b1, c1, keep0, give0, act0, tables
    )
    a2 = jnp.concatenate([low, high], axis=0)
    a3 = pair(a2)
    b2 = column(a2)
    d1 = sibling(b1)
    c2 = sibling(a2)
    keep1, give1, give1_side, act1 = expert(1, a1, b1, c1, d1, pieces=(tok, tok))
    got1_side = sibling(give1_side)
    a3, b2, c2, keep1, give1, act1, got1_side = together(
        a3, b2, c2, keep1, give1, act1, got1_side
    )
    b3 = pair(b2)
    came1_low = column(summed(keep1[tok : tok + half], got1_side[:half]))
    got1 = sibling(give1)
    d2 = sibling(b2)
    c3 = sibling(a3)
    keep2, give2, give2_low, give2_high, act2 = expert(
        2, a2, b2, c2, d2, pieces=(tok, half, half)
    )
    got2_high = sibling(give2_high)
    keep3, give3, act3 = expert(3, a3, c3, picked=(0, 2))
    got0 = sibling(give0)
    b3, came1_low, got0, got1, got2_high, keep2, give2, give2_low, act2, keep3, give3, act3 = (
        together(
            b3, came1_low, got0, got1, got2_high, keep2, give2, give2_low, act2, keep3, give3, act3
        )
    )
    d3 = sibling(b3)
    near1 = summed(keep1[:half], got1[:half], came1_low)

    side_high = column(summed(keep2[tok + half :], got2_high))
    got2 = sibling(give2)
    keep3_side, give3_low, give3_high, act4 = expert(
        3, b3, d3, pieces=(half, half), picked=(1, 3)
    )
    got3_low, got3_high = sibling(give3_low), sibling(give3_high)
    keep3_side, got3_low, got3_high, act4, got2, side_high, near1 = together(
        keep3_side, got3_low, got3_high, act4, got2, side_high, near1
    )
    got2_low, got3 = sibling(give2_low), sibling(give3)
    far2_high = far(summed(keep2[half:tok], got2[half:], side_high))
    came3_low = column(summed(keep3_side[:half], got3_low))
    came3_high = column(summed(keep3_side[half:], got3_high))
    near1_low = pair(near1)
    side0 = summed(keep0[tok:], got0[tok:])
    side1 = summed(keep1[tok + half :], got1_side[half:])
    came3_low, came3_high, far2_high, near1_low, side0, side1, got2_low, got3 = together(
        came3_low, came3_high, far2_high, near1_low, side0, side1, got2_low, got3
    )
    far3_high = far(summed(keep3[half:], got3[half:], came3_high))
    pair3_low = pair(summed(keep3[:half], got3[:half], came3_low))
    side_low = column(summed(keep2[tok : tok + half], got2_low))
    came1_high = column(side1)
    gram = gram_pass(tables, act0, act1, act2, act3, act4)
    far3_high, pair3_low, side_low, came1_high, side0, gram = together(
        far3_high, pair3_low, side_low, came1_high, side0, gram
    )
    far2_low = summed(keep2[:half], got2[:half], pair3_low, side_low)
    far2_low, far3_high, came1_high, side0 = together(far2_low, far3_high, came1_high, side0)
    far2_low = far(far2_low)
    near1_high = pair(summed(keep1[half:tok], got1[half:], came1_high, far3_high))
    last0 = column(side0)
    mixed = mix_pass(
        far2_low, far2_high, near1_high, near1_low, last0, keep0, got0
    )

    return gram[None], mixed


def gathered(routes, probs, tokens, w_gate, w_up, w_down):
    tok_rows, top = routes.shape
    size = lax.axis_size("expert")
    capacity = tok_rows * top // 2
    every_token = lax.all_gather(tokens, "expert", tiled=True)
    weight = weights_for_me(routes, probs, size)
    named = (weight >= 0.0).astype(jnp.int32)
    within = jnp.cumsum(named, axis=1) - named
    per_device = jnp.sum(named, axis=1)
    before = jnp.cumsum(per_device) - per_device
    rank = within + before[:, None]
    kept = (named == 1) & (rank < capacity)
    count = jnp.minimum(jnp.sum(per_device), capacity)
    slot = jnp.where(kept, rank, -1).reshape(size * tok_rows)
    place = jnp.arange(capacity, dtype=jnp.int32)
    select = (place[:, None] == slot[None, :]).astype(jnp.bfloat16)
    rows = jnp.dot(select, every_token, preferred_element_type=jnp.float32).astype(jnp.bfloat16)
    gram_sum, made = expert_pass(rows, w_gate, w_up, w_down)
    gram = gram_sum * (2.0 / count.astype(jnp.float32))
    spread = lax.dot_general(
        select, made, (((0,), (0,)), ((), ())), preferred_element_type=jnp.float32
    )
    partial = (spread * weight.reshape(size * tok_rows, 1)).astype(jnp.bfloat16)
    mixed = lax.psum_scatter(partial, "expert", scatter_dimension=0, tiled=True)
    return gram[None], mixed.astype(jnp.bfloat16)


def shards(routes, probs, tokens, gate_weight, up_weight, down_weight):
    body = staged if lax.axis_size("expert") == 16 else gathered
    return body(routes, probs, tokens, gate_weight[0], up_weight[0], down_weight[0])


def solution(mesh):
    placed = (
        P(("parts", "expert"), None),
        P(("parts", "expert"), None),
        P(("parts", "expert"), None),
        P("expert", None, None),
        P("expert", None, None),
        P("expert", None, None),
    )
    return jax.shard_map(
        shards,
        mesh=mesh,
        in_specs=placed,
        out_specs=(P(("parts", "expert"), None, None), P(("parts", "expert"), None)),
        check_vma=False,
    )
```

```python
import functools

import jax
import jax.numpy as jnp
from jax import lax
from jax.experimental import pallas as pl
from jax.experimental.pallas import tpu as pltpu
from jax.sharding import PartitionSpec as P


def gram_of(rows):
    return lax.dot_general(rows, rows, (((0,), (0,)), ((), ())), preferred_element_type=jnp.float32)


def expert_pass(rows, w_gate, w_up, w_down):
    gate = jnp.dot(rows, w_gate, preferred_element_type=jnp.float32)
    up = jnp.dot(rows, w_up, preferred_element_type=jnp.float32)
    act = (jax.nn.silu(gate) * up).astype(jnp.bfloat16)
    gram_sum = gram_of(act)
    made = jnp.dot(act, w_down, preferred_element_type=jnp.float32).astype(jnp.bfloat16)
    return (gram_sum, made)


def weights_for_me(routes, probs, experts):
    names = routes.T[None, :, :] == jnp.arange(experts, dtype=jnp.int32)[:, None, None]
    weight = jnp.sum(jnp.where(names, probs.T[None, :, :], 0.0), axis=1)
    mine = jnp.where(jnp.any(names, axis=1), weight, -1.0)
    return lax.all_to_all(mine, "expert", split_axis=0, concat_axis=0, tiled=True)


def prepare_kernel(routes, probs, tokens, mine, low, high, names, shares, sems):
    half = low.shape[0]
    pairs = (
        (routes, names),
        (probs, shares),
        (tokens.at[pl.ds(0, half), :], low),
        (tokens.at[pl.ds(half, half), :], high),
    )
    copies = [pltpu.make_async_copy(*pair, sems.at[i]) for i, pair in enumerate(pairs)]
    for copy in copies:
        copy.start()
    for copy in copies[:2]:
        copy.wait()
    for e in range(mine.shape[0]):
        hit = (names[...] == e).astype(jnp.float32)
        named = jnp.sum(hit, axis=0, keepdims=True)
        share = jnp.sum(hit * shares[...], axis=0, keepdims=True)
        mine[pl.ds(e, 1), :] = jnp.where(named > 0.0, share, -1.0)
    for copy in copies[2:]:
        copy.wait()


def prepare_pass(routes, probs, tokens, experts):
    tok, top = routes.shape
    half = jax.ShapeDtypeStruct((tok // 2, tokens.shape[1]), tokens.dtype)
    vmem = pl.BlockSpec(memory_space=pltpu.VMEM)
    return pl.pallas_call(
        prepare_kernel,
        out_shape=(jax.ShapeDtypeStruct((experts, tok), jnp.float32), half, half),
        in_specs=[pl.BlockSpec(memory_space=pl.ANY)] * 3,
        out_specs=[vmem] * 3,
        scratch_shapes=[
            pltpu.VMEM((top, tok), routes.dtype),
            pltpu.VMEM((top, tok), probs.dtype),
            pltpu.SemaphoreType.DMA((4,)),
        ],
        compiler_params=pltpu.CompilerParams(vmem_limit_bytes=4 * 1024 * 1024),
    )(routes.T, probs.T, tokens)


def summed(*parts):
    total = parts[0].astype(jnp.float32)
    for part in parts[1:]:
        total = total + part.astype(jnp.float32)
    return total.astype(jnp.bfloat16)


def ranks_kernel(capacity, spots, weight, tables, ranks, chip_ranks):
    blocks, tok = weight.shape
    planes = blocks // 4
    named = (weight[...] >= 0.0).astype(jnp.float32)
    lane = lax.broadcasted_iota(jnp.int32, (tok, tok), 0)
    below = (lane < lax.broadcasted_iota(jnp.int32, (tok, tok), 1)).astype(jnp.float32)
    within = jnp.dot(named, below, preferred_element_type=jnp.float32)
    totals = jnp.broadcast_to(jnp.sum(named, axis=1, keepdims=True), (blocks, tok))
    row = lax.broadcasted_iota(jnp.int32, (blocks, blocks), 0)
    column = lax.broadcasted_iota(jnp.int32, (blocks, blocks), 1)
    earlier = (column < row).astype(jnp.float32)
    before = jnp.dot(earlier, totals, preferred_element_type=jnp.float32)
    rank = within + before
    kept = (named > 0.0) & (rank < capacity)
    first = (column < row // 4 * 4).astype(jnp.float32)
    start = jnp.dot(first, totals, preferred_element_type=jnp.float32)
    ranks[...] = jnp.where(kept, rank - start, -1.0)
    first = (column < row // 2 * 2).astype(jnp.float32)
    start = jnp.dot(first, totals, preferred_element_type=jnp.float32)
    chip_ranks[...] = jnp.where(kept, rank - start, -1.0)
    for i in range(4):
        span = pl.ds(i * tok, tok)
        tables[pl.ds(2 * planes, 1), span] = chip_ranks[pl.ds(spots[4 * planes - 4 + i], 1), :]
    for k in range(planes):
        for i in range(4):
            span = pl.ds(i * tok, tok)
            tables[pl.ds(k, 1), span] = ranks[pl.ds(spots[4 * k + i], 1), :]
            tables[pl.ds(planes + k, 1), span] = weight[pl.ds(spots[4 * k + i], 1), :]
    count = jnp.minimum(jnp.sum(totals[:, :1], axis=0, keepdims=True), float(capacity))
    rest = (tables.shape[0] - 2 * planes - 1, tables.shape[1])
    tables[2 * planes + 1 :, :] = jnp.broadcast_to(2.0 / count, rest)


def ranks_pass(capacity, spots, weight):
    blocks, tok = weight.shape
    vmem = pl.BlockSpec(memory_space=pltpu.VMEM)
    return pl.pallas_call(
        functools.partial(ranks_kernel, capacity),
        out_shape=jax.ShapeDtypeStruct((blocks // 4 * 2 + 8, 4 * tok), jnp.float32),
        in_specs=[pl.BlockSpec(memory_space=pltpu.SMEM), vmem],
        out_specs=vmem,
        scratch_shapes=[pltpu.VMEM(weight.shape, jnp.float32)] * 2,
        compiler_params=pltpu.CompilerParams(vmem_limit_bytes=4 * 1024 * 1024),
    )(spots, weight)


def plane_kernel(k, picked, gives, tables, *refs):
    *xs, w_gate, w_up, w_down, keep = refs[: -gives - 2]
    *gives, act, rows = refs[-gives - 2 :]
    slots, hidden = act.shape
    features = rows.shape[1]
    half, width = keep.shape[0], tables.shape[1]
    wide, cut = 256, 512
    place = tables[pl.ds(8 if picked else k, 1), :]
    share = tables[pl.ds(4 + k, 1), :]
    if picked:
        tok = width // 4
        place, share = (
            jnp.concatenate([row[:, i * tok : (i + 1) * tok] for i in picked], axis=1)
            for row in (place, share)
        )
        width = 2 * tok
    slot = lax.broadcasted_iota(jnp.int32, (slots, width), 0).astype(jnp.float32)
    hits = slot == place
    scale = jnp.sum(jnp.where(hits, share, 0.0), axis=1, keepdims=True)
    select = hits.astype(jnp.float32).astype(jnp.bfloat16)
    for i in range(features // cut):
        span = pl.ds(i * cut, cut)
        x = jnp.concatenate([block[:, span] for block in xs], axis=0)
        rows[:, span] = jnp.dot(select, x, preferred_element_type=jnp.float32).astype(jnp.bfloat16)
    for i in range(hidden // wide):
        span = pl.ds(i * wide, wide)
        gate = jnp.dot(rows[...], w_gate[:, span], preferred_element_type=jnp.float32)
        up = jnp.dot(rows[...], w_up[:, span], preferred_element_type=jnp.float32)
        act[:, span] = (gate / (1.0 + jnp.exp(-gate)) * up).astype(jnp.bfloat16)
    back = select.T
    for i in range(features // cut):
        span = pl.ds(i * cut, cut)
        result = jnp.dot(act[...], w_down[:, span], preferred_element_type=jnp.float32)
        made = (result * scale).astype(jnp.bfloat16)
        spread = jnp.dot(back, made, preferred_element_type=jnp.float32).astype(jnp.bfloat16)
        keep[:, span] = spread[:half]
        start = half
        for give in gives:
            give[:, span] = spread[start : start + give.shape[0]]
            start += give.shape[0]


def plane_pass(k, tables, xs, w_gate, w_up, w_down, slots, pieces=None, picked=None):
    tok, features = xs[0].shape
    hidden = w_gate.shape[1]
    blocks = 2 if picked else 4
    rows = blocks * slots
    half = blocks // 2 * tok
    pieces = pieces or (half,)
    outs = tuple(jax.ShapeDtypeStruct((some, features), jnp.bfloat16) for some in (half, *pieces))
    outs += (jax.ShapeDtypeStruct((rows, hidden), jnp.bfloat16),)
    vmem = pl.BlockSpec(memory_space=pltpu.VMEM)
    flops = 2 * rows * (3 * features * hidden + 2 * blocks * tok * features)
    moved = 2 * (3 * features * hidden + 2 * blocks * tok * features)
    return pl.pallas_call(
        functools.partial(plane_kernel, k, picked, len(pieces)),
        out_shape=outs,
        in_specs=[vmem] * (len(xs) + 4),
        out_specs=[vmem] * len(outs),
        scratch_shapes=[pltpu.VMEM((rows, features), jnp.bfloat16)],
        compiler_params=pltpu.CompilerParams(vmem_limit_bytes=12 * 1024 * 1024),
        cost_estimate=pl.CostEstimate(
            flops=flops, bytes_accessed=moved, transcendentals=rows * hidden
        ),
    )(tables, *xs, w_gate, w_up, w_down)


def gram_kernel(tables, *refs):
    *acts, gram = refs
    wide = 256
    scale = tables[9:10, :1]
    rows = jnp.concatenate([act[...] for act in acts], axis=0)
    for i in range(gram.shape[0] // wide):
        some = rows[:, i * wide : (i + 1) * wide]
        gram[pl.ds(i * wide, wide), :] = gram_of_two(some, rows) * scale


def gram_of_two(left, right):
    return lax.dot_general(left, right, (((0,), (0,)), ((), ())), preferred_element_type=jnp.float32)


def gram_pass(tables, *acts):
    hidden = acts[0].shape[1]
    rows = sum(act.shape[0] for act in acts)
    vmem = pl.BlockSpec(memory_space=pltpu.VMEM)
    return pl.pallas_call(
        gram_kernel,
        out_shape=jax.ShapeDtypeStruct((hidden, hidden), jnp.float32),
        in_specs=[vmem] * (len(acts) + 1),
        out_specs=vmem,
        compiler_params=pltpu.CompilerParams(vmem_limit_bytes=16 * 1024 * 1024),
        cost_estimate=pl.CostEstimate(
            flops=2 * rows * hidden * hidden,
            bytes_accessed=4 * hidden * hidden + 2 * rows * hidden,
            transcendentals=0,
        ),
    )(tables, *acts)


def mix_kernel(far_low, far_high, near_high, near_low, side, keep, got, mixed):
    most, tok = near_low.shape[0], mixed.shape[0]
    for start, stop, near, far in (
        (0, most, near_low, far_low),
        (most, tok, near_high, far_high),
    ):
        total = keep[start:stop, :].astype(jnp.float32) + got[start:stop, :].astype(jnp.float32)
        total = total + side[start:stop, :].astype(jnp.float32) + near[...].astype(jnp.float32)
        mixed[start:stop, :] = (total + far[...].astype(jnp.float32)).astype(mixed.dtype)


def mix_pass(*parts):
    side = parts[4]
    vmem = pl.BlockSpec(memory_space=pltpu.VMEM)
    return pl.pallas_call(
        mix_kernel,
        out_shape=jax.ShapeDtypeStruct(side.shape, side.dtype),
        in_specs=[vmem] * len(parts),
        out_specs=vmem,
        compiler_params=pltpu.CompilerParams(vmem_limit_bytes=12 * 1024 * 1024),
    )(*parts)


def staged(routes, probs, tokens, w_gate, w_up, w_down):
    tok, top = routes.shape
    size = lax.axis_size("expert")
    slots = 5 * tok * top // (4 * size)
    capacity = tok * top // 2
    half = tok // 2
    me = lax.axis_index("expert")
    z, y, core = me // 4, me // 2 % 2, me % 2

    def swapped(array, bit):
        return lax.ppermute(array, "expert", [(i, i ^ bit) for i in range(size)])

    sibling = functools.partial(swapped, bit=1)
    column = functools.partial(swapped, bit=2)
    pair = functools.partial(swapped, bit=4)
    far = functools.partial(swapped, bit=8)

    def together(*arrays):
        return lax.optimization_barrier(arrays)

    spots = jnp.stack(
        [
            (z ^ k) * 4 + (y ^ column_bit) * 2 + (core ^ core_bit)
            for k in range(4)
            for core_bit in range(2)
            for column_bit in range(2)
        ]
    ).astype(jnp.int32)

    def expert(k, *xs, pieces=None, picked=None):
        return plane_pass(k, tables, xs, w_gate, w_up, w_down, slots, pieces, picked)

    mine, a0_low, a0_high = prepare_pass(routes, probs, tokens, size)
    a0 = tokens
    a1, low, b0, c0, weight, a0_high = together(
        pair(a0),
        far(a0_low),
        column(a0),
        sibling(a0),
        lax.all_to_all(mine, "expert", split_axis=0, concat_axis=0, tiled=True),
        a0_high,
    )
    tables = ranks_pass(capacity, spots, weight)
    high = far(a0_high)
    b1 = column(a1)
    d0 = sibling(b0)
    c1 = sibling(a1)
    keep0, give0, act0 = expert(0, a0, b0, c0, d0)
    high, b1, c1, keep0, give0, act0, tables = together(
        high, b1, c1, keep0, give0, act0, tables
    )
    a2 = jnp.concatenate([low, high], axis=0)
    a3 = pair(a2)
    b2 = column(a2)
    d1 = sibling(b1)
    c2 = sibling(a2)
    keep1, give1, give1_side, act1 = expert(1, a1, b1, c1, d1, pieces=(tok, tok))
    got1_side = sibling(give1_side)
    a3, b2, c2, keep1, give1, act1, got1_side = together(
        a3, b2, c2, keep1, give1, act1, got1_side
    )
    b3 = pair(b2)
    came1_low = column(summed(keep1[tok : tok + half], got1_side[:half]))
    got1 = sibling(give1)
    d2 = sibling(b2)
    c3 = sibling(a3)
    keep2, give2, give2_low, give2_high, act2 = expert(
        2, a2, b2, c2, d2, pieces=(tok, half, half)
    )
    got2_high = sibling(give2_high)
    keep3, give3, act3 = expert(3, a3, c3, picked=(0, 2))
    got0 = sibling(give0)
    b3, came1_low, got0, got1, got2_high, keep2, give2, give2_low, act2, keep3, give3, act3 = (
        together(
            b3, came1_low, got0, got1, got2_high, keep2, give2, give2_low, act2, keep3, give3, act3
        )
    )
    d3 = sibling(b3)
    near1 = summed(keep1[:half], got1[:half], came1_low)

    side_high = column(summed(keep2[tok + half :], got2_high))
    got2 = sibling(give2)
    keep3_side, give3_low, give3_high, act4 = expert(
        3, b3, d3, pieces=(half, half), picked=(1, 3)
    )
    got3_low, got3_high = sibling(give3_low), sibling(give3_high)
    keep3_side, got3_low, got3_high, act4, got2, side_high, near1 = together(
        keep3_side, got3_low, got3_high, act4, got2, side_high, near1
    )
    got2_low, got3 = sibling(give2_low), sibling(give3)
    far2_high = far(summed(keep2[half:tok], got2[half:], side_high))
    came3_low = column(summed(keep3_side[:half], got3_low))
    came3_high = column(summed(keep3_side[half:], got3_high))
    near1_low = pair(near1)
    side0 = summed(keep0[tok:], got0[tok:])
    side1 = summed(keep1[tok + half :], got1_side[half:])
    far2_high, came3_low, came3_high, near1_low, side0, side1, got2_low, got3 = together(
        far2_high, came3_low, came3_high, near1_low, side0, side1, got2_low, got3
    )
    far3_high = far(summed(keep3[half:], got3[half:], came3_high))
    pair3_low = pair(summed(keep3[:half], got3[:half], came3_low))
    side_low = column(summed(keep2[tok : tok + half], got2_low))
    came1_high = column(side1)
    gram = gram_pass(tables, act0, act1, act2, act3, act4)
    far3_high, pair3_low, side_low, came1_high, side0, gram = together(
        far3_high, pair3_low, side_low, came1_high, side0, gram
    )
    far2_low = summed(keep2[:half], got2[:half], pair3_low, side_low)
    far2_low, far3_high, came1_high, side0 = together(far2_low, far3_high, came1_high, side0)
    far2_low = far(far2_low)
    near1_high = pair(summed(keep1[half:tok], got1[half:], came1_high, far3_high))
    last0 = column(side0)
    mixed = mix_pass(
        far2_low, far2_high, near1_high, near1_low, last0, keep0, got0
    )

    return gram[None], mixed


def gathered(routes, probs, tokens, w_gate, w_up, w_down):
    tok_rows, top = routes.shape
    size = lax.axis_size("expert")
    capacity = tok_rows * top // 2
    every_token = lax.all_gather(tokens, "expert", tiled=True)
    weight = weights_for_me(routes, probs, size)
    named = (weight >= 0.0).astype(jnp.int32)
    within = jnp.cumsum(named, axis=1) - named
    per_device = jnp.sum(named, axis=1)
    before = jnp.cumsum(per_device) - per_device
    rank = within + before[:, None]
    kept = (named == 1) & (rank < capacity)
    count = jnp.minimum(jnp.sum(per_device), capacity)
    slot = jnp.where(kept, rank, -1).reshape(size * tok_rows)
    place = jnp.arange(capacity, dtype=jnp.int32)
    select = (place[:, None] == slot[None, :]).astype(jnp.bfloat16)
    rows = jnp.dot(select, every_token, preferred_element_type=jnp.float32).astype(jnp.bfloat16)
    gram_sum, made = expert_pass(rows, w_gate, w_up, w_down)
    gram = gram_sum * (2.0 / count.astype(jnp.float32))
    spread = lax.dot_general(
        select, made, (((0,), (0,)), ((), ())), preferred_element_type=jnp.float32
    )
    partial = (spread * weight.reshape(size * tok_rows, 1)).astype(jnp.bfloat16)
    mixed = lax.psum_scatter(partial, "expert", scatter_dimension=0, tiled=True)
    return gram[None], mixed.astype(jnp.bfloat16)


def shards(routes, probs, tokens, gate_weight, up_weight, down_weight):
    body = staged if lax.axis_size("expert") == 16 else gathered
    return body(routes, probs, tokens, gate_weight[0], up_weight[0], down_weight[0])


def solution(mesh):
    placed = (
        P(("parts", "expert"), None),
        P(("parts", "expert"), None),
        P(("parts", "expert"), None),
        P("expert", None, None),
        P("expert", None, None),
        P("expert", None, None),
    )
    return jax.shard_map(
        shards,
        mesh=mesh,
        in_specs=placed,
        out_specs=(P(("parts", "expert"), None, None), P(("parts", "expert"), None)),
        check_vma=False,
    )
```

```python
import functools

import jax
import jax.numpy as jnp
from jax import lax
from jax.experimental import pallas as pl
from jax.experimental.pallas import tpu as pltpu
from jax.sharding import PartitionSpec as P


def gram_of(rows):
    return lax.dot_general(rows, rows, (((0,), (0,)), ((), ())), preferred_element_type=jnp.float32)


def expert_pass(rows, w_gate, w_up, w_down):
    gate = jnp.dot(rows, w_gate, preferred_element_type=jnp.float32)
    up = jnp.dot(rows, w_up, preferred_element_type=jnp.float32)
    act = (jax.nn.silu(gate) * up).astype(jnp.bfloat16)
    gram_sum = gram_of(act)
    made = jnp.dot(act, w_down, preferred_element_type=jnp.float32).astype(jnp.bfloat16)
    return (gram_sum, made)


def weights_for_me(routes, probs, experts):
    names = routes.T[None, :, :] == jnp.arange(experts, dtype=jnp.int32)[:, None, None]
    weight = jnp.sum(jnp.where(names, probs.T[None, :, :], 0.0), axis=1)
    mine = jnp.where(jnp.any(names, axis=1), weight, -1.0)
    return lax.all_to_all(mine, "expert", split_axis=0, concat_axis=0, tiled=True)


def prepare_kernel(routes, probs, tokens, mine, low, high, names, shares, sems):
    half = low.shape[0]
    pairs = (
        (routes, names),
        (probs, shares),
        (tokens.at[pl.ds(0, half), :], low),
        (tokens.at[pl.ds(half, half), :], high),
    )
    copies = [pltpu.make_async_copy(*pair, sems.at[i]) for i, pair in enumerate(pairs)]
    for copy in copies:
        copy.start()
    for copy in copies[:2]:
        copy.wait()
    for e in range(mine.shape[0]):
        hit = (names[...] == e).astype(jnp.float32)
        named = jnp.sum(hit, axis=0, keepdims=True)
        share = jnp.sum(hit * shares[...], axis=0, keepdims=True)
        mine[pl.ds(e, 1), :] = jnp.where(named > 0.0, share, -1.0)
    for copy in copies[2:]:
        copy.wait()


def prepare_pass(routes, probs, tokens, experts):
    tok, top = routes.shape
    half = jax.ShapeDtypeStruct((tok // 2, tokens.shape[1]), tokens.dtype)
    vmem = pl.BlockSpec(memory_space=pltpu.VMEM)
    return pl.pallas_call(
        prepare_kernel,
        out_shape=(jax.ShapeDtypeStruct((experts, tok), jnp.float32), half, half),
        in_specs=[pl.BlockSpec(memory_space=pl.ANY)] * 3,
        out_specs=[vmem] * 3,
        scratch_shapes=[
            pltpu.VMEM((top, tok), routes.dtype),
            pltpu.VMEM((top, tok), probs.dtype),
            pltpu.SemaphoreType.DMA((4,)),
        ],
        compiler_params=pltpu.CompilerParams(vmem_limit_bytes=4 * 1024 * 1024),
    )(routes.T, probs.T, tokens)


def summed(*parts):
    total = parts[0].astype(jnp.float32)
    for part in parts[1:]:
        total = total + part.astype(jnp.float32)
    return total.astype(jnp.bfloat16)


def ranks_kernel(capacity, spots, weight, tables, ranks, chip_ranks):
    blocks, tok = weight.shape
    planes = blocks // 4
    named = (weight[...] >= 0.0).astype(jnp.float32)
    lane = lax.broadcasted_iota(jnp.int32, (tok, tok), 0)
    below = (lane < lax.broadcasted_iota(jnp.int32, (tok, tok), 1)).astype(jnp.float32)
    within = jnp.dot(named, below, preferred_element_type=jnp.float32)
    totals = jnp.broadcast_to(jnp.sum(named, axis=1, keepdims=True), (blocks, tok))
    row = lax.broadcasted_iota(jnp.int32, (blocks, blocks), 0)
    column = lax.broadcasted_iota(jnp.int32, (blocks, blocks), 1)
    earlier = (column < row).astype(jnp.float32)
    before = jnp.dot(earlier, totals, preferred_element_type=jnp.float32)
    rank = within + before
    kept = (named > 0.0) & (rank < capacity)
    first = (column < row // 4 * 4).astype(jnp.float32)
    start = jnp.dot(first, totals, preferred_element_type=jnp.float32)
    ranks[...] = jnp.where(kept, rank - start, -1.0)
    first = (column < row // 2 * 2).astype(jnp.float32)
    start = jnp.dot(first, totals, preferred_element_type=jnp.float32)
    chip_ranks[...] = jnp.where(kept, rank - start, -1.0)
    for i in range(4):
        span = pl.ds(i * tok, tok)
        tables[pl.ds(2 * planes, 1), span] = chip_ranks[pl.ds(spots[4 * planes - 4 + i], 1), :]
    for k in range(planes):
        for i in range(4):
            span = pl.ds(i * tok, tok)
            tables[pl.ds(k, 1), span] = ranks[pl.ds(spots[4 * k + i], 1), :]
            tables[pl.ds(planes + k, 1), span] = weight[pl.ds(spots[4 * k + i], 1), :]
    count = jnp.minimum(jnp.sum(totals[:, :1], axis=0, keepdims=True), float(capacity))
    rest = (tables.shape[0] - 2 * planes - 1, tables.shape[1])
    tables[2 * planes + 1 :, :] = jnp.broadcast_to(2.0 / count, rest)


def ranks_pass(capacity, spots, weight):
    blocks, tok = weight.shape
    vmem = pl.BlockSpec(memory_space=pltpu.VMEM)
    return pl.pallas_call(
        functools.partial(ranks_kernel, capacity),
        out_shape=jax.ShapeDtypeStruct((blocks // 4 * 2 + 8, 4 * tok), jnp.float32),
        in_specs=[pl.BlockSpec(memory_space=pltpu.SMEM), vmem],
        out_specs=vmem,
        scratch_shapes=[pltpu.VMEM(weight.shape, jnp.float32)] * 2,
        compiler_params=pltpu.CompilerParams(vmem_limit_bytes=4 * 1024 * 1024),
    )(spots, weight)


def plane_kernel(k, picked, gives, tables, *refs):
    *xs, w_gate, w_up, w_down, keep = refs[: -gives - 2]
    *gives, act, rows = refs[-gives - 2 :]
    slots, hidden = act.shape
    features = rows.shape[1]
    half, width = keep.shape[0], tables.shape[1]
    wide, cut = 256, 512
    place = tables[pl.ds(8 if picked else k, 1), :]
    share = tables[pl.ds(4 + k, 1), :]
    if picked:
        tok = width // 4
        place, share = (
            jnp.concatenate([row[:, i * tok : (i + 1) * tok] for i in picked], axis=1)
            for row in (place, share)
        )
        width = 2 * tok
    slot = lax.broadcasted_iota(jnp.int32, (slots, width), 0).astype(jnp.float32)
    hits = slot == place
    scale = jnp.sum(jnp.where(hits, share, 0.0), axis=1, keepdims=True)
    select = hits.astype(jnp.float32).astype(jnp.bfloat16)
    for i in range(features // cut):
        span = pl.ds(i * cut, cut)
        x = jnp.concatenate([block[:, span] for block in xs], axis=0)
        rows[:, span] = jnp.dot(select, x, preferred_element_type=jnp.float32).astype(jnp.bfloat16)
    for i in range(hidden // wide):
        span = pl.ds(i * wide, wide)
        gate = jnp.dot(rows[...], w_gate[:, span], preferred_element_type=jnp.float32)
        up = jnp.dot(rows[...], w_up[:, span], preferred_element_type=jnp.float32)
        act[:, span] = (gate / (1.0 + jnp.exp(-gate)) * up).astype(jnp.bfloat16)
    back = select.T
    for i in range(features // cut):
        span = pl.ds(i * cut, cut)
        result = jnp.dot(act[...], w_down[:, span], preferred_element_type=jnp.float32)
        made = (result * scale).astype(jnp.bfloat16)
        spread = jnp.dot(back, made, preferred_element_type=jnp.float32).astype(jnp.bfloat16)
        keep[:, span] = spread[:half]
        start = half
        for give in gives:
            give[:, span] = spread[start : start + give.shape[0]]
            start += give.shape[0]


def plane_pass(k, tables, xs, w_gate, w_up, w_down, slots, pieces=None, picked=None):
    tok, features = xs[0].shape
    hidden = w_gate.shape[1]
    blocks = 2 if picked else 4
    rows = blocks * slots
    half = blocks // 2 * tok
    pieces = pieces or (half,)
    outs = tuple(jax.ShapeDtypeStruct((some, features), jnp.bfloat16) for some in (half, *pieces))
    outs += (jax.ShapeDtypeStruct((rows, hidden), jnp.bfloat16),)
    vmem = pl.BlockSpec(memory_space=pltpu.VMEM)
    flops = 2 * rows * (3 * features * hidden + 2 * blocks * tok * features)
    moved = 2 * (3 * features * hidden + 2 * blocks * tok * features)
    return pl.pallas_call(
        functools.partial(plane_kernel, k, picked, len(pieces)),
        out_shape=outs,
        in_specs=[vmem] * (len(xs) + 4),
        out_specs=[vmem] * len(outs),
        scratch_shapes=[pltpu.VMEM((rows, features), jnp.bfloat16)],
        compiler_params=pltpu.CompilerParams(vmem_limit_bytes=12 * 1024 * 1024),
        cost_estimate=pl.CostEstimate(
            flops=flops, bytes_accessed=moved, transcendentals=rows * hidden
        ),
    )(tables, *xs, w_gate, w_up, w_down)


def gram_kernel(tables, *refs):
    *acts, gram = refs
    wide = 256
    scale = tables[9:10, :1]
    rows = jnp.concatenate([act[...] for act in acts], axis=0)
    for i in range(gram.shape[0] // wide):
        some = rows[:, i * wide : (i + 1) * wide]
        gram[pl.ds(i * wide, wide), :] = gram_of_two(some, rows) * scale


def gram_of_two(left, right):
    return lax.dot_general(left, right, (((0,), (0,)), ((), ())), preferred_element_type=jnp.float32)


def gram_pass(tables, *acts):
    hidden = acts[0].shape[1]
    rows = sum(act.shape[0] for act in acts)
    vmem = pl.BlockSpec(memory_space=pltpu.VMEM)
    return pl.pallas_call(
        gram_kernel,
        out_shape=jax.ShapeDtypeStruct((hidden, hidden), jnp.float32),
        in_specs=[vmem] * (len(acts) + 1),
        out_specs=vmem,
        compiler_params=pltpu.CompilerParams(vmem_limit_bytes=16 * 1024 * 1024),
        cost_estimate=pl.CostEstimate(
            flops=2 * rows * hidden * hidden,
            bytes_accessed=4 * hidden * hidden + 2 * rows * hidden,
            transcendentals=0,
        ),
    )(tables, *acts)


def mix_kernel(far_low, far_high, near_high, near_low, side, keep, got, mixed):
    most, tok = near_low.shape[0], mixed.shape[0]
    for start, stop, near, far in (
        (0, most, near_low, far_low),
        (most, tok, near_high, far_high),
    ):
        total = keep[start:stop, :].astype(jnp.float32) + got[start:stop, :].astype(jnp.float32)
        total = total + side[start:stop, :].astype(jnp.float32) + near[...].astype(jnp.float32)
        mixed[start:stop, :] = (total + far[...].astype(jnp.float32)).astype(mixed.dtype)


def mix_pass(*parts):
    side = parts[4]
    vmem = pl.BlockSpec(memory_space=pltpu.VMEM)
    return pl.pallas_call(
        mix_kernel,
        out_shape=jax.ShapeDtypeStruct(side.shape, side.dtype),
        in_specs=[vmem] * len(parts),
        out_specs=vmem,
        compiler_params=pltpu.CompilerParams(vmem_limit_bytes=12 * 1024 * 1024),
    )(*parts)


def staged(routes, probs, tokens, w_gate, w_up, w_down):
    tok, top = routes.shape
    size = lax.axis_size("expert")
    slots = 5 * tok * top // (4 * size)
    capacity = tok * top // 2
    half = tok // 2
    me = lax.axis_index("expert")
    z, y, core = me // 4, me // 2 % 2, me % 2

    def swapped(array, bit):
        return lax.ppermute(array, "expert", [(i, i ^ bit) for i in range(size)])

    sibling = functools.partial(swapped, bit=1)
    column = functools.partial(swapped, bit=2)
    pair = functools.partial(swapped, bit=4)
    far = functools.partial(swapped, bit=8)

    def together(*arrays):
        return lax.optimization_barrier(arrays)

    spots = jnp.stack(
        [
            (z ^ k) * 4 + (y ^ column_bit) * 2 + (core ^ core_bit)
            for k in range(4)
            for core_bit in range(2)
            for column_bit in range(2)
        ]
    ).astype(jnp.int32)

    def expert(k, *xs, pieces=None, picked=None):
        return plane_pass(k, tables, xs, w_gate, w_up, w_down, slots, pieces, picked)

    mine, a0_low, a0_high = prepare_pass(routes, probs, tokens, size)
    a0 = tokens
    a1, low, b0, c0, weight, a0_high = together(
        pair(a0),
        far(a0_low),
        column(a0),
        sibling(a0),
        lax.all_to_all(mine, "expert", split_axis=0, concat_axis=0, tiled=True),
        a0_high,
    )
    tables = ranks_pass(capacity, spots, weight)
    high = far(a0_high)
    b1 = column(a1)
    d0 = sibling(b0)
    c1 = sibling(a1)
    keep0, give0, act0 = expert(0, a0, b0, c0, d0)
    high, b1, c1, keep0, give0, act0, tables = together(
        high, b1, c1, keep0, give0, act0, tables
    )
    a2 = jnp.concatenate([low, high], axis=0)
    a3 = pair(a2)
    b2 = column(a2)
    d1 = sibling(b1)
    c2 = sibling(a2)
    keep1, give1, give1_side, act1 = expert(1, a1, b1, c1, d1, pieces=(tok, tok))
    got1_side = sibling(give1_side)
    a3, b2, c2, keep1, give1, act1, got1_side = together(
        a3, b2, c2, keep1, give1, act1, got1_side
    )
    b3 = pair(b2)
    came1_low = column(summed(keep1[tok : tok + half], got1_side[:half]))
    got1 = sibling(give1)
    d2 = sibling(b2)
    c3 = sibling(a3)
    keep2, give2, give2_low, give2_high, act2 = expert(
        2, a2, b2, c2, d2, pieces=(tok, half, half)
    )
    got2_high = sibling(give2_high)
    keep3, give3, act3 = expert(3, a3, c3, picked=(0, 2))
    got0 = sibling(give0)
    b3, came1_low, got0, got1, got2_high, keep2, give2, give2_low, act2, keep3, give3, act3 = (
        together(
            b3, came1_low, got0, got1, got2_high, keep2, give2, give2_low, act2, keep3, give3, act3
        )
    )
    d3 = sibling(b3)
    near1 = summed(keep1[:half], got1[:half], came1_low)

    side_high = column(summed(keep2[tok + half :], got2_high))
    got2 = sibling(give2)
    keep3_side, give3_low, give3_high, act4 = expert(
        3, b3, d3, pieces=(half, half), picked=(1, 3)
    )
    got3_low, got3_high = sibling(give3_low), sibling(give3_high)
    near1_low = pair(near1)
    side_high, near1_low, keep3_side, got3_low, got3_high, act4, got2 = together(
        side_high, near1_low, keep3_side, got3_low, got3_high, act4, got2
    )
    got2_low, got3 = sibling(give2_low), sibling(give3)
    far2_high = far(summed(keep2[half:tok], got2[half:], side_high))
    came3_low = column(summed(keep3_side[:half], got3_low))
    came3_high = column(summed(keep3_side[half:], got3_high))
    side0 = summed(keep0[tok:], got0[tok:])
    side1 = summed(keep1[tok + half :], got1_side[half:])
    far2_high, came3_low, came3_high, side0, side1, got2_low, got3 = together(
        far2_high, came3_low, came3_high, side0, side1, got2_low, got3
    )
    far3_high = far(summed(keep3[half:], got3[half:], came3_high))
    pair3_low = pair(summed(keep3[:half], got3[:half], came3_low))
    side_low = column(summed(keep2[tok : tok + half], got2_low))
    came1_high = column(side1)
    gram = gram_pass(tables, act0, act1, act2, act3, act4)
    far3_high, pair3_low, side_low, came1_high, side0, gram = together(
        far3_high, pair3_low, side_low, came1_high, side0, gram
    )
    far2_low = summed(keep2[:half], got2[:half], pair3_low, side_low)
    far2_low, far3_high, came1_high, side0 = together(far2_low, far3_high, came1_high, side0)
    far2_low = far(far2_low)
    near1_high = pair(summed(keep1[half:tok], got1[half:], came1_high, far3_high))
    last0 = column(side0)
    mixed = mix_pass(
        far2_low, far2_high, near1_high, near1_low, last0, keep0, got0
    )

    return gram[None], mixed


def gathered(routes, probs, tokens, w_gate, w_up, w_down):
    tok_rows, top = routes.shape
    size = lax.axis_size("expert")
    capacity = tok_rows * top // 2
    every_token = lax.all_gather(tokens, "expert", tiled=True)
    weight = weights_for_me(routes, probs, size)
    named = (weight >= 0.0).astype(jnp.int32)
    within = jnp.cumsum(named, axis=1) - named
    per_device = jnp.sum(named, axis=1)
    before = jnp.cumsum(per_device) - per_device
    rank = within + before[:, None]
    kept = (named == 1) & (rank < capacity)
    count = jnp.minimum(jnp.sum(per_device), capacity)
    slot = jnp.where(kept, rank, -1).reshape(size * tok_rows)
    place = jnp.arange(capacity, dtype=jnp.int32)
    select = (place[:, None] == slot[None, :]).astype(jnp.bfloat16)
    rows = jnp.dot(select, every_token, preferred_element_type=jnp.float32).astype(jnp.bfloat16)
    gram_sum, made = expert_pass(rows, w_gate, w_up, w_down)
    gram = gram_sum * (2.0 / count.astype(jnp.float32))
    spread = lax.dot_general(
        select, made, (((0,), (0,)), ((), ())), preferred_element_type=jnp.float32
    )
    partial = (spread * weight.reshape(size * tok_rows, 1)).astype(jnp.bfloat16)
    mixed = lax.psum_scatter(partial, "expert", scatter_dimension=0, tiled=True)
    return gram[None], mixed.astype(jnp.bfloat16)


def shards(routes, probs, tokens, gate_weight, up_weight, down_weight):
    body = staged if lax.axis_size("expert") == 16 else gathered
    return body(routes, probs, tokens, gate_weight[0], up_weight[0], down_weight[0])


def solution(mesh):
    placed = (
        P(("parts", "expert"), None),
        P(("parts", "expert"), None),
        P(("parts", "expert"), None),
        P("expert", None, None),
        P("expert", None, None),
        P("expert", None, None),
    )
    return jax.shard_map(
        shards,
        mesh=mesh,
        in_specs=placed,
        out_specs=(P(("parts", "expert"), None, None), P(("parts", "expert"), None)),
        check_vma=False,
    )
```

```python
import functools

import jax
import jax.numpy as jnp
from jax import lax
from jax.experimental import pallas as pl
from jax.experimental.pallas import tpu as pltpu
from jax.sharding import PartitionSpec as P


def gram_of(rows):
    return lax.dot_general(rows, rows, (((0,), (0,)), ((), ())), preferred_element_type=jnp.float32)


def expert_pass(rows, w_gate, w_up, w_down):
    gate = jnp.dot(rows, w_gate, preferred_element_type=jnp.float32)
    up = jnp.dot(rows, w_up, preferred_element_type=jnp.float32)
    act = (jax.nn.silu(gate) * up).astype(jnp.bfloat16)
    gram_sum = gram_of(act)
    made = jnp.dot(act, w_down, preferred_element_type=jnp.float32).astype(jnp.bfloat16)
    return (gram_sum, made)


def weights_for_me(routes, probs, experts):
    names = routes.T[None, :, :] == jnp.arange(experts, dtype=jnp.int32)[:, None, None]
    weight = jnp.sum(jnp.where(names, probs.T[None, :, :], 0.0), axis=1)
    mine = jnp.where(jnp.any(names, axis=1), weight, -1.0)
    return lax.all_to_all(mine, "expert", split_axis=0, concat_axis=0, tiled=True)


def prepare_kernel(routes, probs, tokens, mine, low, high, names, shares, sems):
    half = low.shape[0]
    pairs = (
        (routes, names),
        (probs, shares),
        (tokens.at[pl.ds(0, half), :], low),
        (tokens.at[pl.ds(half, half), :], high),
    )
    copies = [pltpu.make_async_copy(*pair, sems.at[i]) for i, pair in enumerate(pairs)]
    for copy in copies:
        copy.start()
    for copy in copies[:2]:
        copy.wait()
    for e in range(mine.shape[0]):
        hit = (names[...] == e).astype(jnp.float32)
        named = jnp.sum(hit, axis=0, keepdims=True)
        share = jnp.sum(hit * shares[...], axis=0, keepdims=True)
        mine[pl.ds(e, 1), :] = jnp.where(named > 0.0, share, -1.0)
    for copy in copies[2:]:
        copy.wait()


def prepare_pass(routes, probs, tokens, experts):
    tok, top = routes.shape
    half = jax.ShapeDtypeStruct((tok // 2, tokens.shape[1]), tokens.dtype)
    vmem = pl.BlockSpec(memory_space=pltpu.VMEM)
    return pl.pallas_call(
        prepare_kernel,
        out_shape=(jax.ShapeDtypeStruct((experts, tok), jnp.float32), half, half),
        in_specs=[pl.BlockSpec(memory_space=pl.ANY)] * 3,
        out_specs=[vmem] * 3,
        scratch_shapes=[
            pltpu.VMEM((top, tok), routes.dtype),
            pltpu.VMEM((top, tok), probs.dtype),
            pltpu.SemaphoreType.DMA((4,)),
        ],
        compiler_params=pltpu.CompilerParams(vmem_limit_bytes=4 * 1024 * 1024),
    )(routes.T, probs.T, tokens)


def summed(*parts):
    total = parts[0].astype(jnp.float32)
    for part in parts[1:]:
        total = total + part.astype(jnp.float32)
    return total.astype(jnp.bfloat16)


def ranks_kernel(capacity, spots, weight, tables, ranks, chip_ranks):
    blocks, tok = weight.shape
    planes = blocks // 4
    named = (weight[...] >= 0.0).astype(jnp.float32)
    lane = lax.broadcasted_iota(jnp.int32, (tok, tok), 0)
    below = (lane < lax.broadcasted_iota(jnp.int32, (tok, tok), 1)).astype(jnp.float32)
    within = jnp.dot(named, below, preferred_element_type=jnp.float32)
    totals = jnp.broadcast_to(jnp.sum(named, axis=1, keepdims=True), (blocks, tok))
    row = lax.broadcasted_iota(jnp.int32, (blocks, blocks), 0)
    column = lax.broadcasted_iota(jnp.int32, (blocks, blocks), 1)
    earlier = (column < row).astype(jnp.float32)
    before = jnp.dot(earlier, totals, preferred_element_type=jnp.float32)
    rank = within + before
    kept = (named > 0.0) & (rank < capacity)
    first = (column < row // 4 * 4).astype(jnp.float32)
    start = jnp.dot(first, totals, preferred_element_type=jnp.float32)
    ranks[...] = jnp.where(kept, rank - start, -1.0)
    first = (column < row // 2 * 2).astype(jnp.float32)
    start = jnp.dot(first, totals, preferred_element_type=jnp.float32)
    chip_ranks[...] = jnp.where(kept, rank - start, -1.0)
    for i in range(4):
        span = pl.ds(i * tok, tok)
        tables[pl.ds(2 * planes, 1), span] = chip_ranks[pl.ds(spots[4 * planes - 4 + i], 1), :]
    for k in range(planes):
        for i in range(4):
            span = pl.ds(i * tok, tok)
            tables[pl.ds(k, 1), span] = ranks[pl.ds(spots[4 * k + i], 1), :]
            tables[pl.ds(planes + k, 1), span] = weight[pl.ds(spots[4 * k + i], 1), :]
    count = jnp.minimum(jnp.sum(totals[:, :1], axis=0, keepdims=True), float(capacity))
    rest = (tables.shape[0] - 2 * planes - 1, tables.shape[1])
    tables[2 * planes + 1 :, :] = jnp.broadcast_to(2.0 / count, rest)


def ranks_pass(capacity, spots, weight):
    blocks, tok = weight.shape
    vmem = pl.BlockSpec(memory_space=pltpu.VMEM)
    return pl.pallas_call(
        functools.partial(ranks_kernel, capacity),
        out_shape=jax.ShapeDtypeStruct((blocks // 4 * 2 + 8, 4 * tok), jnp.float32),
        in_specs=[pl.BlockSpec(memory_space=pltpu.SMEM), vmem],
        out_specs=vmem,
        scratch_shapes=[pltpu.VMEM(weight.shape, jnp.float32)] * 2,
        compiler_params=pltpu.CompilerParams(vmem_limit_bytes=4 * 1024 * 1024),
    )(spots, weight)


def plane_kernel(k, picked, gives, tables, *refs):
    *xs, w_gate, w_up, w_down, keep = refs[: -gives - 2]
    *gives, act, rows = refs[-gives - 2 :]
    slots, hidden = act.shape
    features = rows.shape[1]
    half, width = keep.shape[0], tables.shape[1]
    wide, cut = 256, 512
    place = tables[pl.ds(8 if picked else k, 1), :]
    share = tables[pl.ds(4 + k, 1), :]
    if picked:
        tok = width // 4
        place, share = (
            jnp.concatenate([row[:, i * tok : (i + 1) * tok] for i in picked], axis=1)
            for row in (place, share)
        )
        width = 2 * tok
    slot = lax.broadcasted_iota(jnp.int32, (slots, width), 0).astype(jnp.float32)
    hits = slot == place
    scale = jnp.sum(jnp.where(hits, share, 0.0), axis=1, keepdims=True)
    select = hits.astype(jnp.float32).astype(jnp.bfloat16)
    for i in range(features // cut):
        span = pl.ds(i * cut, cut)
        x = jnp.concatenate([block[:, span] for block in xs], axis=0)
        rows[:, span] = jnp.dot(select, x, preferred_element_type=jnp.float32).astype(jnp.bfloat16)
    for i in range(hidden // wide):
        span = pl.ds(i * wide, wide)
        gate = jnp.dot(rows[...], w_gate[:, span], preferred_element_type=jnp.float32)
        up = jnp.dot(rows[...], w_up[:, span], preferred_element_type=jnp.float32)
        act[:, span] = (gate / (1.0 + jnp.exp(-gate)) * up).astype(jnp.bfloat16)
    back = select.T
    for i in range(features // cut):
        span = pl.ds(i * cut, cut)
        result = jnp.dot(act[...], w_down[:, span], preferred_element_type=jnp.float32)
        made = (result * scale).astype(jnp.bfloat16)
        spread = jnp.dot(back, made, preferred_element_type=jnp.float32).astype(jnp.bfloat16)
        keep[:, span] = spread[:half]
        start = half
        for give in gives:
            give[:, span] = spread[start : start + give.shape[0]]
            start += give.shape[0]


def plane_pass(k, tables, xs, w_gate, w_up, w_down, slots, pieces=None, picked=None):
    tok, features = xs[0].shape
    hidden = w_gate.shape[1]
    blocks = 2 if picked else 4
    rows = blocks * slots
    half = blocks // 2 * tok
    pieces = pieces or (half,)
    outs = tuple(jax.ShapeDtypeStruct((some, features), jnp.bfloat16) for some in (half, *pieces))
    outs += (jax.ShapeDtypeStruct((rows, hidden), jnp.bfloat16),)
    vmem = pl.BlockSpec(memory_space=pltpu.VMEM)
    flops = 2 * rows * (3 * features * hidden + 2 * blocks * tok * features)
    moved = 2 * (3 * features * hidden + 2 * blocks * tok * features)
    return pl.pallas_call(
        functools.partial(plane_kernel, k, picked, len(pieces)),
        out_shape=outs,
        in_specs=[vmem] * (len(xs) + 4),
        out_specs=[vmem] * len(outs),
        scratch_shapes=[pltpu.VMEM((rows, features), jnp.bfloat16)],
        compiler_params=pltpu.CompilerParams(vmem_limit_bytes=12 * 1024 * 1024),
        cost_estimate=pl.CostEstimate(
            flops=flops, bytes_accessed=moved, transcendentals=rows * hidden
        ),
    )(tables, *xs, w_gate, w_up, w_down)


def gram_kernel(tables, *refs):
    *acts, gram = refs
    wide = 256
    scale = tables[9:10, :1]
    rows = jnp.concatenate([act[...] for act in acts], axis=0)
    for i in range(gram.shape[0] // wide):
        some = rows[:, i * wide : (i + 1) * wide]
        gram[pl.ds(i * wide, wide), :] = gram_of_two(some, rows) * scale


def gram_of_two(left, right):
    return lax.dot_general(left, right, (((0,), (0,)), ((), ())), preferred_element_type=jnp.float32)


def gram_pass(tables, *acts):
    hidden = acts[0].shape[1]
    rows = sum(act.shape[0] for act in acts)
    vmem = pl.BlockSpec(memory_space=pltpu.VMEM)
    return pl.pallas_call(
        gram_kernel,
        out_shape=jax.ShapeDtypeStruct((hidden, hidden), jnp.float32),
        in_specs=[vmem] * (len(acts) + 1),
        out_specs=vmem,
        compiler_params=pltpu.CompilerParams(vmem_limit_bytes=16 * 1024 * 1024),
        cost_estimate=pl.CostEstimate(
            flops=2 * rows * hidden * hidden,
            bytes_accessed=4 * hidden * hidden + 2 * rows * hidden,
            transcendentals=0,
        ),
    )(tables, *acts)


def mix_kernel(far_low, far_high, near_high, near_low, side, keep, got, mixed):
    most, tok = near_low.shape[0], mixed.shape[0]
    for start, stop, near, far in (
        (0, most, near_low, far_low),
        (most, tok, near_high, far_high),
    ):
        total = keep[start:stop, :].astype(jnp.float32) + got[start:stop, :].astype(jnp.float32)
        total = total + side[start:stop, :].astype(jnp.float32) + near[...].astype(jnp.float32)
        mixed[start:stop, :] = (total + far[...].astype(jnp.float32)).astype(mixed.dtype)


def mix_pass(*parts):
    side = parts[4]
    vmem = pl.BlockSpec(memory_space=pltpu.VMEM)
    return pl.pallas_call(
        mix_kernel,
        out_shape=jax.ShapeDtypeStruct(side.shape, side.dtype),
        in_specs=[vmem] * len(parts),
        out_specs=vmem,
        compiler_params=pltpu.CompilerParams(vmem_limit_bytes=12 * 1024 * 1024),
    )(*parts)


def staged(routes, probs, tokens, w_gate, w_up, w_down):
    tok, top = routes.shape
    size = lax.axis_size("expert")
    slots = 5 * tok * top // (4 * size)
    capacity = tok * top // 2
    half = tok // 2
    me = lax.axis_index("expert")
    z, y, core = me // 4, me // 2 % 2, me % 2

    def swapped(array, bit):
        return lax.ppermute(array, "expert", [(i, i ^ bit) for i in range(size)])

    sibling = functools.partial(swapped, bit=1)
    column = functools.partial(swapped, bit=2)
    pair = functools.partial(swapped, bit=4)
    far = functools.partial(swapped, bit=8)

    def together(*arrays):
        return lax.optimization_barrier(arrays)

    spots = jnp.stack(
        [
            (z ^ k) * 4 + (y ^ column_bit) * 2 + (core ^ core_bit)
            for k in range(4)
            for core_bit in range(2)
            for column_bit in range(2)
        ]
    ).astype(jnp.int32)

    def expert(k, *xs, pieces=None, picked=None):
        return plane_pass(k, tables, xs, w_gate, w_up, w_down, slots, pieces, picked)

    mine, a0_low, a0_high = prepare_pass(routes, probs, tokens, size)
    a0 = tokens
    all_mine = lax.all_gather(mine, "expert")
    a1, low, b0, c0, a0_high = together(
        pair(a0), far(a0_low), column(a0), sibling(a0), a0_high
    )
    weight = lax.dynamic_index_in_dim(all_mine, me, 1, False)
    tables = ranks_pass(capacity, spots, weight)
    high = far(a0_high)
    b1 = column(a1)
    d0 = sibling(b0)
    c1 = sibling(a1)
    keep0, give0, act0 = expert(0, a0, b0, c0, d0)
    high, b1, c1, keep0, give0, act0, tables = together(
        high, b1, c1, keep0, give0, act0, tables
    )
    a2 = jnp.concatenate([low, high], axis=0)
    a3 = pair(a2)
    b2 = column(a2)
    d1 = sibling(b1)
    c2 = sibling(a2)
    keep1, give1, give1_side, act1 = expert(1, a1, b1, c1, d1, pieces=(tok, tok))
    got1_side = sibling(give1_side)
    a3, b2, c2, keep1, give1, act1, got1_side = together(
        a3, b2, c2, keep1, give1, act1, got1_side
    )
    b3 = pair(b2)
    came1_low = column(summed(keep1[tok : tok + half], got1_side[:half]))
    got1 = sibling(give1)
    d2 = sibling(b2)
    c3 = sibling(a3)
    keep2, give2, give2_low, give2_high, act2 = expert(
        2, a2, b2, c2, d2, pieces=(tok, half, half)
    )
    got2_high = sibling(give2_high)
    keep3, give3, act3 = expert(3, a3, c3, picked=(0, 2))
    got0 = sibling(give0)
    b3, came1_low, got0, got1, got2_high, keep2, give2, give2_low, act2, keep3, give3, act3 = (
        together(
            b3, came1_low, got0, got1, got2_high, keep2, give2, give2_low, act2, keep3, give3, act3
        )
    )
    d3 = sibling(b3)
    near1 = summed(keep1[:half], got1[:half], came1_low)

    side_high = column(summed(keep2[tok + half :], got2_high))
    got2 = sibling(give2)
    keep3_side, give3_side, act4 = expert(3, b3, d3, picked=(1, 3))
    keep3_side, give3_side, act4, got2, side_high, near1 = together(
        keep3_side, give3_side, act4, got2, side_high, near1
    )
    got2_low, got3 = sibling(give2_low), sibling(give3)
    far2_high = far(summed(keep2[half:tok], got2[half:], side_high))
    got3_side = sibling(give3_side)
    came3_low = column(summed(keep3_side[:half], got3_side[:half]))
    came3_high = column(summed(keep3_side[half:], got3_side[half:]))
    near1_low = pair(near1)
    side0 = summed(keep0[tok:], got0[tok:])
    side1 = summed(keep1[tok + half :], got1_side[half:])
    came3_low, came3_high, far2_high, near1_low, side0, side1, got2_low, got3 = together(
        came3_low, came3_high, far2_high, near1_low, side0, side1, got2_low, got3
    )
    far3_high = far(summed(keep3[half:], got3[half:], came3_high))
    pair3_low = pair(summed(keep3[:half], got3[:half], came3_low))
    side_low = column(summed(keep2[tok : tok + half], got2_low))
    came1_high = column(side1)
    gram = gram_pass(tables, act0, act1, act2, act3, act4)
    far3_high, pair3_low, side_low, came1_high, side0, gram = together(
        far3_high, pair3_low, side_low, came1_high, side0, gram
    )
    far2_low = summed(keep2[:half], got2[:half], pair3_low, side_low)
    far2_low, far3_high, came1_high, side0 = together(far2_low, far3_high, came1_high, side0)
    far2_low = far(far2_low)
    near1_high = pair(summed(keep1[half:tok], got1[half:], came1_high, far3_high))
    last0 = column(side0)
    mixed = mix_pass(
        far2_low, far2_high, near1_high, near1_low, last0, keep0, got0
    )

    return gram[None], mixed


def gathered(routes, probs, tokens, w_gate, w_up, w_down):
    tok_rows, top = routes.shape
    size = lax.axis_size("expert")
    capacity = tok_rows * top // 2
    every_token = lax.all_gather(tokens, "expert", tiled=True)
    weight = weights_for_me(routes, probs, size)
    named = (weight >= 0.0).astype(jnp.int32)
    within = jnp.cumsum(named, axis=1) - named
    per_device = jnp.sum(named, axis=1)
    before = jnp.cumsum(per_device) - per_device
    rank = within + before[:, None]
    kept = (named == 1) & (rank < capacity)
    count = jnp.minimum(jnp.sum(per_device), capacity)
    slot = jnp.where(kept, rank, -1).reshape(size * tok_rows)
    place = jnp.arange(capacity, dtype=jnp.int32)
    select = (place[:, None] == slot[None, :]).astype(jnp.bfloat16)
    rows = jnp.dot(select, every_token, preferred_element_type=jnp.float32).astype(jnp.bfloat16)
    gram_sum, made = expert_pass(rows, w_gate, w_up, w_down)
    gram = gram_sum * (2.0 / count.astype(jnp.float32))
    spread = lax.dot_general(
        select, made, (((0,), (0,)), ((), ())), preferred_element_type=jnp.float32
    )
    partial = (spread * weight.reshape(size * tok_rows, 1)).astype(jnp.bfloat16)
    mixed = lax.psum_scatter(partial, "expert", scatter_dimension=0, tiled=True)
    return gram[None], mixed.astype(jnp.bfloat16)


def shards(routes, probs, tokens, gate_weight, up_weight, down_weight):
    body = staged if lax.axis_size("expert") == 16 else gathered
    return body(routes, probs, tokens, gate_weight[0], up_weight[0], down_weight[0])


def solution(mesh):
    placed = (
        P(("parts", "expert"), None),
        P(("parts", "expert"), None),
        P(("parts", "expert"), None),
        P("expert", None, None),
        P("expert", None, None),
        P("expert", None, None),
    )
    return jax.shard_map(
        shards,
        mesh=mesh,
        in_specs=placed,
        out_specs=(P(("parts", "expert"), None, None), P(("parts", "expert"), None)),
        check_vma=False,
    )
```

```python
import functools

import jax
import jax.numpy as jnp
from jax import lax
from jax.experimental import pallas as pl
from jax.experimental.pallas import tpu as pltpu
from jax.sharding import PartitionSpec as P


def gram_of(rows):
    return lax.dot_general(rows, rows, (((0,), (0,)), ((), ())), preferred_element_type=jnp.float32)


def expert_pass(rows, w_gate, w_up, w_down):
    gate = jnp.dot(rows, w_gate, preferred_element_type=jnp.float32)
    up = jnp.dot(rows, w_up, preferred_element_type=jnp.float32)
    act = (jax.nn.silu(gate) * up).astype(jnp.bfloat16)
    gram_sum = gram_of(act)
    made = jnp.dot(act, w_down, preferred_element_type=jnp.float32).astype(jnp.bfloat16)
    return (gram_sum, made)


def weights_for_me(routes, probs, experts):
    names = routes.T[None, :, :] == jnp.arange(experts, dtype=jnp.int32)[:, None, None]
    weight = jnp.sum(jnp.where(names, probs.T[None, :, :], 0.0), axis=1)
    mine = jnp.where(jnp.any(names, axis=1), weight, -1.0)
    return lax.all_to_all(mine, "expert", split_axis=0, concat_axis=0, tiled=True)


def prepare_kernel(routes, probs, tokens, mine, low, high, names, shares, sems):
    half = low.shape[0]
    pairs = (
        (routes, names),
        (probs, shares),
        (tokens.at[pl.ds(0, half), :], low),
        (tokens.at[pl.ds(half, half), :], high),
    )
    copies = [pltpu.make_async_copy(*pair, sems.at[i]) for i, pair in enumerate(pairs)]
    for copy in copies:
        copy.start()
    for copy in copies[:2]:
        copy.wait()
    for e in range(mine.shape[0]):
        hit = (names[...] == e).astype(jnp.float32)
        named = jnp.sum(hit, axis=0, keepdims=True)
        share = jnp.sum(hit * shares[...], axis=0, keepdims=True)
        mine[pl.ds(e, 1), :] = jnp.where(named > 0.0, share, -1.0)
    for copy in copies[2:]:
        copy.wait()


def prepare_pass(routes, probs, tokens, experts):
    tok, top = routes.shape
    half = jax.ShapeDtypeStruct((tok // 2, tokens.shape[1]), tokens.dtype)
    vmem = pl.BlockSpec(memory_space=pltpu.VMEM)
    return pl.pallas_call(
        prepare_kernel,
        out_shape=(jax.ShapeDtypeStruct((experts, tok), jnp.float32), half, half),
        in_specs=[pl.BlockSpec(memory_space=pl.ANY)] * 3,
        out_specs=[vmem] * 3,
        scratch_shapes=[
            pltpu.VMEM((top, tok), routes.dtype),
            pltpu.VMEM((top, tok), probs.dtype),
            pltpu.SemaphoreType.DMA((4,)),
        ],
        compiler_params=pltpu.CompilerParams(vmem_limit_bytes=58 * 1024 * 1024),
    )(routes.T, probs.T, tokens)


def summed(*parts):
    total = parts[0].astype(jnp.float32)
    for part in parts[1:]:
        total = total + part.astype(jnp.float32)
    return total.astype(jnp.bfloat16)


def ranks_kernel(capacity, spots, weight, tables, ranks, chip_ranks):
    blocks, tok = weight.shape
    planes = blocks // 4
    named = (weight[...] >= 0.0).astype(jnp.float32)
    lane = lax.broadcasted_iota(jnp.int32, (tok, tok), 0)
    below = (lane < lax.broadcasted_iota(jnp.int32, (tok, tok), 1)).astype(jnp.float32)
    within = jnp.dot(named, below, preferred_element_type=jnp.float32)
    totals = jnp.broadcast_to(jnp.sum(named, axis=1, keepdims=True), (blocks, tok))
    row = lax.broadcasted_iota(jnp.int32, (blocks, blocks), 0)
    column = lax.broadcasted_iota(jnp.int32, (blocks, blocks), 1)
    earlier = (column < row).astype(jnp.float32)
    before = jnp.dot(earlier, totals, preferred_element_type=jnp.float32)
    rank = within + before
    kept = (named > 0.0) & (rank < capacity)
    first = (column < row // 4 * 4).astype(jnp.float32)
    start = jnp.dot(first, totals, preferred_element_type=jnp.float32)
    ranks[...] = jnp.where(kept, rank - start, -1.0)
    first = (column < row // 2 * 2).astype(jnp.float32)
    start = jnp.dot(first, totals, preferred_element_type=jnp.float32)
    chip_ranks[...] = jnp.where(kept, rank - start, -1.0)
    for i in range(4):
        span = pl.ds(i * tok, tok)
        tables[pl.ds(2 * planes, 1), span] = chip_ranks[pl.ds(spots[4 * planes - 4 + i], 1), :]
    for k in range(planes):
        for i in range(4):
            span = pl.ds(i * tok, tok)
            tables[pl.ds(k, 1), span] = ranks[pl.ds(spots[4 * k + i], 1), :]
            tables[pl.ds(planes + k, 1), span] = weight[pl.ds(spots[4 * k + i], 1), :]
    count = jnp.minimum(jnp.sum(totals[:, :1], axis=0, keepdims=True), float(capacity))
    rest = (tables.shape[0] - 2 * planes - 1, tables.shape[1])
    tables[2 * planes + 1 :, :] = jnp.broadcast_to(2.0 / count, rest)


def ranks_pass(capacity, spots, weight):
    blocks, tok = weight.shape
    vmem = pl.BlockSpec(memory_space=pltpu.VMEM)
    return pl.pallas_call(
        functools.partial(ranks_kernel, capacity),
        out_shape=jax.ShapeDtypeStruct((blocks // 4 * 2 + 8, 4 * tok), jnp.float32),
        in_specs=[pl.BlockSpec(memory_space=pltpu.SMEM), vmem],
        out_specs=vmem,
        scratch_shapes=[pltpu.VMEM(weight.shape, jnp.float32)] * 2,
        compiler_params=pltpu.CompilerParams(vmem_limit_bytes=4 * 1024 * 1024),
    )(spots, weight)


def plane_kernel(k, picked, gives, tables, *refs):
    *xs, w_gate, w_up, w_down, keep = refs[: -gives - 2]
    *gives, act, rows = refs[-gives - 2 :]
    slots, hidden = act.shape
    features = rows.shape[1]
    half, width = keep.shape[0], tables.shape[1]
    wide, cut = 256, 512
    place = tables[pl.ds(8 if picked else k, 1), :]
    share = tables[pl.ds(4 + k, 1), :]
    if picked:
        tok = width // 4
        place, share = (
            jnp.concatenate([row[:, i * tok : (i + 1) * tok] for i in picked], axis=1)
            for row in (place, share)
        )
        width = 2 * tok
    slot = lax.broadcasted_iota(jnp.int32, (slots, width), 0).astype(jnp.float32)
    hits = slot == place
    scale = jnp.sum(jnp.where(hits, share, 0.0), axis=1, keepdims=True)
    select = hits.astype(jnp.float32).astype(jnp.bfloat16)
    for i in range(features // cut):
        span = pl.ds(i * cut, cut)
        x = jnp.concatenate([block[:, span] for block in xs], axis=0)
        rows[:, span] = jnp.dot(select, x, preferred_element_type=jnp.float32).astype(jnp.bfloat16)
    for i in range(hidden // wide):
        span = pl.ds(i * wide, wide)
        gate = jnp.dot(rows[...], w_gate[:, span], preferred_element_type=jnp.float32)
        up = jnp.dot(rows[...], w_up[:, span], preferred_element_type=jnp.float32)
        act[:, span] = (gate / (1.0 + jnp.exp(-gate)) * up).astype(jnp.bfloat16)
    back = select.T
    for i in range(features // cut):
        span = pl.ds(i * cut, cut)
        result = jnp.dot(act[...], w_down[:, span], preferred_element_type=jnp.float32)
        made = (result * scale).astype(jnp.bfloat16)
        spread = jnp.dot(back, made, preferred_element_type=jnp.float32).astype(jnp.bfloat16)
        keep[:, span] = spread[:half]
        start = half
        for give in gives:
            give[:, span] = spread[start : start + give.shape[0]]
            start += give.shape[0]


def plane_pass(k, tables, xs, w_gate, w_up, w_down, slots, pieces=None, picked=None):
    tok, features = xs[0].shape
    hidden = w_gate.shape[1]
    blocks = 2 if picked else 4
    rows = blocks * slots
    half = blocks // 2 * tok
    pieces = pieces or (half,)
    outs = tuple(jax.ShapeDtypeStruct((some, features), jnp.bfloat16) for some in (half, *pieces))
    outs += (jax.ShapeDtypeStruct((rows, hidden), jnp.bfloat16),)
    vmem = pl.BlockSpec(memory_space=pltpu.VMEM)
    flops = 2 * rows * (3 * features * hidden + 2 * blocks * tok * features)
    moved = 2 * (3 * features * hidden + 2 * blocks * tok * features)
    return pl.pallas_call(
        functools.partial(plane_kernel, k, picked, len(pieces)),
        out_shape=outs,
        in_specs=[vmem] * (len(xs) + 4),
        out_specs=[vmem] * len(outs),
        scratch_shapes=[pltpu.VMEM((rows, features), jnp.bfloat16)],
        compiler_params=pltpu.CompilerParams(vmem_limit_bytes=12 * 1024 * 1024),
        cost_estimate=pl.CostEstimate(
            flops=flops, bytes_accessed=moved, transcendentals=rows * hidden
        ),
    )(tables, *xs, w_gate, w_up, w_down)


def gram_kernel(tables, *refs):
    *acts, gram = refs
    wide = 256
    scale = tables[9:10, :1]
    rows = jnp.concatenate([act[...] for act in acts], axis=0)
    for i in range(gram.shape[0] // wide):
        some = rows[:, i * wide : (i + 1) * wide]
        gram[pl.ds(i * wide, wide), :] = gram_of_two(some, rows) * scale


def gram_of_two(left, right):
    return lax.dot_general(left, right, (((0,), (0,)), ((), ())), preferred_element_type=jnp.float32)


def gram_pass(tables, *acts):
    hidden = acts[0].shape[1]
    rows = sum(act.shape[0] for act in acts)
    vmem = pl.BlockSpec(memory_space=pltpu.VMEM)
    return pl.pallas_call(
        gram_kernel,
        out_shape=jax.ShapeDtypeStruct((hidden, hidden), jnp.float32),
        in_specs=[vmem] * (len(acts) + 1),
        out_specs=vmem,
        compiler_params=pltpu.CompilerParams(vmem_limit_bytes=16 * 1024 * 1024),
        cost_estimate=pl.CostEstimate(
            flops=2 * rows * hidden * hidden,
            bytes_accessed=4 * hidden * hidden + 2 * rows * hidden,
            transcendentals=0,
        ),
    )(tables, *acts)


def mix_kernel(far_low, far_high, near_high, near_low, side, keep, got, mixed):
    most, tok = near_low.shape[0], mixed.shape[0]
    for start, stop, near, far in (
        (0, most, near_low, far_low),
        (most, tok, near_high, far_high),
    ):
        total = keep[start:stop, :].astype(jnp.float32) + got[start:stop, :].astype(jnp.float32)
        total = total + side[start:stop, :].astype(jnp.float32) + near[...].astype(jnp.float32)
        mixed[start:stop, :] = (total + far[...].astype(jnp.float32)).astype(mixed.dtype)


def mix_pass(*parts):
    side = parts[4]
    vmem = pl.BlockSpec(memory_space=pltpu.VMEM)
    return pl.pallas_call(
        mix_kernel,
        out_shape=jax.ShapeDtypeStruct(side.shape, side.dtype),
        in_specs=[vmem] * len(parts),
        out_specs=vmem,
        compiler_params=pltpu.CompilerParams(vmem_limit_bytes=12 * 1024 * 1024),
    )(*parts)


def staged(routes, probs, tokens, w_gate, w_up, w_down):
    tok, top = routes.shape
    size = lax.axis_size("expert")
    slots = 5 * tok * top // (4 * size)
    capacity = tok * top // 2
    half = tok // 2
    me = lax.axis_index("expert")
    z, y, core = me // 4, me // 2 % 2, me % 2

    def swapped(array, bit):
        return lax.ppermute(array, "expert", [(i, i ^ bit) for i in range(size)])

    sibling = functools.partial(swapped, bit=1)
    column = functools.partial(swapped, bit=2)
    pair = functools.partial(swapped, bit=4)
    far = functools.partial(swapped, bit=8)

    def together(*arrays):
        return lax.optimization_barrier(arrays)

    spots = jnp.stack(
        [
            (z ^ k) * 4 + (y ^ column_bit) * 2 + (core ^ core_bit)
            for k in range(4)
            for core_bit in range(2)
            for column_bit in range(2)
        ]
    ).astype(jnp.int32)

    def expert(k, *xs, pieces=None, picked=None):
        return plane_pass(k, tables, xs, w_gate, w_up, w_down, slots, pieces, picked)

    mine, a0_low, a0_high = prepare_pass(routes, probs, tokens, size)
    a0 = tokens
    a1, low, b0, c0, weight, a0_high = together(
        pair(a0),
        far(a0_low),
        column(a0),
        sibling(a0),
        lax.all_to_all(mine, "expert", split_axis=0, concat_axis=0, tiled=True),
        a0_high,
    )
    tables = ranks_pass(capacity, spots, weight)
    high = far(a0_high)
    b1 = column(a1)
    d0 = sibling(b0)
    c1 = sibling(a1)
    keep0, give0, act0 = expert(0, a0, b0, c0, d0)
    high, b1, c1, keep0, give0, act0, tables = together(
        high, b1, c1, keep0, give0, act0, tables
    )
    a2 = jnp.concatenate([low, high], axis=0)
    a3 = pair(a2)
    b2 = column(a2)
    d1 = sibling(b1)
    c2 = sibling(a2)
    keep1, give1, give1_side, act1 = expert(1, a1, b1, c1, d1, pieces=(tok, tok))
    got1_side = sibling(give1_side)
    a3, b2, c2, keep1, give1, act1, got1_side = together(
        a3, b2, c2, keep1, give1, act1, got1_side
    )
    b3 = pair(b2)
    came1_low = column(summed(keep1[tok : tok + half], got1_side[:half]))
    got1 = sibling(give1)
    d2 = sibling(b2)
    c3 = sibling(a3)
    keep2, give2, give2_low, give2_high, act2 = expert(
        2, a2, b2, c2, d2, pieces=(tok, half, half)
    )
    got2_high = sibling(give2_high)
    keep3, give3, act3 = expert(3, a3, c3, picked=(0, 2))
    got0 = sibling(give0)
    b3, came1_low, got0, got1, got2_high, keep2, give2, give2_low, act2, keep3, give3, act3 = (
        together(
            b3, came1_low, got0, got1, got2_high, keep2, give2, give2_low, act2, keep3, give3, act3
        )
    )
    d3 = sibling(b3)
    near1 = summed(keep1[:half], got1[:half], came1_low)

    side_high = column(summed(keep2[tok + half :], got2_high))
    got2 = sibling(give2)
    keep3_side, give3_side, act4 = expert(3, b3, d3, picked=(1, 3))
    keep3_side, give3_side, act4, got2, side_high, near1 = together(
        keep3_side, give3_side, act4, got2, side_high, near1
    )
    got2_low, got3 = sibling(give2_low), sibling(give3)
    far2_high = far(summed(keep2[half:tok], got2[half:], side_high))
    got3_side = sibling(give3_side)
    came3_low = column(summed(keep3_side[:half], got3_side[:half]))
    came3_high = column(summed(keep3_side[half:], got3_side[half:]))
    near1_low = pair(near1)
    side0 = summed(keep0[tok:], got0[tok:])
    side1 = summed(keep1[tok + half :], got1_side[half:])
    came3_low, came3_high, far2_high, near1_low, side0, side1, got2_low, got3 = together(
        came3_low, came3_high, far2_high, near1_low, side0, side1, got2_low, got3
    )
    far3_high = far(summed(keep3[half:], got3[half:], came3_high))
    pair3_low = pair(summed(keep3[:half], got3[:half], came3_low))
    side_low = column(summed(keep2[tok : tok + half], got2_low))
    came1_high = column(side1)
    gram = gram_pass(tables, act0, act1, act2, act3, act4)
    far3_high, pair3_low, side_low, came1_high, side0, gram = together(
        far3_high, pair3_low, side_low, came1_high, side0, gram
    )
    far2_low = summed(keep2[:half], got2[:half], pair3_low, side_low)
    far2_low, far3_high, came1_high, side0 = together(far2_low, far3_high, came1_high, side0)
    far2_low = far(far2_low)
    near1_high = pair(summed(keep1[half:tok], got1[half:], came1_high, far3_high))
    last0 = column(side0)
    mixed = mix_pass(
        far2_low, far2_high, near1_high, near1_low, last0, keep0, got0
    )

    return gram[None], mixed


def gathered(routes, probs, tokens, w_gate, w_up, w_down):
    tok_rows, top = routes.shape
    size = lax.axis_size("expert")
    capacity = tok_rows * top // 2
    every_token = lax.all_gather(tokens, "expert", tiled=True)
    weight = weights_for_me(routes, probs, size)
    named = (weight >= 0.0).astype(jnp.int32)
    within = jnp.cumsum(named, axis=1) - named
    per_device = jnp.sum(named, axis=1)
    before = jnp.cumsum(per_device) - per_device
    rank = within + before[:, None]
    kept = (named == 1) & (rank < capacity)
    count = jnp.minimum(jnp.sum(per_device), capacity)
    slot = jnp.where(kept, rank, -1).reshape(size * tok_rows)
    place = jnp.arange(capacity, dtype=jnp.int32)
    select = (place[:, None] == slot[None, :]).astype(jnp.bfloat16)
    rows = jnp.dot(select, every_token, preferred_element_type=jnp.float32).astype(jnp.bfloat16)
    gram_sum, made = expert_pass(rows, w_gate, w_up, w_down)
    gram = gram_sum * (2.0 / count.astype(jnp.float32))
    spread = lax.dot_general(
        select, made, (((0,), (0,)), ((), ())), preferred_element_type=jnp.float32
    )
    partial = (spread * weight.reshape(size * tok_rows, 1)).astype(jnp.bfloat16)
    mixed = lax.psum_scatter(partial, "expert", scatter_dimension=0, tiled=True)
    return gram[None], mixed.astype(jnp.bfloat16)


def shards(routes, probs, tokens, gate_weight, up_weight, down_weight):
    body = staged if lax.axis_size("expert") == 16 else gathered
    return body(routes, probs, tokens, gate_weight[0], up_weight[0], down_weight[0])


def solution(mesh):
    placed = (
        P(("parts", "expert"), None),
        P(("parts", "expert"), None),
        P(("parts", "expert"), None),
        P("expert", None, None),
        P("expert", None, None),
        P("expert", None, None),
    )
    return jax.shard_map(
        shards,
        mesh=mesh,
        in_specs=placed,
        out_specs=(P(("parts", "expert"), None, None), P(("parts", "expert"), None)),
        check_vma=False,
    )
```

```python
import functools

import jax
import jax.numpy as jnp
from jax import lax
from jax.experimental import pallas as pl
from jax.experimental.pallas import tpu as pltpu
from jax.sharding import PartitionSpec as P


def gram_of(rows):
    return lax.dot_general(rows, rows, (((0,), (0,)), ((), ())), preferred_element_type=jnp.float32)


def expert_pass(rows, w_gate, w_up, w_down):
    gate = jnp.dot(rows, w_gate, preferred_element_type=jnp.float32)
    up = jnp.dot(rows, w_up, preferred_element_type=jnp.float32)
    act = (jax.nn.silu(gate) * up).astype(jnp.bfloat16)
    gram_sum = gram_of(act)
    made = jnp.dot(act, w_down, preferred_element_type=jnp.float32).astype(jnp.bfloat16)
    return (gram_sum, made)


def weights_for_me(routes, probs, experts):
    names = routes.T[None, :, :] == jnp.arange(experts, dtype=jnp.int32)[:, None, None]
    weight = jnp.sum(jnp.where(names, probs.T[None, :, :], 0.0), axis=1)
    mine = jnp.where(jnp.any(names, axis=1), weight, -1.0)
    return lax.all_to_all(mine, "expert", split_axis=0, concat_axis=0, tiled=True)


def prepare_kernel(routes, probs, tokens, mine, low, high, names, shares, sems):
    half = low.shape[0]
    pairs = (
        (routes, names),
        (probs, shares),
        (tokens.at[pl.ds(0, half), :], low),
        (tokens.at[pl.ds(half, half), :], high),
    )
    copies = [pltpu.make_async_copy(*pair, sems.at[i]) for i, pair in enumerate(pairs)]
    for copy in copies:
        copy.start()
    for copy in copies[:2]:
        copy.wait()
    for e in range(mine.shape[0]):
        hit = (names[...] == e).astype(jnp.float32)
        named = jnp.sum(hit, axis=0, keepdims=True)
        share = jnp.sum(hit * shares[...], axis=0, keepdims=True)
        mine[pl.ds(e, 1), :] = jnp.where(named > 0.0, share, -1.0)
    for copy in copies[2:]:
        copy.wait()


def prepare_pass(routes, probs, tokens, experts):
    tok, top = routes.shape
    half = jax.ShapeDtypeStruct((tok // 2, tokens.shape[1]), tokens.dtype)
    vmem = pl.BlockSpec(memory_space=pltpu.VMEM)
    return pl.pallas_call(
        prepare_kernel,
        out_shape=(jax.ShapeDtypeStruct((experts, tok), jnp.float32), half, half),
        in_specs=[pl.BlockSpec(memory_space=pl.ANY)] * 3,
        out_specs=[vmem] * 3,
        scratch_shapes=[
            pltpu.VMEM((top, tok), routes.dtype),
            pltpu.VMEM((top, tok), probs.dtype),
            pltpu.SemaphoreType.DMA((4,)),
        ],
        compiler_params=pltpu.CompilerParams(vmem_limit_bytes=58 * 1024 * 1024),
    )(routes.T, probs.T, tokens)


def summed(*parts):
    total = parts[0].astype(jnp.float32)
    for part in parts[1:]:
        total = total + part.astype(jnp.float32)
    return total.astype(jnp.bfloat16)


def ranks_kernel(capacity, spots, weight, tables, ranks, chip_ranks):
    blocks, tok = weight.shape
    planes = blocks // 4
    named = (weight[...] >= 0.0).astype(jnp.float32)
    lane = lax.broadcasted_iota(jnp.int32, (tok, tok), 0)
    below = (lane < lax.broadcasted_iota(jnp.int32, (tok, tok), 1)).astype(jnp.float32)
    within = jnp.dot(named, below, preferred_element_type=jnp.float32)
    totals = jnp.broadcast_to(jnp.sum(named, axis=1, keepdims=True), (blocks, tok))
    row = lax.broadcasted_iota(jnp.int32, (blocks, blocks), 0)
    column = lax.broadcasted_iota(jnp.int32, (blocks, blocks), 1)
    earlier = (column < row).astype(jnp.float32)
    before = jnp.dot(earlier, totals, preferred_element_type=jnp.float32)
    rank = within + before
    kept = (named > 0.0) & (rank < capacity)
    first = (column < row // 4 * 4).astype(jnp.float32)
    start = jnp.dot(first, totals, preferred_element_type=jnp.float32)
    ranks[...] = jnp.where(kept, rank - start, -1.0)
    first = (column < row // 2 * 2).astype(jnp.float32)
    start = jnp.dot(first, totals, preferred_element_type=jnp.float32)
    chip_ranks[...] = jnp.where(kept, rank - start, -1.0)
    for i in range(4):
        span = pl.ds(i * tok, tok)
        tables[pl.ds(2 * planes, 1), span] = chip_ranks[pl.ds(spots[4 * planes - 4 + i], 1), :]
    for k in range(planes):
        for i in range(4):
            span = pl.ds(i * tok, tok)
            tables[pl.ds(k, 1), span] = ranks[pl.ds(spots[4 * k + i], 1), :]
            tables[pl.ds(planes + k, 1), span] = weight[pl.ds(spots[4 * k + i], 1), :]
    count = jnp.minimum(jnp.sum(totals[:, :1], axis=0, keepdims=True), float(capacity))
    rest = (tables.shape[0] - 2 * planes - 1, tables.shape[1])
    tables[2 * planes + 1 :, :] = jnp.broadcast_to(2.0 / count, rest)


def ranks_pass(capacity, spots, weight):
    blocks, tok = weight.shape
    vmem = pl.BlockSpec(memory_space=pltpu.VMEM)
    return pl.pallas_call(
        functools.partial(ranks_kernel, capacity),
        out_shape=jax.ShapeDtypeStruct((blocks // 4 * 2 + 8, 4 * tok), jnp.float32),
        in_specs=[pl.BlockSpec(memory_space=pltpu.SMEM), vmem],
        out_specs=vmem,
        scratch_shapes=[pltpu.VMEM(weight.shape, jnp.float32)] * 2,
        compiler_params=pltpu.CompilerParams(vmem_limit_bytes=4 * 1024 * 1024),
    )(spots, weight)


def plane_kernel(k, picked, gives, tables, *refs):
    *xs, w_gate, w_up, w_down, keep = refs[: -gives - 2]
    *gives, act, rows = refs[-gives - 2 :]
    slots, hidden = act.shape
    features = rows.shape[1]
    half, width = keep.shape[0], tables.shape[1]
    wide, cut = 256, 512
    place = tables[pl.ds(8 if picked else k, 1), :]
    share = tables[pl.ds(4 + k, 1), :]
    if picked:
        tok = width // 4
        place, share = (
            jnp.concatenate([row[:, i * tok : (i + 1) * tok] for i in picked], axis=1)
            for row in (place, share)
        )
        width = 2 * tok
    slot = lax.broadcasted_iota(jnp.int32, (slots, width), 0).astype(jnp.float32)
    hits = slot == place
    scale = jnp.sum(jnp.where(hits, share, 0.0), axis=1, keepdims=True)
    select = hits.astype(jnp.float32).astype(jnp.bfloat16)
    for i in range(features // cut):
        span = pl.ds(i * cut, cut)
        x = jnp.concatenate([block[:, span] for block in xs], axis=0)
        rows[:, span] = jnp.dot(select, x, preferred_element_type=jnp.float32).astype(jnp.bfloat16)
    for i in range(hidden // wide):
        span = pl.ds(i * wide, wide)
        gate = jnp.dot(rows[...], w_gate[:, span], preferred_element_type=jnp.float32)
        up = jnp.dot(rows[...], w_up[:, span], preferred_element_type=jnp.float32)
        act[:, span] = (gate / (1.0 + jnp.exp(-gate)) * up).astype(jnp.bfloat16)
    back = select.T
    for i in range(features // cut):
        span = pl.ds(i * cut, cut)
        result = jnp.dot(act[...], w_down[:, span], preferred_element_type=jnp.float32)
        made = (result * scale).astype(jnp.bfloat16)
        spread = jnp.dot(back, made, preferred_element_type=jnp.float32).astype(jnp.bfloat16)
        keep[:, span] = spread[:half]
        start = half
        for give in gives:
            give[:, span] = spread[start : start + give.shape[0]]
            start += give.shape[0]


def plane_pass(k, tables, xs, w_gate, w_up, w_down, slots, pieces=None, picked=None):
    tok, features = xs[0].shape
    hidden = w_gate.shape[1]
    blocks = 2 if picked else 4
    rows = blocks * slots
    half = blocks // 2 * tok
    pieces = pieces or (half,)
    outs = tuple(jax.ShapeDtypeStruct((some, features), jnp.bfloat16) for some in (half, *pieces))
    outs += (jax.ShapeDtypeStruct((rows, hidden), jnp.bfloat16),)
    vmem = pl.BlockSpec(memory_space=pltpu.VMEM)
    flops = 2 * rows * (3 * features * hidden + 2 * blocks * tok * features)
    moved = 2 * (3 * features * hidden + 2 * blocks * tok * features)
    return pl.pallas_call(
        functools.partial(plane_kernel, k, picked, len(pieces)),
        out_shape=outs,
        in_specs=[vmem] * (len(xs) + 4),
        out_specs=[vmem] * len(outs),
        scratch_shapes=[pltpu.VMEM((rows, features), jnp.bfloat16)],
        compiler_params=pltpu.CompilerParams(vmem_limit_bytes=12 * 1024 * 1024),
        cost_estimate=pl.CostEstimate(
            flops=flops, bytes_accessed=moved, transcendentals=rows * hidden
        ),
    )(tables, *xs, w_gate, w_up, w_down)


def gram_kernel(tables, *refs):
    *acts, gram = refs
    wide = 256
    scale = tables[9:10, :1]
    rows = jnp.concatenate([act[...] for act in acts], axis=0)
    for i in range(gram.shape[0] // wide):
        some = rows[:, i * wide : (i + 1) * wide]
        gram[pl.ds(i * wide, wide), :] = gram_of_two(some, rows) * scale


def gram_of_two(left, right):
    return lax.dot_general(left, right, (((0,), (0,)), ((), ())), preferred_element_type=jnp.float32)


def gram_pass(tables, *acts):
    hidden = acts[0].shape[1]
    rows = sum(act.shape[0] for act in acts)
    vmem = pl.BlockSpec(memory_space=pltpu.VMEM)
    return pl.pallas_call(
        gram_kernel,
        out_shape=jax.ShapeDtypeStruct((hidden, hidden), jnp.float32),
        in_specs=[vmem] * (len(acts) + 1),
        out_specs=vmem,
        compiler_params=pltpu.CompilerParams(vmem_limit_bytes=16 * 1024 * 1024),
        cost_estimate=pl.CostEstimate(
            flops=2 * rows * hidden * hidden,
            bytes_accessed=4 * hidden * hidden + 2 * rows * hidden,
            transcendentals=0,
        ),
    )(tables, *acts)


def mix_kernel(far_low, far_high, near_high, near_low, side, keep, got, mixed):
    most, tok = near_low.shape[0], mixed.shape[0]
    for start, stop, near, far in (
        (0, most, near_low, far_low),
        (most, tok, near_high, far_high),
    ):
        total = keep[start:stop, :].astype(jnp.float32) + got[start:stop, :].astype(jnp.float32)
        total = total + side[start:stop, :].astype(jnp.float32) + near[...].astype(jnp.float32)
        mixed[start:stop, :] = (total + far[...].astype(jnp.float32)).astype(mixed.dtype)


def mix_pass(*parts):
    side = parts[4]
    vmem = pl.BlockSpec(memory_space=pltpu.VMEM)
    return pl.pallas_call(
        mix_kernel,
        out_shape=jax.ShapeDtypeStruct(side.shape, side.dtype),
        in_specs=[vmem] * len(parts),
        out_specs=vmem,
        compiler_params=pltpu.CompilerParams(vmem_limit_bytes=12 * 1024 * 1024),
    )(*parts)


def staged(routes, probs, tokens, w_gate, w_up, w_down):
    tok, top = routes.shape
    size = lax.axis_size("expert")
    slots = 5 * tok * top // (4 * size)
    capacity = tok * top // 2
    half = tok // 2
    me = lax.axis_index("expert")
    z, y, core = me // 4, me // 2 % 2, me % 2

    def swapped(array, bit):
        return lax.ppermute(array, "expert", [(i, i ^ bit) for i in range(size)])

    sibling = functools.partial(swapped, bit=1)
    column = functools.partial(swapped, bit=2)
    pair = functools.partial(swapped, bit=4)
    far = functools.partial(swapped, bit=8)

    def together(*arrays):
        return lax.optimization_barrier(arrays)

    spots = jnp.stack(
        [
            (z ^ k) * 4 + (y ^ column_bit) * 2 + (core ^ core_bit)
            for k in range(4)
            for core_bit in range(2)
            for column_bit in range(2)
        ]
    ).astype(jnp.int32)

    def expert(k, *xs, pieces=None, picked=None):
        return plane_pass(k, tables, xs, w_gate, w_up, w_down, slots, pieces, picked)

    mine, a0_low, a0_high = prepare_pass(routes, probs, tokens, size)
    a0 = tokens
    a1, low, b0, c0, weight, a0_high = together(
        pair(a0),
        far(a0_low),
        column(a0),
        sibling(a0),
        lax.all_to_all(mine, "expert", split_axis=0, concat_axis=0, tiled=True),
        a0_high,
    )
    tables = ranks_pass(capacity, spots, weight)
    high = far(a0_high)
    b1 = column(a1)
    d0 = sibling(b0)
    c1 = sibling(a1)
    keep0, give0, act0 = expert(0, a0, b0, c0, d0)
    high, b1, c1, keep0, give0, act0, tables = together(
        high, b1, c1, keep0, give0, act0, tables
    )
    a2 = jnp.concatenate([low, high], axis=0)
    a3 = pair(a2)
    b2 = column(a2)
    d1 = sibling(b1)
    c2 = sibling(a2)
    keep1, give1, give1_side, act1 = expert(1, a1, b1, c1, d1, pieces=(tok, tok))
    got1_side = sibling(give1_side)
    a3, b2, c2, keep1, give1, act1, got1_side = together(
        a3, b2, c2, keep1, give1, act1, got1_side
    )
    b3 = pair(b2)
    came1_low = column(summed(keep1[tok : tok + half], got1_side[:half]))
    got1 = sibling(give1)
    d2 = sibling(b2)
    c3 = sibling(a3)
    keep2, give2, give2_low, give2_high, act2 = expert(
        2, a2, b2, c2, d2, pieces=(tok, half, half)
    )
    got2_high = sibling(give2_high)
    keep3, give3, act3 = expert(3, a3, c3, picked=(0, 2))
    b3, came1_low, got1, got2_high, keep2, give2, give2_low, act2, keep3, give3, act3 = (
        together(
            b3, came1_low, got1, got2_high, keep2, give2, give2_low, act2, keep3, give3, act3
        )
    )
    d3 = sibling(b3)
    near1 = summed(keep1[:half], got1[:half], came1_low)

    side_high = column(summed(keep2[tok + half :], got2_high))
    got2 = sibling(give2)
    keep3_side, give3_side, act4 = expert(3, b3, d3, picked=(1, 3))
    keep3_side, give3_side, act4, got2, side_high, near1 = together(
        keep3_side, give3_side, act4, got2, side_high, near1
    )
    got2_low, got3 = sibling(give2_low), sibling(give3)
    far2_high = far(summed(keep2[half:tok], got2[half:], side_high))
    got3_side = sibling(give3_side)
    came3_low = column(summed(keep3_side[:half], got3_side[:half]))
    came3_high = column(summed(keep3_side[half:], got3_side[half:]))
    near1_low = pair(near1)
    got0 = sibling(give0)
    side1 = summed(keep1[tok + half :], got1_side[half:])
    came3_low, came3_high, far2_high, near1_low, got0, side1, got2_low, got3 = together(
        came3_low, came3_high, far2_high, near1_low, got0, side1, got2_low, got3
    )
    far3_high = far(summed(keep3[half:], got3[half:], came3_high))
    pair3_low = pair(summed(keep3[:half], got3[:half], came3_low))
    side_low = column(summed(keep2[tok : tok + half], got2_low))
    came1_high = column(side1)
    side0 = summed(keep0[tok:], got0[tok:])
    gram = gram_pass(tables, act0, act1, act2, act3, act4)
    far3_high, pair3_low, side_low, came1_high, side0, gram = together(
        far3_high, pair3_low, side_low, came1_high, side0, gram
    )
    far2_low = summed(keep2[:half], got2[:half], pair3_low, side_low)
    far2_low, far3_high, came1_high, side0 = together(far2_low, far3_high, came1_high, side0)
    far2_low = far(far2_low)
    near1_high = pair(summed(keep1[half:tok], got1[half:], came1_high, far3_high))
    last0 = column(side0)
    mixed = mix_pass(
        far2_low, far2_high, near1_high, near1_low, last0, keep0, got0
    )

    return gram[None], mixed


def gathered(routes, probs, tokens, w_gate, w_up, w_down):
    tok_rows, top = routes.shape
    size = lax.axis_size("expert")
    capacity = tok_rows * top // 2
    every_token = lax.all_gather(tokens, "expert", tiled=True)
    weight = weights_for_me(routes, probs, size)
    named = (weight >= 0.0).astype(jnp.int32)
    within = jnp.cumsum(named, axis=1) - named
    per_device = jnp.sum(named, axis=1)
    before = jnp.cumsum(per_device) - per_device
    rank = within + before[:, None]
    kept = (named == 1) & (rank < capacity)
    count = jnp.minimum(jnp.sum(per_device), capacity)
    slot = jnp.where(kept, rank, -1).reshape(size * tok_rows)
    place = jnp.arange(capacity, dtype=jnp.int32)
    select = (place[:, None] == slot[None, :]).astype(jnp.bfloat16)
    rows = jnp.dot(select, every_token, preferred_element_type=jnp.float32).astype(jnp.bfloat16)
    gram_sum, made = expert_pass(rows, w_gate, w_up, w_down)
    gram = gram_sum * (2.0 / count.astype(jnp.float32))
    spread = lax.dot_general(
        select, made, (((0,), (0,)), ((), ())), preferred_element_type=jnp.float32
    )
    partial = (spread * weight.reshape(size * tok_rows, 1)).astype(jnp.bfloat16)
    mixed = lax.psum_scatter(partial, "expert", scatter_dimension=0, tiled=True)
    return gram[None], mixed.astype(jnp.bfloat16)


def shards(routes, probs, tokens, gate_weight, up_weight, down_weight):
    body = staged if lax.axis_size("expert") == 16 else gathered
    return body(routes, probs, tokens, gate_weight[0], up_weight[0], down_weight[0])


def solution(mesh):
    placed = (
        P(("parts", "expert"), None),
        P(("parts", "expert"), None),
        P(("parts", "expert"), None),
        P("expert", None, None),
        P("expert", None, None),
        P("expert", None, None),
    )
    return jax.shard_map(
        shards,
        mesh=mesh,
        in_specs=placed,
        out_specs=(P(("parts", "expert"), None, None), P(("parts", "expert"), None)),
        check_vma=False,
    )
```

```python
import functools

import jax
import jax.numpy as jnp
from jax import lax
from jax.experimental import pallas as pl
from jax.experimental.pallas import tpu as pltpu
from jax.sharding import PartitionSpec as P


def gram_of(rows):
    return lax.dot_general(rows, rows, (((0,), (0,)), ((), ())), preferred_element_type=jnp.float32)


def expert_pass(rows, w_gate, w_up, w_down):
    gate = jnp.dot(rows, w_gate, preferred_element_type=jnp.float32)
    up = jnp.dot(rows, w_up, preferred_element_type=jnp.float32)
    act = (jax.nn.silu(gate) * up).astype(jnp.bfloat16)
    gram_sum = gram_of(act)
    made = jnp.dot(act, w_down, preferred_element_type=jnp.float32).astype(jnp.bfloat16)
    return (gram_sum, made)


def weights_for_me(routes, probs, experts):
    names = routes.T[None, :, :] == jnp.arange(experts, dtype=jnp.int32)[:, None, None]
    weight = jnp.sum(jnp.where(names, probs.T[None, :, :], 0.0), axis=1)
    mine = jnp.where(jnp.any(names, axis=1), weight, -1.0)
    return lax.all_to_all(mine, "expert", split_axis=0, concat_axis=0, tiled=True)


def prepare_kernel(routes, probs, tokens, mine, low, high, names, shares, sems):
    half = low.shape[0]
    pairs = (
        (routes, names),
        (probs, shares),
        (tokens.at[pl.ds(0, half), :], low),
        (tokens.at[pl.ds(half, half), :], high),
    )
    copies = [pltpu.make_async_copy(*pair, sems.at[i]) for i, pair in enumerate(pairs)]
    for copy in copies:
        copy.start()
    for copy in copies[:2]:
        copy.wait()
    for e in range(mine.shape[0]):
        hit = (names[...] == e).astype(jnp.float32)
        named = jnp.sum(hit, axis=0, keepdims=True)
        share = jnp.sum(hit * shares[...], axis=0, keepdims=True)
        mine[pl.ds(e, 1), :] = jnp.where(named > 0.0, share, -1.0)
    for copy in copies[2:]:
        copy.wait()


def prepare_pass(routes, probs, tokens, experts):
    tok, top = routes.shape
    half = jax.ShapeDtypeStruct((tok // 2, tokens.shape[1]), tokens.dtype)
    vmem = pl.BlockSpec(memory_space=pltpu.VMEM)
    return pl.pallas_call(
        prepare_kernel,
        out_shape=(jax.ShapeDtypeStruct((experts, tok), jnp.float32), half, half),
        in_specs=[pl.BlockSpec(memory_space=pl.ANY)] * 3,
        out_specs=[vmem] * 3,
        scratch_shapes=[
            pltpu.VMEM((top, tok), routes.dtype),
            pltpu.VMEM((top, tok), probs.dtype),
            pltpu.SemaphoreType.DMA((4,)),
        ],
        compiler_params=pltpu.CompilerParams(vmem_limit_bytes=58 * 1024 * 1024),
    )(routes.T, probs.T, tokens)


def summed(*parts):
    total = parts[0].astype(jnp.float32)
    for part in parts[1:]:
        total = total + part.astype(jnp.float32)
    return total.astype(jnp.bfloat16)


def ranks_kernel(capacity, spots, weight, tables, ranks, chip_ranks):
    blocks, tok = weight.shape
    planes = blocks // 4
    named = (weight[...] >= 0.0).astype(jnp.float32)
    lane = lax.broadcasted_iota(jnp.int32, (tok, tok), 0)
    below = (lane < lax.broadcasted_iota(jnp.int32, (tok, tok), 1)).astype(jnp.float32)
    within = jnp.dot(named, below, preferred_element_type=jnp.float32)
    totals = jnp.broadcast_to(jnp.sum(named, axis=1, keepdims=True), (blocks, tok))
    row = lax.broadcasted_iota(jnp.int32, (blocks, blocks), 0)
    column = lax.broadcasted_iota(jnp.int32, (blocks, blocks), 1)
    earlier = (column < row).astype(jnp.float32)
    before = jnp.dot(earlier, totals, preferred_element_type=jnp.float32)
    rank = within + before
    kept = (named > 0.0) & (rank < capacity)
    first = (column < row // 4 * 4).astype(jnp.float32)
    start = jnp.dot(first, totals, preferred_element_type=jnp.float32)
    ranks[...] = jnp.where(kept, rank - start, -1.0)
    first = (column < row // 2 * 2).astype(jnp.float32)
    start = jnp.dot(first, totals, preferred_element_type=jnp.float32)
    chip_ranks[...] = jnp.where(kept, rank - start, -1.0)
    for i in range(4):
        span = pl.ds(i * tok, tok)
        tables[pl.ds(2 * planes, 1), span] = chip_ranks[pl.ds(spots[4 * planes - 4 + i], 1), :]
    for k in range(planes):
        for i in range(4):
            span = pl.ds(i * tok, tok)
            tables[pl.ds(k, 1), span] = ranks[pl.ds(spots[4 * k + i], 1), :]
            tables[pl.ds(planes + k, 1), span] = weight[pl.ds(spots[4 * k + i], 1), :]
    count = jnp.minimum(jnp.sum(totals[:, :1], axis=0, keepdims=True), float(capacity))
    rest = (tables.shape[0] - 2 * planes - 1, tables.shape[1])
    tables[2 * planes + 1 :, :] = jnp.broadcast_to(2.0 / count, rest)


def ranks_pass(capacity, spots, weight):
    blocks, tok = weight.shape
    vmem = pl.BlockSpec(memory_space=pltpu.VMEM)
    return pl.pallas_call(
        functools.partial(ranks_kernel, capacity),
        out_shape=jax.ShapeDtypeStruct((blocks // 4 * 2 + 8, 4 * tok), jnp.float32),
        in_specs=[pl.BlockSpec(memory_space=pltpu.SMEM), vmem],
        out_specs=vmem,
        scratch_shapes=[pltpu.VMEM(weight.shape, jnp.float32)] * 2,
        compiler_params=pltpu.CompilerParams(vmem_limit_bytes=4 * 1024 * 1024),
    )(spots, weight)


def plane_kernel(k, picked, gives, tables, *refs):
    *xs, w_gate, w_up, w_down, keep = refs[: -gives - 2]
    *gives, act, rows = refs[-gives - 2 :]
    slots, hidden = act.shape
    features = rows.shape[1]
    half, width = keep.shape[0], tables.shape[1]
    wide, cut = 256, 512
    place = tables[pl.ds(8 if picked else k, 1), :]
    share = tables[pl.ds(4 + k, 1), :]
    if picked:
        tok = width // 4
        place, share = (
            jnp.concatenate([row[:, i * tok : (i + 1) * tok] for i in picked], axis=1)
            for row in (place, share)
        )
        width = 2 * tok
    slot = lax.broadcasted_iota(jnp.int32, (slots, width), 0).astype(jnp.float32)
    hits = slot == place
    scale = jnp.sum(jnp.where(hits, share, 0.0), axis=1, keepdims=True)
    select = hits.astype(jnp.float32).astype(jnp.bfloat16)
    for i in range(features // cut):
        span = pl.ds(i * cut, cut)
        x = jnp.concatenate([block[:, span] for block in xs], axis=0)
        rows[:, span] = jnp.dot(select, x, preferred_element_type=jnp.float32).astype(jnp.bfloat16)
    for i in range(hidden // wide):
        span = pl.ds(i * wide, wide)
        gate = jnp.dot(rows[...], w_gate[:, span], preferred_element_type=jnp.float32)
        up = jnp.dot(rows[...], w_up[:, span], preferred_element_type=jnp.float32)
        act[:, span] = (gate / (1.0 + jnp.exp(-gate)) * up).astype(jnp.bfloat16)
    back = select.T
    for i in range(features // cut):
        span = pl.ds(i * cut, cut)
        result = jnp.dot(act[...], w_down[:, span], preferred_element_type=jnp.float32)
        made = (result * scale).astype(jnp.bfloat16)
        spread = jnp.dot(back, made, preferred_element_type=jnp.float32).astype(jnp.bfloat16)
        keep[:, span] = spread[:half]
        start = half
        for give in gives:
            give[:, span] = spread[start : start + give.shape[0]]
            start += give.shape[0]


def plane_pass(k, tables, xs, w_gate, w_up, w_down, slots, pieces=None, picked=None):
    tok, features = xs[0].shape
    hidden = w_gate.shape[1]
    blocks = 2 if picked else 4
    rows = blocks * slots
    half = blocks // 2 * tok
    pieces = pieces or (half,)
    outs = tuple(jax.ShapeDtypeStruct((some, features), jnp.bfloat16) for some in (half, *pieces))
    outs += (jax.ShapeDtypeStruct((rows, hidden), jnp.bfloat16),)
    vmem = pl.BlockSpec(memory_space=pltpu.VMEM)
    flops = 2 * rows * (3 * features * hidden + 2 * blocks * tok * features)
    moved = 2 * (3 * features * hidden + 2 * blocks * tok * features)
    return pl.pallas_call(
        functools.partial(plane_kernel, k, picked, len(pieces)),
        out_shape=outs,
        in_specs=[vmem] * (len(xs) + 4),
        out_specs=[vmem] * len(outs),
        scratch_shapes=[pltpu.VMEM((rows, features), jnp.bfloat16)],
        compiler_params=pltpu.CompilerParams(vmem_limit_bytes=12 * 1024 * 1024),
        cost_estimate=pl.CostEstimate(
            flops=flops, bytes_accessed=moved, transcendentals=rows * hidden
        ),
    )(tables, *xs, w_gate, w_up, w_down)


def gram_kernel(tables, *refs):
    *acts, gram = refs
    wide = 256
    scale = tables[9:10, :1]
    rows = jnp.concatenate([act[...] for act in acts], axis=0)
    for i in range(gram.shape[0] // wide):
        some = rows[:, i * wide : (i + 1) * wide]
        gram[pl.ds(i * wide, wide), :] = gram_of_two(some, rows) * scale


def gram_of_two(left, right):
    return lax.dot_general(left, right, (((0,), (0,)), ((), ())), preferred_element_type=jnp.float32)


def gram_pass(tables, *acts):
    hidden = acts[0].shape[1]
    rows = sum(act.shape[0] for act in acts)
    vmem = pl.BlockSpec(memory_space=pltpu.VMEM)
    return pl.pallas_call(
        gram_kernel,
        out_shape=jax.ShapeDtypeStruct((hidden, hidden), jnp.float32),
        in_specs=[vmem] * (len(acts) + 1),
        out_specs=vmem,
        compiler_params=pltpu.CompilerParams(vmem_limit_bytes=16 * 1024 * 1024),
        cost_estimate=pl.CostEstimate(
            flops=2 * rows * hidden * hidden,
            bytes_accessed=4 * hidden * hidden + 2 * rows * hidden,
            transcendentals=0,
        ),
    )(tables, *acts)


def mix_kernel(far_low, far_high, near_high, near_low, side, keep, got, mixed):
    most, tok = near_low.shape[0], mixed.shape[0]
    for start, stop, near, far in (
        (0, most, near_low, far_low),
        (most, tok, near_high, far_high),
    ):
        total = keep[start:stop, :].astype(jnp.float32) + got[start:stop, :].astype(jnp.float32)
        total = total + side[start:stop, :].astype(jnp.float32) + near[...].astype(jnp.float32)
        mixed[start:stop, :] = (total + far[...].astype(jnp.float32)).astype(mixed.dtype)


def mix_pass(*parts):
    side = parts[4]
    vmem = pl.BlockSpec(memory_space=pltpu.VMEM)
    return pl.pallas_call(
        mix_kernel,
        out_shape=jax.ShapeDtypeStruct(side.shape, side.dtype),
        in_specs=[vmem] * len(parts),
        out_specs=vmem,
        compiler_params=pltpu.CompilerParams(vmem_limit_bytes=12 * 1024 * 1024),
    )(*parts)


def staged(routes, probs, tokens, w_gate, w_up, w_down):
    tok, top = routes.shape
    size = lax.axis_size("expert")
    slots = 5 * tok * top // (4 * size)
    capacity = tok * top // 2
    half = tok // 2
    me = lax.axis_index("expert")
    z, y, core = me // 4, me // 2 % 2, me % 2

    def swapped(array, bit):
        return lax.ppermute(array, "expert", [(i, i ^ bit) for i in range(size)])

    sibling = functools.partial(swapped, bit=1)
    column = functools.partial(swapped, bit=2)
    pair = functools.partial(swapped, bit=4)
    far = functools.partial(swapped, bit=8)

    def together(*arrays):
        return lax.optimization_barrier(arrays)

    spots = jnp.stack(
        [
            (z ^ k) * 4 + (y ^ column_bit) * 2 + (core ^ core_bit)
            for k in range(4)
            for core_bit in range(2)
            for column_bit in range(2)
        ]
    ).astype(jnp.int32)

    def expert(k, *xs, pieces=None, picked=None):
        return plane_pass(k, tables, xs, w_gate, w_up, w_down, slots, pieces, picked)

    mine, a0_low, a0_high = prepare_pass(routes, probs, tokens, size)
    a0 = tokens
    a1, low, b0, c0, weight, a0_high = together(
        pair(a0),
        far(a0_low),
        column(a0),
        sibling(a0),
        lax.all_to_all(mine, "expert", split_axis=0, concat_axis=0, tiled=True),
        a0_high,
    )
    tables = ranks_pass(capacity, spots, weight)
    high = far(a0_high)
    b1 = column(a1)
    d0 = sibling(b0)
    c1 = sibling(a1)
    keep0, give0, act0 = expert(0, a0, b0, c0, d0)
    high, b1, c1, keep0, give0, act0, tables = together(
        high, b1, c1, keep0, give0, act0, tables
    )
    a2 = jnp.concatenate([low, high], axis=0)
    a3 = pair(a2)
    b2 = column(a2)
    d1 = sibling(b1)
    c2 = sibling(a2)
    keep1, give1, give1_side, act1 = expert(1, a1, b1, c1, d1, pieces=(tok, tok))
    got1_side = sibling(give1_side)
    a3, b2, c2, keep1, give1, act1, got1_side = together(
        a3, b2, c2, keep1, give1, act1, got1_side
    )
    b3 = pair(b2)
    came1_low = column(summed(keep1[tok : tok + half], got1_side[:half]))
    got1 = sibling(give1)
    d2 = sibling(b2)
    c3 = sibling(a3)
    keep2, give2, give2_low, give2_high, act2 = expert(
        2, a2, b2, c2, d2, pieces=(tok, half, half)
    )
    got2_high = sibling(give2_high)
    keep3, give3, act3 = expert(3, a3, c3, picked=(0, 2))
    got0 = sibling(give0)
    b3, came1_low, got0, got1, got2_high, keep2, give2, give2_low, act2, keep3, give3, act3 = (
        together(
            b3, came1_low, got0, got1, got2_high, keep2, give2, give2_low, act2, keep3, give3, act3
        )
    )
    d3 = sibling(b3)
    near1 = summed(keep1[:half], got1[:half], came1_low)

    side_high = column(summed(keep2[tok + half :], got2_high))
    got2 = sibling(give2)
    keep3_side, give3_side, act4 = expert(3, b3, d3, picked=(1, 3))
    side_high, keep3_side, give3_side, act4, got2, near1 = together(
        side_high, keep3_side, give3_side, act4, got2, near1
    )
    got2_low, got3 = sibling(give2_low), sibling(give3)
    far2_high = far(summed(keep2[half:tok], got2[half:], side_high))
    got3_side = sibling(give3_side)
    came3_low = column(summed(keep3_side[:half], got3_side[:half]))
    came3_high = column(summed(keep3_side[half:], got3_side[half:]))
    near1_low = pair(near1)
    side0 = summed(keep0[tok:], got0[tok:])
    side1 = summed(keep1[tok + half :], got1_side[half:])
    came3_low, came3_high, far2_high, near1_low, side0, side1, got2_low, got3 = together(
        came3_low, came3_high, far2_high, near1_low, side0, side1, got2_low, got3
    )
    far3_high = far(summed(keep3[half:], got3[half:], came3_high))
    pair3_low = pair(summed(keep3[:half], got3[:half], came3_low))
    side_low = column(summed(keep2[tok : tok + half], got2_low))
    came1_high = column(side1)
    gram = gram_pass(tables, act0, act1, act2, act3, act4)
    far3_high, pair3_low, side_low, came1_high, side0, gram = together(
        far3_high, pair3_low, side_low, came1_high, side0, gram
    )
    far2_low = summed(keep2[:half], got2[:half], pair3_low, side_low)
    far2_low, far3_high, came1_high, side0 = together(far2_low, far3_high, came1_high, side0)
    far2_low = far(far2_low)
    near1_high = pair(summed(keep1[half:tok], got1[half:], came1_high, far3_high))
    last0 = column(side0)
    mixed = mix_pass(
        far2_low, far2_high, near1_high, near1_low, last0, keep0, got0
    )

    return gram[None], mixed


def gathered(routes, probs, tokens, w_gate, w_up, w_down):
    tok_rows, top = routes.shape
    size = lax.axis_size("expert")
    capacity = tok_rows * top // 2
    every_token = lax.all_gather(tokens, "expert", tiled=True)
    weight = weights_for_me(routes, probs, size)
    named = (weight >= 0.0).astype(jnp.int32)
    within = jnp.cumsum(named, axis=1) - named
    per_device = jnp.sum(named, axis=1)
    before = jnp.cumsum(per_device) - per_device
    rank = within + before[:, None]
    kept = (named == 1) & (rank < capacity)
    count = jnp.minimum(jnp.sum(per_device), capacity)
    slot = jnp.where(kept, rank, -1).reshape(size * tok_rows)
    place = jnp.arange(capacity, dtype=jnp.int32)
    select = (place[:, None] == slot[None, :]).astype(jnp.bfloat16)
    rows = jnp.dot(select, every_token, preferred_element_type=jnp.float32).astype(jnp.bfloat16)
    gram_sum, made = expert_pass(rows, w_gate, w_up, w_down)
    gram = gram_sum * (2.0 / count.astype(jnp.float32))
    spread = lax.dot_general(
        select, made, (((0,), (0,)), ((), ())), preferred_element_type=jnp.float32
    )
    partial = (spread * weight.reshape(size * tok_rows, 1)).astype(jnp.bfloat16)
    mixed = lax.psum_scatter(partial, "expert", scatter_dimension=0, tiled=True)
    return gram[None], mixed.astype(jnp.bfloat16)


def shards(routes, probs, tokens, gate_weight, up_weight, down_weight):
    body = staged if lax.axis_size("expert") == 16 else gathered
    return body(routes, probs, tokens, gate_weight[0], up_weight[0], down_weight[0])


def solution(mesh):
    placed = (
        P(("parts", "expert"), None),
        P(("parts", "expert"), None),
        P(("parts", "expert"), None),
        P("expert", None, None),
        P("expert", None, None),
        P("expert", None, None),
    )
    return jax.shard_map(
        shards,
        mesh=mesh,
        in_specs=placed,
        out_specs=(P(("parts", "expert"), None, None), P(("parts", "expert"), None)),
        check_vma=False,
    )
```
